32 devices in a mesh: dp: 8 (over y, x, core), seq: 4 (over z).
Axes of the slice: x: 2, y: 2, z: 4, core: 2. Of those that a mesh axis runs over, the one named last changes fastest.
Arguments:
- tokens: bfloat16 [2, 8, 1024, 512], P(None, 'dp', 'seq'), may hold values from -6 to 6
- memory: bfloat16 [2, 8, 1024, 512], P(None, 'dp', 'seq'), may hold values from -6 to 6
- target_segments: int32 [2, 8, 1024], P(None, 'dp', 'seq'), may hold values from 0 to 7, never falling along the last dimension, each value on 1 to 512 neighbouring positions
- source_segments: int32 [2, 8, 1024], P(None, 'dp', 'seq'), may hold values from 0 to 7, never falling along the last dimension, each value on 1 to 512 neighbouring positions
- cotangent: bfloat16 [2, 8, 1024, 512], P(None, 'dp', 'seq'), may hold values from -6 to 6
- query_weight: bfloat16 [512, 512], P('dp'), may hold values from -0.25 to 0.25
- key_weight: bfloat16 [512, 512], P('dp'), may hold values from -0.25 to 0.25
- value_weight: bfloat16 [512, 512], P('dp'), may hold values from -0.25 to 0.25
- output_weight: bfloat16 [512, 512], P('dp'), may hold values from -2 to 2
- cross_query: bfloat16 [512, 512], P('dp'), may hold values from -0.25 to 0.25
- cross_key: bfloat16 [512, 512], P('dp'), may hold values from -0.25 to 0.25
- cross_value: bfloat16 [512, 512], P('dp'), may hold values from -0.25 to 0.25
- cross_output: bfloat16 [512, 512], P('dp'), may hold values from -2 to 2
- inner_weight: bfloat16 [512, 2048], P('dp'), may hold values from -0.25 to 0.25
- outer_weight: bfloat16 [2048, 512], P('dp'), may hold values from -0.125 to 0.125
- self_gain: bfloat16 [512], P('dp'), may hold values from 0.25 to 1.75
- self_shift: bfloat16 [512], P('dp'), may hold values from -2 to 2
- cross_gain: bfloat16 [512], P('dp'), may hold values from 0.25 to 1.75
- cross_shift: bfloat16 [512], P('dp'), may hold values from -2 to 2
- feed_gain: bfloat16 [512], P('dp'), may hold values from 0.25 to 1.75
- feed_shift: bfloat16 [512], P('dp'), may hold values from -2 to 2
Outputs:
- out_tokens: bfloat16 [2, 8, 1024, 512], P(None, 'dp', 'seq')
- grad_tokens: float32 [2, 8, 1024, 512], P(None, 'dp', 'seq')
- grad_memory: float32 [2, 8, 1024, 512], P(None, 'dp', 'seq')
- grad_query: float32 [512, 512], P('dp')
- grad_key: float32 [512, 512], P('dp')
- grad_value: float32 [512, 512], P('dp')
- grad_output: float32 [512, 512], P('dp')
- grad_cross_query: float32 [512, 512], P('dp')
- grad_cross_key: float32 [512, 512], P('dp')
- grad_cross_value: float32 [512, 512], P('dp')
- grad_cross_output: float32 [512, 512], P('dp')
- grad_inner: float32 [512, 2048], P('dp')
- grad_outer: float32 [2048, 512], P('dp')
- grad_self_gain: float32 [512], P('dp')
- grad_self_shift: float32 [512], P('dp')
- grad_cross_gain: float32 [512], P('dp')
- grad_cross_shift: float32 [512], P('dp')
- grad_feed_gain: float32 [512], P('dp')
- grad_feed_shift: float32 [512], P('dp')
The draws below stay inside these ranges and needn't reach their ends.
Inputs may be any that keep to these rules, and one draw needn't show every extreme that they name: `target_segments`: each sequence's document ids never fall, and every one of the 8 ids has at least one position; the longest target document has exactly 512 positions. `source_segments`: each sequence's document ids never fall, and every one of the 8 ids has at least one position; the longest source document has exactly 512 positions.
All inputs are finite; a program needn't handle non-finite values.
Results may differ from the reference program's by a relative error of at most 0.028.
Values may be sent and summed in bfloat16 or wider, within the bound.
No kernel may reach another device: no remote copies, remote signals or barrier semaphores. Data moves between devices by JAX's collectives and lax.ppermute only.
A program may use at most 128 MiB of HBM per device.

```python
import math
import jax
import jax.numpy as jnp
import numpy as np
from jax import lax

D = 512
H = 8
DH = 64
FF = 2048
MB = 2
DOCS = 8
LEN = 1024
SRC = 1024
SEQS = 8
MOST_T = 512
MOST_S = 512


def block_scale(own_key, extent, split, low, high):
    level = 1.0
    for position, shards_of in split:
        heights = jax.random.uniform(jax.random.fold_in(jax.random.fold_in(own_key, 6), position), (shards_of,), jnp.float32, low / len(split), high / len(split))
        level = level * jnp.repeat(jnp.exp(heights), extent[position] // shards_of).reshape((-1,) + (1,) * (len(extent) - 1 - position))
    return level


def profile(amount, total, most, skew):
    weights = [(1 << 20) // math.isqrt(standing ** skew) + 1 for standing in range(2, amount + 1)]
    rest, given = total - most - (amount - 1), [1] * (amount - 1)
    while rest > 0:
        free = [i for i in range(amount - 1) if given[i] < most]
        mass, left = sum([weights[i] for i in free]), rest
        for i in free:
            addition = min(most - given[i], max(1, left * weights[i] // mass), rest)
            given[i] = given[i] + addition
            rest = rest - addition
    return np.array([most] + given)


def uneven_parts(rng, amount, total, bound, lean):
    if amount == 2:
        one = jax.random.randint(rng, (), max(1, total - bound), min(bound, total - 1) + 1)
        return jnp.stack([one, total - one])
    tallies = jnp.asarray(profile(amount, total, bound, lean), jnp.int32)
    twos = (amount - 1) // 2
    donor, receiver = tallies[1:1 + 2 * twos:2], tallies[2:2 + 2 * twos:2]
    slack = jnp.minimum(donor - 1, bound - receiver)
    passed = jax.random.randint(jax.random.fold_in(rng, 1), (twos,), 0, 1 << 20) % (slack + 1)
    tallies = tallies.at[1:1 + 2 * twos:2].set(donor - passed).at[2:2 + 2 * twos:2].set(receiver + passed)
    return tallies[jax.random.permutation(jax.random.fold_in(rng, 2), amount)]


def gaussian(rng, shape, width, bound, shards=(), kind=jnp.bfloat16):
    drawn = width * jax.random.normal(rng, shape, jnp.float32)
    if shards:
        drawn = drawn * block_scale(rng, shape, shards, -0.22, 0.18)
    return jnp.clip(drawn, -bound, bound).astype(kind)


def setup_inputs(seed: int = 0) -> dict:
    streams_of = jax.random.split(jax.random.key(seed), 22)
    tokens = gaussian(streams_of[0], (MB, SEQS, LEN, D), 1.0, 6.0, ((1, 8), (2, 4)))
    memory = gaussian(streams_of[1], (MB, SEQS, SRC, D), 1.0, 6.0, ((1, 8), (2, 4)))
    target_segments = jax.vmap(lambda own: jnp.searchsorted(jnp.cumsum(uneven_parts(own, DOCS, LEN, MOST_T, 2)), jnp.arange(LEN), side="right"))(jax.random.split(streams_of[2], MB * SEQS)).reshape((MB, SEQS, LEN)).astype(jnp.int32)
    source_segments = jax.vmap(lambda own: jnp.searchsorted(jnp.cumsum(uneven_parts(own, DOCS, SRC, MOST_S, 2)), jnp.arange(SRC), side="right"))(jax.random.split(streams_of[3], MB * SEQS)).reshape((MB, SEQS, SRC)).astype(jnp.int32)
    cotangent = gaussian(streams_of[4], (MB, SEQS, LEN, D), 1.0, 6.0, ((1, 8), (2, 4)))
    query_weight = gaussian(streams_of[5], (D, D), D ** -0.5, 0.25, ((0, 8),))
    key_weight = gaussian(streams_of[6], (D, D), D ** -0.5, 0.25, ((0, 8),))
    value_weight = gaussian(streams_of[7], (D, D), D ** -0.5, 0.25, ((0, 8),))
    output_weight = gaussian(streams_of[8], (D, D), (max(D // 64, 8)) ** -0.5, 2.0, ((0, 8),))
    cross_query = gaussian(streams_of[9], (D, D), D ** -0.5, 0.25, ((0, 8),))
    cross_key = gaussian(streams_of[10], (D, D), D ** -0.5, 0.25, ((0, 8),))
    cross_value = gaussian(streams_of[11], (D, D), D ** -0.5, 0.25, ((0, 8),))
    cross_output = gaussian(streams_of[12], (D, D), (max(D // 64, 8)) ** -0.5, 2.0, ((0, 8),))
    inner_weight = gaussian(streams_of[13], (D, FF), D ** -0.5, 0.25, ((0, 8),))
    outer_weight = gaussian(streams_of[14], (FF, D), FF ** -0.5, 0.125, ((0, 8),))
    self_gain = jnp.clip(1.0 + 0.15 * jax.random.normal(streams_of[15], (D,), jnp.float32), 0.25, 1.75).astype(jnp.bfloat16)
    self_shift = gaussian(streams_of[16], (D,), 0.3, 2.0, ((0, 8),))
    cross_gain = jnp.clip(1.0 + 0.15 * jax.random.normal(streams_of[17], (D,), jnp.float32), 0.25, 1.75).astype(jnp.bfloat16)
    cross_shift = gaussian(streams_of[18], (D,), 0.3, 2.0, ((0, 8),))
    feed_gain = jnp.clip(1.0 + 0.15 * jax.random.normal(streams_of[19], (D,), jnp.float32), 0.25, 1.75).astype(jnp.bfloat16)
    feed_shift = gaussian(streams_of[20], (D,), 0.3, 2.0, ((0, 8),))
    return {"tokens": tokens, "memory": memory, "target_segments": target_segments, "source_segments": source_segments, "cotangent": cotangent, "query_weight": query_weight, "key_weight": key_weight, "value_weight": value_weight, "output_weight": output_weight, "cross_query": cross_query, "cross_key": cross_key, "cross_value": cross_value, "cross_output": cross_output, "inner_weight": inner_weight, "outer_weight": outer_weight, "self_gain": self_gain, "self_shift": self_shift, "cross_gain": cross_gain, "cross_shift": cross_shift, "feed_gain": feed_gain, "feed_shift": feed_shift}


@jax.custom_vjp
def low(v):
    return lax.optimization_barrier(v.astype(jnp.bfloat16)).astype(jnp.float32)

@jax.custom_vjp
def low_back(v):
    return v

def low_keep(v):
    return (low(v), None)

def low_pass(kept, grad):
    return (grad,)

def back_keep(v):
    return (v, None)

def back_low(kept, grad):
    return (low(grad),)
low.defvjp(low_keep, low_pass)
low_back.defvjp(back_keep, back_low)
EPSILON = 1e-05
NEGATIVE = -1e+30
HIGHEST = lax.Precision.HIGHEST

def product(first_operand, second_operand):
    return jnp.dot(first_operand, second_operand, precision=HIGHEST, preferred_element_type=jnp.float32)

def layer_norm(values, gain_vector, shift_vector):
    centred = values - lax.optimization_barrier(jnp.mean(values, axis=-1, keepdims=True))
    spread = lax.optimization_barrier(jnp.mean(centred * centred, axis=-1, keepdims=True))
    return centred * lax.rsqrt(spread + EPSILON) * gain_vector + shift_vector

def rounded(values):
    return low_back(low(values))

def attend(query_rows, key_rows, value_rows, query_seg, key_seg, causal):
    length = query_rows.shape[0]
    block_rows = min(512, length)
    block_count = length // block_rows
    factor = DH ** (-0.5)
    key_heads = key_rows.reshape(key_rows.shape[0], H, DH)
    value_heads = value_rows.reshape(value_rows.shape[0], H, DH)
    key_places = jnp.arange(key_rows.shape[0], dtype=jnp.int32)

    def one_block(inputs):
        query_block, seg_block, place_block = inputs
        scores = low_back(factor * jnp.einsum('qhd,khd->hqk', query_block, key_heads, precision=HIGHEST))
        allowed = seg_block[:, None] == key_seg[None, :]
        if causal:
            allowed = jnp.logical_and(allowed, place_block[:, None] >= key_places[None, :])
        scores = jnp.where(allowed[None], scores, NEGATIVE)
        shifted = scores - lax.optimization_barrier(jnp.max(scores, axis=-1, keepdims=True))
        exponent = jnp.exp(shifted)
        probs = low(exponent / lax.optimization_barrier(jnp.sum(exponent, axis=-1, keepdims=True)))
        return jnp.einsum('hqk,khd->qhd', probs, value_heads, precision=HIGHEST)
    blocks = lax.map(jax.checkpoint(one_block), (query_rows.reshape(block_count, block_rows, H, DH), query_seg.reshape(block_count, block_rows), jnp.arange(length, dtype=jnp.int32).reshape(block_count, block_rows)))
    return blocks.reshape(length, H * DH)

def layer(params, token_rows, memory_rows, target_ids, source_ids):
    query_weight, key_weight, value_weight, output_weight, cross_query, cross_key, cross_value, cross_output, inner_weight, outer_weight, self_gain, self_shift, cross_gain, cross_shift, feed_gain, feed_shift = params
    queries = rounded(product(token_rows, query_weight))
    keys_self = rounded(product(token_rows, key_weight))
    values_self = rounded(product(token_rows, value_weight))
    context = rounded(attend(queries, keys_self, values_self, target_ids, target_ids, True))
    first = layer_norm(token_rows + low_back(product(context, output_weight)), self_gain, self_shift)
    first_low = low(first)
    cross_queries = rounded(product(first_low, cross_query))
    cross_keys = rounded(product(memory_rows, cross_key))
    cross_values = rounded(product(memory_rows, cross_value))
    cross_context = rounded(attend(cross_queries, cross_keys, cross_values, target_ids, source_ids, False))
    second = layer_norm(first + low_back(product(cross_context, cross_output)), cross_gain, cross_shift)
    second_low = low(second)
    hidden = product(second_low, inner_weight)
    activated = low(low_back(jax.nn.gelu(hidden, approximate=False)))
    return layer_norm(second + low_back(product(activated, outer_weight)), feed_gain, feed_shift)

def reference(tokens, memory, target_segments, source_segments, cotangent, query_weight, key_weight, value_weight, output_weight, cross_query, cross_key, cross_value, cross_output, inner_weight, outer_weight, self_gain, self_shift, cross_gain, cross_shift, feed_gain, feed_shift):
    params = tuple((element.astype(jnp.float32) for element in (query_weight, key_weight, value_weight, output_weight, cross_query, cross_key, cross_value, cross_output, inner_weight, outer_weight, self_gain, self_shift, cross_gain, cross_shift, feed_gain, feed_shift)))

    def per_sequence(carry, inputs):
        token_rows, memory_rows, target_ids, source_ids, grad_rows = inputs

        def forward(weights_all, token_part, memory_part):
            return layer(weights_all, token_part, memory_part, target_ids, source_ids)
        result, pullback = jax.vjp(forward, params, token_rows.astype(jnp.float32), memory_rows.astype(jnp.float32))
        weight_grads, token_grad, memory_grad = pullback(grad_rows.astype(jnp.float32))
        carry = jax.tree.map(jnp.add, carry, weight_grads)
        return (carry, (result.astype(jnp.bfloat16), token_grad, memory_grad))
    zeros = jax.tree.map(jnp.zeros_like, params)
    sequences = (tokens.reshape(MB * SEQS, LEN, D), memory.reshape(MB * SEQS, SRC, D), target_segments.reshape(MB * SEQS, LEN).astype(jnp.int32), source_segments.reshape(MB * SEQS, SRC).astype(jnp.int32), cotangent.reshape(MB * SEQS, LEN, D))
    grads, (outputs, token_grads, memory_grads) = lax.scan(per_sequence, zeros, sequences)
    scale_factor = 1.0 / (MB * SEQS)
    grads = tuple((element * scale_factor for element in grads))
    return (outputs.reshape(MB, SEQS, LEN, D), token_grads.reshape(MB, SEQS, LEN, D), memory_grads.reshape(MB, SEQS, SRC, D), grads[0], grads[1], grads[2], grads[3], grads[4], grads[5], grads[6], grads[7], grads[8], grads[9], grads[10], grads[11], grads[12], grads[13], grads[14], grads[15])
```

```python
import functools

import jax
import jax.numpy as jnp
from jax import lax
from jax.experimental import pallas as pl
from jax.experimental.pallas import tpu as pltpu
from jax.sharding import PartitionSpec as P

DH = 64
PAIR = 2 * DH
BLOCK = 256
TILE = 16
EPSILON = 1e-05
NEGATIVE = -1e30
FACTOR = DH ** (-0.5)
AXES = ("dp", "seq")
LOW = jnp.bfloat16
WIDE = jnp.float32
VMEM_LIMIT = 56 * 1024 * 1024


def dot_nn(a, b):
    return jnp.dot(a, b, preferred_element_type=WIDE)


def dot_nt(a, b):
    return lax.dot_general(a, b, (((1,), (1,)), ((), ())), preferred_element_type=WIDE)


def dot_tn(a, b):
    return lax.dot_general(a, b, (((0,), (0,)), ((), ())), preferred_element_type=WIDE)


def normalise(values):
    centred = values - jnp.mean(values, axis=-1, keepdims=True)
    inverse = lax.rsqrt(jnp.mean(centred * centred, axis=-1, keepdims=True) + EPSILON)
    return centred * inverse, inverse


def norm_backward(upstream, normed, inverse, gain_row):
    scaled = upstream * gain_row
    plain_mean = jnp.mean(scaled, axis=-1, keepdims=True)
    along_mean = jnp.mean(scaled * normed, axis=-1, keepdims=True)
    return inverse * (scaled - plain_mean - normed * along_mean)


def row_blocks(length, size=BLOCK):
    return [pl.ds(start, size) for start in range(0, length, size)]


def copy_all(copies):
    for copy in copies:
        copy.start()
    for copy in copies:
        copy.wait()


def piece_copies(pieces, orders, first, place, semaphores):
    copies = []
    for piece in pieces:
        for slab in range(piece.shape[0]):
            index = orders[first + len(copies)]
            copies.append((piece.at[slab], index))
    return [
        pltpu.make_async_copy(source, place(index), semaphores.at[number])
        for number, (source, index) in enumerate(copies)
    ]


def weight_of(weight_ref, which, rows):
    count, _, width = weight_ref.shape
    return weight_ref[:, which * rows : (which + 1) * rows, :].reshape(count * rows, width)


def seg_columns(seg_row):
    return jnp.transpose(jnp.broadcast_to(seg_row, (128, seg_row.shape[1])))


def stack_heads(pair):
    lane = lax.broadcasted_iota(jnp.int32, pair.shape, 1)
    zero = jnp.zeros_like(pair)
    return jnp.concatenate(
        [jnp.where(lane < DH, pair, zero), jnp.where(lane < DH, zero, pair)], axis=0
    )


def unstack_heads(columns):
    row = lax.broadcasted_iota(jnp.int32, (PAIR, BLOCK), 0)
    return jnp.where(row < DH, columns[:, :BLOCK], columns[:, BLOCK:])


def mask_bias(key_ids, query_ids, key_start, query_start, causal):
    ids = jnp.concatenate([key_ids, key_ids], axis=1)
    allowed = ids == query_ids
    if causal:
        key_place = key_start + lax.broadcasted_iota(jnp.int32, (BLOCK, BLOCK), 0)
        query_place = query_start + lax.broadcasted_iota(jnp.int32, (BLOCK, BLOCK), 1)
        allowed = jnp.logical_and(allowed, key_place <= query_place)
    bias = jnp.where(allowed, 0.0, NEGATIVE)
    return jnp.concatenate([bias, bias], axis=1)


def key_bounds(key_row, query_ids, query_start, causal):
    below = jnp.sum(jnp.where(key_row < jnp.min(query_ids), 1.0, 0.0)).astype(jnp.int32)
    first = lax.div(below, BLOCK)
    if causal:
        return first, lax.div(query_start, BLOCK) + 1
    upto = jnp.sum(jnp.where(key_row <= jnp.max(query_ids), 1.0, 0.0)).astype(jnp.int32)
    return first, lax.div(upto + (BLOCK - 1), BLOCK)


def attend_forward(
    q_ref, k_ref, v_ref, o_ref, lse_ref, key_row, columns_ref, query_row, start, causal, scratch
):
    stack_ref, sum_ref, top_ref, total_ref = scratch
    pairs = q_ref.shape[1] // PAIR
    for number, rows in enumerate(row_blocks(q_ref.shape[0])):
        query_ids = query_row[:, number * BLOCK : (number + 1) * BLOCK]
        query_start = start + number * BLOCK
        low, high = key_bounds(key_row, query_ids, query_start, causal)
        for pair in range(pairs):
            stack_ref[pair] = stack_heads(q_ref[rows, pair * PAIR : (pair + 1) * PAIR])
        sum_ref[...] = jnp.zeros_like(sum_ref)
        top_ref[...] = jnp.full_like(top_ref, NEGATIVE)
        total_ref[...] = jnp.zeros_like(total_ref)

        def one_block(block, carry):
            key_start = pl.multiple_of(block * BLOCK, BLOCK)
            keys = pl.ds(key_start, BLOCK)
            bias = mask_bias(columns_ref[keys, :], query_ids, key_start, query_start, causal)
            for pair in range(pairs):
                lanes = slice(pair * PAIR, (pair + 1) * PAIR)
                scores = dot_nt(k_ref[keys, lanes], stack_ref[pair]) + bias
                before = top_ref[pair : pair + 1, :]
                top = jnp.maximum(before, jnp.max(scores, axis=0, keepdims=True))
                shrink = jnp.exp(before - top)
                exponent = jnp.exp(scores - top)
                top_ref[pair : pair + 1, :] = top
                total_ref[pair : pair + 1, :] = total_ref[
                    pair : pair + 1, :
                ] * shrink + jnp.sum(exponent, axis=0, keepdims=True)
                sum_ref[pair] = sum_ref[pair] * shrink + dot_tn(
                    v_ref[keys, lanes], exponent.astype(LOW)
                )
            return carry

        lax.fori_loop(low, high, one_block, 0)
        for pair in range(pairs):
            total = total_ref[pair : pair + 1, :]
            context = unstack_heads(sum_ref[pair] / total)
            o_ref[rows, pair * PAIR : (pair + 1) * PAIR] = jnp.transpose(context).astype(LOW)
            place = number * pairs + pair
            lse_ref[place : place + 1, :] = top_ref[pair : pair + 1, :] + jnp.log(total)


def attend_backward(
    q_ref,
    k_ref,
    v_ref,
    o_ref,
    grad_ref,
    lse_ref,
    dq_ref,
    dk_ref,
    dv_ref,
    key_row,
    columns_ref,
    query_row,
    start,
    causal,
    scratch,
):
    stack_ref, stack_grad_ref, sum_ref, along_ref = scratch
    pairs = q_ref.shape[1] // PAIR
    dk_ref[...] = jnp.zeros_like(dk_ref)
    dv_ref[...] = jnp.zeros_like(dv_ref)
    for number, rows in enumerate(row_blocks(q_ref.shape[0])):
        query_ids = query_row[:, number * BLOCK : (number + 1) * BLOCK]
        query_start = start + number * BLOCK
        low, high = key_bounds(key_row, query_ids, query_start, causal)
        for pair in range(pairs):
            lanes = slice(pair * PAIR, (pair + 1) * PAIR)
            grad = grad_ref[rows, lanes]
            stack_ref[pair] = stack_heads(q_ref[rows, lanes])
            stack_grad_ref[pair] = stack_heads(grad)
            along = jnp.transpose(grad.astype(WIDE) * o_ref[rows, lanes].astype(WIDE))
            along_ref[pair : pair + 1, :] = jnp.concatenate(
                [
                    jnp.sum(along[:DH], axis=0, keepdims=True),
                    jnp.sum(along[DH:], axis=0, keepdims=True),
                ],
                axis=1,
            )
        sum_ref[...] = jnp.zeros_like(sum_ref)

        def one_block(block, carry):
            key_start = pl.multiple_of(block * BLOCK, BLOCK)
            keys = pl.ds(key_start, BLOCK)
            bias = mask_bias(columns_ref[keys, :], query_ids, key_start, query_start, causal)
            for pair in range(pairs):
                lanes = slice(pair * PAIR, (pair + 1) * PAIR)
                place = number * pairs + pair
                key_pair = k_ref[keys, lanes]
                scores = dot_nt(key_pair, stack_ref[pair]) + bias
                probs = jnp.exp(scores - lse_ref[place : place + 1, :])
                prob_grad = dot_nt(v_ref[keys, lanes], stack_grad_ref[pair])
                score_grad = (probs * (prob_grad - along_ref[pair : pair + 1, :])).astype(LOW)
                dv_ref[keys, lanes] += dot_nn(probs.astype(LOW), stack_grad_ref[pair])
                dk_ref[keys, lanes] += dot_nn(score_grad, stack_ref[pair])
                sum_ref[pair] += dot_tn(key_pair, score_grad)
            return carry

        lax.fori_loop(low, high, one_block, 0)
        for pair in range(pairs):
            grad = jnp.transpose(unstack_heads(sum_ref[pair])) * FACTOR
            dq_ref[rows, pair * PAIR : (pair + 1) * PAIR] = grad.astype(LOW)


def store_pieces(grad_ref, keep_ref, send_ref, info_ref, order, offset, count, rows):
    half = count // 2
    for number in range(count):
        owner = info_ref[order + number]
        block = grad_ref[pl.ds(pl.multiple_of(owner * rows, rows), rows), :].astype(LOW)
        target = keep_ref if number < half else send_ref
        target[number % half, offset : offset + rows, :] = block


class Plan:
    def __init__(self, tokens, inner_weight):
        self.dp = lax.axis_size("dp")
        self.seq = lax.axis_size("seq")
        self.batches, _, self.chunk, self.width = tokens.shape
        self.hidden = inner_weight.shape[1]
        self.length = self.chunk * self.seq
        self.group = self.seq // self.batches
        self.rows = self.batches * self.chunk
        self.chunks = self.seq
        self.shard = self.width // self.dp
        self.outer_shard = self.hidden // self.dp
        self.hidden_blocks = self.hidden // self.width
        self.pairs = self.width // PAIR
        self.query_blocks = self.rows // BLOCK
        self.order = 0
        self.grad_order = self.dp
        self.chunk_order = 2 * self.dp
        self.own = self.chunk_order + self.chunks
        self.round = self.own + 1
        self.mates = self.round + self.batches
        self.info_length = self.mates + self.group


def seg_rows(plan, raw_ref, seg_ref):
    for number in range(plan.chunks):
        lanes = slice(number * plan.chunk, (number + 1) * plan.chunk)
        seg_ref[0:1, lanes] = raw_ref[number, 0:1, : plan.chunk].astype(WIDE)
        seg_ref[1:2, lanes] = raw_ref[number, 0:1, plan.chunk : 2 * plan.chunk].astype(WIDE)


def own_rows(plan, info_ref):
    return pl.multiple_of(info_ref[plan.own] * plan.rows, plan.rows)


def self_forward_kernel(plan, chunk_count, piece_count, info_ref, *refs):
    chunks, refs = refs[:chunk_count], refs[chunk_count:]
    pieces, refs = refs[:piece_count], refs[piece_count:]
    (q_ref, k_ref, v_ref, o_ref, lse_ref, a_ref, seg_ref, vec_ref), refs = refs[:8], refs[8:]
    x_ref, raw_ref, w_ref, columns_ref, chunk_sems, piece_sems, *scratch = refs
    load_chunks = chunk_copies(plan, chunks, info_ref, x_ref, raw_ref, chunk_sems)
    load_pieces = piece_copies(
        pieces, info_ref, plan.order, lambda index: w_ref.at[index], piece_sems
    )
    copy_all(load_chunks + load_pieces)
    shard = plan.shard
    start = own_rows(plan, info_ref)
    vec_ref[...] = jnp.sum(w_ref[:, 4 * shard :, :].astype(WIDE), axis=0)
    seg_rows(plan, raw_ref, seg_ref)
    columns_ref[...] = seg_columns(seg_ref[0:1, :])
    for rows in row_blocks(plan.rows):
        own = x_ref[pl.ds(start + rows.start, BLOCK), :]
        q_ref[rows, :] = (dot_nn(own, weight_of(w_ref, 0, shard)) * FACTOR).astype(LOW)

    def project_block(block, carry):
        rows = pl.ds(pl.multiple_of(block * BLOCK, BLOCK), BLOCK)
        k_ref[rows, :] = dot_nn(x_ref[rows, :], weight_of(w_ref, 1, shard)).astype(LOW)
        v_ref[rows, :] = dot_nn(x_ref[rows, :], weight_of(w_ref, 2, shard)).astype(LOW)
        return carry

    lax.fori_loop(0, plan.length // BLOCK, project_block, 0)
    attend_forward(
        q_ref,
        k_ref,
        v_ref,
        o_ref,
        lse_ref,
        seg_ref[0:1, :],
        columns_ref,
        seg_ref[0:1, pl.ds(start, plan.rows)],
        start,
        True,
        scratch,
    )
    for rows in row_blocks(plan.rows):
        own = x_ref[pl.ds(start + rows.start, BLOCK), :].astype(WIDE)
        a_ref[rows, :] = own + dot_nn(o_ref[rows, :], weight_of(w_ref, 3, shard))


def chunk_copies(plan, chunks, info_ref, x_ref, raw_ref, semaphores):
    copies = []
    for number, chunk in enumerate(chunks):
        index = info_ref[plan.chunk_order + number]
        rows = pl.ds(pl.multiple_of(index * plan.chunk, plan.chunk), plan.chunk)
        copies.append(
            pltpu.make_async_copy(
                chunk.at[pl.ds(0, plan.chunk)], x_ref.at[rows], semaphores.at[0, number]
            )
        )
        if raw_ref is not None:
            copies.append(
                pltpu.make_async_copy(
                    chunk.at[pl.ds(plan.chunk, TILE)], raw_ref.at[index], semaphores.at[1, number]
                )
            )
    return copies


def cross_forward_kernel(plan, chunk_count, piece_count, info_ref, *refs):
    chunks, refs = refs[:chunk_count], refs[chunk_count:]
    pieces, refs = refs[:piece_count], refs[piece_count:]
    (a_ref, seg_ref, vec_ref), refs = refs[:3], refs[3:]
    (q_ref, k_ref, v_ref, o_ref, lse_ref, z_ref), refs = refs[:6], refs[6:]
    m_ref, w_ref, columns_ref, chunk_sems, piece_sems, *scratch = refs
    load_chunks = chunk_copies(plan, chunks, info_ref, m_ref, None, chunk_sems)
    load_pieces = piece_copies(
        pieces, info_ref, plan.order, lambda index: w_ref.at[index], piece_sems
    )
    copy_all(load_chunks + load_pieces)
    shard = plan.shard
    start = own_rows(plan, info_ref)
    columns_ref[...] = seg_columns(seg_ref[1:2, :])
    gain, shift = vec_ref[0:1, :], vec_ref[1:2, :]
    for rows in row_blocks(plan.rows):
        normed, _ = normalise(a_ref[rows, :])
        first = normed * gain + shift
        z_ref[rows, :] = first
        q_ref[rows, :] = (
            dot_nn(first.astype(LOW), weight_of(w_ref, 0, shard)) * FACTOR
        ).astype(LOW)

    def project_block(block, carry):
        rows = pl.ds(pl.multiple_of(block * BLOCK, BLOCK), BLOCK)
        k_ref[rows, :] = dot_nn(m_ref[rows, :], weight_of(w_ref, 1, shard)).astype(LOW)
        v_ref[rows, :] = dot_nn(m_ref[rows, :], weight_of(w_ref, 2, shard)).astype(LOW)
        return carry

    lax.fori_loop(0, plan.length // BLOCK, project_block, 0)
    attend_forward(
        q_ref,
        k_ref,
        v_ref,
        o_ref,
        lse_ref,
        seg_ref[1:2, :],
        columns_ref,
        seg_ref[0:1, pl.ds(start, plan.rows)],
        start,
        False,
        scratch,
    )
    for rows in row_blocks(plan.rows):
        z_ref[rows, :] += dot_nn(o_ref[rows, :], weight_of(w_ref, 3, shard))


def feed_kernel(plan, piece_count, info_ref, *refs):
    batches = plan.batches
    upstreams, refs = refs[:batches], refs[batches:]
    pieces, refs = refs[:piece_count], refs[piece_count:]
    (z_ref, vec_ref), refs = refs[:2], refs[2:]
    outs, refs = refs[:batches], refs[batches:]
    (dh_ref, dvec_ref, keep_ref, send_ref), refs = refs[:4], refs[4:]
    inner_ref, outer_ref, low_ref, u_ref, r_ref, f_ref, up_ref, res_ref, gw_ref, piece_sems = refs
    width, shard, blocks, outer_shard = (
        plan.width,
        plan.shard,
        plan.hidden_blocks,
        plan.outer_shard,
    )
    copies = []
    number = 0
    for piece in pieces:
        for slab in range(piece.shape[0]):
            owner = info_ref[plan.order + number]
            for block in range(blocks):
                copies.append(
                    pltpu.make_async_copy(
                        piece.at[slab, pl.ds(block * shard, shard)],
                        inner_ref.at[block, pl.ds(pl.multiple_of(owner * shard, shard), shard)],
                        piece_sems.at[block, number],
                    )
                )
            copies.append(
                pltpu.make_async_copy(
                    piece.at[slab, pl.ds(blocks * shard, outer_shard)],
                    outer_ref.at[pl.ds(pl.multiple_of(owner * outer_shard, outer_shard), outer_shard)],
                    piece_sems.at[blocks, number],
                )
            )
            number += 1
    copy_all(copies)
    for number in range(batches):
        index = info_ref[plan.round + number]
        rows = pl.ds(pl.multiple_of(index * plan.chunk, plan.chunk), plan.chunk)
        up_ref[rows, :] = upstreams[number][...]
    gain_two, shift_two = vec_ref[2:3, :], vec_ref[3:4, :]
    gain_three, shift_three = vec_ref[4:5, :], vec_ref[5:6, :]
    gain_grad = jnp.zeros((1, width), WIDE)
    shift_grad = jnp.zeros((1, width), WIDE)
    for rows in row_blocks(plan.rows):
        normed, _ = normalise(z_ref[rows, :])
        second = normed * gain_two + shift_two
        f_ref[rows, :] = second
        low_ref[rows, :] = second.astype(LOW)

    def inner_block(block, carry):
        for rows in row_blocks(plan.rows):
            u = dot_nn(low_ref[rows, :], inner_ref[block])
            phi = 0.5 + 0.5 * lax.erf(u * (0.5**0.5))
            r_ref[block, rows, :] = (u * phi).astype(LOW)
            u_ref[block, rows, :] = phi + u * (jnp.exp(-0.5 * u * u) * 0.3989422804014327)
            outer = outer_ref[pl.ds(pl.multiple_of(block * width, width), width), :]
            f_ref[rows, :] += dot_nn(r_ref[block, rows, :], outer)
        return carry

    lax.fori_loop(0, blocks, inner_block, 0)
    for rows in row_blocks(plan.rows):
        normed, inverse = normalise(f_ref[rows, :])
        res_ref[rows, :] = (normed * gain_three + shift_three).astype(LOW)
        upstream = up_ref[rows, :].astype(WIDE)
        gain_grad += jnp.sum(upstream * normed, axis=0, keepdims=True)
        shift_grad += jnp.sum(upstream, axis=0, keepdims=True)
        feed_grad = norm_backward(upstream, normed, inverse, gain_three)
        dh_ref[rows, :] = feed_grad
        up_ref[rows, :] = feed_grad.astype(LOW)
    for number in range(batches):
        index = info_ref[plan.round + number]
        outs[number][...] = res_ref[pl.ds(pl.multiple_of(index * plan.chunk, plan.chunk), plan.chunk), :]

    def back_block(block, carry):
        outer = outer_ref[pl.ds(pl.multiple_of(block * width, width), width), :]
        du_ref = r_ref
        gw_ref[block] = dot_tn(r_ref[block], up_ref[...])
        for rows in row_blocks(plan.rows):
            dr = dot_nt(up_ref[rows, :], outer).astype(LOW).astype(WIDE)
            du_ref[block, rows, :] = (dr * u_ref[block, rows, :]).astype(LOW)
        for rows in row_blocks(plan.rows):
            dh_ref[rows, :] += dot_nt(du_ref[block, rows, :], inner_ref[block])
        return carry

    lax.fori_loop(0, blocks, back_block, 0)
    half = plan.dp // 2
    for number in range(plan.dp):
        owner = info_ref[plan.grad_order + number]
        target = keep_ref if number < half else send_ref
        first = owner * outer_shard
        block = lax.div(first, width)
        inside = pl.multiple_of(lax.rem(first, width), outer_shard)
        target[number % half, blocks * shard : blocks * shard + outer_shard, :] = gw_ref[
            block, pl.ds(inside, outer_shard), :
        ].astype(LOW)

    def inner_grad(block, carry):
        gw_ref[block] = dot_tn(low_ref[...], r_ref[block])
        return carry

    lax.fori_loop(0, blocks, inner_grad, 0)
    for block in range(blocks):
        store_pieces(
            gw_ref.at[block],
            keep_ref,
            send_ref,
            info_ref,
            plan.grad_order,
            block * shard,
            plan.dp,
            shard,
        )
    dvec_ref[...] = jnp.zeros_like(dvec_ref)
    dvec_ref[4:5, :] = gain_grad
    dvec_ref[5:6, :] = shift_grad


def cross_backward_kernel(plan, chunk_count, piece_count, info_ref, *refs):
    chunks, refs = refs[:chunk_count], refs[chunk_count:]
    pieces, refs = refs[:piece_count], refs[piece_count:]
    (a_ref, z_ref, seg_ref, vec_ref, dvec_in_ref, dh_ref), refs = refs[:6], refs[6:]
    (q_ref, k_ref, v_ref, o_ref, lse_ref), refs = refs[:5], refs[5:]
    own_ref, refs = refs[0], refs[1:]
    mates, refs = refs[: plan.group - 1], refs[plan.group - 1 :]
    (dfirst_ref, dvec_ref, keep_ref, send_ref), refs = refs[:4], refs[4:]
    m_ref, w_ref, columns_ref, chunk_sems, piece_sems, refs = *refs[:5], refs[5:]
    low_ref, do_ref, h_ref, dq_ref, dk_ref, dv_ref, dkl_ref, dvl_ref, gw_ref, *scratch = refs
    load_chunks = chunk_copies(plan, chunks, info_ref, m_ref, None, chunk_sems)
    load_pieces = piece_copies(
        pieces, info_ref, plan.order, lambda index: w_ref.at[index], piece_sems
    )
    copy_all(load_chunks + load_pieces)
    shard = plan.shard
    start = own_rows(plan, info_ref)
    columns_ref[...] = seg_columns(seg_ref[1:2, :])
    gain_grad = jnp.zeros((1, plan.width), WIDE)
    shift_grad = jnp.zeros((1, plan.width), WIDE)
    for rows in row_blocks(plan.rows):
        normed, inverse = normalise(z_ref[rows, :])
        upstream = dh_ref[rows, :]
        gain_grad += jnp.sum(upstream * normed, axis=0, keepdims=True)
        shift_grad += jnp.sum(upstream, axis=0, keepdims=True)
        grad = norm_backward(upstream, normed, inverse, vec_ref[2:3, :])
        dfirst_ref[rows, :] = grad
        low_ref[rows, :] = grad.astype(LOW)
        do_ref[rows, :] = dot_nt(low_ref[rows, :], weight_of(w_ref, 3, shard)).astype(LOW)
        normed, _ = normalise(a_ref[rows, :])
        h_ref[rows, :] = (normed * vec_ref[0:1, :] + vec_ref[1:2, :]).astype(LOW)
    dvec_ref[...] = dvec_in_ref[...]
    dvec_ref[2:3, :] = gain_grad
    dvec_ref[3:4, :] = shift_grad
    attend_backward(
        q_ref,
        k_ref,
        v_ref,
        o_ref,
        do_ref,
        lse_ref,
        dq_ref,
        dk_ref,
        dv_ref,
        seg_ref[1:2, :],
        columns_ref,
        seg_ref[0:1, pl.ds(start, plan.rows)],
        start,
        False,
        scratch,
    )
    finish_backward(
        plan,
        info_ref,
        w_ref,
        m_ref,
        h_ref,
        o_ref,
        low_ref,
        dq_ref,
        dk_ref,
        dv_ref,
        dkl_ref,
        dvl_ref,
        gw_ref,
        keep_ref,
        send_ref,
        own_ref,
        mates,
    )
    for rows in row_blocks(plan.rows):
        dfirst_ref[rows, :] += dot_nt(dq_ref[rows, :], weight_of(w_ref, 0, shard))


def finish_backward(
    plan,
    info_ref,
    w_ref,
    source_ref,
    query_source_ref,
    o_ref,
    low_ref,
    dq_ref,
    dk_ref,
    dv_ref,
    dkl_ref,
    dvl_ref,
    gw_ref,
    keep_ref,
    send_ref,
    own_ref,
    mates,
):
    shard = plan.shard

    def round_block(block, carry):
        rows = pl.ds(pl.multiple_of(block * BLOCK, BLOCK), BLOCK)
        dkl_ref[rows, :] = dk_ref[rows, :].astype(LOW)
        dvl_ref[rows, :] = dv_ref[rows, :].astype(LOW)
        return carry

    lax.fori_loop(0, plan.length // BLOCK, round_block, 0)
    for number in range(plan.group):
        first = pl.multiple_of(info_ref[plan.mates + number] * plan.rows, plan.rows)
        for rows in row_blocks(plan.rows):
            source = pl.ds(first + rows.start, BLOCK)
            part = dot_nt(dkl_ref[source, :], weight_of(w_ref, 1, shard)) + dot_nt(
                dvl_ref[source, :], weight_of(w_ref, 2, shard)
            )
            if number == 0:
                own_ref[rows, :] = part
            else:
                mates[number - 1][rows, :] = part.astype(LOW)
    products = (
        (query_source_ref, dq_ref),
        (source_ref, dkl_ref),
        (source_ref, dvl_ref),
        (o_ref, low_ref),
    )
    for which, (left, right) in enumerate(products):
        gw_ref[...] = dot_tn(left[...], right[...])
        store_pieces(
            gw_ref, keep_ref, send_ref, info_ref, plan.grad_order, which * shard, plan.dp, shard
        )


def self_backward_kernel(plan, chunk_count, piece_count, info_ref, *refs):
    chunks, refs = refs[:chunk_count], refs[chunk_count:]
    pieces, refs = refs[:piece_count], refs[piece_count:]
    (a_ref, seg_ref, vec_ref, dvec_in_ref, dh_ref), refs = refs[:5], refs[5:]
    (q_ref, k_ref, v_ref, o_ref, lse_ref), refs = refs[:5], refs[5:]
    own_ref, refs = refs[0], refs[1:]
    mates, refs = refs[: plan.group - 1], refs[plan.group - 1 :]
    (keep_ref, send_ref), refs = refs[:2], refs[2:]
    x_ref, raw_ref, w_ref, columns_ref, chunk_sems, piece_sems, refs = *refs[:6], refs[6:]
    low_ref, do_ref, own_x_ref, da_ref, dq_ref, dk_ref, dv_ref, dkl_ref, dvl_ref, gw_ref, *scratch = refs
    load_chunks = chunk_copies(plan, chunks, info_ref, x_ref, raw_ref, chunk_sems)
    load_pieces = piece_copies(
        pieces, info_ref, plan.order, lambda index: w_ref.at[index], piece_sems
    )
    copy_all(load_chunks + load_pieces)
    shard = plan.shard
    start = own_rows(plan, info_ref)
    columns_ref[...] = seg_columns(seg_ref[0:1, :])
    gain_grad = jnp.zeros((1, plan.width), WIDE)
    shift_grad = jnp.zeros((1, plan.width), WIDE)
    for rows in row_blocks(plan.rows):
        normed, inverse = normalise(a_ref[rows, :])
        upstream = dh_ref[rows, :]
        gain_grad += jnp.sum(upstream * normed, axis=0, keepdims=True)
        shift_grad += jnp.sum(upstream, axis=0, keepdims=True)
        grad = norm_backward(upstream, normed, inverse, vec_ref[0:1, :])
        da_ref[rows, :] = grad
        low_ref[rows, :] = grad.astype(LOW)
        do_ref[rows, :] = dot_nt(low_ref[rows, :], weight_of(w_ref, 3, shard)).astype(LOW)
        own_x_ref[rows, :] = x_ref[pl.ds(start + rows.start, BLOCK), :]
    attend_backward(
        q_ref,
        k_ref,
        v_ref,
        o_ref,
        do_ref,
        lse_ref,
        dq_ref,
        dk_ref,
        dv_ref,
        seg_ref[0:1, :],
        columns_ref,
        seg_ref[0:1, pl.ds(start, plan.rows)],
        start,
        True,
        scratch,
    )
    finish_backward(
        plan,
        info_ref,
        w_ref,
        x_ref,
        own_x_ref,
        o_ref,
        low_ref,
        dq_ref,
        dk_ref,
        dv_ref,
        dkl_ref,
        dvl_ref,
        gw_ref,
        keep_ref,
        send_ref,
        own_ref,
        mates,
    )
    for rows in row_blocks(plan.rows):
        own_ref[rows, :] += da_ref[rows, :] + dot_nt(dq_ref[rows, :], weight_of(w_ref, 0, shard))
    tail = jnp.concatenate(
        [
            gain_grad,
            shift_grad,
            dvec_in_ref[2:8, :],
            jnp.zeros((TILE - 8, plan.width), WIDE),
        ],
        axis=0,
    ).astype(LOW)
    for number in range(plan.dp // 2):
        keep_ref[number, 4 * shard :, :] = tail
        send_ref[number, 4 * shard :, :] = tail


SMEM = pl.BlockSpec(memory_space=pltpu.SMEM)
VMEM = pl.BlockSpec(memory_space=pltpu.VMEM)
ANY = pl.BlockSpec(memory_space=pl.ANY)


def call(kernel, specs, operands, outs, scratch, flops, moved):
    return pl.pallas_call(
        kernel,
        in_specs=specs,
        out_specs=[VMEM] * len(outs),
        out_shape=outs,
        scratch_shapes=scratch,
        compiler_params=pltpu.CompilerParams(vmem_limit_bytes=VMEM_LIMIT),
        cost_estimate=pl.CostEstimate(flops=flops, bytes_accessed=moved, transcendentals=0),
    )(*operands)


def shape(dims, dtype):
    return jax.ShapeDtypeStruct(dims, dtype)


def forward_scratch(plan):
    return [
        pltpu.VMEM((plan.pairs, 2 * BLOCK, PAIR), LOW),
        pltpu.VMEM((plan.pairs, PAIR, 2 * BLOCK), WIDE),
        pltpu.VMEM((8, 2 * BLOCK), WIDE),
        pltpu.VMEM((8, 2 * BLOCK), WIDE),
    ]


def backward_scratch(plan):
    return [
        pltpu.VMEM((plan.pairs, 2 * BLOCK, PAIR), LOW),
        pltpu.VMEM((plan.pairs, 2 * BLOCK, PAIR), LOW),
        pltpu.VMEM((plan.pairs, PAIR, 2 * BLOCK), WIDE),
        pltpu.VMEM((8, 2 * BLOCK), WIDE),
    ]


def flat(pieces):
    return sum(piece.shape[0] for piece in pieces)


def self_forward(plan, info, chunks, pieces):
    rows, length, width = plan.rows, plan.length, plan.width
    outs = [
        shape((rows, width), LOW),
        shape((length, width), LOW),
        shape((length, width), LOW),
        shape((rows, width), LOW),
        shape((plan.query_blocks * plan.pairs, 2 * BLOCK), WIDE),
        shape((rows, width), WIDE),
        shape((8, length), WIDE),
        shape((TILE, width), WIDE),
    ]
    scratch = [
        pltpu.VMEM((length, width), LOW),
        pltpu.VMEM((plan.chunks, TILE, width), LOW),
        pltpu.VMEM((plan.dp, 4 * plan.shard + TILE, width), LOW),
        pltpu.VMEM((length, 128), WIDE),
        pltpu.SemaphoreType.DMA((2, plan.chunks)),
        pltpu.SemaphoreType.DMA((plan.dp,)),
    ] + forward_scratch(plan)
    return call(
        functools.partial(self_forward_kernel, plan, len(chunks), len(pieces)),
        [SMEM] + [ANY] * (len(chunks) + len(pieces)),
        [info, *chunks, *pieces],
        outs,
        scratch,
        4 * 10**9,
        8 * 10**6,
    )


def cross_forward(plan, info, chunks, pieces, a, segs, vecs):
    rows, length, width = plan.rows, plan.length, plan.width
    outs = [
        shape((rows, width), LOW),
        shape((length, width), LOW),
        shape((length, width), LOW),
        shape((rows, width), LOW),
        shape((plan.query_blocks * plan.pairs, 2 * BLOCK), WIDE),
        shape((rows, width), WIDE),
    ]
    scratch = [
        pltpu.VMEM((length, width), LOW),
        pltpu.VMEM((plan.dp, 4 * plan.shard, width), LOW),
        pltpu.VMEM((length, 128), WIDE),
        pltpu.SemaphoreType.DMA((2, plan.chunks)),
        pltpu.SemaphoreType.DMA((plan.dp,)),
    ] + forward_scratch(plan)
    return call(
        functools.partial(cross_forward_kernel, plan, len(chunks), len(pieces)),
        [SMEM] + [ANY] * (len(chunks) + len(pieces)) + [VMEM] * 3,
        [info, *chunks, *pieces, a, segs, vecs],
        outs,
        scratch,
        4 * 10**9,
        8 * 10**6,
    )


def feed(plan, info, upstreams, pieces, z, vecs):
    rows, width, blocks = plan.rows, plan.width, plan.hidden_blocks
    piece_rows = blocks * plan.shard + plan.outer_shard
    outs = (
        [shape((plan.chunk, width), LOW)] * plan.batches
        + [shape((rows, width), WIDE), shape((8, width), WIDE)]
        + [shape((plan.dp // 2, piece_rows, width), LOW)] * 2
    )
    scratch = [
        pltpu.VMEM((blocks, width, width), LOW),
        pltpu.VMEM((plan.hidden, width), LOW),
        pltpu.VMEM((rows, width), LOW),
        pltpu.VMEM((blocks, rows, width), WIDE),
        pltpu.VMEM((blocks, rows, width), LOW),
        pltpu.VMEM((rows, width), WIDE),
        pltpu.VMEM((rows, width), LOW),
        pltpu.VMEM((rows, width), LOW),
        pltpu.VMEM((blocks, width, width), WIDE),
        pltpu.SemaphoreType.DMA((blocks + 1, plan.dp)),
    ]
    return call(
        functools.partial(feed_kernel, plan, len(pieces)),
        [SMEM] + [VMEM] * plan.batches + [ANY] * len(pieces) + [VMEM] * 2,
        [info, *upstreams, *pieces, z, vecs],
        outs,
        scratch,
        7 * 10**9,
        12 * 10**6,
    )


def backward_buffers(plan):
    rows, length, width = plan.rows, plan.length, plan.width
    return [
        pltpu.VMEM((rows, width), LOW),
        pltpu.VMEM((length, width), WIDE),
        pltpu.VMEM((length, width), WIDE),
        pltpu.VMEM((length, width), LOW),
        pltpu.VMEM((length, width), LOW),
        pltpu.VMEM((width, width), WIDE),
    ] + backward_scratch(plan)


def cross_backward(plan, info, chunks, pieces, operands):
    rows, length, width = plan.rows, plan.length, plan.width
    outs = (
        [shape((rows, width), WIDE)]
        + [shape((rows, width), LOW)] * (plan.group - 1)
        + [shape((rows, width), WIDE), shape((8, width), WIDE)]
        + [shape((plan.dp // 2, 4 * plan.shard, width), LOW)] * 2
    )
    scratch = [
        pltpu.VMEM((length, width), LOW),
        pltpu.VMEM((plan.dp, 4 * plan.shard, width), LOW),
        pltpu.VMEM((length, 128), WIDE),
        pltpu.SemaphoreType.DMA((2, plan.chunks)),
        pltpu.SemaphoreType.DMA((plan.dp,)),
        pltpu.VMEM((rows, width), LOW),
        pltpu.VMEM((rows, width), LOW),
        pltpu.VMEM((rows, width), LOW),
    ] + backward_buffers(plan)
    return call(
        functools.partial(cross_backward_kernel, plan, len(chunks), len(pieces)),
        [SMEM] + [ANY] * (len(chunks) + len(pieces)) + [VMEM] * len(operands),
        [info, *chunks, *pieces, *operands],
        outs,
        scratch,
        8 * 10**9,
        12 * 10**6,
    )


def self_backward(plan, info, chunks, pieces, operands):
    rows, length, width = plan.rows, plan.length, plan.width
    outs = (
        [shape((rows, width), WIDE)]
        + [shape((rows, width), LOW)] * (plan.group - 1)
        + [shape((plan.dp // 2, 4 * plan.shard + TILE, width), LOW)] * 2
    )
    scratch = [
        pltpu.VMEM((length, width), LOW),
        pltpu.VMEM((plan.chunks, TILE, width), LOW),
        pltpu.VMEM((plan.dp, 4 * plan.shard + TILE, width), LOW),
        pltpu.VMEM((length, 128), WIDE),
        pltpu.SemaphoreType.DMA((2, plan.chunks)),
        pltpu.SemaphoreType.DMA((plan.dp,)),
        pltpu.VMEM((rows, width), LOW),
        pltpu.VMEM((rows, width), LOW),
        pltpu.VMEM((rows, width), LOW),
        pltpu.VMEM((rows, width), WIDE),
    ] + backward_buffers(plan)
    return call(
        functools.partial(self_backward_kernel, plan, len(chunks), len(pieces)),
        [SMEM] + [ANY] * (len(chunks) + len(pieces)) + [VMEM] * len(operands),
        [info, *chunks, *pieces, *operands],
        outs,
        scratch,
        8 * 10**9,
        12 * 10**6,
    )


def pairs_of(plan, move):
    return [
        (dp * plan.seq + seq, to[0] * plan.seq + to[1])
        for dp in range(plan.dp)
        for seq in range(plan.seq)
        for to in [move(dp, seq)]
    ]


def home(plan, dp, batch, seq):
    position = (2 * batch + dp % 2) * plan.group + seq // plan.batches
    return (dp - dp % 2 + position % 2, position // 2)


def round_batch(plan, seq, number):
    return (seq + number) % plan.batches


def inward(plan, number):
    return pairs_of(plan, lambda dp, seq: home(plan, dp, round_batch(plan, seq, number), seq))


def outward(plan, number):
    return [(to, source) for source, to in inward(plan, number)]


def mate(plan, turn):
    def move(dp, seq):
        position = 2 * seq + dp % 2
        group, own = position // plan.group, position % plan.group
        to = group * plan.group + (own + turn) % plan.group
        return (dp - dp % 2 + to % 2, to // 2)

    return pairs_of(plan, move)


def permute(values, pairs):
    return lax.ppermute(values, AXES, pairs)


def dp_flip(plan, bits):
    return pairs_of(plan, lambda dp, seq: (dp ^ bits, seq))


def seq_flip(plan, bits):
    return pairs_of(plan, lambda dp, seq: (dp, seq ^ bits))


def share_inputs(plan, values):
    seq = lax.axis_index("seq")
    received = []
    for number in range(plan.batches):
        piece = lax.dynamic_index_in_dim(
            values, round_batch(plan, seq, number), axis=0, keepdims=False
        )
        received.append(permute(piece, inward(plan, number)))
    return received


def share_mates(plan, received):
    chunks = list(received)
    for turn in range(1, plan.group):
        chunks += [permute(piece, mate(plan, turn)) for piece in received]
    return chunks


def return_outputs(plan, pieces):
    seq = lax.axis_index("seq")
    landed = [permute(piece, outward(plan, number)) for number, piece in enumerate(pieces)]
    landed = jnp.stack(landed)
    order = [lax.rem(batch - seq % plan.batches + plan.batches, plan.batches) for batch in range(plan.batches)]
    return jnp.stack([lax.dynamic_index_in_dim(landed, index, 0, keepdims=False) for index in order])


def gather_pieces(plan, shard):
    if plan.dp != 8:
        return [lax.all_gather(shard, "dp", axis=0)]
    direct = [shard] + [permute(shard, dp_flip(plan, bits)) for bits in (2, 4, 6)]
    pieces = []
    for piece in direct:
        pieces += [piece[None], permute(piece, dp_flip(plan, 1))[None]]
    return pieces


def reduce_pieces(plan, keep, send):
    if plan.dp != 8:
        stacked = jnp.concatenate([keep, send], axis=0)
        part = lax.psum_scatter(stacked, "dp", scatter_dimension=0)
        return lax.psum(part, "seq").astype(WIDE)
    other = permute(send, dp_flip(plan, 1))
    parts = [
        (keep[number].astype(WIDE) + other[number].astype(WIDE)).astype(LOW) for number in range(4)
    ]
    landed = [permute(parts[number], dp_flip(plan, 2 * number)) for number in range(1, 4)]
    total = parts[0].astype(WIDE)
    for piece in landed:
        total = total + piece.astype(WIDE)
    bits = 1
    while bits < plan.seq:
        total = total.astype(LOW)
        total = total.astype(WIDE) + permute(total, seq_flip(plan, bits)).astype(WIDE)
        bits *= 2
    return total


def plan_info(plan):
    dp, seq = lax.axis_index("dp"), lax.axis_index("seq")
    position = 2 * seq + dp % 2
    own = position % plan.group
    batch = position // plan.group // 2
    flips = list(range(8)) if plan.dp == 8 else None
    entries = []
    if flips:
        entries += [dp ^ bits for bits in (0, 1, 2, 3, 4, 5, 6, 7)]
        entries += [dp ^ bits for bits in (0, 2, 4, 6, 1, 3, 5, 7)]
    else:
        entries += list(range(plan.dp)) * 2
    places = [(batch - number) % plan.batches for number in range(plan.batches)]
    for turn in range(plan.group):
        source = (own - turn) % plan.group
        entries += [source * plan.batches + place for place in places]
    entries.append(own)
    entries += places
    entries += [(own + turn) % plan.group for turn in range(plan.group)]
    return jnp.stack([jnp.asarray(entry, jnp.int32) for entry in entries])


def on_device(
    tokens,
    memory,
    target_segments,
    source_segments,
    cotangent,
    query_weight,
    key_weight,
    value_weight,
    output_weight,
    cross_query,
    cross_key,
    cross_value,
    cross_output,
    inner_weight,
    outer_weight,
    self_gain,
    self_shift,
    cross_gain,
    cross_shift,
    feed_gain,
    feed_shift,
):
    plan = Plan(tokens, inner_weight)
    width, shard = plan.width, plan.shard
    info = plan_info(plan)
    dp = lax.axis_index("dp")

    vectors = jnp.stack([self_gain, self_shift, cross_gain, cross_shift, feed_gain, feed_shift])
    vectors = lax.dynamic_update_slice(jnp.zeros((TILE, width), LOW), vectors, (0, dp * shard))
    self_pieces = gather_pieces(
        plan, jnp.concatenate([query_weight, key_weight, value_weight, output_weight, vectors])
    )
    ids = jnp.concatenate([target_segments, source_segments], axis=2).astype(LOW)
    ids = jnp.pad(ids, ((0, 0), (0, TILE - 1), (0, width - 2 * plan.chunk)))
    token_pieces = share_inputs(plan, jnp.concatenate([tokens[:, 0], ids], axis=1))
    token_chunks = share_mates(plan, token_pieces)
    cross_pieces = gather_pieces(
        plan, jnp.concatenate([cross_query, cross_key, cross_value, cross_output])
    )
    memory_chunks = share_mates(plan, share_inputs(plan, memory[:, 0]))
    inner_blocks = [
        inner_weight[:, block * width : (block + 1) * width] for block in range(plan.hidden_blocks)
    ]
    feed_pieces = gather_pieces(plan, jnp.concatenate(inner_blocks + [outer_weight]))
    upstreams = share_inputs(plan, cotangent[:, 0])

    q, k, v, o, lse, a, segs, vecs = self_forward(plan, info, token_chunks, self_pieces)
    cq, ck, cv, co, cross_lse, z = cross_forward(
        plan, info, memory_chunks, cross_pieces, a, segs, vecs
    )
    *results, dsecond, dvec, feed_keep, feed_send = feed(
        plan, info, upstreams, feed_pieces, z, vecs
    )
    out_tokens = return_outputs(plan, results)
    own, *others = cross_backward(
        plan,
        info,
        memory_chunks,
        cross_pieces,
        [a, z, segs, vecs, dvec, dsecond, cq, ck, cv, co, cross_lse],
    )
    mates, (dfirst, dvec, cross_keep, cross_send) = (
        others[: plan.group - 1],
        others[plan.group - 1 :],
    )
    grad_memory = finish_source(plan, info, own, mates)
    own, *others = self_backward(
        plan, info, token_chunks, self_pieces, [a, segs, vecs, dvec, dfirst, q, k, v, o, lse]
    )
    mates, (self_keep, self_send) = others[: plan.group - 1], others[plan.group - 1 :]
    grad_tokens = finish_source(plan, info, own, mates)

    scale = 1.0 / (plan.batches * plan.dp)
    feed_grads = reduce_pieces(plan, feed_keep, feed_send) * scale
    cross_grads = reduce_pieces(plan, cross_keep, cross_send) * scale
    self_grads = reduce_pieces(plan, self_keep, self_send) * scale
    inner_grads = [
        feed_grads[block * shard : (block + 1) * shard] for block in range(plan.hidden_blocks)
    ]
    vector_grads = lax.dynamic_slice(
        self_grads, (4 * shard, dp * shard), (TILE, shard)
    )
    return (
        out_tokens[:, None],
        grad_tokens[:, None],
        grad_memory[:, None],
        *[self_grads[which * shard : (which + 1) * shard] for which in range(4)],
        *[cross_grads[which * shard : (which + 1) * shard] for which in range(4)],
        jnp.concatenate(inner_grads, axis=1),
        feed_grads[plan.hidden_blocks * shard :],
        *[vector_grads[which] for which in range(6)],
    )


def finish_source(plan, info, own, mates):
    for turn, part in enumerate(mates, 1):
        own = own + permute(part, mate(plan, turn)).astype(WIDE)
    own = own.reshape(plan.batches, plan.chunk, plan.width)
    pieces = [
        lax.dynamic_index_in_dim(own, info[plan.round + number], 0, keepdims=False).astype(LOW)
        for number in range(plan.batches)
    ]
    return return_outputs(plan, pieces).astype(WIDE)


def solution(mesh):
    tokens = P(None, "dp", "seq", None)
    ids = P(None, "dp", "seq")
    weight = P("dp", None)
    vector = P("dp")
    return jax.shard_map(
        on_device,
        mesh=mesh,
        in_specs=(tokens, tokens, ids, ids, tokens) + (weight,) * 10 + (vector,) * 6,
        out_specs=(tokens,) * 3 + (weight,) * 10 + (vector,) * 6,
        check_vma=False,
    )
```

```python
import functools

import jax
import jax.numpy as jnp
from jax import lax
from jax.experimental import pallas as pl
from jax.experimental.pallas import tpu as pltpu
from jax.sharding import PartitionSpec as P

DH = 64
PAIR = 2 * DH
BLOCK = 256
TILE = 16
VECTOR_ROWS = 64
FORWARD_COST = 10**6
EPSILON = 1e-05
NEGATIVE = -1e30
FACTOR = DH ** (-0.5)
AXES = ("dp", "seq")
LOW = jnp.bfloat16
WIDE = jnp.float32
VMEM_LIMIT = 56 * 1024 * 1024


def dot_nn(a, b):
    return jnp.dot(a, b, preferred_element_type=WIDE)


def dot_nt(a, b):
    return lax.dot_general(a, b, (((1,), (1,)), ((), ())), preferred_element_type=WIDE)


def dot_tn(a, b):
    return lax.dot_general(a, b, (((0,), (0,)), ((), ())), preferred_element_type=WIDE)


def normalise(values):
    centred = values - jnp.mean(values, axis=-1, keepdims=True)
    inverse = lax.rsqrt(jnp.mean(centred * centred, axis=-1, keepdims=True) + EPSILON)
    return centred * inverse, inverse


def norm_backward(upstream, normed, inverse, gain_row):
    scaled = upstream * gain_row
    plain_mean = jnp.mean(scaled, axis=-1, keepdims=True)
    along_mean = jnp.mean(scaled * normed, axis=-1, keepdims=True)
    return inverse * (scaled - plain_mean - normed * along_mean)


def row_blocks(length, size=BLOCK):
    return [pl.ds(start, size) for start in range(0, length, size)]


def copy_all(copies):
    for copy in copies:
        copy.start()
    for copy in copies:
        copy.wait()


def piece_copies(plan, pieces, info_ref, w_ref, semaphores):
    copies = []
    for piece in pieces:
        for slab in range(piece.shape[0]):
            number = len(copies)
            owner = info_ref[plan.order + number]
            copies.append(
                pltpu.make_async_copy(piece.at[slab], w_ref.at[owner], semaphores.at[number])
            )
    return copies


def weight_of(weight_ref, which, rows):
    count, _, width = weight_ref.shape
    return weight_ref[:, which * rows : (which + 1) * rows, :].reshape(count * rows, width)


def seg_columns(seg_row):
    return jnp.transpose(jnp.broadcast_to(seg_row, (128, seg_row.shape[1])))


def stack_heads(pair):
    lane = lax.broadcasted_iota(jnp.int32, pair.shape, 1)
    zero = jnp.zeros_like(pair)
    return jnp.concatenate(
        [jnp.where(lane < DH, pair, zero), jnp.where(lane < DH, zero, pair)], axis=0
    )


def unstack_heads(columns):
    row = lax.broadcasted_iota(jnp.int32, (PAIR, BLOCK), 0)
    return jnp.where(row < DH, columns[:, :BLOCK], columns[:, BLOCK:])


def mask_bias(key_ids, query_ids, key_start, query_start, causal):
    ids = jnp.concatenate([key_ids, key_ids], axis=1)
    allowed = ids == query_ids
    if causal:
        key_place = key_start + lax.broadcasted_iota(jnp.int32, (BLOCK, BLOCK), 0)
        query_place = query_start + lax.broadcasted_iota(jnp.int32, (BLOCK, BLOCK), 1)
        allowed = jnp.logical_and(allowed, key_place <= query_place)
    bias = jnp.where(allowed, 0.0, NEGATIVE)
    return jnp.concatenate([bias, bias], axis=1)


def key_bounds(key_row, query_ids, query_start, causal):
    below = jnp.sum(jnp.where(key_row < jnp.min(query_ids), 1.0, 0.0)).astype(jnp.int32)
    first = lax.div(below, BLOCK)
    if causal:
        return first, lax.div(query_start, BLOCK) + 1
    upto = jnp.sum(jnp.where(key_row <= jnp.max(query_ids), 1.0, 0.0)).astype(jnp.int32)
    return first, lax.div(upto + (BLOCK - 1), BLOCK)


def attend_forward(
    q_ref, k_ref, v_ref, o_ref, lse_ref, key_row, columns_ref, query_row, start, causal, scratch
):
    stack_ref, sum_ref, top_ref, total_ref = scratch
    pairs = q_ref.shape[1] // PAIR
    for number, rows in enumerate(row_blocks(q_ref.shape[0])):
        query_ids = query_row[:, number * BLOCK : (number + 1) * BLOCK]
        query_start = start + number * BLOCK
        low, high = key_bounds(key_row, query_ids, query_start, causal)
        for pair in range(pairs):
            stack_ref[pair] = stack_heads(q_ref[rows, pair * PAIR : (pair + 1) * PAIR])
        sum_ref[...] = jnp.zeros_like(sum_ref)
        top_ref[...] = jnp.full_like(top_ref, NEGATIVE)
        total_ref[...] = jnp.zeros_like(total_ref)

        def one_block(block, carry):
            key_start = pl.multiple_of(block * BLOCK, BLOCK)
            keys = pl.ds(key_start, BLOCK)
            bias = mask_bias(columns_ref[keys, :], query_ids, key_start, query_start, causal)
            for pair in range(pairs):
                lanes = slice(pair * PAIR, (pair + 1) * PAIR)
                scores = dot_nt(k_ref[keys, lanes], stack_ref[pair]) + bias
                before = top_ref[pair : pair + 1, :]
                top = jnp.maximum(before, jnp.max(scores, axis=0, keepdims=True))
                shrink = jnp.exp(before - top)
                exponent = jnp.exp(scores - top)
                top_ref[pair : pair + 1, :] = top
                total_ref[pair : pair + 1, :] = total_ref[
                    pair : pair + 1, :
                ] * shrink + jnp.sum(exponent, axis=0, keepdims=True)
                sum_ref[pair] = sum_ref[pair] * shrink + dot_tn(
                    v_ref[keys, lanes], exponent.astype(LOW)
                )
            return carry

        lax.fori_loop(low, high, one_block, 0)
        for pair in range(pairs):
            total = total_ref[pair : pair + 1, :]
            context = unstack_heads(sum_ref[pair] / total)
            o_ref[rows, pair * PAIR : (pair + 1) * PAIR] = jnp.transpose(context).astype(LOW)
            place = number * pairs + pair
            lse_ref[place : place + 1, :] = top_ref[pair : pair + 1, :] + jnp.log(total)


def attend_backward(
    q_ref,
    k_ref,
    v_ref,
    o_ref,
    grad_ref,
    lse_ref,
    dq_ref,
    dk_ref,
    dv_ref,
    key_row,
    columns_ref,
    query_row,
    start,
    causal,
    scratch,
):
    stack_ref, stack_grad_ref, sum_ref, along_ref = scratch
    pairs = q_ref.shape[1] // PAIR
    dk_ref[...] = jnp.zeros_like(dk_ref)
    dv_ref[...] = jnp.zeros_like(dv_ref)
    for number, rows in enumerate(row_blocks(q_ref.shape[0])):
        query_ids = query_row[:, number * BLOCK : (number + 1) * BLOCK]
        query_start = start + number * BLOCK
        low, high = key_bounds(key_row, query_ids, query_start, causal)
        for pair in range(pairs):
            lanes = slice(pair * PAIR, (pair + 1) * PAIR)
            grad = grad_ref[rows, lanes]
            stack_ref[pair] = stack_heads(q_ref[rows, lanes])
            stack_grad_ref[pair] = stack_heads(grad)
            along = jnp.transpose(grad.astype(WIDE) * o_ref[rows, lanes].astype(WIDE))
            along_ref[pair : pair + 1, :] = jnp.concatenate(
                [
                    jnp.sum(along[:DH], axis=0, keepdims=True),
                    jnp.sum(along[DH:], axis=0, keepdims=True),
                ],
                axis=1,
            )
        sum_ref[...] = jnp.zeros_like(sum_ref)

        def one_block(block, carry):
            key_start = pl.multiple_of(block * BLOCK, BLOCK)
            keys = pl.ds(key_start, BLOCK)
            bias = mask_bias(columns_ref[keys, :], query_ids, key_start, query_start, causal)
            for pair in range(pairs):
                lanes = slice(pair * PAIR, (pair + 1) * PAIR)
                place = number * pairs + pair
                key_pair = k_ref[keys, lanes]
                scores = dot_nt(key_pair, stack_ref[pair]) + bias
                probs = jnp.exp(scores - lse_ref[place : place + 1, :])
                prob_grad = dot_nt(v_ref[keys, lanes], stack_grad_ref[pair])
                score_grad = (probs * (prob_grad - along_ref[pair : pair + 1, :])).astype(LOW)
                dv_ref[keys, lanes] += dot_nn(probs.astype(LOW), stack_grad_ref[pair])
                dk_ref[keys, lanes] += dot_nn(score_grad, stack_ref[pair])
                sum_ref[pair] += dot_tn(key_pair, score_grad)
            return carry

        lax.fori_loop(low, high, one_block, 0)
        for pair in range(pairs):
            grad = jnp.transpose(unstack_heads(sum_ref[pair])) * FACTOR
            dq_ref[rows, pair * PAIR : (pair + 1) * PAIR] = grad.astype(LOW)


def store_pieces(grad_ref, keep_ref, send_ref, info_ref, order, offset, count, rows):
    half = count // 2
    for number in range(count):
        owner = info_ref[order + number]
        block = grad_ref[pl.ds(pl.multiple_of(owner * rows, rows), rows), :].astype(LOW)
        target = keep_ref if number < half else send_ref
        target[number % half, offset : offset + rows, :] = block


class Plan:
    def __init__(self, tokens, inner_weight):
        self.dp = lax.axis_size("dp")
        self.seq = lax.axis_size("seq")
        self.batches, _, self.chunk, self.width = tokens.shape
        self.hidden = inner_weight.shape[1]
        self.length = self.chunk * self.seq
        self.group = self.seq // self.batches
        self.rows = self.batches * self.chunk
        self.chunks = self.seq
        self.shard = self.width // self.dp
        self.outer_shard = self.hidden // self.dp
        self.hidden_blocks = self.hidden // self.width
        self.pairs = self.width // PAIR
        self.query_blocks = self.rows // BLOCK
        self.order = 0
        self.grad_order = self.dp
        self.chunk_order = 2 * self.dp
        self.own = self.chunk_order + self.chunks
        self.round = self.own + 1
        self.mates = self.round + self.batches
        self.batch = self.mates + self.group
        self.own_dp = self.batch + self.batches


def seg_rows(plan, raw_ref, seg_ref):
    for number in range(plan.chunks):
        lanes = slice(number * plan.chunk, (number + 1) * plan.chunk)
        seg_ref[0:1, lanes] = raw_ref[number, 0:1, : plan.chunk].astype(WIDE)
        seg_ref[1:2, lanes] = raw_ref[number, 0:1, plan.chunk : 2 * plan.chunk].astype(WIDE)


def own_rows(plan, info_ref):
    return pl.multiple_of(info_ref[plan.own] * plan.rows, plan.rows)


def chunk_copies(plan, chunks, info_ref, first, x_ref, raw_ref, semaphores):
    copies = []
    for number, chunk in enumerate(chunks):
        index = info_ref[plan.chunk_order + number]
        rows = pl.ds(pl.multiple_of(index * plan.chunk, plan.chunk), plan.chunk)
        copies.append(
            pltpu.make_async_copy(
                chunk.at[pl.ds(first, plan.chunk)], x_ref.at[rows], semaphores.at[0, number]
            )
        )
        if raw_ref is not None:
            copies.append(
                pltpu.make_async_copy(
                    chunk.at[pl.ds(2 * plan.chunk, TILE)],
                    raw_ref.at[index],
                    semaphores.at[1, number],
                )
            )
    return copies


def project_rows(count, source_ref, weight_of_key, weight_of_value, k_ref, v_ref):
    def project_block(block, carry):
        rows = pl.ds(pl.multiple_of(block * BLOCK, BLOCK), BLOCK)
        k_ref[rows, :] = dot_nn(source_ref[rows, :], weight_of_key()).astype(LOW)
        v_ref[rows, :] = dot_nn(source_ref[rows, :], weight_of_value()).astype(LOW)
        return carry

    lax.fori_loop(0, count // BLOCK, project_block, 0)


def forward_kernel(plan, chunk_count, piece_count, info_ref, *refs):
    chunks, refs = refs[:chunk_count], refs[chunk_count:]
    pieces, refs = refs[:piece_count], refs[piece_count:]
    (q_ref, k_ref, v_ref, o_ref, lse_ref, a_ref, seg_ref, vec_ref), refs = refs[:8], refs[8:]
    (cq_ref, ck_ref, cv_ref, co_ref, cross_lse_ref, z_ref), refs = refs[:6], refs[6:]
    x_ref, m_ref, raw_ref, w_ref, columns_ref, chunk_sems, m_sems, piece_sems, *scratch = refs
    load = chunk_copies(plan, chunks, info_ref, 0, x_ref, raw_ref, chunk_sems)
    load += chunk_copies(plan, chunks, info_ref, plan.chunk, m_ref, None, m_sems)
    load += piece_copies(plan, pieces, info_ref, w_ref, piece_sems)
    copy_all(load)
    shard = plan.shard
    start = own_rows(plan, info_ref)
    vec_ref[...] = jnp.sum(w_ref[:, 8 * shard :, :].astype(WIDE), axis=0)
    seg_rows(plan, raw_ref, seg_ref)
    columns_ref[...] = seg_columns(seg_ref[0:1, :])
    for rows in row_blocks(plan.rows):
        own = x_ref[pl.ds(start + rows.start, BLOCK), :]
        q_ref[rows, :] = (dot_nn(own, weight_of(w_ref, 0, shard)) * FACTOR).astype(LOW)
    project_rows(
        plan.length,
        x_ref,
        lambda: weight_of(w_ref, 1, shard),
        lambda: weight_of(w_ref, 2, shard),
        k_ref,
        v_ref,
    )
    attend_forward(
        q_ref,
        k_ref,
        v_ref,
        o_ref,
        lse_ref,
        seg_ref[0:1, :],
        columns_ref,
        seg_ref[0:1, pl.ds(start, plan.rows)],
        start,
        True,
        scratch,
    )
    gain, shift = vec_ref[0:1, :], vec_ref[1:2, :]
    for rows in row_blocks(plan.rows):
        own = x_ref[pl.ds(start + rows.start, BLOCK), :].astype(WIDE)
        a = own + dot_nn(o_ref[rows, :], weight_of(w_ref, 3, shard))
        a_ref[rows, :] = a
        normed, _ = normalise(a)
        first = normed * gain + shift
        z_ref[rows, :] = first
        cq_ref[rows, :] = (
            dot_nn(first.astype(LOW), weight_of(w_ref, 4, shard)) * FACTOR
        ).astype(LOW)
    project_rows(
        plan.length,
        m_ref,
        lambda: weight_of(w_ref, 5, shard),
        lambda: weight_of(w_ref, 6, shard),
        ck_ref,
        cv_ref,
    )
    columns_ref[...] = seg_columns(seg_ref[1:2, :])
    attend_forward(
        cq_ref,
        ck_ref,
        cv_ref,
        co_ref,
        cross_lse_ref,
        seg_ref[1:2, :],
        columns_ref,
        seg_ref[0:1, pl.ds(start, plan.rows)],
        start,
        False,
        scratch,
    )
    for rows in row_blocks(plan.rows):
        z_ref[rows, :] += dot_nn(co_ref[rows, :], weight_of(w_ref, 7, shard))


def feed_kernel(plan, piece_count, info_ref, *refs):
    batches = plan.batches
    upstreams, refs = refs[:batches], refs[batches:]
    pieces, refs = refs[:piece_count], refs[piece_count:]
    (z_ref, vec_ref), refs = refs[:2], refs[2:]
    outs, refs = refs[:batches], refs[batches:]
    (dh_ref, dvec_ref, keep_ref, send_ref), refs = refs[:4], refs[4:]
    inner_ref, outer_ref, low_ref, u_ref, r_ref, f_ref, up_ref, res_ref, gw_ref, *sems = refs
    piece_sems, up_sems = sems
    width, shard, blocks, outer_shard = (
        plan.width,
        plan.shard,
        plan.hidden_blocks,
        plan.outer_shard,
    )
    copies = []
    number = 0
    for piece in pieces:
        for slab in range(piece.shape[0]):
            owner = info_ref[plan.order + number]
            for block in range(blocks):
                copies.append(
                    pltpu.make_async_copy(
                        piece.at[slab, pl.ds(block * shard, shard)],
                        inner_ref.at[block, pl.ds(pl.multiple_of(owner * shard, shard), shard)],
                        piece_sems.at[block, number],
                    )
                )
            copies.append(
                pltpu.make_async_copy(
                    piece.at[slab, pl.ds(blocks * shard, outer_shard)],
                    outer_ref.at[pl.ds(pl.multiple_of(owner * outer_shard, outer_shard), outer_shard)],
                    piece_sems.at[blocks, number],
                )
            )
            number += 1
    for number in range(batches):
        index = info_ref[plan.round + number]
        rows = pl.ds(pl.multiple_of(index * plan.chunk, plan.chunk), plan.chunk)
        copies.append(
            pltpu.make_async_copy(
                upstreams[number],
                up_ref.at[rows],
                up_sems.at[number],
            )
        )
    copy_all(copies)
    gain_two, shift_two = vec_ref[2:3, :], vec_ref[3:4, :]
    gain_three, shift_three = vec_ref[4:5, :], vec_ref[5:6, :]
    gain_grad = jnp.zeros((1, width), WIDE)
    shift_grad = jnp.zeros((1, width), WIDE)
    for rows in row_blocks(plan.rows):
        normed, _ = normalise(z_ref[rows, :])
        second = normed * gain_two + shift_two
        f_ref[rows, :] = second
        low_ref[rows, :] = second.astype(LOW)

    def inner_block(block, carry):
        for rows in row_blocks(plan.rows):
            u = dot_nn(low_ref[rows, :], inner_ref[block])
            phi = 0.5 + 0.5 * lax.erf(u * (0.5**0.5))
            r_ref[block, rows, :] = (u * phi).astype(LOW)
            u_ref[block, rows, :] = phi + u * (jnp.exp(-0.5 * u * u) * 0.3989422804014327)
            outer = outer_ref[pl.ds(pl.multiple_of(block * width, width), width), :]
            f_ref[rows, :] += dot_nn(r_ref[block, rows, :], outer)
        return carry

    lax.fori_loop(0, blocks, inner_block, 0)
    for rows in row_blocks(plan.rows):
        normed, inverse = normalise(f_ref[rows, :])
        res_ref[rows, :] = (normed * gain_three + shift_three).astype(LOW)
        upstream = up_ref[rows, :].astype(WIDE)
        gain_grad += jnp.sum(upstream * normed, axis=0, keepdims=True)
        shift_grad += jnp.sum(upstream, axis=0, keepdims=True)
        feed_grad = norm_backward(upstream, normed, inverse, gain_three)
        dh_ref[rows, :] = feed_grad
        up_ref[rows, :] = feed_grad.astype(LOW)
    for number in range(batches):
        index = info_ref[plan.round + number]
        outs[number][...] = res_ref[pl.ds(pl.multiple_of(index * plan.chunk, plan.chunk), plan.chunk), :]

    def back_block(block, carry):
        outer = outer_ref[pl.ds(pl.multiple_of(block * width, width), width), :]
        du_ref = r_ref
        gw_ref[block] = dot_tn(r_ref[block], up_ref[...])
        for rows in row_blocks(plan.rows):
            dr = dot_nt(up_ref[rows, :], outer).astype(LOW).astype(WIDE)
            du_ref[block, rows, :] = (dr * u_ref[block, rows, :]).astype(LOW)
        for rows in row_blocks(plan.rows):
            dh_ref[rows, :] += dot_nt(du_ref[block, rows, :], inner_ref[block])
        return carry

    lax.fori_loop(0, blocks, back_block, 0)
    half = plan.dp // 2
    for number in range(plan.dp):
        owner = info_ref[plan.grad_order + number]
        target = keep_ref if number < half else send_ref
        first = owner * outer_shard
        block = lax.div(first, width)
        inside = pl.multiple_of(lax.rem(first, width), outer_shard)
        target[number % half, blocks * shard : blocks * shard + outer_shard, :] = gw_ref[
            block, pl.ds(inside, outer_shard), :
        ].astype(LOW)

    def inner_grad(block, carry):
        gw_ref[block] = dot_tn(low_ref[...], r_ref[block])
        return carry

    lax.fori_loop(0, blocks, inner_grad, 0)
    for block in range(blocks):
        store_pieces(
            gw_ref.at[block],
            keep_ref,
            send_ref,
            info_ref,
            plan.grad_order,
            block * shard,
            plan.dp,
            shard,
        )
    dvec_ref[...] = jnp.zeros_like(dvec_ref)
    dvec_ref[4:5, :] = gain_grad
    dvec_ref[5:6, :] = shift_grad


def norm_back(plan, line, z_ref, upstream_ref, vec_ref, w_ref, which, grad_ref, low_ref, do_ref):
    gain_grad = jnp.zeros((1, plan.width), WIDE)
    shift_grad = jnp.zeros((1, plan.width), WIDE)
    for rows in row_blocks(plan.rows):
        normed, inverse = normalise(z_ref[rows, :])
        upstream = upstream_ref[rows, :]
        gain_grad += jnp.sum(upstream * normed, axis=0, keepdims=True)
        shift_grad += jnp.sum(upstream, axis=0, keepdims=True)
        grad = norm_backward(upstream, normed, inverse, vec_ref[2 * line : 2 * line + 1, :])
        grad_ref[rows, :] = grad
        low_ref[rows, :] = grad.astype(LOW)
        do_ref[rows, :] = dot_nt(low_ref[rows, :], weight_of(w_ref, which, plan.shard)).astype(LOW)
    return gain_grad, shift_grad


def attention_back(plan, causal, info_ref, seg_ref, operands, results, buffers):
    q_ref, k_ref, v_ref, o_ref, do_ref, lse_ref = operands
    dq_ref, dkl_ref, dvl_ref = results
    columns_ref, dk_ref, dv_ref, *scratch = buffers
    start = own_rows(plan, info_ref)
    line = 0 if causal else 1
    columns_ref[...] = seg_columns(seg_ref[line : line + 1, :])
    attend_backward(
        q_ref,
        k_ref,
        v_ref,
        o_ref,
        do_ref,
        lse_ref,
        dq_ref,
        dk_ref,
        dv_ref,
        seg_ref[line : line + 1, :],
        columns_ref,
        seg_ref[0:1, pl.ds(start, plan.rows)],
        start,
        causal,
        scratch,
    )

    def round_block(block, carry):
        rows = pl.ds(pl.multiple_of(block * BLOCK, BLOCK), BLOCK)
        dkl_ref[rows, :] = dk_ref[rows, :].astype(LOW)
        dvl_ref[rows, :] = dv_ref[rows, :].astype(LOW)
        return carry

    lax.fori_loop(0, plan.length // BLOCK, round_block, 0)


def source_parts(plan, info_ref, dkl_ref, dvl_ref, w_ref, which, own_ref, add, mates):
    shard = plan.shard
    for number in range(plan.group):
        first = pl.multiple_of(info_ref[plan.mates + number] * plan.rows, plan.rows)
        for rows in row_blocks(plan.rows):
            source = pl.ds(first + rows.start, BLOCK)
            part = dot_nt(dkl_ref[source, :], weight_of(w_ref, which, shard)) + dot_nt(
                dvl_ref[source, :], weight_of(w_ref, which + 1, shard)
            )
            if number:
                mates[number - 1][rows, :] = part.astype(LOW)
            elif add:
                own_ref[rows, :] += part
            else:
                own_ref[rows, :] = part


def weight_products(plan, info_ref, products, gw_ref, keep_ref, send_ref):
    for which, (left, right) in enumerate(products):
        gw_ref[...] = dot_tn(left[...], right[...])
        store_pieces(
            gw_ref,
            keep_ref,
            send_ref,
            info_ref,
            plan.grad_order,
            which * plan.shard,
            plan.dp,
            plan.shard,
        )


def cross_backward_kernel(plan, chunk_count, piece_count, info_ref, *refs):
    chunks, refs = refs[:chunk_count], refs[chunk_count:]
    pieces, refs = refs[:piece_count], refs[piece_count:]
    (a_ref, z_ref, seg_ref, vec_ref, dvec_ref, dsecond_ref, context_ref), refs = refs[:7], refs[7:]
    (q_ref, k_ref, v_ref, o_ref, lse_ref), refs = refs[:5], refs[5:]
    own_ref, refs = refs[0], refs[1:]
    mates, refs = refs[: plan.group - 1], refs[plan.group - 1 :]
    (da_ref, self_do_ref, keep_ref, send_ref), refs = refs[:4], refs[4:]
    m_ref, w_ref, h_ref, gw_ref, grad_ref, low_ref, self_low_ref, *refs = refs
    do_ref, dq_ref, dkl_ref, dvl_ref, chunk_sems, piece_sems, *buffers = refs
    shard = plan.shard
    copies = chunk_copies(plan, chunks, info_ref, plan.chunk, m_ref, None, chunk_sems)
    copies += piece_copies(
        plan,
        [piece.at[:, pl.ds(3 * shard, 5 * shard)] for piece in pieces],
        info_ref,
        w_ref,
        piece_sems,
    )
    copy_all(copies)
    cross_terms = norm_back(
        plan, 1, z_ref, dsecond_ref, vec_ref, w_ref, 4, grad_ref, low_ref, do_ref
    )
    attention_back(
        plan,
        False,
        info_ref,
        seg_ref,
        (q_ref, k_ref, v_ref, o_ref, do_ref, lse_ref),
        (dq_ref, dkl_ref, dvl_ref),
        buffers,
    )
    for rows in row_blocks(plan.rows):
        grad_ref[rows, :] += dot_nt(dq_ref[rows, :], weight_of(w_ref, 1, shard))
        normed, _ = normalise(a_ref[rows, :])
        h_ref[rows, :] = (normed * vec_ref[0:1, :] + vec_ref[1:2, :]).astype(LOW)
    self_terms = norm_back(
        plan, 0, a_ref, grad_ref, vec_ref, w_ref, 0, da_ref, self_low_ref, self_do_ref
    )
    source_parts(plan, info_ref, dkl_ref, dvl_ref, w_ref, 2, own_ref, False, mates)
    products = (
        (h_ref, dq_ref),
        (m_ref, dkl_ref),
        (m_ref, dvl_ref),
        (o_ref, low_ref),
        (context_ref, self_low_ref),
    )
    weight_products(plan, info_ref, products, gw_ref, keep_ref, send_ref)
    tail = jnp.concatenate(
        [*self_terms, *cross_terms, dvec_ref[4:8, :], jnp.zeros((VECTOR_ROWS - 8, plan.width), WIDE)],
        axis=0,
    ).astype(LOW)
    for number in range(plan.dp // 2):
        keep_ref[number, 5 * shard :, :] = tail
        send_ref[number, 5 * shard :, :] = tail


def self_backward_kernel(plan, piece_count, info_ref, *refs):
    pieces, refs = refs[:piece_count], refs[piece_count:]
    (seg_ref, da_ref, do_ref, q_ref, k_ref, v_ref, o_ref, lse_ref), refs = refs[:8], refs[8:]
    (dq_ref, dkl_ref, dvl_ref, own_ref), refs = refs[:4], refs[4:]
    mates, refs = refs[: plan.group - 1], refs[plan.group - 1 :]
    w_ref, piece_sems, *buffers = refs
    copies = piece_copies(
        plan,
        [piece.at[:, pl.ds(0, 3 * plan.shard)] for piece in pieces],
        info_ref,
        w_ref,
        piece_sems,
    )
    copy_all(copies)
    attention_back(
        plan,
        True,
        info_ref,
        seg_ref,
        (q_ref, k_ref, v_ref, o_ref, do_ref, lse_ref),
        (dq_ref, dkl_ref, dvl_ref),
        buffers,
    )
    for rows in row_blocks(plan.rows):
        own_ref[rows, :] = da_ref[rows, :] + dot_nt(
            dq_ref[rows, :], weight_of(w_ref, 0, plan.shard)
        )
    source_parts(plan, info_ref, dkl_ref, dvl_ref, w_ref, 1, own_ref, True, mates)


def self_weights_kernel(plan, chunk_count, info_ref, *refs):
    chunks, refs = refs[:chunk_count], refs[chunk_count:]
    (dq_ref, dkl_ref, dvl_ref, keep_ref, send_ref), refs = refs[:5], refs[5:]
    x_ref, own_x_ref, gw_ref, chunk_sems = refs
    copy_all(chunk_copies(plan, chunks, info_ref, 0, x_ref, None, chunk_sems))
    start = own_rows(plan, info_ref)
    for rows in row_blocks(plan.rows):
        own_x_ref[rows, :] = x_ref[pl.ds(start + rows.start, BLOCK), :]
    products = ((own_x_ref, dq_ref), (x_ref, dkl_ref), (x_ref, dvl_ref))
    weight_products(plan, info_ref, products, gw_ref, keep_ref, send_ref)


SMEM = pl.BlockSpec(memory_space=pltpu.SMEM)
VMEM = pl.BlockSpec(memory_space=pltpu.VMEM)
ANY = pl.BlockSpec(memory_space=pl.ANY)


def call(kernel, specs, operands, outs, scratch, flops, moved):
    return pl.pallas_call(
        kernel,
        in_specs=specs,
        out_specs=[VMEM] * len(outs),
        out_shape=outs,
        scratch_shapes=scratch,
        compiler_params=pltpu.CompilerParams(vmem_limit_bytes=VMEM_LIMIT),
        cost_estimate=pl.CostEstimate(flops=flops, bytes_accessed=moved, transcendentals=0),
    )(*operands)


def shape(dims, dtype):
    return jax.ShapeDtypeStruct(dims, dtype)


def forward_scratch(plan):
    return [
        pltpu.VMEM((plan.pairs, 2 * BLOCK, PAIR), LOW),
        pltpu.VMEM((plan.pairs, PAIR, 2 * BLOCK), WIDE),
        pltpu.VMEM((8, 2 * BLOCK), WIDE),
        pltpu.VMEM((8, 2 * BLOCK), WIDE),
    ]


def backward_scratch(plan):
    return [
        pltpu.VMEM((plan.pairs, 2 * BLOCK, PAIR), LOW),
        pltpu.VMEM((plan.pairs, 2 * BLOCK, PAIR), LOW),
        pltpu.VMEM((plan.pairs, PAIR, 2 * BLOCK), WIDE),
        pltpu.VMEM((8, 2 * BLOCK), WIDE),
    ]


def flat(pieces):
    return sum(piece.shape[0] for piece in pieces)


def forward(plan, info, chunks, pieces):
    rows, length, width = plan.rows, plan.length, plan.width
    heads = [
        shape((rows, width), LOW),
        shape((length, width), LOW),
        shape((length, width), LOW),
        shape((rows, width), LOW),
        shape((plan.query_blocks * plan.pairs, 2 * BLOCK), WIDE),
        shape((rows, width), WIDE),
    ]
    outs = heads + [shape((8, length), WIDE), shape((TILE, width), WIDE)] + heads
    scratch = [
        pltpu.VMEM((length, width), LOW),
        pltpu.VMEM((length, width), LOW),
        pltpu.VMEM((plan.chunks, TILE, width), LOW),
        pltpu.VMEM((plan.dp, 8 * plan.shard + TILE, width), LOW),
        pltpu.VMEM((length, 128), WIDE),
        pltpu.SemaphoreType.DMA((2, plan.chunks)),
        pltpu.SemaphoreType.DMA((2, plan.chunks)),
        pltpu.SemaphoreType.DMA((plan.dp,)),
    ] + forward_scratch(plan)
    return call(
        functools.partial(forward_kernel, plan, len(chunks), len(pieces)),
        [SMEM] + [ANY] * (len(chunks) + len(pieces)),
        [info, *chunks, *pieces],
        outs,
        scratch,
        FORWARD_COST,
        10**5,
    )


def feed(plan, info, upstreams, pieces, z, vecs):
    rows, width, blocks = plan.rows, plan.width, plan.hidden_blocks
    piece_rows = blocks * plan.shard + plan.outer_shard
    outs = (
        [shape((plan.chunk, width), LOW)] * plan.batches
        + [shape((rows, width), WIDE), shape((8, width), WIDE)]
        + [shape((plan.dp // 2, piece_rows, width), LOW)] * 2
    )
    scratch = [
        pltpu.VMEM((blocks, width, width), LOW),
        pltpu.VMEM((plan.hidden, width), LOW),
        pltpu.VMEM((rows, width), LOW),
        pltpu.VMEM((blocks, rows, width), WIDE),
        pltpu.VMEM((blocks, rows, width), LOW),
        pltpu.VMEM((rows, width), WIDE),
        pltpu.VMEM((rows, width), LOW),
        pltpu.VMEM((rows, width), LOW),
        pltpu.VMEM((blocks, width, width), WIDE),
        pltpu.SemaphoreType.DMA((blocks + 1, plan.dp)),
        pltpu.SemaphoreType.DMA((plan.batches,)),
    ]
    return call(
        functools.partial(feed_kernel, plan, len(pieces)),
        [SMEM] + [ANY] * (plan.batches + len(pieces)) + [VMEM] * 2,
        [info, *upstreams, *pieces, z, vecs],
        outs,
        scratch,
        20 * 10**9,
        12 * 10**6,
    )


def backward_buffers(plan):
    length, width = plan.length, plan.width
    return [
        pltpu.VMEM((length, 128), WIDE),
        pltpu.VMEM((length, width), WIDE),
        pltpu.VMEM((length, width), WIDE),
        pltpu.VMEM((plan.pairs, 2 * BLOCK, PAIR), LOW),
        pltpu.VMEM((plan.pairs, 2 * BLOCK, PAIR), LOW),
        pltpu.VMEM((plan.pairs, PAIR, 2 * BLOCK), WIDE),
        pltpu.VMEM((8, 2 * BLOCK), WIDE),
    ]


def cross_backward(plan, info, chunks, pieces, operands):
    rows, length, width = plan.rows, plan.length, plan.width
    outs = (
        [shape((rows, width), WIDE)]
        + [shape((rows, width), LOW)] * (plan.group - 1)
        + [shape((rows, width), WIDE), shape((rows, width), LOW)]
        + [shape((plan.dp // 2, 5 * plan.shard + VECTOR_ROWS, width), LOW)] * 2
    )
    scratch = [
        pltpu.VMEM((length, width), LOW),
        pltpu.VMEM((plan.dp, 5 * plan.shard, width), LOW),
        pltpu.VMEM((rows, width), LOW),
        pltpu.VMEM((width, width), WIDE),
        pltpu.VMEM((rows, width), WIDE),
        pltpu.VMEM((rows, width), LOW),
        pltpu.VMEM((rows, width), LOW),
        pltpu.VMEM((rows, width), LOW),
        pltpu.VMEM((rows, width), LOW),
        pltpu.VMEM((length, width), LOW),
        pltpu.VMEM((length, width), LOW),
        pltpu.SemaphoreType.DMA((2, plan.chunks)),
        pltpu.SemaphoreType.DMA((plan.dp,)),
    ] + backward_buffers(plan)
    return call(
        functools.partial(cross_backward_kernel, plan, len(chunks), len(pieces)),
        [SMEM] + [ANY] * (len(chunks) + len(pieces)) + [VMEM] * len(operands),
        [info, *chunks, *pieces, *operands],
        outs,
        scratch,
        22 * 10**9,
        12 * 10**6,
    )


def self_backward(plan, info, pieces, operands):
    rows, length, width = plan.rows, plan.length, plan.width
    outs = [
        shape((rows, width), LOW),
        shape((length, width), LOW),
        shape((length, width), LOW),
        shape((rows, width), WIDE),
    ] + [shape((rows, width), LOW)] * (plan.group - 1)
    scratch = [
        pltpu.VMEM((plan.dp, 3 * plan.shard, width), LOW),
        pltpu.SemaphoreType.DMA((plan.dp,)),
    ] + backward_buffers(plan)
    return call(
        functools.partial(self_backward_kernel, plan, len(pieces)),
        [SMEM] + [ANY] * len(pieces) + [VMEM] * len(operands),
        [info, *pieces, *operands],
        outs,
        scratch,
        15 * 10**9,
        12 * 10**6,
    )


def self_weights(plan, info, chunks, operands):
    rows, length, width = plan.rows, plan.length, plan.width
    outs = [shape((plan.dp // 2, 3 * plan.shard, width), LOW)] * 2
    scratch = [
        pltpu.VMEM((length, width), LOW),
        pltpu.VMEM((rows, width), LOW),
        pltpu.VMEM((width, width), WIDE),
        pltpu.SemaphoreType.DMA((2, plan.chunks)),
    ]
    return call(
        functools.partial(self_weights_kernel, plan, len(chunks)),
        [SMEM] + [ANY] * len(chunks) + [VMEM] * len(operands),
        [info, *chunks, *operands],
        outs,
        scratch,
        6 * 10**9,
        6 * 10**6,
    )


def pack_first_kernel(plan, info_ref, *refs):
    weights, refs = refs[:8], refs[8:]
    (vectors, tokens, memory, target, source, piece_ref), rounds = refs[:6], refs[6:]
    shard, chunk, width = plan.shard, plan.chunk, plan.width
    for which in range(8):
        piece_ref[0, which * shard : (which + 1) * shard, :] = weights[which][...]
    lanes = pltpu.roll(vectors[...].astype(WIDE), info_ref[plan.own_dp] * shard, 1)
    piece_ref[0, 8 * shard :, :] = lanes.astype(LOW)
    first_row = lax.broadcasted_iota(jnp.int32, (TILE, width), 0) == 0
    for number in range(plan.batches):
        batch = info_ref[plan.batch + number]
        rounds[number][:chunk, :] = tokens[batch, 0]
        rounds[number][chunk : 2 * chunk, :] = memory[batch, 0]
        row = jnp.concatenate([target[batch], source[batch]], axis=1).astype(WIDE)
        if width > 2 * chunk:
            row = jnp.concatenate([row, jnp.zeros((1, width - 2 * chunk), WIDE)], axis=1)
        rounds[number][2 * chunk :, :] = jnp.where(first_row, row, 0.0).astype(LOW)


def pack_first(plan, info, weights, vectors, tokens, memory, target, source):
    outs = [shape((1, 8 * plan.shard + TILE, plan.width), LOW)]
    outs += [shape((2 * plan.chunk + TILE, plan.width), LOW)] * plan.batches
    return call(
        functools.partial(pack_first_kernel, plan),
        [SMEM] + [VMEM] * 13,
        [info, *weights, vectors, tokens, memory, target, source],
        outs,
        [],
        0,
        2 * 10**6,
    )


def pack_rest_kernel(plan, info_ref, inner, outer, cotangent, feed_ref, *rounds):
    shard, width, blocks = plan.shard, plan.width, plan.hidden_blocks
    for number in range(plan.batches):
        rounds[number][...] = cotangent[info_ref[plan.batch + number], 0]
    for block in range(blocks):
        feed_ref[0, block * shard : (block + 1) * shard, :] = inner[
            :, block * width : (block + 1) * width
        ]
    feed_ref[0, blocks * shard :, :] = outer[...]


def pack_rest(plan, info, inner, outer, cotangent):
    outs = [shape((1, plan.hidden_blocks * plan.shard + plan.outer_shard, plan.width), LOW)]
    outs += [shape((plan.chunk, plan.width), LOW)] * plan.batches
    return call(
        functools.partial(pack_rest_kernel, plan),
        [SMEM] + [VMEM] * 3,
        [info, inner, outer, cotangent],
        outs,
        [],
        0,
        2 * 10**6,
    )


def pairs_of(plan, move):
    return [
        (dp * plan.seq + seq, to[0] * plan.seq + to[1])
        for dp in range(plan.dp)
        for seq in range(plan.seq)
        for to in [move(dp, seq)]
    ]


def home(plan, dp, batch, seq):
    position = (2 * batch + dp % 2) * plan.group + seq // plan.batches
    return (dp - dp % 2 + position % 2, position // 2)


def round_batch(plan, seq, number):
    return (seq + number) % plan.batches


def inward(plan, number):
    return pairs_of(plan, lambda dp, seq: home(plan, dp, round_batch(plan, seq, number), seq))


def outward(plan, number):
    return [(to, source) for source, to in inward(plan, number)]


def mate(plan, turn):
    def move(dp, seq):
        position = 2 * seq + dp % 2
        group, own = position // plan.group, position % plan.group
        to = group * plan.group + (own + turn) % plan.group
        return (dp - dp % 2 + to % 2, to // 2)

    return pairs_of(plan, move)


def permute(values, pairs):
    return lax.ppermute(values, AXES, pairs)


def dp_flip(plan, bits):
    return pairs_of(plan, lambda dp, seq: (dp ^ bits, seq))


def seq_flip(plan, bits):
    return pairs_of(plan, lambda dp, seq: (dp, seq ^ bits))


def share_inputs(plan, rounds):
    return [permute(piece, inward(plan, number)) for number, piece in enumerate(rounds)]


def share_mates(plan, received):
    chunks = list(received)
    for turn in range(1, plan.group):
        chunks += [permute(piece, mate(plan, turn)) for piece in received]
    return chunks


def send_home(plan, pieces):
    return [permute(piece, outward(plan, number)) for number, piece in enumerate(pieces)]


def order_home(plan, landed, dtype):
    seq = lax.axis_index("seq")
    landed = jnp.stack(landed).astype(dtype)
    order = [(batch - seq) % plan.batches for batch in range(plan.batches)]
    return jnp.stack(
        [lax.dynamic_index_in_dim(landed, index, 0, keepdims=False) for index in order]
    )


def gather_direct(plan, shard):
    if plan.dp != 8:
        return [lax.all_gather(shard[0], "dp", axis=0)]
    return [shard] + [permute(shard, dp_flip(plan, bits)) for bits in (2, 4, 6)]


def gather_rest(plan, direct):
    if plan.dp != 8:
        return direct
    pieces = []
    for piece in direct:
        pieces += [piece, permute(piece, dp_flip(plan, 1))]
    return pieces


def add_low(values):
    total = values[0].astype(WIDE)
    for value in values[1:]:
        total = total + value.astype(WIDE)
    return total.astype(LOW)


def core_send(plan, send):
    return permute(send, dp_flip(plan, 1)) if plan.dp == 8 else send


def core_sum(plan, keep, other):
    if plan.dp != 8:
        return [jnp.concatenate([keep, other], axis=0)]
    return [add_low([keep[number], other[number]]) for number in range(4)]


def plane_send(plan, parts):
    if plan.dp != 8:
        return [lax.psum_scatter(parts[0], "dp", scatter_dimension=0)]
    return [permute(parts[number], dp_flip(plan, 2 * number)) for number in range(1, 4)]


def plane_sum(plan, parts, landed):
    total = landed[0] if plan.dp != 8 else add_low([parts[0], *landed])
    return total if plan.seq == 4 else lax.psum(total, "seq")


def halves(plan, total, bits):
    if plan.seq != 4:
        return total, jnp.zeros_like(total)
    half = total.shape[0] // 2
    own = lax.axis_index("seq") // bits % 2
    return (
        lax.dynamic_slice_in_dim(total, own * half, half),
        lax.dynamic_slice_in_dim(total, (1 - own) * half, half),
    )


def seq_send(plan, values, bits):
    return permute(values, seq_flip(plan, bits)) if plan.seq == 4 else jnp.zeros_like(values)


def join(plan, own_part, other, bits):
    if plan.seq != 4:
        return own_part
    own = lax.axis_index("seq") // bits % 2
    return jnp.where(
        own == 0, jnp.concatenate([own_part, other]), jnp.concatenate([other, own_part])
    )


def add_wide(first, second):
    return first.astype(WIDE) + second.astype(WIDE)


def after(values, *others):
    return lax.optimization_barrier((values, others))[0]


def plan_info(plan):
    dp, seq = lax.axis_index("dp"), lax.axis_index("seq")
    position = 2 * seq + dp % 2
    own = position % plan.group
    batch = position // plan.group // 2
    flips = list(range(8)) if plan.dp == 8 else None
    entries = []
    if flips:
        entries += [dp ^ bits for bits in (0, 1, 2, 3, 4, 5, 6, 7)]
        entries += [dp ^ bits for bits in (0, 2, 4, 6, 1, 3, 5, 7)]
    else:
        entries += list(range(plan.dp)) * 2
    places = [(batch - number) % plan.batches for number in range(plan.batches)]
    for turn in range(plan.group):
        source = (own - turn) % plan.group
        entries += [source * plan.batches + place for place in places]
    entries.append(own)
    entries += places
    entries += [(own + turn) % plan.group for turn in range(plan.group)]
    entries += [(seq + number) % plan.batches for number in range(plan.batches)]
    entries.append(dp)
    return jnp.stack([jnp.asarray(entry, jnp.int32) for entry in entries])


def on_device(
    tokens,
    memory,
    target_segments,
    source_segments,
    cotangent,
    query_weight,
    key_weight,
    value_weight,
    output_weight,
    cross_query,
    cross_key,
    cross_value,
    cross_output,
    inner_weight,
    outer_weight,
    self_gain,
    self_shift,
    cross_gain,
    cross_shift,
    feed_gain,
    feed_shift,
):
    plan = Plan(tokens, inner_weight)
    width, shard = plan.width, plan.shard
    info = plan_info(plan)
    dp = lax.axis_index("dp")

    vectors = jnp.stack([self_gain, self_shift, cross_gain, cross_shift, feed_gain, feed_shift])
    vectors = jnp.pad(vectors, ((0, TILE - 6), (0, width - shard)))
    shard_piece, *rounds = pack_first(
        plan,
        info,
        [
            query_weight,
            key_weight,
            value_weight,
            output_weight,
            cross_query,
            cross_key,
            cross_value,
            cross_output,
        ],
        vectors,
        tokens,
        memory,
        target_segments,
        source_segments,
    )
    direct = gather_direct(plan, shard_piece)
    landed = share_inputs(plan, rounds)

    feed_shard, *rounds = pack_rest(plan, info, inner_weight, outer_weight, cotangent)
    first = landed[0]
    direct, landed = after((direct, landed), feed_shard)
    feed_shard, rounds = after((feed_shard, rounds), first)
    feed_direct = gather_direct(plan, feed_shard)
    upstreams = share_inputs(plan, rounds)
    pieces = gather_rest(plan, direct)
    chunks = share_mates(plan, landed)
    q, k, v, o, lse, a, segs, vecs, cq, ck, cv, co, cross_lse, z = forward(
        plan, info, chunks, pieces
    )

    feed_direct, upstreams = after((feed_direct, upstreams), z)
    feed_pieces = gather_rest(plan, feed_direct)
    *results, dsecond, dvec, feed_keep, feed_send = feed(
        plan, info, upstreams, feed_pieces, z, vecs
    )

    feed_parts = core_sum(plan, feed_keep, core_send(plan, feed_send))
    out_landed = send_home(plan, results)
    feed_landed = plane_send(plan, feed_parts)
    dsecond = after(dsecond, feed_parts)
    back = cross_backward(
        plan,
        info,
        chunks,
        pieces,
        [a, z, segs, vecs, dvec, dsecond, o, cq, ck, cv, co, cross_lse],
    )
    back, feed_landed, out_landed = lax.optimization_barrier((back, feed_landed, out_landed))
    own_memory, *others = back
    mate_memory, (da, do, cross_keep, cross_send) = (
        others[: plan.group - 1],
        others[plan.group - 1 :],
    )

    feed_keep, feed_send = halves(plan, plane_sum(plan, feed_parts, feed_landed), 1)
    cross_parts = core_sum(plan, cross_keep, core_send(plan, cross_send))
    memory_pieces = add_mates(plan, info, own_memory, mate_memory)
    feed_landed = seq_send(plan, feed_send, 1)
    cross_landed = plane_send(plan, cross_parts)
    memory_landed = send_home(plan, memory_pieces)
    do = after(do, feed_send, cross_parts, memory_pieces)
    back = self_backward(plan, info, pieces, [segs, da, do, q, k, v, o, lse])
    back, feed_landed, cross_landed, memory_landed = lax.optimization_barrier(
        (back, feed_landed, cross_landed, memory_landed)
    )
    dq, dk, dv, own_tokens, *mate_tokens = back

    feed_keep, feed_send = halves(plan, add_low([feed_keep, feed_landed]), 2)
    cross_keep, cross_send = halves(plan, plane_sum(plan, cross_parts, cross_landed), 1)
    feed_landed = seq_send(plan, feed_send, 2)
    cross_landed = seq_send(plan, cross_send, 1)
    mate_landed = send_mates(plan, mate_tokens)
    dq = after(dq, feed_send, cross_send)
    self_keep, self_send = self_weights(plan, info, chunks, [dq, dk, dv])
    self_keep, self_send, feed_landed, cross_landed, mate_landed = lax.optimization_barrier(
        (self_keep, self_send, feed_landed, cross_landed, mate_landed)
    )

    self_landed = core_send(plan, self_send)
    token_pieces = sum_mates(plan, info, own_tokens, mate_landed)
    self_parts = core_sum(plan, self_keep, after(self_landed, token_pieces))
    self_landed = plane_send(plan, self_parts)
    token_landed = send_home(plan, after(token_pieces, self_parts))
    feed_quarter = add_low([after(feed_keep, token_pieces), feed_landed])
    cross_keep, cross_send = halves(
        plan, add_low([after(cross_keep, token_pieces), cross_landed]), 2
    )
    feed_landed = seq_send(plan, feed_quarter, 2)
    cross_landed = seq_send(plan, cross_send, 2)
    self_landed = after(self_landed, feed_quarter, cross_send)
    self_total = plane_sum(plan, self_parts, self_landed)
    self_landed = seq_send(plan, self_total, 1)
    feed_landed, cross_landed = after((feed_landed, cross_landed), self_total)
    feed_half = join(plan, feed_quarter, feed_landed, 2)
    cross_quarter = add_low([cross_keep, cross_landed])
    feed_landed = seq_send(plan, feed_half, 1)
    cross_landed = seq_send(plan, cross_quarter, 2)
    self_landed = after(self_landed, feed_half, cross_quarter)
    self_total = add_low([self_total, self_landed])
    self_landed = seq_send(plan, self_total, 2)
    cross_half = join(plan, cross_quarter, after(cross_landed, self_total), 2)
    cross_landed = seq_send(plan, cross_half, 1)
    feed_total = join(plan, feed_half, feed_landed, 1).astype(WIDE)
    cross_total = join(plan, cross_half, cross_landed, 1).astype(WIDE)
    self_total = add_wide(self_total, self_landed)
    out_tokens = order_home(plan, out_landed, LOW)
    grad_memory = order_home(plan, memory_landed, WIDE)
    grad_tokens = order_home(plan, token_landed, WIDE)
    scale = 1.0 / (plan.batches * plan.dp)
    feed_grads, cross_grads, self_grads = (
        feed_total * scale,
        cross_total * scale,
        self_total * scale,
    )
    inner_grads = [
        feed_grads[block * shard : (block + 1) * shard] for block in range(plan.hidden_blocks)
    ]
    vector_grads = lax.dynamic_slice(cross_grads, (5 * shard, dp * shard), (TILE, shard))
    return (
        out_tokens[:, None],
        grad_tokens[:, None],
        grad_memory[:, None],
        *[self_grads[which * shard : (which + 1) * shard] for which in range(3)],
        cross_grads[4 * shard : 5 * shard],
        *[cross_grads[which * shard : (which + 1) * shard] for which in range(4)],
        jnp.concatenate(inner_grads, axis=1),
        feed_grads[plan.hidden_blocks * shard :],
        *[vector_grads[which] for which in range(6)],
    )


def send_mates(plan, mates):
    return [permute(part, mate(plan, turn)) for turn, part in enumerate(mates, 1)]


def sum_mates(plan, info, own, landed):
    for part in landed:
        own = own + part.astype(WIDE)
    own = own.reshape(plan.batches, plan.chunk, plan.width)
    return [
        lax.dynamic_index_in_dim(own, info[plan.round + number], 0, keepdims=False).astype(LOW)
        for number in range(plan.batches)
    ]


def add_mates(plan, info, own, mates):
    return sum_mates(plan, info, own, send_mates(plan, mates))


def solution(mesh):
    tokens = P(None, "dp", "seq", None)
    ids = P(None, "dp", "seq")
    weight = P("dp", None)
    vector = P("dp")
    return jax.shard_map(
        on_device,
        mesh=mesh,
        in_specs=(tokens, tokens, ids, ids, tokens) + (weight,) * 10 + (vector,) * 6,
        out_specs=(tokens,) * 3 + (weight,) * 10 + (vector,) * 6,
        check_vma=False,
    )
```

```python
import functools

import jax
import jax.numpy as jnp
from jax import lax
from jax.experimental import pallas as pl
from jax.experimental.pallas import tpu as pltpu
from jax.sharding import PartitionSpec as P

DH = 64
PAIR = 2 * DH
BLOCK = 256
TILE = 16
VECTOR_ROWS = 64
FORWARD_COST = 10**6
EPSILON = 1e-05
NEGATIVE = -1e30
FACTOR = DH ** (-0.5)
AXES = ("dp", "seq")
LOW = jnp.bfloat16
WIDE = jnp.float32
MEGABYTE = 1024 * 1024


def dot_nn(a, b):
    return jnp.dot(a, b, preferred_element_type=WIDE)


def dot_nt(a, b):
    return lax.dot_general(a, b, (((1,), (1,)), ((), ())), preferred_element_type=WIDE)


def dot_tn(a, b):
    return lax.dot_general(a, b, (((0,), (0,)), ((), ())), preferred_element_type=WIDE)


def normalise(values):
    centred = values - jnp.mean(values, axis=-1, keepdims=True)
    inverse = lax.rsqrt(jnp.mean(centred * centred, axis=-1, keepdims=True) + EPSILON)
    return centred * inverse, inverse


def norm_backward(upstream, normed, inverse, gain_row):
    scaled = upstream * gain_row
    plain_mean = jnp.mean(scaled, axis=-1, keepdims=True)
    along_mean = jnp.mean(scaled * normed, axis=-1, keepdims=True)
    return inverse * (scaled - plain_mean - normed * along_mean)


def row_blocks(length, size=BLOCK):
    return [pl.ds(start, size) for start in range(0, length, size)]


def copy_all(copies):
    for copy in copies:
        copy.start()
    for copy in copies:
        copy.wait()


def piece_copies(plan, pieces, info_ref, w_ref, semaphores):
    copies = []
    for piece in pieces:
        for slab in range(piece.shape[0]):
            number = len(copies)
            owner = info_ref[plan.order + number]
            copies.append(
                pltpu.make_async_copy(piece.at[slab], w_ref.at[owner], semaphores.at[number])
            )
    return copies


def weight_of(weight_ref, which, rows):
    count, _, width = weight_ref.shape
    return weight_ref[:, which * rows : (which + 1) * rows, :].reshape(count * rows, width)


def seg_columns(seg_row):
    return jnp.transpose(jnp.broadcast_to(seg_row, (128, seg_row.shape[1])))


def stack_heads(pair):
    lane = lax.broadcasted_iota(jnp.int32, pair.shape, 1)
    zero = jnp.zeros_like(pair)
    return jnp.concatenate(
        [jnp.where(lane < DH, pair, zero), jnp.where(lane < DH, zero, pair)], axis=0
    )


def unstack_heads(columns):
    row = lax.broadcasted_iota(jnp.int32, (PAIR, BLOCK), 0)
    return jnp.where(row < DH, columns[:, :BLOCK], columns[:, BLOCK:])


def mask_bias(key_ids, query_ids, key_start, query_start, causal):
    ids = jnp.concatenate([key_ids, key_ids], axis=1)
    allowed = ids == query_ids
    if causal:
        key_place = key_start + lax.broadcasted_iota(jnp.int32, (BLOCK, BLOCK), 0)
        query_place = query_start + lax.broadcasted_iota(jnp.int32, (BLOCK, BLOCK), 1)
        allowed = jnp.logical_and(allowed, key_place <= query_place)
    bias = jnp.where(allowed, 0.0, NEGATIVE)
    return jnp.concatenate([bias, bias], axis=1)


def key_bounds(key_row, query_ids, query_start, causal):
    below = jnp.sum(jnp.where(key_row < jnp.min(query_ids), 1.0, 0.0)).astype(jnp.int32)
    first = lax.div(below, BLOCK)
    if causal:
        return first, lax.div(query_start, BLOCK) + 1
    upto = jnp.sum(jnp.where(key_row <= jnp.max(query_ids), 1.0, 0.0)).astype(jnp.int32)
    return first, lax.div(upto + (BLOCK - 1), BLOCK)


def attend_forward(
    q_ref, k_ref, v_ref, o_ref, lse_ref, key_row, columns_ref, query_row, start, causal, scratch
):
    stack_ref, sum_ref, top_ref, total_ref = scratch
    pairs = q_ref.shape[1] // PAIR
    for number, rows in enumerate(row_blocks(q_ref.shape[0])):
        query_ids = query_row[:, number * BLOCK : (number + 1) * BLOCK]
        query_start = start + number * BLOCK
        low, high = key_bounds(key_row, query_ids, query_start, causal)
        for pair in range(pairs):
            stack_ref[pair] = stack_heads(q_ref[rows, pair * PAIR : (pair + 1) * PAIR])
        sum_ref[...] = jnp.zeros_like(sum_ref)
        top_ref[...] = jnp.full_like(top_ref, NEGATIVE)
        total_ref[...] = jnp.zeros_like(total_ref)

        def one_block(block, carry):
            key_start = pl.multiple_of(block * BLOCK, BLOCK)
            keys = pl.ds(key_start, BLOCK)
            bias = mask_bias(columns_ref[keys, :], query_ids, key_start, query_start, causal)
            values = [
                (
                    k_ref[keys, pair * PAIR : (pair + 1) * PAIR],
                    v_ref[keys, pair * PAIR : (pair + 1) * PAIR],
                    stack_ref[pair],
                    top_ref[pair : pair + 1, :],
                    total_ref[pair : pair + 1, :],
                    sum_ref[pair],
                )
                for pair in range(pairs)
            ]
            scores = [dot_nt(key_pair, queries) + bias for key_pair, _, queries, *_ in values]
            tops = [
                jnp.maximum(value[3], jnp.max(score, axis=0, keepdims=True))
                for value, score in zip(values, scores)
            ]
            exponents = [jnp.exp(score - top) for score, top in zip(scores, tops)]
            shrinks = [jnp.exp(value[3] - top) for value, top in zip(values, tops)]
            totals = [
                value[4] * shrink + jnp.sum(exponent, axis=0, keepdims=True)
                for value, shrink, exponent in zip(values, shrinks, exponents)
            ]
            sums = [
                value[5] * shrink + dot_tn(value[1], exponent.astype(LOW))
                for value, shrink, exponent in zip(values, shrinks, exponents)
            ]
            for pair in range(pairs):
                top_ref[pair : pair + 1, :] = tops[pair]
                total_ref[pair : pair + 1, :] = totals[pair]
                sum_ref[pair] = sums[pair]
            return carry

        lax.fori_loop(low, high, one_block, 0)
        for pair in range(pairs):
            total = total_ref[pair : pair + 1, :]
            context = unstack_heads(sum_ref[pair] / total)
            o_ref[rows, pair * PAIR : (pair + 1) * PAIR] = jnp.transpose(context).astype(LOW)
            place = number * pairs + pair
            lse_ref[place : place + 1, :] = top_ref[pair : pair + 1, :] + jnp.log(total)


def attend_backward(
    q_ref,
    k_ref,
    v_ref,
    o_ref,
    grad_ref,
    lse_ref,
    dq_ref,
    dk_ref,
    dv_ref,
    key_row,
    columns_ref,
    query_row,
    start,
    causal,
    scratch,
):
    stack_ref, stack_grad_ref, sum_ref, along_ref = scratch
    pairs = q_ref.shape[1] // PAIR
    dk_ref[...] = jnp.zeros_like(dk_ref)
    dv_ref[...] = jnp.zeros_like(dv_ref)
    for number, rows in enumerate(row_blocks(q_ref.shape[0])):
        query_ids = query_row[:, number * BLOCK : (number + 1) * BLOCK]
        query_start = start + number * BLOCK
        low, high = key_bounds(key_row, query_ids, query_start, causal)
        for pair in range(pairs):
            lanes = slice(pair * PAIR, (pair + 1) * PAIR)
            grad = grad_ref[rows, lanes]
            stack_ref[pair] = stack_heads(q_ref[rows, lanes])
            stack_grad_ref[pair] = stack_heads(grad)
            along = jnp.transpose(grad.astype(WIDE) * o_ref[rows, lanes].astype(WIDE))
            along_ref[pair : pair + 1, :] = jnp.concatenate(
                [
                    jnp.sum(along[:DH], axis=0, keepdims=True),
                    jnp.sum(along[DH:], axis=0, keepdims=True),
                ],
                axis=1,
            )
        sum_ref[...] = jnp.zeros_like(sum_ref)

        def one_block(block, carry):
            key_start = pl.multiple_of(block * BLOCK, BLOCK)
            keys = pl.ds(key_start, BLOCK)
            bias = mask_bias(columns_ref[keys, :], query_ids, key_start, query_start, causal)
            for pair in range(pairs):
                lanes = slice(pair * PAIR, (pair + 1) * PAIR)
                place = number * pairs + pair
                key_pair = k_ref[keys, lanes]
                scores = dot_nt(key_pair, stack_ref[pair]) + bias
                probs = jnp.exp(scores - lse_ref[place : place + 1, :])
                prob_grad = dot_nt(v_ref[keys, lanes], stack_grad_ref[pair])
                score_grad = (probs * (prob_grad - along_ref[pair : pair + 1, :])).astype(LOW)
                dv_ref[keys, lanes] += dot_nn(probs.astype(LOW), stack_grad_ref[pair])
                dk_ref[keys, lanes] += dot_nn(score_grad, stack_ref[pair])
                sum_ref[pair] += dot_tn(key_pair, score_grad)
            return carry

        lax.fori_loop(low, high, one_block, 0)
        for pair in range(pairs):
            grad = jnp.transpose(unstack_heads(sum_ref[pair])) * FACTOR
            dq_ref[rows, pair * PAIR : (pair + 1) * PAIR] = grad.astype(LOW)


def store_pieces(grad_ref, keep_ref, send_ref, info_ref, order, offset, count, rows):
    half = count // 2
    for number in range(count):
        owner = info_ref[order + number]
        block = grad_ref[pl.ds(pl.multiple_of(owner * rows, rows), rows), :]
        target = keep_ref if number < half else send_ref
        target[number % half, offset : offset + rows, :] = block


class Plan:
    def __init__(self, tokens, inner_weight):
        self.dp = lax.axis_size("dp")
        self.seq = lax.axis_size("seq")
        self.batches, _, self.chunk, self.width = tokens.shape
        self.hidden = inner_weight.shape[1]
        self.length = self.chunk * self.seq
        self.group = self.seq // self.batches
        self.rows = self.batches * self.chunk
        self.chunks = self.seq
        self.shard = self.width // self.dp
        self.outer_shard = self.hidden // self.dp
        self.hidden_blocks = self.hidden // self.width
        self.pairs = self.width // PAIR
        self.query_blocks = self.rows // BLOCK
        self.order = 0
        self.grad_order = self.dp
        self.chunk_order = 2 * self.dp
        self.own = self.chunk_order + self.chunks
        self.round = self.own + 1
        self.mates = self.round + self.batches
        self.batch = self.mates + self.group
        self.own_dp = self.batch + self.batches


def megabytes(plan, fixed, by_length):
    return fixed + -(-by_length * plan.length // 1024)


def seg_rows(plan, raw_ref, seg_ref):
    for number in range(plan.chunks):
        lanes = slice(number * plan.chunk, (number + 1) * plan.chunk)
        seg_ref[0:1, lanes] = raw_ref[number, 0:1, : plan.chunk].astype(WIDE)
        seg_ref[1:2, lanes] = raw_ref[number, 0:1, plan.chunk : 2 * plan.chunk].astype(WIDE)


def own_rows(plan, info_ref):
    return pl.multiple_of(info_ref[plan.own] * plan.rows, plan.rows)


def chunk_copies(plan, chunks, info_ref, first, x_ref, raw_ref, semaphores):
    copies = []
    for number, chunk in enumerate(chunks):
        index = info_ref[plan.chunk_order + number]
        rows = pl.ds(pl.multiple_of(index * plan.chunk, plan.chunk), plan.chunk)
        copies.append(
            pltpu.make_async_copy(
                chunk.at[pl.ds(first, plan.chunk)], x_ref.at[rows], semaphores.at[0, number]
            )
        )
        if raw_ref is not None:
            copies.append(
                pltpu.make_async_copy(
                    chunk.at[pl.ds(2 * plan.chunk, TILE)],
                    raw_ref.at[index],
                    semaphores.at[1, number],
                )
            )
    return copies


def project_rows(length, source_ref, key_weight, value_weight, k_ref, v_ref):
    for rows in row_blocks(length, 2 * BLOCK):
        k_ref[rows, :] = dot_nn(source_ref[rows, :], key_weight).astype(LOW)
        v_ref[rows, :] = dot_nn(source_ref[rows, :], value_weight).astype(LOW)


def forward_kernel(plan, chunk_count, piece_count, info_ref, *refs):
    chunks, refs = refs[:chunk_count], refs[chunk_count:]
    pieces, refs = refs[:piece_count], refs[piece_count:]
    (q_ref, k_ref, v_ref, o_ref, lse_ref, a_ref, seg_ref, vec_ref), refs = refs[:8], refs[8:]
    (cq_ref, ck_ref, cv_ref, co_ref, cross_lse_ref, z_ref), refs = refs[:6], refs[6:]
    x_ref, m_ref, raw_ref, w_ref, columns_ref, chunk_sems, m_sems, piece_sems, *scratch = refs
    load = chunk_copies(plan, chunks, info_ref, 0, x_ref, raw_ref, chunk_sems)
    load += chunk_copies(plan, chunks, info_ref, plan.chunk, m_ref, None, m_sems)
    load += piece_copies(plan, pieces, info_ref, w_ref, piece_sems)
    copy_all(load)
    shard = plan.shard
    start = own_rows(plan, info_ref)
    vec_ref[...] = jnp.sum(w_ref[:, 8 * shard :, :].astype(WIDE), axis=0)
    seg_rows(plan, raw_ref, seg_ref)
    columns_ref[...] = seg_columns(seg_ref[0:1, :])
    for rows in row_blocks(plan.rows):
        own = x_ref[pl.ds(start + rows.start, BLOCK), :]
        q_ref[rows, :] = (dot_nn(own, weight_of(w_ref, 0, shard)) * FACTOR).astype(LOW)
    project_rows(
        plan.length,
        x_ref,
        weight_of(w_ref, 1, shard),
        weight_of(w_ref, 2, shard),
        k_ref,
        v_ref,
    )
    attend_forward(
        q_ref,
        k_ref,
        v_ref,
        o_ref,
        lse_ref,
        seg_ref[0:1, :],
        columns_ref,
        seg_ref[0:1, pl.ds(start, plan.rows)],
        start,
        True,
        scratch,
    )
    gain, shift = vec_ref[0:1, :], vec_ref[1:2, :]
    for rows in row_blocks(plan.rows):
        own = x_ref[pl.ds(start + rows.start, BLOCK), :].astype(WIDE)
        a = own + dot_nn(o_ref[rows, :], weight_of(w_ref, 3, shard))
        a_ref[rows, :] = a
        normed, _ = normalise(a)
        first = normed * gain + shift
        z_ref[rows, :] = first
        cq_ref[rows, :] = (
            dot_nn(first.astype(LOW), weight_of(w_ref, 4, shard)) * FACTOR
        ).astype(LOW)
    project_rows(
        plan.length,
        m_ref,
        weight_of(w_ref, 5, shard),
        weight_of(w_ref, 6, shard),
        ck_ref,
        cv_ref,
    )
    columns_ref[...] = seg_columns(seg_ref[1:2, :])
    attend_forward(
        cq_ref,
        ck_ref,
        cv_ref,
        co_ref,
        cross_lse_ref,
        seg_ref[1:2, :],
        columns_ref,
        seg_ref[0:1, pl.ds(start, plan.rows)],
        start,
        False,
        scratch,
    )
    for rows in row_blocks(plan.rows):
        z_ref[rows, :] += dot_nn(co_ref[rows, :], weight_of(w_ref, 7, shard))


def feed_kernel(plan, piece_count, info_ref, *refs):
    batches = plan.batches
    upstreams, refs = refs[:batches], refs[batches:]
    pieces, refs = refs[:piece_count], refs[piece_count:]
    (z_ref, vec_ref), refs = refs[:2], refs[2:]
    outs, refs = refs[:batches], refs[batches:]
    (dh_ref, dvec_ref, keep_ref, send_ref), refs = refs[:4], refs[4:]
    inner_ref, outer_ref, low_ref, u_ref, r_ref, du_ref, f_ref, up_ref, res_ref, *refs = refs
    inner_gw_ref, outer_gw_ref, piece_sems, up_sems = refs
    width, shard, blocks, outer_shard = (
        plan.width,
        plan.shard,
        plan.hidden_blocks,
        plan.outer_shard,
    )
    copies = []
    number = 0
    for piece in pieces:
        for slab in range(piece.shape[0]):
            owner = info_ref[plan.order + number]
            for block in range(blocks):
                copies.append(
                    pltpu.make_async_copy(
                        piece.at[slab, pl.ds(block * shard, shard)],
                        inner_ref.at[
                            pl.ds(pl.multiple_of(owner * shard, shard), shard),
                            pl.ds(block * width, width),
                        ],
                        piece_sems.at[block, number],
                    )
                )
            copies.append(
                pltpu.make_async_copy(
                    piece.at[slab, pl.ds(blocks * shard, outer_shard)],
                    outer_ref.at[pl.ds(pl.multiple_of(owner * outer_shard, outer_shard), outer_shard)],
                    piece_sems.at[blocks, number],
                )
            )
            number += 1
    for number in range(batches):
        index = info_ref[plan.round + number]
        rows = pl.ds(pl.multiple_of(index * plan.chunk, plan.chunk), plan.chunk)
        copies.append(
            pltpu.make_async_copy(upstreams[number], up_ref.at[rows], up_sems.at[number])
        )
    for copy in copies:
        copy.start()
    gain_two, shift_two = vec_ref[2:3, :], vec_ref[3:4, :]
    gain_three, shift_three = vec_ref[4:5, :], vec_ref[5:6, :]
    gain_grad = jnp.zeros((1, width), WIDE)
    shift_grad = jnp.zeros((1, width), WIDE)
    for rows in row_blocks(plan.rows):
        normed, _ = normalise(z_ref[rows, :])
        second = normed * gain_two + shift_two
        f_ref[rows, :] = second
        low_ref[rows, :] = second.astype(LOW)
    for copy in copies:
        copy.wait()
    lanes = [slice(block * width, (block + 1) * width) for block in range(blocks)]
    for part in lanes:
        u = dot_nn(low_ref[...], inner_ref[:, part])
        phi = 0.5 + 0.5 * lax.erf(u * (0.5**0.5))
        r_ref[:, part] = (u * phi).astype(LOW)
        u_ref[:, part] = phi + u * (jnp.exp(-0.5 * u * u) * 0.3989422804014327)
    for rows in row_blocks(plan.rows):
        f = f_ref[rows, :] + dot_nn(r_ref[rows, :], outer_ref[...])
        normed, inverse = normalise(f)
        res_ref[rows, :] = (normed * gain_three + shift_three).astype(LOW)
        upstream = up_ref[rows, :].astype(WIDE)
        gain_grad += jnp.sum(upstream * normed, axis=0, keepdims=True)
        shift_grad += jnp.sum(upstream, axis=0, keepdims=True)
        feed_grad = norm_backward(upstream, normed, inverse, gain_three)
        dh_ref[rows, :] = feed_grad
        up_ref[rows, :] = feed_grad.astype(LOW)
    for number in range(batches):
        index = info_ref[plan.round + number]
        outs[number][...] = res_ref[pl.ds(pl.multiple_of(index * plan.chunk, plan.chunk), plan.chunk), :]
    for part in lanes:
        dr = dot_nt(up_ref[...], outer_ref[part, :]).astype(LOW).astype(WIDE)
        du_ref[:, part] = (dr * u_ref[:, part]).astype(LOW)
        outer_gw_ref[part, :] = dot_tn(r_ref[:, part], up_ref[...]).astype(LOW)
    for block, part in enumerate(lanes):
        inner_gw_ref[block] = dot_tn(low_ref[...], du_ref[:, part]).astype(LOW)
    for rows in row_blocks(plan.rows):
        dh_ref[rows, :] += dot_nt(du_ref[rows, :], inner_ref[...])
    for block in range(blocks):
        store_pieces(
            inner_gw_ref.at[block],
            keep_ref,
            send_ref,
            info_ref,
            plan.grad_order,
            block * shard,
            plan.dp,
            shard,
        )
    store_pieces(
        outer_gw_ref,
        keep_ref,
        send_ref,
        info_ref,
        plan.grad_order,
        blocks * shard,
        plan.dp,
        outer_shard,
    )
    dvec_ref[...] = jnp.zeros_like(dvec_ref)
    dvec_ref[4:5, :] = gain_grad
    dvec_ref[5:6, :] = shift_grad


def norm_back(plan, line, z_ref, upstream_ref, vec_ref, w_ref, which, grad_ref, low_ref, do_ref):
    gain_grad = jnp.zeros((1, plan.width), WIDE)
    shift_grad = jnp.zeros((1, plan.width), WIDE)
    for rows in row_blocks(plan.rows):
        normed, inverse = normalise(z_ref[rows, :])
        upstream = upstream_ref[rows, :]
        gain_grad += jnp.sum(upstream * normed, axis=0, keepdims=True)
        shift_grad += jnp.sum(upstream, axis=0, keepdims=True)
        grad = norm_backward(upstream, normed, inverse, vec_ref[2 * line : 2 * line + 1, :])
        grad_ref[rows, :] = grad
        low_ref[rows, :] = grad.astype(LOW)
        do_ref[rows, :] = dot_nt(low_ref[rows, :], weight_of(w_ref, which, plan.shard)).astype(LOW)
    return gain_grad, shift_grad


def attention_back(plan, causal, info_ref, seg_ref, operands, results, buffers):
    q_ref, k_ref, v_ref, o_ref, do_ref, lse_ref = operands
    dq_ref, dkl_ref, dvl_ref = results
    columns_ref, dk_ref, dv_ref, *scratch = buffers
    start = own_rows(plan, info_ref)
    line = 0 if causal else 1
    columns_ref[...] = seg_columns(seg_ref[line : line + 1, :])
    attend_backward(
        q_ref,
        k_ref,
        v_ref,
        o_ref,
        do_ref,
        lse_ref,
        dq_ref,
        dk_ref,
        dv_ref,
        seg_ref[line : line + 1, :],
        columns_ref,
        seg_ref[0:1, pl.ds(start, plan.rows)],
        start,
        causal,
        scratch,
    )

    def round_block(block, carry):
        rows = pl.ds(pl.multiple_of(block * BLOCK, BLOCK), BLOCK)
        dkl_ref[rows, :] = dk_ref[rows, :].astype(LOW)
        dvl_ref[rows, :] = dv_ref[rows, :].astype(LOW)
        return carry

    lax.fori_loop(0, plan.length // BLOCK, round_block, 0)


def source_parts(plan, info_ref, dkl_ref, dvl_ref, w_ref, which, own_ref, add, mates):
    shard = plan.shard
    for number in range(plan.group):
        first = pl.multiple_of(info_ref[plan.mates + number] * plan.rows, plan.rows)
        for rows in row_blocks(plan.rows):
            source = pl.ds(first + rows.start, BLOCK)
            part = dot_nt(dkl_ref[source, :], weight_of(w_ref, which, shard)) + dot_nt(
                dvl_ref[source, :], weight_of(w_ref, which + 1, shard)
            )
            if number:
                mates[number - 1][rows, :] = part.astype(LOW)
            elif add:
                own_ref[rows, :] += part
            else:
                own_ref[rows, :] = part


def weight_products(plan, info_ref, products, gw_ref, keep_ref, send_ref):
    for which, (left, right) in enumerate(products):
        gw_ref[which] = dot_tn(left[...], right[...]).astype(LOW)
    for which in range(len(products)):
        store_pieces(
            gw_ref.at[which],
            keep_ref,
            send_ref,
            info_ref,
            plan.grad_order,
            which * plan.shard,
            plan.dp,
            plan.shard,
        )


def cross_backward_kernel(plan, chunk_count, piece_count, info_ref, *refs):
    chunks, refs = refs[:chunk_count], refs[chunk_count:]
    pieces, refs = refs[:piece_count], refs[piece_count:]
    (a_ref, z_ref, seg_ref, vec_ref, dvec_ref, dsecond_ref, context_ref), refs = refs[:7], refs[7:]
    (q_ref, k_ref, v_ref, o_ref, lse_ref), refs = refs[:5], refs[5:]
    own_ref, refs = refs[0], refs[1:]
    mates, refs = refs[: plan.group - 1], refs[plan.group - 1 :]
    (da_ref, self_do_ref, keep_ref, send_ref), refs = refs[:4], refs[4:]
    m_ref, w_ref, h_ref, gw_ref, grad_ref, low_ref, self_low_ref, *refs = refs
    do_ref, dq_ref, dkl_ref, dvl_ref, chunk_sems, piece_sems, *buffers = refs
    shard = plan.shard
    copies = chunk_copies(plan, chunks, info_ref, plan.chunk, m_ref, None, chunk_sems)
    copies += piece_copies(
        plan,
        [piece.at[:, pl.ds(3 * shard, 5 * shard)] for piece in pieces],
        info_ref,
        w_ref,
        piece_sems,
    )
    copy_all(copies)
    cross_terms = norm_back(
        plan, 1, z_ref, dsecond_ref, vec_ref, w_ref, 4, grad_ref, low_ref, do_ref
    )
    attention_back(
        plan,
        False,
        info_ref,
        seg_ref,
        (q_ref, k_ref, v_ref, o_ref, do_ref, lse_ref),
        (dq_ref, dkl_ref, dvl_ref),
        buffers,
    )
    for rows in row_blocks(plan.rows):
        grad_ref[rows, :] += dot_nt(dq_ref[rows, :], weight_of(w_ref, 1, shard))
        normed, _ = normalise(a_ref[rows, :])
        h_ref[rows, :] = (normed * vec_ref[0:1, :] + vec_ref[1:2, :]).astype(LOW)
    self_terms = norm_back(
        plan, 0, a_ref, grad_ref, vec_ref, w_ref, 0, da_ref, self_low_ref, self_do_ref
    )
    source_parts(plan, info_ref, dkl_ref, dvl_ref, w_ref, 2, own_ref, False, mates)
    products = (
        (h_ref, dq_ref),
        (m_ref, dkl_ref),
        (m_ref, dvl_ref),
        (o_ref, low_ref),
        (context_ref, self_low_ref),
    )
    weight_products(plan, info_ref, products, gw_ref, keep_ref, send_ref)
    tail = jnp.concatenate(
        [*self_terms, *cross_terms, dvec_ref[4:8, :], jnp.zeros((VECTOR_ROWS - 8, plan.width), WIDE)],
        axis=0,
    ).astype(LOW)
    for number in range(plan.dp // 2):
        keep_ref[number, 5 * shard :, :] = tail
        send_ref[number, 5 * shard :, :] = tail


def self_backward_kernel(plan, piece_count, info_ref, *refs):
    pieces, refs = refs[:piece_count], refs[piece_count:]
    (seg_ref, da_ref, do_ref, q_ref, k_ref, v_ref, o_ref, lse_ref), refs = refs[:8], refs[8:]
    (dq_ref, dkl_ref, dvl_ref, own_ref), refs = refs[:4], refs[4:]
    mates, refs = refs[: plan.group - 1], refs[plan.group - 1 :]
    w_ref, piece_sems, *buffers = refs
    copies = piece_copies(
        plan,
        [piece.at[:, pl.ds(0, 3 * plan.shard)] for piece in pieces],
        info_ref,
        w_ref,
        piece_sems,
    )
    copy_all(copies)
    attention_back(
        plan,
        True,
        info_ref,
        seg_ref,
        (q_ref, k_ref, v_ref, o_ref, do_ref, lse_ref),
        (dq_ref, dkl_ref, dvl_ref),
        buffers,
    )
    for rows in row_blocks(plan.rows):
        own_ref[rows, :] = da_ref[rows, :] + dot_nt(
            dq_ref[rows, :], weight_of(w_ref, 0, plan.shard)
        )
    source_parts(plan, info_ref, dkl_ref, dvl_ref, w_ref, 1, own_ref, True, mates)


def self_weights_kernel(plan, chunk_count, info_ref, *refs):
    chunks, refs = refs[:chunk_count], refs[chunk_count:]
    (dq_ref, dkl_ref, dvl_ref, keep_ref, send_ref), refs = refs[:5], refs[5:]
    x_ref, own_x_ref, gw_ref, chunk_sems = refs
    copy_all(chunk_copies(plan, chunks, info_ref, 0, x_ref, None, chunk_sems))
    start = own_rows(plan, info_ref)
    for rows in row_blocks(plan.rows):
        own_x_ref[rows, :] = x_ref[pl.ds(start + rows.start, BLOCK), :]
    products = ((own_x_ref, dq_ref), (x_ref, dkl_ref), (x_ref, dvl_ref))
    weight_products(plan, info_ref, products, gw_ref, keep_ref, send_ref)


SMEM = pl.BlockSpec(memory_space=pltpu.SMEM)
VMEM = pl.BlockSpec(memory_space=pltpu.VMEM)
ANY = pl.BlockSpec(memory_space=pl.ANY)
HBM = pl.BlockSpec(memory_space=pltpu.HBM)


def call(kernel, specs, operands, outs, scratch, flops, moved, megabytes):
    return pl.pallas_call(
        kernel,
        in_specs=specs,
        out_specs=[VMEM] * len(outs),
        out_shape=outs,
        scratch_shapes=scratch,
        compiler_params=pltpu.CompilerParams(vmem_limit_bytes=megabytes * MEGABYTE),
        cost_estimate=pl.CostEstimate(flops=flops, bytes_accessed=moved, transcendentals=0),
    )(*operands)


def shape(dims, dtype):
    return jax.ShapeDtypeStruct(dims, dtype)


def forward_scratch(plan):
    return [
        pltpu.VMEM((plan.pairs, 2 * BLOCK, PAIR), LOW),
        pltpu.VMEM((plan.pairs, PAIR, 2 * BLOCK), WIDE),
        pltpu.VMEM((8, 2 * BLOCK), WIDE),
        pltpu.VMEM((8, 2 * BLOCK), WIDE),
    ]


def backward_scratch(plan):
    return [
        pltpu.VMEM((plan.pairs, 2 * BLOCK, PAIR), LOW),
        pltpu.VMEM((plan.pairs, 2 * BLOCK, PAIR), LOW),
        pltpu.VMEM((plan.pairs, PAIR, 2 * BLOCK), WIDE),
        pltpu.VMEM((8, 2 * BLOCK), WIDE),
    ]


def flat(pieces):
    return sum(piece.shape[0] for piece in pieces)


def forward(plan, info, chunks, pieces):
    rows, length, width = plan.rows, plan.length, plan.width
    heads = [
        shape((rows, width), LOW),
        shape((length, width), LOW),
        shape((length, width), LOW),
        shape((rows, width), LOW),
        shape((plan.query_blocks * plan.pairs, 2 * BLOCK), WIDE),
        shape((rows, width), WIDE),
    ]
    outs = heads + [shape((8, length), WIDE), shape((TILE, width), WIDE)] + heads
    scratch = [
        pltpu.VMEM((length, width), LOW),
        pltpu.VMEM((length, width), LOW),
        pltpu.VMEM((plan.chunks, TILE, width), LOW),
        pltpu.VMEM((plan.dp, 8 * plan.shard + TILE, width), LOW),
        pltpu.VMEM((length, 128), WIDE),
        pltpu.SemaphoreType.DMA((2, plan.chunks)),
        pltpu.SemaphoreType.DMA((2, plan.chunks)),
        pltpu.SemaphoreType.DMA((plan.dp,)),
    ] + forward_scratch(plan)
    return call(
        functools.partial(forward_kernel, plan, len(chunks), len(pieces)),
        [SMEM] + [ANY] * (len(chunks) + len(pieces)),
        [info, *chunks, *pieces],
        outs,
        scratch,
        FORWARD_COST,
        10**5,
        megabytes(plan, 18, 10),
    )


def feed(plan, info, upstreams, pieces, z, vecs):
    rows, width, blocks = plan.rows, plan.width, plan.hidden_blocks
    piece_rows = blocks * plan.shard + plan.outer_shard
    outs = (
        [shape((plan.chunk, width), LOW)] * plan.batches
        + [shape((rows, width), WIDE), shape((8, width), WIDE)]
        + [shape((plan.dp // 2, piece_rows, width), LOW)] * 2
    )
    scratch = [
        pltpu.VMEM((width, plan.hidden), LOW),
        pltpu.VMEM((plan.hidden, width), LOW),
        pltpu.VMEM((rows, width), LOW),
        pltpu.VMEM((rows, plan.hidden), WIDE),
        pltpu.VMEM((rows, plan.hidden), LOW),
        pltpu.VMEM((rows, plan.hidden), LOW),
        pltpu.VMEM((rows, width), WIDE),
        pltpu.VMEM((rows, width), LOW),
        pltpu.VMEM((rows, width), LOW),
        pltpu.VMEM((blocks, width, width), LOW),
        pltpu.VMEM((plan.hidden, width), LOW),
        pltpu.SemaphoreType.DMA((blocks + 1, plan.dp)),
        pltpu.SemaphoreType.DMA((plan.batches,)),
    ]
    return call(
        functools.partial(feed_kernel, plan, len(pieces)),
        [SMEM] + [ANY] * (plan.batches + len(pieces)) + [VMEM] * 2,
        [info, *upstreams, *pieces, z, vecs],
        outs,
        scratch,
        20 * 10**9,
        12 * 10**6,
        28,
    )


def backward_buffers(plan):
    length, width = plan.length, plan.width
    return [
        pltpu.VMEM((length, 128), WIDE),
        pltpu.VMEM((length, width), WIDE),
        pltpu.VMEM((length, width), WIDE),
        pltpu.VMEM((plan.pairs, 2 * BLOCK, PAIR), LOW),
        pltpu.VMEM((plan.pairs, 2 * BLOCK, PAIR), LOW),
        pltpu.VMEM((plan.pairs, PAIR, 2 * BLOCK), WIDE),
        pltpu.VMEM((8, 2 * BLOCK), WIDE),
    ]


def cross_backward(plan, info, chunks, pieces, operands):
    rows, length, width = plan.rows, plan.length, plan.width
    outs = (
        [shape((rows, width), WIDE)]
        + [shape((rows, width), LOW)] * (plan.group - 1)
        + [shape((rows, width), WIDE), shape((rows, width), LOW)]
        + [shape((plan.dp // 2, 5 * plan.shard + VECTOR_ROWS, width), LOW)] * 2
    )
    scratch = [
        pltpu.VMEM((length, width), LOW),
        pltpu.VMEM((plan.dp, 5 * plan.shard, width), LOW),
        pltpu.VMEM((rows, width), LOW),
        pltpu.VMEM((5, width, width), LOW),
        pltpu.VMEM((rows, width), WIDE),
        pltpu.VMEM((rows, width), LOW),
        pltpu.VMEM((rows, width), LOW),
        pltpu.VMEM((rows, width), LOW),
        pltpu.VMEM((rows, width), LOW),
        pltpu.VMEM((length, width), LOW),
        pltpu.VMEM((length, width), LOW),
        pltpu.SemaphoreType.DMA((2, plan.chunks)),
        pltpu.SemaphoreType.DMA((plan.dp,)),
    ] + backward_buffers(plan)
    return call(
        functools.partial(cross_backward_kernel, plan, len(chunks), len(pieces)),
        [SMEM] + [ANY] * (len(chunks) + len(pieces)) + [VMEM] * len(operands),
        [info, *chunks, *pieces, *operands],
        outs,
        scratch,
        22 * 10**9,
        12 * 10**6,
        megabytes(plan, 18, 16),
    )


def self_backward(plan, info, pieces, operands):
    rows, length, width = plan.rows, plan.length, plan.width
    outs = [
        shape((rows, width), LOW),
        shape((length, width), LOW),
        shape((length, width), LOW),
        shape((rows, width), WIDE),
    ] + [shape((rows, width), LOW)] * (plan.group - 1)
    scratch = [
        pltpu.VMEM((plan.dp, 3 * plan.shard, width), LOW),
        pltpu.SemaphoreType.DMA((plan.dp,)),
    ] + backward_buffers(plan)
    return call(
        functools.partial(self_backward_kernel, plan, len(pieces)),
        [SMEM] + [ANY] * len(pieces) + [VMEM] * len(operands),
        [info, *pieces, *operands],
        outs,
        scratch,
        15 * 10**9,
        12 * 10**6,
        megabytes(plan, 10, 14),
    )


def self_weights(plan, info, chunks, operands):
    rows, length, width = plan.rows, plan.length, plan.width
    outs = [shape((plan.dp // 2, 3 * plan.shard, width), LOW)] * 2
    scratch = [
        pltpu.VMEM((length, width), LOW),
        pltpu.VMEM((rows, width), LOW),
        pltpu.VMEM((3, width, width), LOW),
        pltpu.SemaphoreType.DMA((2, plan.chunks)),
    ]
    return call(
        functools.partial(self_weights_kernel, plan, len(chunks)),
        [SMEM] + [ANY] * len(chunks) + [VMEM] * len(operands),
        [info, *chunks, *operands],
        outs,
        scratch,
        6 * 10**9,
        6 * 10**6,
        megabytes(plan, 6, 5),
    )


def pack_first_kernel(plan, info_ref, *refs):
    weights, refs = refs[:8], refs[8:]
    (tokens, memory, vectors, target, source, piece_ref), refs = refs[:6], refs[6:]
    rounds, semaphores = refs[: plan.batches], refs[-1]
    shard, chunk, width = plan.shard, plan.chunk, plan.width
    moves = [
        (weights[which], piece_ref.at[0, pl.ds(which * shard, shard)]) for which in range(8)
    ]
    for number in range(plan.batches):
        batch = info_ref[plan.batch + number]
        moves.append((tokens.at[batch, 0], rounds[number].at[pl.ds(0, chunk)]))
        moves.append((memory.at[batch, 0], rounds[number].at[pl.ds(chunk, chunk)]))
    copies = [
        pltpu.make_async_copy(here, there, semaphores.at[number])
        for number, (here, there) in enumerate(moves)
    ]
    for copy in copies:
        copy.start()
    lanes = pltpu.roll(vectors[...].astype(WIDE), info_ref[plan.own_dp] * shard, 1)
    piece_ref[0, 8 * shard :, :] = lanes.astype(LOW)
    first_row = lax.broadcasted_iota(jnp.int32, (TILE, width), 0) == 0
    for number in range(plan.batches):
        batch = info_ref[plan.batch + number]
        row = jnp.concatenate([target[batch], source[batch]], axis=1).astype(WIDE)
        if width > 2 * chunk:
            row = jnp.concatenate([row, jnp.zeros((1, width - 2 * chunk), WIDE)], axis=1)
        rounds[number][2 * chunk :, :] = jnp.where(first_row, row, 0.0).astype(LOW)
    for copy in copies:
        copy.wait()


def pack_first(plan, info, weights, vectors, tokens, memory, target, source):
    outs = [shape((1, 8 * plan.shard + TILE, plan.width), LOW)]
    outs += [shape((2 * plan.chunk + TILE, plan.width), LOW)] * plan.batches
    return call(
        functools.partial(pack_first_kernel, plan),
        [SMEM] + [HBM] * 10 + [VMEM] * 3,
        [info, *weights, tokens, memory, vectors, target, source],
        outs,
        [pltpu.SemaphoreType.DMA((8 + 2 * plan.batches,))],
        0,
        2 * 10**6,
        60,
    )


def pack_rest_kernel(plan, info_ref, inner, outer, cotangent, feed_ref, *refs):
    rounds, semaphores = refs[: plan.batches], refs[-1]
    shard, width, blocks = plan.shard, plan.width, plan.hidden_blocks
    moves = [
        (
            inner.at[:, pl.ds(block * width, width)],
            feed_ref.at[0, pl.ds(block * shard, shard)],
        )
        for block in range(blocks)
    ]
    moves.append((outer, feed_ref.at[0, pl.ds(blocks * shard, plan.outer_shard)]))
    for number in range(plan.batches):
        moves.append((cotangent.at[info_ref[plan.batch + number], 0], rounds[number]))
    copy_all(
        [
            pltpu.make_async_copy(here, there, semaphores.at[number])
            for number, (here, there) in enumerate(moves)
        ]
    )


def pack_rest(plan, info, inner, outer, cotangent):
    outs = [shape((1, plan.hidden_blocks * plan.shard + plan.outer_shard, plan.width), LOW)]
    outs += [shape((plan.chunk, plan.width), LOW)] * plan.batches
    return call(
        functools.partial(pack_rest_kernel, plan),
        [SMEM] + [HBM] * 3,
        [info, inner, outer, cotangent],
        outs,
        [pltpu.SemaphoreType.DMA((plan.hidden_blocks + 1 + plan.batches,))],
        0,
        2 * 10**6,
        60,
    )


def pairs_of(plan, move):
    return [
        (dp * plan.seq + seq, to[0] * plan.seq + to[1])
        for dp in range(plan.dp)
        for seq in range(plan.seq)
        for to in [move(dp, seq)]
    ]


def home(plan, dp, batch, seq):
    position = (2 * batch + dp % 2) * plan.group + seq // plan.batches
    return (dp - dp % 2 + position % 2, position // 2)


def round_batch(plan, seq, number):
    return (seq + number) % plan.batches


def inward(plan, number):
    return pairs_of(plan, lambda dp, seq: home(plan, dp, round_batch(plan, seq, number), seq))


def outward(plan, number):
    return [(to, source) for source, to in inward(plan, number)]


def mate(plan, turn):
    def move(dp, seq):
        position = 2 * seq + dp % 2
        group, own = position // plan.group, position % plan.group
        to = group * plan.group + (own + turn) % plan.group
        return (dp - dp % 2 + to % 2, to // 2)

    return pairs_of(plan, move)


def permute(values, pairs):
    return lax.ppermute(values, AXES, pairs)


def dp_flip(plan, bits):
    return pairs_of(plan, lambda dp, seq: (dp ^ bits, seq))


def seq_flip(plan, bits):
    return pairs_of(plan, lambda dp, seq: (dp, seq ^ bits))


def share_inputs(plan, rounds):
    return [permute(piece, inward(plan, number)) for number, piece in enumerate(rounds)]


def share_mates(plan, received):
    chunks = list(received)
    for turn in range(1, plan.group):
        chunks += [permute(piece, mate(plan, turn)) for piece in received]
    return chunks


def send_home(plan, pieces):
    return [permute(piece, outward(plan, number)) for number, piece in enumerate(pieces)]


def order_home(plan, landed, dtype):
    seq = lax.axis_index("seq")
    landed = jnp.stack(landed).astype(dtype)
    order = [(batch - seq) % plan.batches for batch in range(plan.batches)]
    return jnp.stack(
        [lax.dynamic_index_in_dim(landed, index, 0, keepdims=False) for index in order]
    )


def gather_direct(plan, shard):
    if plan.dp != 8:
        return [lax.all_gather(shard[0], "dp", axis=0)]
    return [shard] + [permute(shard, dp_flip(plan, bits)) for bits in (2, 4, 6)]


def gather_rest(plan, direct):
    if plan.dp != 8:
        return direct
    pieces = []
    for piece in direct:
        pieces += [piece, permute(piece, dp_flip(plan, 1))]
    return pieces


def add_low(values):
    total = values[0].astype(WIDE)
    for value in values[1:]:
        total = total + value.astype(WIDE)
    return total.astype(LOW)


def core_send(plan, send):
    return permute(send, dp_flip(plan, 1)) if plan.dp == 8 else send


def core_sum(plan, keep, other):
    if plan.dp != 8:
        return [jnp.concatenate([keep, other], axis=0)]
    return [add_low([keep[number], other[number]]) for number in range(4)]


def plane_send(plan, parts):
    if plan.dp != 8:
        return [lax.psum_scatter(parts[0], "dp", scatter_dimension=0)]
    return [permute(parts[number], dp_flip(plan, 2 * number)) for number in range(1, 4)]


def plane_sum(plan, parts, landed):
    total = landed[0] if plan.dp != 8 else add_low([parts[0], *landed])
    return total if plan.seq == 4 else lax.psum(total, "seq")


def halves(plan, total, bits):
    if plan.seq != 4:
        return total, jnp.zeros_like(total)
    half = total.shape[0] // 2
    own = lax.axis_index("seq") // bits % 2
    return (
        lax.dynamic_slice_in_dim(total, own * half, half),
        lax.dynamic_slice_in_dim(total, (1 - own) * half, half),
    )


def seq_send(plan, values, bits):
    return permute(values, seq_flip(plan, bits)) if plan.seq == 4 else jnp.zeros_like(values)


def join(plan, own_part, other, bits):
    if plan.seq != 4:
        return own_part
    own = lax.axis_index("seq") // bits % 2
    return jnp.where(
        own == 0, jnp.concatenate([own_part, other]), jnp.concatenate([other, own_part])
    )


def add_wide(first, second):
    return first.astype(WIDE) + second.astype(WIDE)


def after(values, *others):
    return lax.optimization_barrier((values, others))[0]


def plan_info(plan):
    dp, seq = lax.axis_index("dp"), lax.axis_index("seq")
    position = 2 * seq + dp % 2
    own = position % plan.group
    batch = position // plan.group // 2
    flips = list(range(8)) if plan.dp == 8 else None
    entries = []
    if flips:
        entries += [dp ^ bits for bits in (0, 1, 2, 3, 4, 5, 6, 7)]
        entries += [dp ^ bits for bits in (0, 2, 4, 6, 1, 3, 5, 7)]
    else:
        entries += list(range(plan.dp)) * 2
    places = [(batch - number) % plan.batches for number in range(plan.batches)]
    for turn in range(plan.group):
        source = (own - turn) % plan.group
        entries += [source * plan.batches + place for place in places]
    entries.append(own)
    entries += places
    entries += [(own + turn) % plan.group for turn in range(plan.group)]
    entries += [(seq + number) % plan.batches for number in range(plan.batches)]
    entries.append(dp)
    return jnp.stack([jnp.asarray(entry, jnp.int32) for entry in entries])


def on_device(
    tokens,
    memory,
    target_segments,
    source_segments,
    cotangent,
    query_weight,
    key_weight,
    value_weight,
    output_weight,
    cross_query,
    cross_key,
    cross_value,
    cross_output,
    inner_weight,
    outer_weight,
    self_gain,
    self_shift,
    cross_gain,
    cross_shift,
    feed_gain,
    feed_shift,
):
    plan = Plan(tokens, inner_weight)
    width, shard = plan.width, plan.shard
    info = plan_info(plan)
    dp = lax.axis_index("dp")

    vectors = jnp.stack([self_gain, self_shift, cross_gain, cross_shift, feed_gain, feed_shift])
    vectors = jnp.pad(vectors, ((0, TILE - 6), (0, width - shard)))
    shard_piece, *rounds = pack_first(
        plan,
        info,
        [
            query_weight,
            key_weight,
            value_weight,
            output_weight,
            cross_query,
            cross_key,
            cross_value,
            cross_output,
        ],
        vectors,
        tokens,
        memory,
        target_segments,
        source_segments,
    )
    direct = gather_direct(plan, shard_piece)
    landed = share_inputs(plan, rounds)

    feed_shard, *rounds = pack_rest(plan, info, inner_weight, outer_weight, cotangent)
    first = landed[0]
    direct, landed = after((direct, landed), feed_shard)
    feed_shard, rounds = after((feed_shard, rounds), first)
    feed_direct = gather_direct(plan, feed_shard)
    upstreams = share_inputs(plan, rounds)
    pieces = gather_rest(plan, direct)
    chunks = share_mates(plan, landed)
    q, k, v, o, lse, a, segs, vecs, cq, ck, cv, co, cross_lse, z = forward(
        plan, info, chunks, pieces
    )

    feed_direct, upstreams = after((feed_direct, upstreams), z)
    feed_pieces = gather_rest(plan, feed_direct)
    *results, dsecond, dvec, feed_keep, feed_send = feed(
        plan, info, upstreams, feed_pieces, z, vecs
    )

    feed_parts = core_sum(plan, feed_keep, core_send(plan, feed_send))
    out_landed = send_home(plan, results)
    feed_landed = plane_send(plan, feed_parts)
    dsecond = after(dsecond, feed_parts)
    back = cross_backward(
        plan,
        info,
        chunks,
        pieces,
        [a, z, segs, vecs, dvec, dsecond, o, cq, ck, cv, co, cross_lse],
    )
    back, feed_landed, out_landed = lax.optimization_barrier((back, feed_landed, out_landed))
    own_memory, *others = back
    mate_memory, (da, do, cross_keep, cross_send) = (
        others[: plan.group - 1],
        others[plan.group - 1 :],
    )

    feed_keep, feed_send = halves(plan, plane_sum(plan, feed_parts, feed_landed), 1)
    cross_parts = core_sum(plan, cross_keep, core_send(plan, cross_send))
    memory_pieces = add_mates(plan, info, own_memory, mate_memory)
    feed_landed = seq_send(plan, feed_send, 1)
    cross_landed = plane_send(plan, cross_parts)
    memory_landed = send_home(plan, memory_pieces)
    do = after(do, feed_send, cross_parts, memory_pieces)
    back = self_backward(plan, info, pieces, [segs, da, do, q, k, v, o, lse])
    back, feed_landed, cross_landed, memory_landed = lax.optimization_barrier(
        (back, feed_landed, cross_landed, memory_landed)
    )
    dq, dk, dv, own_tokens, *mate_tokens = back

    feed_keep, feed_send = halves(plan, add_low([feed_keep, feed_landed]), 2)
    cross_keep, cross_send = halves(plan, plane_sum(plan, cross_parts, cross_landed), 1)
    feed_landed = seq_send(plan, feed_send, 2)
    cross_landed = seq_send(plan, cross_send, 1)
    mate_landed = send_mates(plan, mate_tokens)
    dq = after(dq, feed_send, cross_send)
    self_keep, self_send = self_weights(plan, info, chunks, [dq, dk, dv])
    self_keep, self_send, feed_landed, cross_landed, mate_landed = lax.optimization_barrier(
        (self_keep, self_send, feed_landed, cross_landed, mate_landed)
    )

    self_landed = core_send(plan, self_send)
    token_pieces = sum_mates(plan, info, own_tokens, mate_landed)
    self_parts = core_sum(plan, self_keep, after(self_landed, token_pieces))
    self_landed = plane_send(plan, self_parts)
    token_landed = send_home(plan, after(token_pieces, self_parts))
    feed_quarter = add_low([after(feed_keep, token_pieces), feed_landed])
    cross_keep, cross_send = halves(
        plan, add_low([after(cross_keep, token_pieces), cross_landed]), 2
    )
    feed_landed = seq_send(plan, feed_quarter, 2)
    cross_landed = seq_send(plan, cross_send, 2)
    self_landed = after(self_landed, feed_quarter, cross_send)
    self_total = plane_sum(plan, self_parts, self_landed)
    self_landed = seq_send(plan, self_total, 1)
    feed_landed, cross_landed = after((feed_landed, cross_landed), self_total)
    feed_half = join(plan, feed_quarter, feed_landed, 2)
    cross_quarter = add_low([cross_keep, cross_landed])
    feed_landed = seq_send(plan, feed_half, 1)
    cross_landed = seq_send(plan, cross_quarter, 2)
    self_landed = after(self_landed, feed_half, cross_quarter)
    self_total = add_low([self_total, self_landed])
    self_landed = seq_send(plan, self_total, 2)
    cross_half = join(plan, cross_quarter, after(cross_landed, self_total), 2)
    cross_landed = seq_send(plan, cross_half, 1)
    feed_total = join(plan, feed_half, feed_landed, 1).astype(WIDE)
    cross_total = join(plan, cross_half, cross_landed, 1).astype(WIDE)
    self_total = add_wide(self_total, self_landed)
    out_tokens = order_home(plan, out_landed, LOW)
    grad_memory = order_home(plan, memory_landed, WIDE)
    grad_tokens = order_home(plan, token_landed, WIDE)
    scale = 1.0 / (plan.batches * plan.dp)
    feed_grads, cross_grads, self_grads = (
        feed_total * scale,
        cross_total * scale,
        self_total * scale,
    )
    inner_grads = [
        feed_grads[block * shard : (block + 1) * shard] for block in range(plan.hidden_blocks)
    ]
    vector_grads = lax.dynamic_slice(cross_grads, (5 * shard, dp * shard), (TILE, shard))
    return (
        out_tokens[:, None],
        grad_tokens[:, None],
        grad_memory[:, None],
        *[self_grads[which * shard : (which + 1) * shard] for which in range(3)],
        cross_grads[4 * shard : 5 * shard],
        *[cross_grads[which * shard : (which + 1) * shard] for which in range(4)],
        jnp.concatenate(inner_grads, axis=1),
        feed_grads[plan.hidden_blocks * shard :],
        *[vector_grads[which] for which in range(6)],
    )


def send_mates(plan, mates):
    return [permute(part, mate(plan, turn)) for turn, part in enumerate(mates, 1)]


def sum_mates(plan, info, own, landed):
    for part in landed:
        own = own + part.astype(WIDE)
    own = own.reshape(plan.batches, plan.chunk, plan.width)
    return [
        lax.dynamic_index_in_dim(own, info[plan.round + number], 0, keepdims=False).astype(LOW)
        for number in range(plan.batches)
    ]


def add_mates(plan, info, own, mates):
    return sum_mates(plan, info, own, send_mates(plan, mates))


def solution(mesh):
    tokens = P(None, "dp", "seq", None)
    ids = P(None, "dp", "seq")
    weight = P("dp", None)
    vector = P("dp")
    return jax.shard_map(
        on_device,
        mesh=mesh,
        in_specs=(tokens, tokens, ids, ids, tokens) + (weight,) * 10 + (vector,) * 6,
        out_specs=(tokens,) * 3 + (weight,) * 10 + (vector,) * 6,
        check_vma=False,
    )
```

```python
import functools

import jax
import jax.numpy as jnp
from jax import lax
from jax.experimental import pallas as pl
from jax.experimental.pallas import tpu as pltpu
from jax.sharding import PartitionSpec as P

DH = 64
PAIR = 2 * DH
BLOCK = 256
TILE = 16
VECTOR_ROWS = 64
FORWARD_COST = 10**6
EPSILON = 1e-05
NEGATIVE = -1e30
FACTOR = DH ** (-0.5)
AXES = ("dp", "seq")
LOW = jnp.bfloat16
WIDE = jnp.float32
MEGABYTE = 1024 * 1024


def dot_nn(a, b):
    return jnp.dot(a, b, preferred_element_type=WIDE)


def dot_nt(a, b):
    return lax.dot_general(a, b, (((1,), (1,)), ((), ())), preferred_element_type=WIDE)


def dot_tn(a, b):
    return lax.dot_general(a, b, (((0,), (0,)), ((), ())), preferred_element_type=WIDE)


def normalise(values):
    centred = values - jnp.mean(values, axis=-1, keepdims=True)
    inverse = lax.rsqrt(jnp.mean(centred * centred, axis=-1, keepdims=True) + EPSILON)
    return centred * inverse, inverse


def norm_backward(upstream, normed, inverse, gain_row):
    scaled = upstream * gain_row
    plain_mean = jnp.mean(scaled, axis=-1, keepdims=True)
    along_mean = jnp.mean(scaled * normed, axis=-1, keepdims=True)
    return inverse * (scaled - plain_mean - normed * along_mean)


def row_blocks(length, size=BLOCK):
    return [pl.ds(start, size) for start in range(0, length, size)]


def copy_all(copies):
    for copy in copies:
        copy.start()
    for copy in copies:
        copy.wait()


def piece_copies(plan, pieces, info_ref, w_ref, semaphores):
    copies = []
    for piece in pieces:
        for slab in range(piece.shape[0]):
            number = len(copies)
            owner = info_ref[plan.order + number]
            copies.append(
                pltpu.make_async_copy(piece.at[slab], w_ref.at[owner], semaphores.at[number])
            )
    return copies


def weight_of(weight_ref, which, rows):
    count, _, width = weight_ref.shape
    return weight_ref[:, which * rows : (which + 1) * rows, :].reshape(count * rows, width)


def seg_columns(seg_row):
    return jnp.transpose(jnp.broadcast_to(seg_row, (128, seg_row.shape[1])))


def stack_heads(pair):
    lane = lax.broadcasted_iota(jnp.int32, pair.shape, 1)
    zero = jnp.zeros_like(pair)
    return jnp.concatenate(
        [jnp.where(lane < DH, pair, zero), jnp.where(lane < DH, zero, pair)], axis=0
    )


def unstack_heads(columns):
    row = lax.broadcasted_iota(jnp.int32, (PAIR, BLOCK), 0)
    return jnp.where(row < DH, columns[:, :BLOCK], columns[:, BLOCK:])


def mask_bias(key_ids, query_ids, key_start, query_start, causal):
    ids = jnp.concatenate([key_ids, key_ids], axis=1)
    allowed = ids == query_ids
    if causal:
        key_place = key_start + lax.broadcasted_iota(jnp.int32, (BLOCK, BLOCK), 0)
        query_place = query_start + lax.broadcasted_iota(jnp.int32, (BLOCK, BLOCK), 1)
        allowed = jnp.logical_and(allowed, key_place <= query_place)
    bias = jnp.where(allowed, 0.0, NEGATIVE)
    return jnp.concatenate([bias, bias], axis=1)


def key_bounds(key_row, query_ids, query_start, causal):
    below = jnp.sum(jnp.where(key_row < jnp.min(query_ids), 1.0, 0.0)).astype(jnp.int32)
    first = lax.div(below, BLOCK)
    if causal:
        return first, lax.div(query_start, BLOCK) + 1
    upto = jnp.sum(jnp.where(key_row <= jnp.max(query_ids), 1.0, 0.0)).astype(jnp.int32)
    return first, lax.div(upto + (BLOCK - 1), BLOCK)


def attend_forward(
    q_ref, k_ref, v_ref, o_ref, lse_ref, key_row, columns_ref, query_row, start, causal, scratch
):
    stack_ref, sum_ref, top_ref, total_ref = scratch
    pairs = q_ref.shape[1] // PAIR
    for number, rows in enumerate(row_blocks(q_ref.shape[0])):
        query_ids = query_row[:, number * BLOCK : (number + 1) * BLOCK]
        query_start = start + number * BLOCK
        low, high = key_bounds(key_row, query_ids, query_start, causal)
        for pair in range(pairs):
            stack_ref[pair] = stack_heads(q_ref[rows, pair * PAIR : (pair + 1) * PAIR])
        sum_ref[...] = jnp.zeros_like(sum_ref)
        top_ref[...] = jnp.full_like(top_ref, NEGATIVE)
        total_ref[...] = jnp.zeros_like(total_ref)

        def one_block(block, carry):
            key_start = pl.multiple_of(block * BLOCK, BLOCK)
            keys = pl.ds(key_start, BLOCK)
            bias = mask_bias(columns_ref[keys, :], query_ids, key_start, query_start, causal)
            values = [
                (
                    k_ref[keys, pair * PAIR : (pair + 1) * PAIR],
                    v_ref[keys, pair * PAIR : (pair + 1) * PAIR],
                    stack_ref[pair],
                    top_ref[pair : pair + 1, :],
                    total_ref[pair : pair + 1, :],
                    sum_ref[pair],
                )
                for pair in range(pairs)
            ]
            scores = [dot_nt(key_pair, queries) + bias for key_pair, _, queries, *_ in values]
            tops = [
                jnp.maximum(value[3], jnp.max(score, axis=0, keepdims=True))
                for value, score in zip(values, scores)
            ]
            exponents = [jnp.exp(score - top) for score, top in zip(scores, tops)]
            shrinks = [jnp.exp(value[3] - top) for value, top in zip(values, tops)]
            totals = [
                value[4] * shrink + jnp.sum(exponent, axis=0, keepdims=True)
                for value, shrink, exponent in zip(values, shrinks, exponents)
            ]
            sums = [
                value[5] * shrink + dot_tn(value[1], exponent.astype(LOW))
                for value, shrink, exponent in zip(values, shrinks, exponents)
            ]
            for pair in range(pairs):
                top_ref[pair : pair + 1, :] = tops[pair]
                total_ref[pair : pair + 1, :] = totals[pair]
                sum_ref[pair] = sums[pair]
            return carry

        lax.fori_loop(low, high, one_block, 0)
        for pair in range(pairs):
            total = total_ref[pair : pair + 1, :]
            context = unstack_heads(sum_ref[pair] / total)
            o_ref[rows, pair * PAIR : (pair + 1) * PAIR] = jnp.transpose(context).astype(LOW)
            place = number * pairs + pair
            lse_ref[place : place + 1, :] = top_ref[pair : pair + 1, :] + jnp.log(total)


def attend_backward(
    q_ref,
    k_ref,
    v_ref,
    o_ref,
    grad_ref,
    lse_ref,
    dq_ref,
    dk_ref,
    dv_ref,
    key_row,
    columns_ref,
    query_row,
    start,
    causal,
    scratch,
):
    stack_ref, stack_grad_ref, sum_ref, along_ref = scratch
    pairs = q_ref.shape[1] // PAIR
    dk_ref[...] = jnp.zeros_like(dk_ref)
    dv_ref[...] = jnp.zeros_like(dv_ref)
    for number, rows in enumerate(row_blocks(q_ref.shape[0])):
        query_ids = query_row[:, number * BLOCK : (number + 1) * BLOCK]
        query_start = start + number * BLOCK
        low, high = key_bounds(key_row, query_ids, query_start, causal)
        for pair in range(pairs):
            lanes = slice(pair * PAIR, (pair + 1) * PAIR)
            grad = grad_ref[rows, lanes]
            stack_ref[pair] = stack_heads(q_ref[rows, lanes])
            stack_grad_ref[pair] = stack_heads(grad)
            along = jnp.transpose(grad.astype(WIDE) * o_ref[rows, lanes].astype(WIDE))
            along_ref[pair : pair + 1, :] = jnp.concatenate(
                [
                    jnp.sum(along[:DH], axis=0, keepdims=True),
                    jnp.sum(along[DH:], axis=0, keepdims=True),
                ],
                axis=1,
            )
        sum_ref[...] = jnp.zeros_like(sum_ref)

        def one_block(block, carry):
            key_start = pl.multiple_of(block * BLOCK, BLOCK)
            keys = pl.ds(key_start, BLOCK)
            bias = mask_bias(columns_ref[keys, :], query_ids, key_start, query_start, causal)
            for pair in range(pairs):
                lanes = slice(pair * PAIR, (pair + 1) * PAIR)
                place = number * pairs + pair
                key_pair = k_ref[keys, lanes]
                scores = dot_nt(key_pair, stack_ref[pair]) + bias
                probs = jnp.exp(scores - lse_ref[place : place + 1, :])
                prob_grad = dot_nt(v_ref[keys, lanes], stack_grad_ref[pair])
                score_grad = (probs * (prob_grad - along_ref[pair : pair + 1, :])).astype(LOW)
                dv_ref[keys, lanes] += dot_nn(probs.astype(LOW), stack_grad_ref[pair])
                dk_ref[keys, lanes] += dot_nn(score_grad, stack_ref[pair])
                sum_ref[pair] += dot_tn(key_pair, score_grad)
            return carry

        lax.fori_loop(low, high, one_block, 0)
        for pair in range(pairs):
            grad = jnp.transpose(unstack_heads(sum_ref[pair])) * FACTOR
            dq_ref[rows, pair * PAIR : (pair + 1) * PAIR] = grad.astype(LOW)


def store_pieces(grad_ref, keep_ref, send_ref, info_ref, order, offset, count, rows):
    half = count // 2
    for number in range(count):
        owner = info_ref[order + number]
        block = grad_ref[pl.ds(pl.multiple_of(owner * rows, rows), rows), :]
        target = keep_ref if number < half else send_ref
        target[number % half, offset : offset + rows, :] = block


class Plan:
    def __init__(self, tokens, inner_weight):
        self.dp = lax.axis_size("dp")
        self.seq = lax.axis_size("seq")
        self.batches, _, self.chunk, self.width = tokens.shape
        self.hidden = inner_weight.shape[1]
        self.length = self.chunk * self.seq
        self.group = self.seq // self.batches
        self.rows = self.batches * self.chunk
        self.chunks = self.seq
        self.shard = self.width // self.dp
        self.outer_shard = self.hidden // self.dp
        self.hidden_blocks = self.hidden // self.width
        self.pairs = self.width // PAIR
        self.query_blocks = self.rows // BLOCK
        self.order = 0
        self.grad_order = self.dp
        self.chunk_order = 2 * self.dp
        self.own = self.chunk_order + self.chunks
        self.round = self.own + 1
        self.mates = self.round + self.batches
        self.batch = self.mates + self.group
        self.own_dp = self.batch + self.batches


def megabytes(plan, fixed, by_length):
    return fixed + -(-by_length * plan.length // 1024)


def seg_rows(plan, raw_ref, seg_ref):
    for number in range(plan.chunks):
        lanes = slice(number * plan.chunk, (number + 1) * plan.chunk)
        seg_ref[0:1, lanes] = raw_ref[number, 0:1, : plan.chunk].astype(WIDE)
        seg_ref[1:2, lanes] = raw_ref[number, 0:1, plan.chunk : 2 * plan.chunk].astype(WIDE)


def own_rows(plan, info_ref):
    return pl.multiple_of(info_ref[plan.own] * plan.rows, plan.rows)


def chunk_copies(plan, chunks, info_ref, first, x_ref, raw_ref, semaphores):
    copies = []
    for number, chunk in enumerate(chunks):
        index = info_ref[plan.chunk_order + number]
        rows = pl.ds(pl.multiple_of(index * plan.chunk, plan.chunk), plan.chunk)
        copies.append(
            pltpu.make_async_copy(
                chunk.at[pl.ds(first, plan.chunk)], x_ref.at[rows], semaphores.at[0, number]
            )
        )
        if raw_ref is not None:
            copies.append(
                pltpu.make_async_copy(
                    chunk.at[pl.ds(2 * plan.chunk, TILE)],
                    raw_ref.at[index],
                    semaphores.at[1, number],
                )
            )
    return copies


def project_rows(length, source_ref, key_weight, value_weight, k_ref, v_ref):
    for rows in row_blocks(length, 2 * BLOCK):
        k_ref[rows, :] = dot_nn(source_ref[rows, :], key_weight).astype(LOW)
        v_ref[rows, :] = dot_nn(source_ref[rows, :], value_weight).astype(LOW)


def forward_kernel(plan, chunk_count, piece_count, info_ref, *refs):
    chunks, refs = refs[:chunk_count], refs[chunk_count:]
    pieces, refs = refs[:piece_count], refs[piece_count:]
    (q_ref, o_ref, lse_ref, a_ref, seg_ref, vec_ref), refs = refs[:6], refs[6:]
    (cq_ref, co_ref, cross_lse_ref, z_ref, k_ref, v_ref), refs = refs[:6], refs[6:]
    x_ref, m_ref, raw_ref, w_ref, columns_ref, chunk_sems, m_sems, piece_sems, *scratch = refs
    load = chunk_copies(plan, chunks, info_ref, 0, x_ref, raw_ref, chunk_sems)
    load += chunk_copies(plan, chunks, info_ref, plan.chunk, m_ref, None, m_sems)
    load += piece_copies(plan, pieces, info_ref, w_ref, piece_sems)
    copy_all(load)
    shard = plan.shard
    start = own_rows(plan, info_ref)
    vec_ref[...] = jnp.sum(w_ref[:, 8 * shard :, :].astype(WIDE), axis=0)
    seg_rows(plan, raw_ref, seg_ref)
    columns_ref[...] = seg_columns(seg_ref[0:1, :])
    for rows in row_blocks(plan.rows):
        own = x_ref[pl.ds(start + rows.start, BLOCK), :]
        q_ref[rows, :] = (dot_nn(own, weight_of(w_ref, 0, shard)) * FACTOR).astype(LOW)
    project_rows(
        plan.length,
        x_ref,
        weight_of(w_ref, 1, shard),
        weight_of(w_ref, 2, shard),
        k_ref,
        v_ref,
    )
    attend_forward(
        q_ref,
        k_ref,
        v_ref,
        o_ref,
        lse_ref,
        seg_ref[0:1, :],
        columns_ref,
        seg_ref[0:1, pl.ds(start, plan.rows)],
        start,
        True,
        scratch,
    )
    gain, shift = vec_ref[0:1, :], vec_ref[1:2, :]
    for rows in row_blocks(plan.rows):
        own = x_ref[pl.ds(start + rows.start, BLOCK), :].astype(WIDE)
        a = own + dot_nn(o_ref[rows, :], weight_of(w_ref, 3, shard))
        a_ref[rows, :] = a
        normed, _ = normalise(a)
        first = normed * gain + shift
        z_ref[rows, :] = first
        cq_ref[rows, :] = (
            dot_nn(first.astype(LOW), weight_of(w_ref, 4, shard)) * FACTOR
        ).astype(LOW)
    project_rows(
        plan.length,
        m_ref,
        weight_of(w_ref, 5, shard),
        weight_of(w_ref, 6, shard),
        k_ref,
        v_ref,
    )
    columns_ref[...] = seg_columns(seg_ref[1:2, :])
    attend_forward(
        cq_ref,
        k_ref,
        v_ref,
        co_ref,
        cross_lse_ref,
        seg_ref[1:2, :],
        columns_ref,
        seg_ref[0:1, pl.ds(start, plan.rows)],
        start,
        False,
        scratch,
    )
    for rows in row_blocks(plan.rows):
        z_ref[rows, :] += dot_nn(co_ref[rows, :], weight_of(w_ref, 7, shard))


def feed_kernel(plan, piece_count, info_ref, *refs):
    batches = plan.batches
    upstreams, refs = refs[:batches], refs[batches:]
    pieces, refs = refs[:piece_count], refs[piece_count:]
    (z_ref, vec_ref), refs = refs[:2], refs[2:]
    outs, refs = refs[:batches], refs[batches:]
    (dh_ref, dvec_ref, keep_ref, send_ref), refs = refs[:4], refs[4:]
    inner_ref, outer_ref, low_ref, u_ref, r_ref, du_ref, f_ref, up_ref, res_ref, *refs = refs
    inner_gw_ref, outer_gw_ref, piece_sems, up_sems = refs
    width, shard, blocks, outer_shard = (
        plan.width,
        plan.shard,
        plan.hidden_blocks,
        plan.outer_shard,
    )
    copies = []
    number = 0
    for piece in pieces:
        for slab in range(piece.shape[0]):
            owner = info_ref[plan.order + number]
            for block in range(blocks):
                copies.append(
                    pltpu.make_async_copy(
                        piece.at[slab, pl.ds(block * shard, shard)],
                        inner_ref.at[
                            pl.ds(pl.multiple_of(owner * shard, shard), shard),
                            pl.ds(block * width, width),
                        ],
                        piece_sems.at[block, number],
                    )
                )
            copies.append(
                pltpu.make_async_copy(
                    piece.at[slab, pl.ds(blocks * shard, outer_shard)],
                    outer_ref.at[pl.ds(pl.multiple_of(owner * outer_shard, outer_shard), outer_shard)],
                    piece_sems.at[blocks, number],
                )
            )
            number += 1
    for number in range(batches):
        index = info_ref[plan.round + number]
        rows = pl.ds(pl.multiple_of(index * plan.chunk, plan.chunk), plan.chunk)
        copies.append(
            pltpu.make_async_copy(upstreams[number], up_ref.at[rows], up_sems.at[number])
        )
    for copy in copies:
        copy.start()
    gain_two, shift_two = vec_ref[2:3, :], vec_ref[3:4, :]
    gain_three, shift_three = vec_ref[4:5, :], vec_ref[5:6, :]
    gain_grad = jnp.zeros((1, width), WIDE)
    shift_grad = jnp.zeros((1, width), WIDE)
    for rows in row_blocks(plan.rows):
        normed, _ = normalise(z_ref[rows, :])
        second = normed * gain_two + shift_two
        f_ref[rows, :] = second
        low_ref[rows, :] = second.astype(LOW)
    for copy in copies:
        copy.wait()
    lanes = [slice(block * width, (block + 1) * width) for block in range(blocks)]
    for part in lanes:
        u = dot_nn(low_ref[...], inner_ref[:, part])
        phi = 0.5 + 0.5 * lax.erf(u * (0.5**0.5))
        r_ref[:, part] = (u * phi).astype(LOW)
        u_ref[:, part] = phi + u * (jnp.exp(-0.5 * u * u) * 0.3989422804014327)
    for rows in row_blocks(plan.rows):
        f = f_ref[rows, :] + dot_nn(r_ref[rows, :], outer_ref[...])
        normed, inverse = normalise(f)
        res_ref[rows, :] = (normed * gain_three + shift_three).astype(LOW)
        upstream = up_ref[rows, :].astype(WIDE)
        gain_grad += jnp.sum(upstream * normed, axis=0, keepdims=True)
        shift_grad += jnp.sum(upstream, axis=0, keepdims=True)
        feed_grad = norm_backward(upstream, normed, inverse, gain_three)
        dh_ref[rows, :] = feed_grad
        up_ref[rows, :] = feed_grad.astype(LOW)
    for number in range(batches):
        index = info_ref[plan.round + number]
        outs[number][...] = res_ref[pl.ds(pl.multiple_of(index * plan.chunk, plan.chunk), plan.chunk), :]
    for part in lanes:
        dr = dot_nt(up_ref[...], outer_ref[part, :]).astype(LOW).astype(WIDE)
        du_ref[:, part] = (dr * u_ref[:, part]).astype(LOW)
        outer_gw_ref[part, :] = dot_tn(r_ref[:, part], up_ref[...]).astype(LOW)
    for block, part in enumerate(lanes):
        inner_gw_ref[block] = dot_tn(low_ref[...], du_ref[:, part]).astype(LOW)
    for rows in row_blocks(plan.rows):
        dh_ref[rows, :] += dot_nt(du_ref[rows, :], inner_ref[...])
    for block in range(blocks):
        store_pieces(
            inner_gw_ref.at[block],
            keep_ref,
            send_ref,
            info_ref,
            plan.grad_order,
            block * shard,
            plan.dp,
            shard,
        )
    store_pieces(
        outer_gw_ref,
        keep_ref,
        send_ref,
        info_ref,
        plan.grad_order,
        blocks * shard,
        plan.dp,
        outer_shard,
    )
    dvec_ref[...] = jnp.zeros_like(dvec_ref)
    dvec_ref[4:5, :] = gain_grad
    dvec_ref[5:6, :] = shift_grad


def norm_back(plan, line, z_ref, upstream_ref, vec_ref, w_ref, which, grad_ref, low_ref, do_ref):
    gain_grad = jnp.zeros((1, plan.width), WIDE)
    shift_grad = jnp.zeros((1, plan.width), WIDE)
    for rows in row_blocks(plan.rows):
        normed, inverse = normalise(z_ref[rows, :])
        upstream = upstream_ref[rows, :]
        gain_grad += jnp.sum(upstream * normed, axis=0, keepdims=True)
        shift_grad += jnp.sum(upstream, axis=0, keepdims=True)
        grad = norm_backward(upstream, normed, inverse, vec_ref[2 * line : 2 * line + 1, :])
        grad_ref[rows, :] = grad
        low_ref[rows, :] = grad.astype(LOW)
        do_ref[rows, :] = dot_nt(low_ref[rows, :], weight_of(w_ref, which, plan.shard)).astype(LOW)
    return gain_grad, shift_grad


def attention_back(plan, causal, info_ref, seg_ref, operands, results, buffers):
    q_ref, k_ref, v_ref, o_ref, do_ref, lse_ref = operands
    dq_ref, dkl_ref, dvl_ref = results
    columns_ref, dk_ref, dv_ref, *scratch = buffers
    start = own_rows(plan, info_ref)
    line = 0 if causal else 1
    columns_ref[...] = seg_columns(seg_ref[line : line + 1, :])
    attend_backward(
        q_ref,
        k_ref,
        v_ref,
        o_ref,
        do_ref,
        lse_ref,
        dq_ref,
        dk_ref,
        dv_ref,
        seg_ref[line : line + 1, :],
        columns_ref,
        seg_ref[0:1, pl.ds(start, plan.rows)],
        start,
        causal,
        scratch,
    )

    def round_block(block, carry):
        rows = pl.ds(pl.multiple_of(block * BLOCK, BLOCK), BLOCK)
        dkl_ref[rows, :] = dk_ref[rows, :].astype(LOW)
        dvl_ref[rows, :] = dv_ref[rows, :].astype(LOW)
        return carry

    lax.fori_loop(0, plan.length // BLOCK, round_block, 0)


def source_parts(plan, info_ref, dkl_ref, dvl_ref, w_ref, which, own_ref, base_ref, mates):
    shard = plan.shard
    for number in range(plan.group):
        first = pl.multiple_of(info_ref[plan.mates + number] * plan.rows, plan.rows)
        for rows in row_blocks(plan.rows):
            source = pl.ds(first + rows.start, BLOCK)
            part = dot_nt(dkl_ref[source, :], weight_of(w_ref, which, shard)) + dot_nt(
                dvl_ref[source, :], weight_of(w_ref, which + 1, shard)
            )
            if number == 0 and base_ref is not None:
                part = part + base_ref[rows, :]
            target = mates[number - 1] if number else own_ref
            target[rows, :] = part.astype(LOW)


def weight_products(plan, info_ref, products, gw_ref, keep_ref, send_ref):
    for which, (left, right) in enumerate(products):
        gw_ref[which] = dot_tn(left[...], right[...]).astype(LOW)
    for which in range(len(products)):
        store_pieces(
            gw_ref.at[which],
            keep_ref,
            send_ref,
            info_ref,
            plan.grad_order,
            which * plan.shard,
            plan.dp,
            plan.shard,
        )


def cross_backward_kernel(plan, chunk_count, piece_count, info_ref, *refs):
    chunks, refs = refs[:chunk_count], refs[chunk_count:]
    pieces, refs = refs[:piece_count], refs[piece_count:]
    (a_ref, z_ref, seg_ref, vec_ref, dvec_ref, dsecond_ref, context_ref), refs = refs[:7], refs[7:]
    (q_ref, o_ref, lse_ref), refs = refs[:3], refs[3:]
    own_ref, refs = refs[0], refs[1:]
    mates, refs = refs[: plan.group - 1], refs[plan.group - 1 :]
    (da_ref, self_do_ref, keep_ref, send_ref), refs = refs[:4], refs[4:]
    m_ref, w_ref, h_ref, gw_ref, grad_ref, low_ref, self_low_ref, *refs = refs
    k_ref, v_ref, do_ref, dq_ref, dkl_ref, dvl_ref, chunk_sems, piece_sems, *buffers = refs
    shard = plan.shard
    copies = chunk_copies(plan, chunks, info_ref, plan.chunk, m_ref, None, chunk_sems)
    copies += piece_copies(
        plan,
        [piece.at[:, pl.ds(3 * shard, 5 * shard)] for piece in pieces],
        info_ref,
        w_ref,
        piece_sems,
    )
    copy_all(copies)
    project_rows(
        plan.length, m_ref, weight_of(w_ref, 2, shard), weight_of(w_ref, 3, shard), k_ref, v_ref
    )
    cross_terms = norm_back(
        plan, 1, z_ref, dsecond_ref, vec_ref, w_ref, 4, grad_ref, low_ref, do_ref
    )
    attention_back(
        plan,
        False,
        info_ref,
        seg_ref,
        (q_ref, k_ref, v_ref, o_ref, do_ref, lse_ref),
        (dq_ref, dkl_ref, dvl_ref),
        buffers,
    )
    for rows in row_blocks(plan.rows):
        grad_ref[rows, :] += dot_nt(dq_ref[rows, :], weight_of(w_ref, 1, shard))
        normed, _ = normalise(a_ref[rows, :])
        h_ref[rows, :] = (normed * vec_ref[0:1, :] + vec_ref[1:2, :]).astype(LOW)
    self_terms = norm_back(
        plan, 0, a_ref, grad_ref, vec_ref, w_ref, 0, da_ref, self_low_ref, self_do_ref
    )
    source_parts(plan, info_ref, dkl_ref, dvl_ref, w_ref, 2, own_ref, None, mates)
    products = (
        (h_ref, dq_ref),
        (m_ref, dkl_ref),
        (m_ref, dvl_ref),
        (o_ref, low_ref),
        (context_ref, self_low_ref),
    )
    weight_products(plan, info_ref, products, gw_ref, keep_ref, send_ref)
    tail = jnp.concatenate(
        [*self_terms, *cross_terms, dvec_ref[4:8, :], jnp.zeros((VECTOR_ROWS - 8, plan.width), WIDE)],
        axis=0,
    ).astype(LOW)
    for number in range(plan.dp // 2):
        keep_ref[number, 5 * shard :, :] = tail
        send_ref[number, 5 * shard :, :] = tail


def self_backward_kernel(plan, chunk_count, piece_count, info_ref, *refs):
    chunks, refs = refs[:chunk_count], refs[chunk_count:]
    pieces, refs = refs[:piece_count], refs[piece_count:]
    (seg_ref, da_ref, do_ref, q_ref, o_ref, lse_ref), refs = refs[:6], refs[6:]
    own_ref, refs = refs[0], refs[1:]
    mates, refs = refs[: plan.group - 1], refs[plan.group - 1 :]
    keep_ref, send_ref, x_ref, own_x_ref, gw_ref, w_ref, *refs = refs
    k_ref, v_ref, base_ref, dq_ref, dkl_ref, dvl_ref, chunk_sems, piece_sems, *buffers = refs
    copies = piece_copies(
        plan,
        [piece.at[:, pl.ds(0, 3 * plan.shard)] for piece in pieces],
        info_ref,
        w_ref,
        piece_sems,
    )
    copies += chunk_copies(plan, chunks, info_ref, 0, x_ref, None, chunk_sems)
    copy_all(copies)
    project_rows(
        plan.length,
        x_ref,
        weight_of(w_ref, 1, plan.shard),
        weight_of(w_ref, 2, plan.shard),
        k_ref,
        v_ref,
    )
    attention_back(
        plan,
        True,
        info_ref,
        seg_ref,
        (q_ref, k_ref, v_ref, o_ref, do_ref, lse_ref),
        (dq_ref, dkl_ref, dvl_ref),
        buffers,
    )
    for rows in row_blocks(plan.rows):
        base_ref[rows, :] = da_ref[rows, :] + dot_nt(
            dq_ref[rows, :], weight_of(w_ref, 0, plan.shard)
        )
    source_parts(plan, info_ref, dkl_ref, dvl_ref, w_ref, 1, own_ref, base_ref, mates)
    start = own_rows(plan, info_ref)
    for rows in row_blocks(plan.rows):
        own_x_ref[rows, :] = x_ref[pl.ds(start + rows.start, BLOCK), :]
    products = ((own_x_ref, dq_ref), (x_ref, dkl_ref), (x_ref, dvl_ref))
    weight_products(plan, info_ref, products, gw_ref, keep_ref, send_ref)


SMEM = pl.BlockSpec(memory_space=pltpu.SMEM)
VMEM = pl.BlockSpec(memory_space=pltpu.VMEM)
ANY = pl.BlockSpec(memory_space=pl.ANY)
HBM = pl.BlockSpec(memory_space=pltpu.HBM)


def call(kernel, specs, operands, outs, scratch, flops, moved, megabytes, out_specs=None):
    return pl.pallas_call(
        kernel,
        in_specs=specs,
        out_specs=out_specs or [VMEM] * len(outs),
        out_shape=outs,
        scratch_shapes=scratch,
        compiler_params=pltpu.CompilerParams(vmem_limit_bytes=megabytes * MEGABYTE),
        cost_estimate=pl.CostEstimate(flops=flops, bytes_accessed=moved, transcendentals=0),
    )(*operands)


def shape(dims, dtype):
    return jax.ShapeDtypeStruct(dims, dtype)


def forward_scratch(plan):
    return [
        pltpu.VMEM((plan.pairs, 2 * BLOCK, PAIR), LOW),
        pltpu.VMEM((plan.pairs, PAIR, 2 * BLOCK), WIDE),
        pltpu.VMEM((8, 2 * BLOCK), WIDE),
        pltpu.VMEM((8, 2 * BLOCK), WIDE),
    ]


def backward_scratch(plan):
    return [
        pltpu.VMEM((plan.pairs, 2 * BLOCK, PAIR), LOW),
        pltpu.VMEM((plan.pairs, 2 * BLOCK, PAIR), LOW),
        pltpu.VMEM((plan.pairs, PAIR, 2 * BLOCK), WIDE),
        pltpu.VMEM((8, 2 * BLOCK), WIDE),
    ]


def flat(pieces):
    return sum(piece.shape[0] for piece in pieces)


def hold_kernel(info_ref, held_ref):
    for place in range(info_ref.shape[0]):
        held_ref[place] = info_ref[place]


def hold(info):
    return call(
        hold_kernel, [SMEM], [info], [shape(info.shape, jnp.int32)], [], 40 * 10**9, 10**5, 1, [SMEM]
    )[0]


def forward(plan, info, chunks, pieces):
    rows, length, width = plan.rows, plan.length, plan.width
    heads = [
        shape((rows, width), LOW),
        shape((rows, width), LOW),
        shape((plan.query_blocks * plan.pairs, 2 * BLOCK), WIDE),
        shape((rows, width), WIDE),
    ]
    outs = heads + [shape((8, length), WIDE), shape((TILE, width), WIDE)] + heads
    scratch = [
        pltpu.VMEM((length, width), LOW),
        pltpu.VMEM((length, width), LOW),
        pltpu.VMEM((length, width), LOW),
        pltpu.VMEM((length, width), LOW),
        pltpu.VMEM((plan.chunks, TILE, width), LOW),
        pltpu.VMEM((plan.dp, 8 * plan.shard + TILE, width), LOW),
        pltpu.VMEM((length, 128), WIDE),
        pltpu.SemaphoreType.DMA((2, plan.chunks)),
        pltpu.SemaphoreType.DMA((2, plan.chunks)),
        pltpu.SemaphoreType.DMA((plan.dp,)),
    ] + forward_scratch(plan)
    return call(
        functools.partial(forward_kernel, plan, len(chunks), len(pieces)),
        [SMEM] + [ANY] * (len(chunks) + len(pieces)),
        [info, *chunks, *pieces],
        outs,
        scratch,
        FORWARD_COST,
        10**5,
        megabytes(plan, 18, 10),
    )


def feed(plan, info, upstreams, pieces, z, vecs):
    rows, width, blocks = plan.rows, plan.width, plan.hidden_blocks
    piece_rows = blocks * plan.shard + plan.outer_shard
    outs = (
        [shape((plan.chunk, width), LOW)] * plan.batches
        + [shape((rows, width), WIDE), shape((8, width), WIDE)]
        + [shape((plan.dp // 2, piece_rows, width), LOW)] * 2
    )
    scratch = [
        pltpu.VMEM((width, plan.hidden), LOW),
        pltpu.VMEM((plan.hidden, width), LOW),
        pltpu.VMEM((rows, width), LOW),
        pltpu.VMEM((rows, plan.hidden), WIDE),
        pltpu.VMEM((rows, plan.hidden), LOW),
        pltpu.VMEM((rows, plan.hidden), LOW),
        pltpu.VMEM((rows, width), WIDE),
        pltpu.VMEM((rows, width), LOW),
        pltpu.VMEM((rows, width), LOW),
        pltpu.VMEM((blocks, width, width), LOW),
        pltpu.VMEM((plan.hidden, width), LOW),
        pltpu.SemaphoreType.DMA((blocks + 1, plan.dp)),
        pltpu.SemaphoreType.DMA((plan.batches,)),
    ]
    return call(
        functools.partial(feed_kernel, plan, len(pieces)),
        [SMEM] + [ANY] * (plan.batches + len(pieces)) + [VMEM] * 2,
        [info, *upstreams, *pieces, z, vecs],
        outs,
        scratch,
        20 * 10**9,
        12 * 10**6,
        28,
    )


def backward_buffers(plan):
    length, width = plan.length, plan.width
    return [
        pltpu.VMEM((length, 128), WIDE),
        pltpu.VMEM((length, width), WIDE),
        pltpu.VMEM((length, width), WIDE),
        pltpu.VMEM((plan.pairs, 2 * BLOCK, PAIR), LOW),
        pltpu.VMEM((plan.pairs, 2 * BLOCK, PAIR), LOW),
        pltpu.VMEM((plan.pairs, PAIR, 2 * BLOCK), WIDE),
        pltpu.VMEM((8, 2 * BLOCK), WIDE),
    ]


def cross_backward(plan, info, chunks, pieces, operands):
    rows, length, width = plan.rows, plan.length, plan.width
    outs = (
        [shape((rows, width), LOW)]
        + [shape((rows, width), LOW)] * (plan.group - 1)
        + [shape((rows, width), WIDE), shape((rows, width), LOW)]
        + [shape((plan.dp // 2, 5 * plan.shard + VECTOR_ROWS, width), LOW)] * 2
    )
    scratch = [
        pltpu.VMEM((length, width), LOW),
        pltpu.VMEM((plan.dp, 5 * plan.shard, width), LOW),
        pltpu.VMEM((rows, width), LOW),
        pltpu.VMEM((5, width, width), LOW),
        pltpu.VMEM((rows, width), WIDE),
        pltpu.VMEM((rows, width), LOW),
        pltpu.VMEM((rows, width), LOW),
        pltpu.VMEM((length, width), LOW),
        pltpu.VMEM((length, width), LOW),
        pltpu.VMEM((rows, width), LOW),
        pltpu.VMEM((rows, width), LOW),
        pltpu.VMEM((length, width), LOW),
        pltpu.VMEM((length, width), LOW),
        pltpu.SemaphoreType.DMA((2, plan.chunks)),
        pltpu.SemaphoreType.DMA((plan.dp,)),
    ] + backward_buffers(plan)
    return call(
        functools.partial(cross_backward_kernel, plan, len(chunks), len(pieces)),
        [SMEM] + [ANY] * (len(chunks) + len(pieces)) + [VMEM] * len(operands),
        [info, *chunks, *pieces, *operands],
        outs,
        scratch,
        22 * 10**9,
        12 * 10**6,
        megabytes(plan, 18, 16),
    )


def self_backward(plan, info, chunks, pieces, operands):
    rows, length, width = plan.rows, plan.length, plan.width
    outs = (
        [shape((rows, width), LOW)]
        + [shape((rows, width), LOW)] * (plan.group - 1)
        + [shape((plan.dp // 2, 3 * plan.shard, width), LOW)] * 2
    )
    scratch = [
        pltpu.VMEM((length, width), LOW),
        pltpu.VMEM((rows, width), LOW),
        pltpu.VMEM((3, width, width), LOW),
        pltpu.VMEM((plan.dp, 3 * plan.shard, width), LOW),
        pltpu.VMEM((length, width), LOW),
        pltpu.VMEM((length, width), LOW),
        pltpu.VMEM((rows, width), WIDE),
        pltpu.VMEM((rows, width), LOW),
        pltpu.VMEM((length, width), LOW),
        pltpu.VMEM((length, width), LOW),
        pltpu.SemaphoreType.DMA((2, plan.chunks)),
        pltpu.SemaphoreType.DMA((plan.dp,)),
    ] + backward_buffers(plan)
    return call(
        functools.partial(self_backward_kernel, plan, len(chunks), len(pieces)),
        [SMEM] + [ANY] * (len(chunks) + len(pieces)) + [VMEM] * len(operands),
        [info, *chunks, *pieces, *operands],
        outs,
        scratch,
        18 * 10**9,
        12 * 10**6,
        megabytes(plan, 12, 12),
    )


def pack_tokens_kernel(plan, info_ref, tokens, memory, target, source, *refs):
    rounds, semaphores = refs[: plan.batches], refs[-1]
    chunk, width = plan.chunk, plan.width
    moves = []
    for number in range(plan.batches):
        batch = info_ref[plan.batch + number]
        moves.append((tokens.at[batch, 0], rounds[number].at[pl.ds(0, chunk)]))
        moves.append((memory.at[batch, 0], rounds[number].at[pl.ds(chunk, chunk)]))
    copies = [
        pltpu.make_async_copy(here, there, semaphores.at[number])
        for number, (here, there) in enumerate(moves)
    ]
    for copy in copies:
        copy.start()
    first_row = lax.broadcasted_iota(jnp.int32, (TILE, width), 0) == 0
    for number in range(plan.batches):
        batch = info_ref[plan.batch + number]
        row = jnp.concatenate([target[batch], source[batch]], axis=1).astype(WIDE)
        if width > 2 * chunk:
            row = jnp.concatenate([row, jnp.zeros((1, width - 2 * chunk), WIDE)], axis=1)
        rounds[number][2 * chunk :, :] = jnp.where(first_row, row, 0.0).astype(LOW)
    for copy in copies:
        copy.wait()


def pack_tokens(plan, info, tokens, memory, target, source):
    return call(
        functools.partial(pack_tokens_kernel, plan),
        [SMEM] + [HBM] * 2 + [VMEM] * 2,
        [info, tokens, memory, target, source],
        [shape((2 * plan.chunk + TILE, plan.width), LOW)] * plan.batches,
        [pltpu.SemaphoreType.DMA((2 * plan.batches,))],
        0,
        10**6,
        60,
    )


def pack_weights_kernel(plan, info_ref, *refs):
    weights, (vectors, piece_ref, lines_ref, semaphores) = refs[:8], refs[8:]
    shard = plan.shard
    copies = [
        pltpu.make_async_copy(
            weight, piece_ref.at[0, pl.ds(which * shard, shard)], semaphores.at[which]
        )
        for which, weight in enumerate(weights)
    ]
    for copy in copies:
        copy.start()
    lines_ref[...] = jnp.zeros_like(lines_ref)
    lines_ref[0:6, 0:shard] = vectors[...].astype(WIDE)
    lanes = pltpu.roll(lines_ref[...], info_ref[plan.own_dp] * shard, 1)
    piece_ref[0, 8 * shard :, :] = lanes.astype(LOW)
    for copy in copies:
        copy.wait()


def pack_weights(plan, info, weights, vectors):
    return call(
        functools.partial(pack_weights_kernel, plan),
        [SMEM] + [HBM] * 8 + [VMEM],
        [info, *weights, vectors],
        [shape((1, 8 * plan.shard + TILE, plan.width), LOW)],
        [pltpu.VMEM((TILE, plan.width), WIDE), pltpu.SemaphoreType.DMA((8,))],
        20 * 10**9,
        10**6,
        60,
    )[0]


def pack_rest_kernel(plan, info_ref, inner, outer, cotangent, feed_ref, *refs):
    rounds, semaphores = refs[: plan.batches], refs[-1]
    shard, width, blocks = plan.shard, plan.width, plan.hidden_blocks
    moves = [
        (
            inner.at[:, pl.ds(block * width, width)],
            feed_ref.at[0, pl.ds(block * shard, shard)],
        )
        for block in range(blocks)
    ]
    moves.append((outer, feed_ref.at[0, pl.ds(blocks * shard, plan.outer_shard)]))
    for number in range(plan.batches):
        moves.append((cotangent.at[info_ref[plan.batch + number], 0], rounds[number]))
    copy_all(
        [
            pltpu.make_async_copy(here, there, semaphores.at[number])
            for number, (here, there) in enumerate(moves)
        ]
    )


def pack_rest(plan, info, inner, outer, cotangent):
    outs = [shape((1, plan.hidden_blocks * plan.shard + plan.outer_shard, plan.width), LOW)]
    outs += [shape((plan.chunk, plan.width), LOW)] * plan.batches
    return call(
        functools.partial(pack_rest_kernel, plan),
        [SMEM] + [HBM] * 3,
        [info, inner, outer, cotangent],
        outs,
        [pltpu.SemaphoreType.DMA((plan.hidden_blocks + 1 + plan.batches,))],
        0,
        2 * 10**6,
        60,
    )


def pairs_of(plan, move):
    return [
        (dp * plan.seq + seq, to[0] * plan.seq + to[1])
        for dp in range(plan.dp)
        for seq in range(plan.seq)
        for to in [move(dp, seq)]
    ]


def home(plan, dp, batch, seq):
    position = (2 * batch + dp % 2) * plan.group + seq // plan.batches
    return (dp - dp % 2 + position % 2, position // 2)


def round_batch(plan, seq, number):
    return (seq + number) % plan.batches


def inward(plan, number):
    return pairs_of(plan, lambda dp, seq: home(plan, dp, round_batch(plan, seq, number), seq))


def outward(plan, number):
    return [(to, source) for source, to in inward(plan, number)]


def mate(plan, turn):
    def move(dp, seq):
        position = 2 * seq + dp % 2
        group, own = position // plan.group, position % plan.group
        to = group * plan.group + (own + turn) % plan.group
        return (dp - dp % 2 + to % 2, to // 2)

    return pairs_of(plan, move)


def permute(values, pairs):
    return lax.ppermute(values, AXES, pairs)


def dp_flip(plan, bits):
    return pairs_of(plan, lambda dp, seq: (dp ^ bits, seq))


def seq_flip(plan, bits):
    return pairs_of(plan, lambda dp, seq: (dp, seq ^ bits))


def share_inputs(plan, rounds):
    return [permute(piece, inward(plan, number)) for number, piece in enumerate(rounds)]


def share_mates(plan, received):
    chunks = list(received)
    for turn in range(1, plan.group):
        chunks += [permute(piece, mate(plan, turn)) for piece in received]
    return chunks


def send_home(plan, pieces):
    return [permute(piece, outward(plan, number)) for number, piece in enumerate(pieces)]


def order_home(plan, landed, dtype):
    seq = lax.axis_index("seq")
    landed = jnp.stack(landed).astype(dtype)
    order = [(batch - seq) % plan.batches for batch in range(plan.batches)]
    return jnp.stack(
        [lax.dynamic_index_in_dim(landed, index, 0, keepdims=False) for index in order]
    )


def gather_direct(plan, shard):
    if plan.dp != 8:
        return [lax.all_gather(shard[0], "dp", axis=0)]
    return [shard] + [permute(shard, dp_flip(plan, bits)) for bits in (2, 4, 6)]


def gather_rest(plan, direct):
    if plan.dp != 8:
        return direct
    pieces = []
    for piece in direct:
        pieces += [piece, permute(piece, dp_flip(plan, 1))]
    return pieces


def add_low(values):
    total = values[0].astype(WIDE)
    for value in values[1:]:
        total = total + value.astype(WIDE)
    return total.astype(LOW)


def core_send(plan, send):
    return permute(send, dp_flip(plan, 1)) if plan.dp == 8 else send


def core_sum(plan, keep, other):
    if plan.dp != 8:
        return [jnp.concatenate([keep, other], axis=0)]
    return [add_low([keep[number], other[number]]) for number in range(4)]


def plane_send(plan, parts):
    if plan.dp != 8:
        return [lax.psum_scatter(parts[0], "dp", scatter_dimension=0)]
    return [permute(parts[number], dp_flip(plan, 2 * number)) for number in range(1, 4)]


def plane_sum(plan, parts, landed):
    total = landed[0] if plan.dp != 8 else add_low([parts[0], *landed])
    return total if plan.seq == 4 else lax.psum(total, "seq")


def halves(plan, total, bits):
    if plan.seq != 4:
        return total, jnp.zeros_like(total)
    half = total.shape[0] // 2
    own = lax.axis_index("seq") // bits % 2
    return (
        lax.dynamic_slice_in_dim(total, own * half, half),
        lax.dynamic_slice_in_dim(total, (1 - own) * half, half),
    )


def seq_send(plan, values, bits):
    return permute(values, seq_flip(plan, bits)) if plan.seq == 4 else jnp.zeros_like(values)


def join(plan, own_part, other, bits):
    if plan.seq != 4:
        return own_part
    own = lax.axis_index("seq") // bits % 2
    return jnp.where(
        own == 0, jnp.concatenate([own_part, other]), jnp.concatenate([other, own_part])
    )


def add_wide(first, second):
    return first.astype(WIDE) + second.astype(WIDE)


def tie(*values):
    return lax.optimization_barrier(values)


def after(values, *others):
    return lax.optimization_barrier((values, others))[0]


def plan_info(plan):
    dp, seq = lax.axis_index("dp"), lax.axis_index("seq")
    position = 2 * seq + dp % 2
    own = position % plan.group
    batch = position // plan.group // 2
    flips = list(range(8)) if plan.dp == 8 else None
    entries = []
    if flips:
        entries += [dp ^ bits for bits in (0, 1, 2, 3, 4, 5, 6, 7)]
        entries += [dp ^ bits for bits in (0, 2, 4, 6, 1, 3, 5, 7)]
    else:
        entries += list(range(plan.dp)) * 2
    places = [(batch - number) % plan.batches for number in range(plan.batches)]
    for turn in range(plan.group):
        source = (own - turn) % plan.group
        entries += [source * plan.batches + place for place in places]
    entries.append(own)
    entries += places
    entries += [(own + turn) % plan.group for turn in range(plan.group)]
    entries += [(seq + number) % plan.batches for number in range(plan.batches)]
    entries.append(dp)
    plan.places = [place.astype(jnp.uint32) for place in places]
    return jnp.stack([jnp.asarray(entry, jnp.int32) for entry in entries])


def on_device(
    tokens,
    memory,
    target_segments,
    source_segments,
    cotangent,
    query_weight,
    key_weight,
    value_weight,
    output_weight,
    cross_query,
    cross_key,
    cross_value,
    cross_output,
    inner_weight,
    outer_weight,
    self_gain,
    self_shift,
    cross_gain,
    cross_shift,
    feed_gain,
    feed_shift,
):
    plan = Plan(tokens, inner_weight)
    width, shard = plan.width, plan.shard
    info = plan_info(plan)
    dp = lax.axis_index("dp")

    vectors = jnp.stack([self_gain, self_shift, cross_gain, cross_shift, feed_gain, feed_shift])
    rounds = pack_tokens(plan, info, tokens, memory, target_segments, source_segments)
    shard_piece = pack_weights(
        plan,
        info,
        [
            query_weight,
            key_weight,
            value_weight,
            output_weight,
            cross_query,
            cross_key,
            cross_value,
            cross_output,
        ],
        vectors,
    )
    direct = gather_direct(plan, shard_piece)
    landed = share_inputs(plan, rounds)

    feed_shard, *rounds = pack_rest(plan, info, inner_weight, outer_weight, cotangent)
    feed_shard, rounds, landed[0] = lax.optimization_barrier((feed_shard, rounds, landed[0]))
    info, feed_shard = lax.optimization_barrier((info, feed_shard))
    feed_direct = gather_direct(plan, feed_shard)
    upstreams = share_inputs(plan, rounds)
    direct, landed, info = lax.optimization_barrier((direct, landed, hold(info)))
    pieces = gather_rest(plan, direct)
    chunks = share_mates(plan, landed)
    q, o, lse, a, segs, vecs, cq, co, cross_lse, z = forward(
        plan, info, chunks, pieces
    )

    feed_direct, upstreams = after((feed_direct, upstreams), z)
    feed_pieces = gather_rest(plan, feed_direct)
    *results, dsecond, dvec, feed_keep, feed_send = feed(
        plan, info, upstreams, feed_pieces, z, vecs
    )

    feed_parts = core_sum(plan, feed_keep, core_send(plan, feed_send))
    out_landed = send_home(plan, results)
    feed_landed = plane_send(plan, feed_parts)
    dsecond = after(dsecond, feed_parts)
    back = cross_backward(
        plan,
        info,
        chunks,
        pieces,
        [a, z, segs, vecs, dvec, dsecond, o, cq, co, cross_lse],
    )
    back, feed_landed, out_landed = lax.optimization_barrier((back, feed_landed, out_landed))
    own_memory, *others = back
    mate_memory, (da, do, cross_keep, cross_send) = (
        others[: plan.group - 1],
        others[plan.group - 1 :],
    )

    feed_keep, feed_send = halves(plan, plane_sum(plan, feed_parts, feed_landed), 1)
    cross_parts = core_sum(plan, cross_keep, core_send(plan, cross_send))
    memory_pieces = add_mates(plan, own_memory, mate_memory)
    feed_landed = seq_send(plan, feed_send, 1)
    cross_landed = plane_send(plan, cross_parts)
    memory_landed = send_home(plan, memory_pieces)
    feed_landed, cross_parts[0], memory_pieces = tie(feed_landed, cross_parts[0], memory_pieces)
    feed_keep, feed_send = halves(plan, add_low([feed_keep, feed_landed]), 2)
    feed_landed = seq_send(plan, feed_send, 2)
    do, feed_keep = tie(do, feed_keep)
    back = self_backward(plan, info, chunks, pieces, [segs, da, do, q, o, lse])
    back, feed_landed, cross_landed, memory_landed = lax.optimization_barrier(
        (back, feed_landed, cross_landed, memory_landed)
    )
    own_tokens, *mate_tokens, self_keep, self_send = back

    mate_landed = send_mates(plan, mate_tokens)
    self_landed = core_send(plan, self_send)
    feed_quarter = add_low([feed_keep, feed_landed])
    feed_landed = seq_send(plan, feed_quarter, 2)
    cross_keep, cross_send = halves(plan, plane_sum(plan, cross_parts, cross_landed), 1)
    cross_landed = seq_send(plan, cross_send, 1)
    token_pieces = sum_mates(plan, own_tokens, mate_landed)
    token_landed = send_home(plan, token_pieces)
    self_landed, token_landed[0], cross_keep, feed_quarter = tie(
        self_landed, token_landed[0], cross_keep, feed_quarter
    )
    self_parts = core_sum(plan, self_keep, self_landed)
    self_landed = plane_send(plan, self_parts)
    feed_landed, cross_landed = after((feed_landed, cross_landed), self_parts)
    feed_half = join(plan, feed_quarter, feed_landed, 2)
    feed_landed = seq_send(plan, feed_half, 1)
    cross_keep, cross_send = halves(plan, add_low([cross_keep, cross_landed]), 2)
    cross_landed = seq_send(plan, cross_send, 2)
    self_landed, feed_half, cross_keep = tie(self_landed, feed_half, cross_keep)
    self_total = plane_sum(plan, self_parts, self_landed)
    self_landed = seq_send(plan, self_total, 1)
    cross_landed, self_total = tie(cross_landed, self_total)
    cross_quarter = add_low([cross_keep, cross_landed])
    cross_landed = seq_send(plan, cross_quarter, 2)
    self_landed, cross_quarter = tie(self_landed, cross_quarter)
    self_total = add_low([self_total, self_landed])
    self_landed = seq_send(plan, self_total, 2)
    cross_landed, self_total, out_landed, memory_landed = tie(
        cross_landed, self_total, out_landed, memory_landed
    )
    cross_half = join(plan, cross_quarter, cross_landed, 2)
    cross_landed = seq_send(plan, cross_half, 1)
    out_tokens = order_home(plan, out_landed, LOW)
    grad_memory = order_home(plan, memory_landed, WIDE)
    grad_tokens = order_home(plan, token_landed, WIDE)
    self_landed, cross_landed, out_tokens, grad_memory, grad_tokens = tie(
        self_landed, cross_landed, out_tokens, grad_memory, grad_tokens
    )
    feed_total = join(plan, feed_half, feed_landed, 1).astype(WIDE)
    cross_total = join(plan, cross_half, cross_landed, 1).astype(WIDE)
    self_total = add_wide(self_total, self_landed)

    scale = 1.0 / (plan.batches * plan.dp)
    feed_grads, cross_grads, self_grads = (
        feed_total * scale,
        cross_total * scale,
        self_total * scale,
    )
    inner_grads = [
        feed_grads[block * shard : (block + 1) * shard] for block in range(plan.hidden_blocks)
    ]
    vector_grads = lax.dynamic_slice(cross_grads, (5 * shard, dp * shard), (TILE, shard))
    return (
        out_tokens[:, None],
        grad_tokens[:, None],
        grad_memory[:, None],
        *[self_grads[which * shard : (which + 1) * shard] for which in range(3)],
        cross_grads[4 * shard : 5 * shard],
        *[cross_grads[which * shard : (which + 1) * shard] for which in range(4)],
        jnp.concatenate(inner_grads, axis=1),
        feed_grads[plan.hidden_blocks * shard :],
        *[vector_grads[which] for which in range(6)],
    )


def send_mates(plan, mates):
    return [permute(part, mate(plan, turn)) for turn, part in enumerate(mates, 1)]


def sum_mates(plan, own, landed):
    own = own.astype(WIDE)
    for part in landed:
        own = own + part.astype(WIDE)
    own = own.reshape(plan.batches, plan.chunk, plan.width)
    return [
        lax.dynamic_index_in_dim(own, place, 0, keepdims=False).astype(LOW)
        for place in plan.places
    ]


def add_mates(plan, own, mates):
    return sum_mates(plan, own, send_mates(plan, mates))


def solution(mesh):
    tokens = P(None, "dp", "seq", None)
    ids = P(None, "dp", "seq")
    weight = P("dp", None)
    vector = P("dp")
    return jax.shard_map(
        on_device,
        mesh=mesh,
        in_specs=(tokens, tokens, ids, ids, tokens) + (weight,) * 10 + (vector,) * 6,
        out_specs=(tokens,) * 3 + (weight,) * 10 + (vector,) * 6,
        check_vma=False,
    )
```

```python
import functools

import jax
import jax.numpy as jnp
from jax import lax
from jax.experimental import pallas as pl
from jax.experimental.pallas import tpu as pltpu
from jax.sharding import PartitionSpec as P

DH = 64
PAIR = 2 * DH
BLOCK = 256
TILE = 16
VECTOR_ROWS = 16
FORWARD_COST = 10**6
EPSILON = 1e-05
NEGATIVE = -1e30
FACTOR = DH ** (-0.5)
AXES = ("dp", "seq")
LOW = jnp.bfloat16
WIDE = jnp.float32
MEGABYTE = 1024 * 1024


def dot_nn(a, b):
    return jnp.dot(a, b, preferred_element_type=WIDE)


def dot_nt(a, b):
    return lax.dot_general(a, b, (((1,), (1,)), ((), ())), preferred_element_type=WIDE)


def dot_tn(a, b):
    return lax.dot_general(a, b, (((0,), (0,)), ((), ())), preferred_element_type=WIDE)


def normalise(values):
    centred = values - jnp.mean(values, axis=-1, keepdims=True)
    inverse = lax.rsqrt(jnp.mean(centred * centred, axis=-1, keepdims=True) + EPSILON)
    return centred * inverse, inverse


def norm_backward(upstream, normed, inverse, gain_row):
    scaled = upstream * gain_row
    plain_mean = jnp.mean(scaled, axis=-1, keepdims=True)
    along_mean = jnp.mean(scaled * normed, axis=-1, keepdims=True)
    return inverse * (scaled - plain_mean - normed * along_mean)


def row_blocks(length, size=BLOCK):
    return [pl.ds(start, size) for start in range(0, length, size)]


def copy_all(copies):
    for copy in copies:
        copy.start()
    for copy in copies:
        copy.wait()


def piece_copies(plan, pieces, info_ref, w_ref, semaphores):
    copies = []
    for piece in pieces:
        for slab in range(piece.shape[0]):
            number = len(copies)
            owner = info_ref[plan.order + number]
            copies.append(
                pltpu.make_async_copy(piece.at[slab], w_ref.at[owner], semaphores.at[number])
            )
    return copies


def weight_of(weight_ref, which, rows):
    count, _, width = weight_ref.shape
    return weight_ref[:, which * rows : (which + 1) * rows, :].reshape(count * rows, width)


def seg_columns(seg_row):
    return jnp.transpose(jnp.broadcast_to(seg_row, (128, seg_row.shape[1])))


def stack_heads(pair):
    lane = lax.broadcasted_iota(jnp.int32, pair.shape, 1)
    zero = jnp.zeros_like(pair)
    return jnp.concatenate(
        [jnp.where(lane < DH, pair, zero), jnp.where(lane < DH, zero, pair)], axis=0
    )


def unstack_heads(columns):
    row = lax.broadcasted_iota(jnp.int32, (PAIR, BLOCK), 0)
    return jnp.where(row < DH, columns[:, :BLOCK], columns[:, BLOCK:])


def mask_bias(key_ids, query_ids, key_start, query_start, causal):
    ids = jnp.concatenate([key_ids, key_ids], axis=1)
    allowed = ids == query_ids
    if causal:
        key_place = key_start + lax.broadcasted_iota(jnp.int32, (BLOCK, BLOCK), 0)
        query_place = query_start + lax.broadcasted_iota(jnp.int32, (BLOCK, BLOCK), 1)
        allowed = jnp.logical_and(allowed, key_place <= query_place)
    bias = jnp.where(allowed, 0.0, NEGATIVE)
    return jnp.concatenate([bias, bias], axis=1)


def key_bounds(key_row, query_ids, query_start, causal):
    below = jnp.sum(jnp.where(key_row < jnp.min(query_ids), 1.0, 0.0)).astype(jnp.int32)
    first = lax.div(below, BLOCK)
    if causal:
        return first, lax.div(query_start, BLOCK) + 1
    upto = jnp.sum(jnp.where(key_row <= jnp.max(query_ids), 1.0, 0.0)).astype(jnp.int32)
    return first, lax.div(upto + (BLOCK - 1), BLOCK)


def attend_forward(
    q_ref, k_ref, v_ref, o_ref, lse_ref, key_row, columns_ref, query_row, start, causal, scratch
):
    stack_ref, sum_ref, top_ref, total_ref = scratch
    pairs = q_ref.shape[1] // PAIR
    for number, rows in enumerate(row_blocks(q_ref.shape[0])):
        query_ids = query_row[:, number * BLOCK : (number + 1) * BLOCK]
        query_start = start + number * BLOCK
        low, high = key_bounds(key_row, query_ids, query_start, causal)
        for pair in range(pairs):
            stack_ref[pair] = stack_heads(q_ref[rows, pair * PAIR : (pair + 1) * PAIR])
        sum_ref[...] = jnp.zeros_like(sum_ref)
        top_ref[...] = jnp.full_like(top_ref, NEGATIVE)
        total_ref[...] = jnp.zeros_like(total_ref)

        def one_block(block, carry):
            key_start = pl.multiple_of(block * BLOCK, BLOCK)
            keys = pl.ds(key_start, BLOCK)
            bias = mask_bias(columns_ref[keys, :], query_ids, key_start, query_start, causal)
            values = [
                (
                    k_ref[keys, pair * PAIR : (pair + 1) * PAIR],
                    v_ref[keys, pair * PAIR : (pair + 1) * PAIR],
                    stack_ref[pair],
                    top_ref[pair : pair + 1, :],
                    total_ref[pair : pair + 1, :],
                    sum_ref[pair],
                )
                for pair in range(pairs)
            ]
            scores = [dot_nt(key_pair, queries) + bias for key_pair, _, queries, *_ in values]
            tops = [
                jnp.maximum(value[3], jnp.max(score, axis=0, keepdims=True))
                for value, score in zip(values, scores)
            ]
            exponents = [jnp.exp(score - top) for score, top in zip(scores, tops)]
            shrinks = [jnp.exp(value[3] - top) for value, top in zip(values, tops)]
            totals = [
                value[4] * shrink + jnp.sum(exponent, axis=0, keepdims=True)
                for value, shrink, exponent in zip(values, shrinks, exponents)
            ]
            sums = [
                value[5] * shrink + dot_tn(value[1], exponent.astype(LOW))
                for value, shrink, exponent in zip(values, shrinks, exponents)
            ]
            for pair in range(pairs):
                top_ref[pair : pair + 1, :] = tops[pair]
                total_ref[pair : pair + 1, :] = totals[pair]
                sum_ref[pair] = sums[pair]
            return carry

        lax.fori_loop(low, high, one_block, 0)
        for pair in range(pairs):
            total = total_ref[pair : pair + 1, :]
            context = unstack_heads(sum_ref[pair] / total)
            o_ref[rows, pair * PAIR : (pair + 1) * PAIR] = jnp.transpose(context).astype(LOW)
            place = number * pairs + pair
            lse_ref[place : place + 1, :] = top_ref[pair : pair + 1, :] + jnp.log(total)


def attend_backward(
    q_ref,
    k_ref,
    v_ref,
    o_ref,
    grad_ref,
    lse_ref,
    dq_ref,
    dk_ref,
    dv_ref,
    key_row,
    columns_ref,
    query_row,
    start,
    causal,
    scratch,
):
    stack_ref, stack_grad_ref, sum_ref, along_ref = scratch
    pairs = q_ref.shape[1] // PAIR
    dk_ref[...] = jnp.zeros_like(dk_ref)
    dv_ref[...] = jnp.zeros_like(dv_ref)
    for number, rows in enumerate(row_blocks(q_ref.shape[0])):
        query_ids = query_row[:, number * BLOCK : (number + 1) * BLOCK]
        query_start = start + number * BLOCK
        low, high = key_bounds(key_row, query_ids, query_start, causal)
        for pair in range(pairs):
            lanes = slice(pair * PAIR, (pair + 1) * PAIR)
            grad = grad_ref[rows, lanes]
            stack_ref[pair] = stack_heads(q_ref[rows, lanes])
            stack_grad_ref[pair] = stack_heads(grad)
            along = jnp.transpose(grad.astype(WIDE) * o_ref[rows, lanes].astype(WIDE))
            along_ref[pair : pair + 1, :] = jnp.concatenate(
                [
                    jnp.sum(along[:DH], axis=0, keepdims=True),
                    jnp.sum(along[DH:], axis=0, keepdims=True),
                ],
                axis=1,
            )
        sum_ref[...] = jnp.zeros_like(sum_ref)

        def one_block(block, carry):
            key_start = pl.multiple_of(block * BLOCK, BLOCK)
            keys = pl.ds(key_start, BLOCK)
            bias = mask_bias(columns_ref[keys, :], query_ids, key_start, query_start, causal)
            for pair in range(pairs):
                lanes = slice(pair * PAIR, (pair + 1) * PAIR)
                place = number * pairs + pair
                key_pair = k_ref[keys, lanes]
                scores = dot_nt(key_pair, stack_ref[pair]) + bias
                probs = jnp.exp(scores - lse_ref[place : place + 1, :])
                prob_grad = dot_nt(v_ref[keys, lanes], stack_grad_ref[pair])
                score_grad = (probs * (prob_grad - along_ref[pair : pair + 1, :])).astype(LOW)
                dv_ref[keys, lanes] += dot_nn(probs.astype(LOW), stack_grad_ref[pair])
                dk_ref[keys, lanes] += dot_nn(score_grad, stack_ref[pair])
                sum_ref[pair] += dot_tn(key_pair, score_grad)
            return carry

        lax.fori_loop(low, high, one_block, 0)
        for pair in range(pairs):
            grad = jnp.transpose(unstack_heads(sum_ref[pair])) * FACTOR
            dq_ref[rows, pair * PAIR : (pair + 1) * PAIR] = grad.astype(LOW)


def store_pieces(grad_ref, keep_ref, send_ref, info_ref, order, offset, count, rows):
    half = count // 2
    for number in range(count):
        owner = info_ref[order + number]
        block = grad_ref[pl.ds(pl.multiple_of(owner * rows, rows), rows), :]
        target = keep_ref if number < half else send_ref
        target[number % half, offset : offset + rows, :] = block


class Plan:
    def __init__(self, tokens, inner_weight):
        self.dp = lax.axis_size("dp")
        self.seq = lax.axis_size("seq")
        self.batches, _, self.chunk, self.width = tokens.shape
        self.hidden = inner_weight.shape[1]
        self.length = self.chunk * self.seq
        self.group = self.seq // self.batches
        self.rows = self.batches * self.chunk
        self.chunks = self.seq
        self.shard = self.width // self.dp
        self.outer_shard = self.hidden // self.dp
        self.hidden_blocks = self.hidden // self.width
        self.pairs = self.width // PAIR
        self.query_blocks = self.rows // BLOCK
        self.order = 0
        self.grad_order = self.dp
        self.chunk_order = 2 * self.dp
        self.own = self.chunk_order + self.chunks
        self.round = self.own + 1
        self.mates = self.round + self.batches
        self.batch = self.mates + self.group
        self.own_dp = self.batch + self.batches


def megabytes(plan, fixed, by_length):
    return fixed + -(-by_length * plan.length // 1024)


def seg_rows(plan, raw_ref, seg_ref):
    for number in range(plan.chunks):
        lanes = slice(number * plan.chunk, (number + 1) * plan.chunk)
        seg_ref[0:1, lanes] = raw_ref[number, 0:1, : plan.chunk].astype(WIDE)
        seg_ref[1:2, lanes] = raw_ref[number, 0:1, plan.chunk : 2 * plan.chunk].astype(WIDE)


def own_rows(plan, info_ref):
    return pl.multiple_of(info_ref[plan.own] * plan.rows, plan.rows)


def chunk_copies(plan, chunks, info_ref, first, x_ref, raw_ref, semaphores):
    copies = []
    for number, chunk in enumerate(chunks):
        index = info_ref[plan.chunk_order + number]
        rows = pl.ds(pl.multiple_of(index * plan.chunk, plan.chunk), plan.chunk)
        copies.append(
            pltpu.make_async_copy(
                chunk.at[pl.ds(first, plan.chunk)], x_ref.at[rows], semaphores.at[0, number]
            )
        )
        if raw_ref is not None:
            copies.append(
                pltpu.make_async_copy(
                    chunk.at[pl.ds(2 * plan.chunk, TILE)],
                    raw_ref.at[index],
                    semaphores.at[1, number],
                )
            )
    return copies


def project_rows(length, source_ref, key_weight, value_weight, k_ref, v_ref):
    for rows in row_blocks(length, 2 * BLOCK):
        k_ref[rows, :] = dot_nn(source_ref[rows, :], key_weight).astype(LOW)
        v_ref[rows, :] = dot_nn(source_ref[rows, :], value_weight).astype(LOW)


def forward_kernel(plan, chunk_count, piece_count, info_ref, *refs):
    chunks, refs = refs[:chunk_count], refs[chunk_count:]
    pieces, refs = refs[:piece_count], refs[piece_count:]
    (q_ref, o_ref, lse_ref, a_ref, seg_ref, vec_ref), refs = refs[:6], refs[6:]
    (cq_ref, co_ref, cross_lse_ref, z_ref, k_ref, v_ref), refs = refs[:6], refs[6:]
    x_ref, m_ref, raw_ref, w_ref, columns_ref, chunk_sems, m_sems, piece_sems, *scratch = refs
    load = chunk_copies(plan, chunks, info_ref, 0, x_ref, raw_ref, chunk_sems)
    load += chunk_copies(plan, chunks, info_ref, plan.chunk, m_ref, None, m_sems)
    load += piece_copies(plan, pieces, info_ref, w_ref, piece_sems)
    copy_all(load)
    shard = plan.shard
    start = own_rows(plan, info_ref)
    vec_ref[...] = jnp.sum(w_ref[:, 8 * shard :, :].astype(WIDE), axis=0)
    seg_rows(plan, raw_ref, seg_ref)
    columns_ref[...] = seg_columns(seg_ref[0:1, :])
    for rows in row_blocks(plan.rows):
        own = x_ref[pl.ds(start + rows.start, BLOCK), :]
        q_ref[rows, :] = (dot_nn(own, weight_of(w_ref, 0, shard)) * FACTOR).astype(LOW)
    project_rows(
        plan.length,
        x_ref,
        weight_of(w_ref, 1, shard),
        weight_of(w_ref, 2, shard),
        k_ref,
        v_ref,
    )
    attend_forward(
        q_ref,
        k_ref,
        v_ref,
        o_ref,
        lse_ref,
        seg_ref[0:1, :],
        columns_ref,
        seg_ref[0:1, pl.ds(start, plan.rows)],
        start,
        True,
        scratch,
    )
    gain, shift = vec_ref[0:1, :], vec_ref[1:2, :]
    for rows in row_blocks(plan.rows):
        own = x_ref[pl.ds(start + rows.start, BLOCK), :].astype(WIDE)
        a = own + dot_nn(o_ref[rows, :], weight_of(w_ref, 3, shard))
        a_ref[rows, :] = a
        normed, _ = normalise(a)
        first = normed * gain + shift
        z_ref[rows, :] = first
        cq_ref[rows, :] = (
            dot_nn(first.astype(LOW), weight_of(w_ref, 4, shard)) * FACTOR
        ).astype(LOW)
    project_rows(
        plan.length,
        m_ref,
        weight_of(w_ref, 5, shard),
        weight_of(w_ref, 6, shard),
        k_ref,
        v_ref,
    )
    columns_ref[...] = seg_columns(seg_ref[1:2, :])
    attend_forward(
        cq_ref,
        k_ref,
        v_ref,
        co_ref,
        cross_lse_ref,
        seg_ref[1:2, :],
        columns_ref,
        seg_ref[0:1, pl.ds(start, plan.rows)],
        start,
        False,
        scratch,
    )
    for rows in row_blocks(plan.rows):
        z_ref[rows, :] += dot_nn(co_ref[rows, :], weight_of(w_ref, 7, shard))


def feed_kernel(plan, piece_count, info_ref, *refs):
    batches = plan.batches
    upstreams, refs = refs[:batches], refs[batches:]
    pieces, refs = refs[:piece_count], refs[piece_count:]
    (z_ref, vec_ref), refs = refs[:2], refs[2:]
    outs, refs = refs[:batches], refs[batches:]
    (dh_ref, dvec_ref, keep_ref, send_ref), refs = refs[:4], refs[4:]
    inner_ref, outer_ref, low_ref, u_ref, r_ref, du_ref, f_ref, up_ref, res_ref, *refs = refs
    inner_gw_ref, outer_gw_ref, piece_sems, up_sems = refs
    width, shard, blocks, outer_shard = (
        plan.width,
        plan.shard,
        plan.hidden_blocks,
        plan.outer_shard,
    )
    copies = []
    number = 0
    for piece in pieces:
        for slab in range(piece.shape[0]):
            owner = info_ref[plan.order + number]
            for block in range(blocks):
                copies.append(
                    pltpu.make_async_copy(
                        piece.at[slab, pl.ds(block * shard, shard)],
                        inner_ref.at[
                            pl.ds(pl.multiple_of(owner * shard, shard), shard),
                            pl.ds(block * width, width),
                        ],
                        piece_sems.at[block, number],
                    )
                )
            copies.append(
                pltpu.make_async_copy(
                    piece.at[slab, pl.ds(blocks * shard, outer_shard)],
                    outer_ref.at[pl.ds(pl.multiple_of(owner * outer_shard, outer_shard), outer_shard)],
                    piece_sems.at[blocks, number],
                )
            )
            number += 1
    for number in range(batches):
        index = info_ref[plan.round + number]
        rows = pl.ds(pl.multiple_of(index * plan.chunk, plan.chunk), plan.chunk)
        copies.append(
            pltpu.make_async_copy(upstreams[number], up_ref.at[rows], up_sems.at[number])
        )
    for copy in copies:
        copy.start()
    gain_two, shift_two = vec_ref[2:3, :], vec_ref[3:4, :]
    gain_three, shift_three = vec_ref[4:5, :], vec_ref[5:6, :]
    gain_grad = jnp.zeros((1, width), WIDE)
    shift_grad = jnp.zeros((1, width), WIDE)
    for rows in row_blocks(plan.rows):
        normed, _ = normalise(z_ref[rows, :])
        second = normed * gain_two + shift_two
        f_ref[rows, :] = second
        low_ref[rows, :] = second.astype(LOW)
    for copy in copies:
        copy.wait()
    lanes = [slice(block * width, (block + 1) * width) for block in range(blocks)]
    for part in lanes:
        u = dot_nn(low_ref[...], inner_ref[:, part])
        phi = 0.5 + 0.5 * lax.erf(u * (0.5**0.5))
        r_ref[:, part] = (u * phi).astype(LOW)
        u_ref[:, part] = phi + u * (jnp.exp(-0.5 * u * u) * 0.3989422804014327)
    for rows in row_blocks(plan.rows):
        f = f_ref[rows, :] + dot_nn(r_ref[rows, :], outer_ref[...])
        normed, inverse = normalise(f)
        res_ref[rows, :] = (normed * gain_three + shift_three).astype(LOW)
        upstream = up_ref[rows, :].astype(WIDE)
        gain_grad += jnp.sum(upstream * normed, axis=0, keepdims=True)
        shift_grad += jnp.sum(upstream, axis=0, keepdims=True)
        feed_grad = norm_backward(upstream, normed, inverse, gain_three)
        dh_ref[rows, :] = feed_grad
        up_ref[rows, :] = feed_grad.astype(LOW)
    for number in range(batches):
        index = info_ref[plan.round + number]
        outs[number][...] = res_ref[pl.ds(pl.multiple_of(index * plan.chunk, plan.chunk), plan.chunk), :]
    for part in lanes:
        dr = dot_nt(up_ref[...], outer_ref[part, :]).astype(LOW).astype(WIDE)
        du_ref[:, part] = (dr * u_ref[:, part]).astype(LOW)
        outer_gw_ref[part, :] = dot_tn(r_ref[:, part], up_ref[...]).astype(LOW)
    for block, part in enumerate(lanes):
        inner_gw_ref[block] = dot_tn(low_ref[...], du_ref[:, part]).astype(LOW)
    for rows in row_blocks(plan.rows):
        dh_ref[rows, :] += dot_nt(du_ref[rows, :], inner_ref[...])
    for block in range(blocks):
        store_pieces(
            inner_gw_ref.at[block],
            keep_ref,
            send_ref,
            info_ref,
            plan.grad_order,
            block * shard,
            plan.dp,
            shard,
        )
    store_pieces(
        outer_gw_ref,
        keep_ref,
        send_ref,
        info_ref,
        plan.grad_order,
        blocks * shard,
        plan.dp,
        outer_shard,
    )
    dvec_ref[...] = jnp.zeros_like(dvec_ref)
    dvec_ref[4:5, :] = gain_grad
    dvec_ref[5:6, :] = shift_grad


def norm_back(plan, line, z_ref, upstream_ref, vec_ref, w_ref, which, grad_ref, low_ref, do_ref):
    gain_grad = jnp.zeros((1, plan.width), WIDE)
    shift_grad = jnp.zeros((1, plan.width), WIDE)
    for rows in row_blocks(plan.rows):
        normed, inverse = normalise(z_ref[rows, :])
        upstream = upstream_ref[rows, :]
        gain_grad += jnp.sum(upstream * normed, axis=0, keepdims=True)
        shift_grad += jnp.sum(upstream, axis=0, keepdims=True)
        grad = norm_backward(upstream, normed, inverse, vec_ref[2 * line : 2 * line + 1, :])
        grad_ref[rows, :] = grad
        low_ref[rows, :] = grad.astype(LOW)
        do_ref[rows, :] = dot_nt(low_ref[rows, :], weight_of(w_ref, which, plan.shard)).astype(LOW)
    return gain_grad, shift_grad


def attention_back(plan, causal, info_ref, seg_ref, operands, results, buffers):
    q_ref, k_ref, v_ref, o_ref, do_ref, lse_ref = operands
    dq_ref, dkl_ref, dvl_ref = results
    columns_ref, dk_ref, dv_ref, *scratch = buffers
    start = own_rows(plan, info_ref)
    line = 0 if causal else 1
    columns_ref[...] = seg_columns(seg_ref[line : line + 1, :])
    attend_backward(
        q_ref,
        k_ref,
        v_ref,
        o_ref,
        do_ref,
        lse_ref,
        dq_ref,
        dk_ref,
        dv_ref,
        seg_ref[line : line + 1, :],
        columns_ref,
        seg_ref[0:1, pl.ds(start, plan.rows)],
        start,
        causal,
        scratch,
    )

    def round_block(block, carry):
        rows = pl.ds(pl.multiple_of(block * BLOCK, BLOCK), BLOCK)
        dkl_ref[rows, :] = dk_ref[rows, :].astype(LOW)
        dvl_ref[rows, :] = dv_ref[rows, :].astype(LOW)
        return carry

    lax.fori_loop(0, plan.length // BLOCK, round_block, 0)


def source_parts(plan, info_ref, dkl_ref, dvl_ref, w_ref, which, own_ref, base_ref, mates):
    shard = plan.shard
    for number in range(plan.group):
        first = pl.multiple_of(info_ref[plan.mates + number] * plan.rows, plan.rows)
        for rows in row_blocks(plan.rows):
            source = pl.ds(first + rows.start, BLOCK)
            part = dot_nt(dkl_ref[source, :], weight_of(w_ref, which, shard)) + dot_nt(
                dvl_ref[source, :], weight_of(w_ref, which + 1, shard)
            )
            if number == 0 and base_ref is not None:
                part = part + base_ref[rows, :]
            target = mates[number - 1] if number else own_ref
            target[rows, :] = part.astype(LOW)


def weight_products(plan, info_ref, products, gw_ref, keep_ref, send_ref):
    for which, (left, right) in enumerate(products):
        gw_ref[which] = dot_tn(left[...], right[...]).astype(LOW)
    for which in range(len(products)):
        store_pieces(
            gw_ref.at[which],
            keep_ref,
            send_ref,
            info_ref,
            plan.grad_order,
            which * plan.shard,
            plan.dp,
            plan.shard,
        )


def cross_backward_kernel(plan, chunk_count, piece_count, info_ref, *refs):
    chunks, refs = refs[:chunk_count], refs[chunk_count:]
    pieces, refs = refs[:piece_count], refs[piece_count:]
    (a_ref, z_ref, seg_ref, vec_ref, dvec_ref, dsecond_ref, context_ref), refs = refs[:7], refs[7:]
    (q_ref, o_ref, lse_ref), refs = refs[:3], refs[3:]
    own_ref, refs = refs[0], refs[1:]
    mates, refs = refs[: plan.group - 1], refs[plan.group - 1 :]
    (da_ref, self_do_ref, terms_ref, keep_ref, send_ref), refs = refs[:5], refs[5:]
    m_ref, w_ref, h_ref, gw_ref, grad_ref, low_ref, self_low_ref, *refs = refs
    k_ref, v_ref, do_ref, dq_ref, dkl_ref, dvl_ref, chunk_sems, piece_sems, *buffers = refs
    shard = plan.shard
    copies = chunk_copies(plan, chunks, info_ref, plan.chunk, m_ref, None, chunk_sems)
    copies += piece_copies(
        plan,
        [piece.at[:, pl.ds(3 * shard, 5 * shard)] for piece in pieces],
        info_ref,
        w_ref,
        piece_sems,
    )
    copy_all(copies)
    project_rows(
        plan.length, m_ref, weight_of(w_ref, 2, shard), weight_of(w_ref, 3, shard), k_ref, v_ref
    )
    cross_terms = norm_back(
        plan, 1, z_ref, dsecond_ref, vec_ref, w_ref, 4, grad_ref, low_ref, do_ref
    )
    attention_back(
        plan,
        False,
        info_ref,
        seg_ref,
        (q_ref, k_ref, v_ref, o_ref, do_ref, lse_ref),
        (dq_ref, dkl_ref, dvl_ref),
        buffers,
    )
    for rows in row_blocks(plan.rows):
        grad_ref[rows, :] += dot_nt(dq_ref[rows, :], weight_of(w_ref, 1, shard))
        normed, _ = normalise(a_ref[rows, :])
        h_ref[rows, :] = (normed * vec_ref[0:1, :] + vec_ref[1:2, :]).astype(LOW)
    self_terms = norm_back(
        plan, 0, a_ref, grad_ref, vec_ref, w_ref, 0, da_ref, self_low_ref, self_do_ref
    )
    source_parts(plan, info_ref, dkl_ref, dvl_ref, w_ref, 2, own_ref, None, mates)
    products = (
        (h_ref, dq_ref),
        (m_ref, dkl_ref),
        (m_ref, dvl_ref),
        (o_ref, low_ref),
        (context_ref, self_low_ref),
    )
    weight_products(plan, info_ref, products, gw_ref, keep_ref, send_ref)
    terms_ref[...] = dvec_ref[...]
    for place, term in enumerate([*self_terms, *cross_terms]):
        terms_ref[place : place + 1, :] = term


def self_backward_kernel(plan, chunk_count, piece_count, info_ref, *refs):
    chunks, refs = refs[:chunk_count], refs[chunk_count:]
    pieces, refs = refs[:piece_count], refs[piece_count:]
    (seg_ref, da_ref, do_ref, terms_ref, q_ref, o_ref, lse_ref), refs = refs[:7], refs[7:]
    own_ref, refs = refs[0], refs[1:]
    mates, refs = refs[: plan.group - 1], refs[plan.group - 1 :]
    keep_ref, send_ref, x_ref, own_x_ref, gw_ref, w_ref, *refs = refs
    k_ref, v_ref, base_ref, dq_ref, dkl_ref, dvl_ref, chunk_sems, piece_sems, *buffers = refs
    copies = piece_copies(
        plan,
        [piece.at[:, pl.ds(0, 3 * plan.shard)] for piece in pieces],
        info_ref,
        w_ref,
        piece_sems,
    )
    copies += chunk_copies(plan, chunks, info_ref, 0, x_ref, None, chunk_sems)
    copy_all(copies)
    project_rows(
        plan.length,
        x_ref,
        weight_of(w_ref, 1, plan.shard),
        weight_of(w_ref, 2, plan.shard),
        k_ref,
        v_ref,
    )
    attention_back(
        plan,
        True,
        info_ref,
        seg_ref,
        (q_ref, k_ref, v_ref, o_ref, do_ref, lse_ref),
        (dq_ref, dkl_ref, dvl_ref),
        buffers,
    )
    for rows in row_blocks(plan.rows):
        base_ref[rows, :] = da_ref[rows, :] + dot_nt(
            dq_ref[rows, :], weight_of(w_ref, 0, plan.shard)
        )
    source_parts(plan, info_ref, dkl_ref, dvl_ref, w_ref, 1, own_ref, base_ref, mates)
    start = own_rows(plan, info_ref)
    for rows in row_blocks(plan.rows):
        own_x_ref[rows, :] = x_ref[pl.ds(start + rows.start, BLOCK), :]
    products = ((own_x_ref, dq_ref), (x_ref, dkl_ref), (x_ref, dvl_ref))
    weight_products(plan, info_ref, products, gw_ref, keep_ref, send_ref)
    tail = jnp.concatenate(
        [terms_ref[...], jnp.zeros((VECTOR_ROWS - 8, plan.width), WIDE)], axis=0
    ).astype(LOW)
    for number in range(plan.dp // 2):
        keep_ref[number, 3 * plan.shard :, :] = tail
        send_ref[number, 3 * plan.shard :, :] = tail


SMEM = pl.BlockSpec(memory_space=pltpu.SMEM)
VMEM = pl.BlockSpec(memory_space=pltpu.VMEM)
ANY = pl.BlockSpec(memory_space=pl.ANY)
HBM = pl.BlockSpec(memory_space=pltpu.HBM)


def call(kernel, specs, operands, outs, scratch, flops, moved, megabytes, out_specs=None):
    return pl.pallas_call(
        kernel,
        in_specs=specs,
        out_specs=out_specs or [VMEM] * len(outs),
        out_shape=outs,
        scratch_shapes=scratch,
        compiler_params=pltpu.CompilerParams(vmem_limit_bytes=megabytes * MEGABYTE),
        cost_estimate=pl.CostEstimate(flops=flops, bytes_accessed=moved, transcendentals=0),
    )(*operands)


def shape(dims, dtype):
    return jax.ShapeDtypeStruct(dims, dtype)


def forward_scratch(plan):
    return [
        pltpu.VMEM((plan.pairs, 2 * BLOCK, PAIR), LOW),
        pltpu.VMEM((plan.pairs, PAIR, 2 * BLOCK), WIDE),
        pltpu.VMEM((8, 2 * BLOCK), WIDE),
        pltpu.VMEM((8, 2 * BLOCK), WIDE),
    ]


def backward_scratch(plan):
    return [
        pltpu.VMEM((plan.pairs, 2 * BLOCK, PAIR), LOW),
        pltpu.VMEM((plan.pairs, 2 * BLOCK, PAIR), LOW),
        pltpu.VMEM((plan.pairs, PAIR, 2 * BLOCK), WIDE),
        pltpu.VMEM((8, 2 * BLOCK), WIDE),
    ]


def flat(pieces):
    return sum(piece.shape[0] for piece in pieces)


def hold_kernel(info_ref, held_ref):
    for place in range(info_ref.shape[0]):
        held_ref[place] = info_ref[place]


def hold(info):
    return call(
        hold_kernel, [SMEM], [info], [shape(info.shape, jnp.int32)], [], 40 * 10**9, 10**5, 1, [SMEM]
    )[0]


def forward(plan, info, chunks, pieces):
    rows, length, width = plan.rows, plan.length, plan.width
    heads = [
        shape((rows, width), LOW),
        shape((rows, width), LOW),
        shape((plan.query_blocks * plan.pairs, 2 * BLOCK), WIDE),
        shape((rows, width), WIDE),
    ]
    outs = heads + [shape((8, length), WIDE), shape((TILE, width), WIDE)] + heads
    scratch = [
        pltpu.VMEM((length, width), LOW),
        pltpu.VMEM((length, width), LOW),
        pltpu.VMEM((length, width), LOW),
        pltpu.VMEM((length, width), LOW),
        pltpu.VMEM((plan.chunks, TILE, width), LOW),
        pltpu.VMEM((plan.dp, 8 * plan.shard + TILE, width), LOW),
        pltpu.VMEM((length, 128), WIDE),
        pltpu.SemaphoreType.DMA((2, plan.chunks)),
        pltpu.SemaphoreType.DMA((2, plan.chunks)),
        pltpu.SemaphoreType.DMA((plan.dp,)),
    ] + forward_scratch(plan)
    return call(
        functools.partial(forward_kernel, plan, len(chunks), len(pieces)),
        [SMEM] + [ANY] * (len(chunks) + len(pieces)),
        [info, *chunks, *pieces],
        outs,
        scratch,
        FORWARD_COST,
        10**5,
        megabytes(plan, 18, 10),
    )


def feed(plan, info, upstreams, pieces, z, vecs):
    rows, width, blocks = plan.rows, plan.width, plan.hidden_blocks
    piece_rows = blocks * plan.shard + plan.outer_shard
    outs = (
        [shape((plan.chunk, width), LOW)] * plan.batches
        + [shape((rows, width), WIDE), shape((8, width), WIDE)]
        + [shape((plan.dp // 2, piece_rows, width), LOW)] * 2
    )
    scratch = [
        pltpu.VMEM((width, plan.hidden), LOW),
        pltpu.VMEM((plan.hidden, width), LOW),
        pltpu.VMEM((rows, width), LOW),
        pltpu.VMEM((rows, plan.hidden), WIDE),
        pltpu.VMEM((rows, plan.hidden), LOW),
        pltpu.VMEM((rows, plan.hidden), LOW),
        pltpu.VMEM((rows, width), WIDE),
        pltpu.VMEM((rows, width), LOW),
        pltpu.VMEM((rows, width), LOW),
        pltpu.VMEM((blocks, width, width), LOW),
        pltpu.VMEM((plan.hidden, width), LOW),
        pltpu.SemaphoreType.DMA((blocks + 1, plan.dp)),
        pltpu.SemaphoreType.DMA((plan.batches,)),
    ]
    return call(
        functools.partial(feed_kernel, plan, len(pieces)),
        [SMEM] + [ANY] * (plan.batches + len(pieces)) + [VMEM] * 2,
        [info, *upstreams, *pieces, z, vecs],
        outs,
        scratch,
        20 * 10**9,
        12 * 10**6,
        28,
    )


def backward_buffers(plan):
    length, width = plan.length, plan.width
    return [
        pltpu.VMEM((length, 128), WIDE),
        pltpu.VMEM((length, width), WIDE),
        pltpu.VMEM((length, width), WIDE),
        pltpu.VMEM((plan.pairs, 2 * BLOCK, PAIR), LOW),
        pltpu.VMEM((plan.pairs, 2 * BLOCK, PAIR), LOW),
        pltpu.VMEM((plan.pairs, PAIR, 2 * BLOCK), WIDE),
        pltpu.VMEM((8, 2 * BLOCK), WIDE),
    ]


def cross_backward(plan, info, chunks, pieces, operands):
    rows, length, width = plan.rows, plan.length, plan.width
    outs = (
        [shape((rows, width), LOW)]
        + [shape((rows, width), LOW)] * (plan.group - 1)
        + [shape((rows, width), WIDE), shape((rows, width), LOW), shape((8, width), WIDE)]
        + [shape((plan.dp // 2, 5 * plan.shard, width), LOW)] * 2
    )
    scratch = [
        pltpu.VMEM((length, width), LOW),
        pltpu.VMEM((plan.dp, 5 * plan.shard, width), LOW),
        pltpu.VMEM((rows, width), LOW),
        pltpu.VMEM((5, width, width), LOW),
        pltpu.VMEM((rows, width), WIDE),
        pltpu.VMEM((rows, width), LOW),
        pltpu.VMEM((rows, width), LOW),
        pltpu.VMEM((length, width), LOW),
        pltpu.VMEM((length, width), LOW),
        pltpu.VMEM((rows, width), LOW),
        pltpu.VMEM((rows, width), LOW),
        pltpu.VMEM((length, width), LOW),
        pltpu.VMEM((length, width), LOW),
        pltpu.SemaphoreType.DMA((2, plan.chunks)),
        pltpu.SemaphoreType.DMA((plan.dp,)),
    ] + backward_buffers(plan)
    return call(
        functools.partial(cross_backward_kernel, plan, len(chunks), len(pieces)),
        [SMEM] + [ANY] * (len(chunks) + len(pieces)) + [VMEM] * len(operands),
        [info, *chunks, *pieces, *operands],
        outs,
        scratch,
        22 * 10**9,
        12 * 10**6,
        megabytes(plan, 18, 16),
    )


def self_backward(plan, info, chunks, pieces, operands):
    rows, length, width = plan.rows, plan.length, plan.width
    outs = (
        [shape((rows, width), LOW)]
        + [shape((rows, width), LOW)] * (plan.group - 1)
        + [shape((plan.dp // 2, 3 * plan.shard + VECTOR_ROWS, width), LOW)] * 2
    )
    scratch = [
        pltpu.VMEM((length, width), LOW),
        pltpu.VMEM((rows, width), LOW),
        pltpu.VMEM((3, width, width), LOW),
        pltpu.VMEM((plan.dp, 3 * plan.shard, width), LOW),
        pltpu.VMEM((length, width), LOW),
        pltpu.VMEM((length, width), LOW),
        pltpu.VMEM((rows, width), WIDE),
        pltpu.VMEM((rows, width), LOW),
        pltpu.VMEM((length, width), LOW),
        pltpu.VMEM((length, width), LOW),
        pltpu.SemaphoreType.DMA((2, plan.chunks)),
        pltpu.SemaphoreType.DMA((plan.dp,)),
    ] + backward_buffers(plan)
    return call(
        functools.partial(self_backward_kernel, plan, len(chunks), len(pieces)),
        [SMEM] + [ANY] * (len(chunks) + len(pieces)) + [VMEM] * len(operands),
        [info, *chunks, *pieces, *operands],
        outs,
        scratch,
        18 * 10**9,
        12 * 10**6,
        megabytes(plan, 12, 12),
    )


def pack_tokens_kernel(plan, info_ref, tokens, memory, target, source, *refs):
    rounds, semaphores = refs[: plan.batches], refs[-1]
    chunk, width = plan.chunk, plan.width
    moves = []
    for number in range(plan.batches):
        batch = info_ref[plan.batch + number]
        moves.append((tokens.at[batch, 0], rounds[number].at[pl.ds(0, chunk)]))
        moves.append((memory.at[batch, 0], rounds[number].at[pl.ds(chunk, chunk)]))
    copies = [
        pltpu.make_async_copy(here, there, semaphores.at[number])
        for number, (here, there) in enumerate(moves)
    ]
    for copy in copies:
        copy.start()
    first_row = lax.broadcasted_iota(jnp.int32, (TILE, width), 0) == 0
    for number in range(plan.batches):
        batch = info_ref[plan.batch + number]
        row = jnp.concatenate([target[batch], source[batch]], axis=1).astype(WIDE)
        if width > 2 * chunk:
            row = jnp.concatenate([row, jnp.zeros((1, width - 2 * chunk), WIDE)], axis=1)
        rounds[number][2 * chunk :, :] = jnp.where(first_row, row, 0.0).astype(LOW)
    for copy in copies:
        copy.wait()


def pack_tokens(plan, info, tokens, memory, target, source):
    return call(
        functools.partial(pack_tokens_kernel, plan),
        [SMEM] + [HBM] * 2 + [VMEM] * 2,
        [info, tokens, memory, target, source],
        [shape((2 * plan.chunk + TILE, plan.width), LOW)] * plan.batches,
        [pltpu.SemaphoreType.DMA((2 * plan.batches,))],
        0,
        10**6,
        60,
    )


def pack_weights_kernel(plan, info_ref, *refs):
    weights, (vectors, piece_ref, lines_ref, semaphores) = refs[:8], refs[8:]
    shard = plan.shard
    copies = [
        pltpu.make_async_copy(
            weight, piece_ref.at[0, pl.ds(which * shard, shard)], semaphores.at[which]
        )
        for which, weight in enumerate(weights)
    ]
    for copy in copies:
        copy.start()
    lines_ref[...] = jnp.zeros_like(lines_ref)
    lines_ref[0:6, 0:shard] = vectors[...].astype(WIDE)
    lanes = pltpu.roll(lines_ref[...], info_ref[plan.own_dp] * shard, 1)
    piece_ref[0, 8 * shard :, :] = lanes.astype(LOW)
    for copy in copies:
        copy.wait()


def pack_weights(plan, info, weights, vectors):
    return call(
        functools.partial(pack_weights_kernel, plan),
        [SMEM] + [HBM] * 8 + [VMEM],
        [info, *weights, vectors],
        [shape((1, 8 * plan.shard + TILE, plan.width), LOW)],
        [pltpu.VMEM((TILE, plan.width), WIDE), pltpu.SemaphoreType.DMA((8,))],
        20 * 10**9,
        10**6,
        60,
    )[0]


def pack_rest_kernel(plan, info_ref, inner, outer, cotangent, feed_ref, *refs):
    rounds, semaphores = refs[: plan.batches], refs[-1]
    shard, width, blocks = plan.shard, plan.width, plan.hidden_blocks
    moves = [
        (
            inner.at[:, pl.ds(block * width, width)],
            feed_ref.at[0, pl.ds(block * shard, shard)],
        )
        for block in range(blocks)
    ]
    moves.append((outer, feed_ref.at[0, pl.ds(blocks * shard, plan.outer_shard)]))
    for number in range(plan.batches):
        moves.append((cotangent.at[info_ref[plan.batch + number], 0], rounds[number]))
    copy_all(
        [
            pltpu.make_async_copy(here, there, semaphores.at[number])
            for number, (here, there) in enumerate(moves)
        ]
    )


def pack_rest(plan, info, inner, outer, cotangent):
    outs = [shape((1, plan.hidden_blocks * plan.shard + plan.outer_shard, plan.width), LOW)]
    outs += [shape((plan.chunk, plan.width), LOW)] * plan.batches
    return call(
        functools.partial(pack_rest_kernel, plan),
        [SMEM] + [HBM] * 3,
        [info, inner, outer, cotangent],
        outs,
        [pltpu.SemaphoreType.DMA((plan.hidden_blocks + 1 + plan.batches,))],
        0,
        2 * 10**6,
        60,
    )


def pairs_of(plan, move):
    return [
        (dp * plan.seq + seq, to[0] * plan.seq + to[1])
        for dp in range(plan.dp)
        for seq in range(plan.seq)
        for to in [move(dp, seq)]
    ]


def home(plan, dp, batch, seq):
    position = (2 * batch + dp % 2) * plan.group + seq // plan.batches
    return (dp - dp % 2 + position % 2, position // 2)


def round_batch(plan, seq, number):
    return (seq + number) % plan.batches


def inward(plan, number):
    return pairs_of(plan, lambda dp, seq: home(plan, dp, round_batch(plan, seq, number), seq))


def outward(plan, number):
    return [(to, source) for source, to in inward(plan, number)]


def mate(plan, turn):
    def move(dp, seq):
        position = 2 * seq + dp % 2
        group, own = position // plan.group, position % plan.group
        to = group * plan.group + (own + turn) % plan.group
        return (dp - dp % 2 + to % 2, to // 2)

    return pairs_of(plan, move)


def permute(values, pairs):
    return lax.ppermute(values, AXES, pairs)


def dp_flip(plan, bits):
    return pairs_of(plan, lambda dp, seq: (dp ^ bits, seq))


def seq_flip(plan, bits):
    return pairs_of(plan, lambda dp, seq: (dp, seq ^ bits))


def share_inputs(plan, rounds):
    return [permute(piece, inward(plan, number)) for number, piece in enumerate(rounds)]


def share_mates(plan, received):
    chunks = list(received)
    for turn in range(1, plan.group):
        chunks += [permute(piece, mate(plan, turn)) for piece in received]
    return chunks


def send_home(plan, pieces):
    return [permute(piece, outward(plan, number)) for number, piece in enumerate(pieces)]


def order_home(plan, landed, dtype):
    seq = lax.axis_index("seq")
    landed = jnp.stack(landed).astype(dtype)
    order = [(batch - seq) % plan.batches for batch in range(plan.batches)]
    return jnp.stack(
        [lax.dynamic_index_in_dim(landed, index, 0, keepdims=False) for index in order]
    )


def gather_direct(plan, shard):
    if plan.dp != 8:
        return [lax.all_gather(shard[0], "dp", axis=0)]
    return [shard] + [permute(shard, dp_flip(plan, bits)) for bits in (2, 4, 6)]


def gather_rest(plan, direct):
    if plan.dp != 8:
        return direct
    pieces = []
    for piece in direct:
        pieces += [piece, permute(piece, dp_flip(plan, 1))]
    return pieces


def add_low(values):
    total = values[0].astype(WIDE)
    for value in values[1:]:
        total = total + value.astype(WIDE)
    return total.astype(LOW)


def core_send(plan, send):
    return permute(send, dp_flip(plan, 1)) if plan.dp == 8 else send


def core_sum(plan, keep, other):
    if plan.dp != 8:
        return [jnp.concatenate([keep, other], axis=0)]
    return [add_low([keep[number], other[number]]) for number in range(4)]


def plane_send(plan, parts):
    if plan.dp != 8:
        return [lax.psum_scatter(parts[0], "dp", scatter_dimension=0)]
    return [permute(parts[number], dp_flip(plan, 2 * number)) for number in range(1, 4)]


def plane_sum(plan, parts, landed):
    total = landed[0] if plan.dp != 8 else add_low([parts[0], *landed])
    return total if plan.seq == 4 else lax.psum(total, "seq")


def halves(plan, total, bits):
    if plan.seq != 4:
        return total, jnp.zeros_like(total)
    half = total.shape[0] // 2
    own = lax.axis_index("seq") // bits % 2
    return (
        lax.dynamic_slice_in_dim(total, own * half, half),
        lax.dynamic_slice_in_dim(total, (1 - own) * half, half),
    )


def seq_send(plan, values, bits):
    return permute(values, seq_flip(plan, bits)) if plan.seq == 4 else jnp.zeros_like(values)


def join(plan, own_part, other, bits):
    if plan.seq != 4:
        return own_part
    own = lax.axis_index("seq") // bits % 2
    return jnp.where(
        own == 0, jnp.concatenate([own_part, other]), jnp.concatenate([other, own_part])
    )


def add_wide(first, second):
    return first.astype(WIDE) + second.astype(WIDE)


def tie(*values):
    return lax.optimization_barrier(values)


def after(values, *others):
    return lax.optimization_barrier((values, others))[0]


def plan_info(plan):
    dp, seq = lax.axis_index("dp"), lax.axis_index("seq")
    position = 2 * seq + dp % 2
    own = position % plan.group
    batch = position // plan.group // 2
    flips = list(range(8)) if plan.dp == 8 else None
    entries = []
    if flips:
        entries += [dp ^ bits for bits in (0, 1, 2, 3, 4, 5, 6, 7)]
        entries += [dp ^ bits for bits in (0, 2, 4, 6, 1, 3, 5, 7)]
    else:
        entries += list(range(plan.dp)) * 2
    places = [(batch - number) % plan.batches for number in range(plan.batches)]
    for turn in range(plan.group):
        source = (own - turn) % plan.group
        entries += [source * plan.batches + place for place in places]
    entries.append(own)
    entries += places
    entries += [(own + turn) % plan.group for turn in range(plan.group)]
    entries += [(seq + number) % plan.batches for number in range(plan.batches)]
    entries.append(dp)
    plan.places = [place.astype(jnp.uint32) for place in places]
    return jnp.stack([jnp.asarray(entry, jnp.int32) for entry in entries])


def on_device(
    tokens,
    memory,
    target_segments,
    source_segments,
    cotangent,
    query_weight,
    key_weight,
    value_weight,
    output_weight,
    cross_query,
    cross_key,
    cross_value,
    cross_output,
    inner_weight,
    outer_weight,
    self_gain,
    self_shift,
    cross_gain,
    cross_shift,
    feed_gain,
    feed_shift,
):
    plan = Plan(tokens, inner_weight)
    width, shard = plan.width, plan.shard
    info = plan_info(plan)
    dp = lax.axis_index("dp")

    vectors = jnp.stack([self_gain, self_shift, cross_gain, cross_shift, feed_gain, feed_shift])
    rounds = pack_tokens(plan, info, tokens, memory, target_segments, source_segments)
    shard_piece = pack_weights(
        plan,
        info,
        [
            query_weight,
            key_weight,
            value_weight,
            output_weight,
            cross_query,
            cross_key,
            cross_value,
            cross_output,
        ],
        vectors,
    )
    direct = gather_direct(plan, shard_piece)
    landed = share_inputs(plan, rounds)

    feed_shard, *rounds = pack_rest(plan, info, inner_weight, outer_weight, cotangent)
    feed_shard, rounds, landed[0] = lax.optimization_barrier((feed_shard, rounds, landed[0]))
    info, feed_shard = lax.optimization_barrier((info, feed_shard))
    feed_direct = gather_direct(plan, feed_shard)
    upstreams = share_inputs(plan, rounds)
    direct, landed, info = lax.optimization_barrier((direct, landed, hold(info)))
    pieces = gather_rest(plan, direct)
    chunks = share_mates(plan, landed)
    q, o, lse, a, segs, vecs, cq, co, cross_lse, z = forward(
        plan, info, chunks, pieces
    )

    feed_direct, upstreams = after((feed_direct, upstreams), z)
    feed_pieces = gather_rest(plan, feed_direct)
    *results, dsecond, dvec, feed_keep, feed_send = feed(
        plan, info, upstreams, feed_pieces, z, vecs
    )

    feed_parts = core_sum(plan, feed_keep, core_send(plan, feed_send))
    out_landed = send_home(plan, results)
    feed_landed = plane_send(plan, feed_parts)
    dsecond = after(dsecond, feed_parts)
    back = cross_backward(
        plan,
        info,
        chunks,
        pieces,
        [a, z, segs, vecs, dvec, dsecond, o, cq, co, cross_lse],
    )
    back, feed_landed, out_landed = lax.optimization_barrier((back, feed_landed, out_landed))
    own_memory, *others = back
    mate_memory, (da, do, terms, cross_keep, cross_send) = (
        others[: plan.group - 1],
        others[plan.group - 1 :],
    )

    feed_keep, feed_send = halves(plan, plane_sum(plan, feed_parts, feed_landed), 1)
    cross_parts = core_sum(plan, cross_keep, core_send(plan, cross_send))
    memory_pieces = add_mates(plan, own_memory, mate_memory)
    feed_landed = seq_send(plan, feed_send, 1)
    cross_landed = plane_send(plan, cross_parts)
    memory_landed = send_home(plan, memory_pieces)
    feed_landed, cross_parts[0], memory_pieces = tie(feed_landed, cross_parts[0], memory_pieces)
    feed_keep, feed_send = halves(plan, add_low([feed_keep, feed_landed]), 2)
    feed_landed = seq_send(plan, feed_send, 2)
    do, feed_keep = tie(do, feed_keep)
    back = self_backward(plan, info, chunks, pieces, [segs, da, do, terms, q, o, lse])
    back, feed_landed, cross_landed, memory_landed = lax.optimization_barrier(
        (back, feed_landed, cross_landed, memory_landed)
    )
    own_tokens, *mate_tokens, self_keep, self_send = back

    mate_landed = send_mates(plan, mate_tokens)
    self_landed = core_send(plan, self_send)
    feed_quarter = add_low([feed_keep, feed_landed])
    feed_landed = seq_send(plan, feed_quarter, 2)
    cross_keep, cross_send = halves(plan, plane_sum(plan, cross_parts, cross_landed), 1)
    cross_landed = seq_send(plan, cross_send, 1)
    token_pieces = sum_mates(plan, own_tokens, mate_landed)
    token_landed = send_home(plan, token_pieces)
    self_landed, cross_keep, feed_quarter = tie(self_landed, cross_keep, feed_quarter)
    self_parts = core_sum(plan, self_keep, self_landed)
    self_landed = plane_send(plan, self_parts)
    feed_landed, cross_landed = after((feed_landed, cross_landed), self_parts)
    feed_half = join(plan, feed_quarter, feed_landed, 2)
    feed_landed = seq_send(plan, feed_half, 1)
    cross_keep, cross_send = halves(plan, add_low([cross_keep, cross_landed]), 2)
    cross_landed = seq_send(plan, cross_send, 2)
    self_landed, feed_half, cross_keep, token_landed[0] = tie(
        self_landed, feed_half, cross_keep, token_landed[0]
    )
    self_total = plane_sum(plan, self_parts, self_landed)
    self_landed = seq_send(plan, self_total, 1)
    cross_landed, self_total = tie(cross_landed, self_total)
    cross_quarter = add_low([cross_keep, cross_landed])
    cross_landed = seq_send(plan, cross_quarter, 2)
    self_landed, cross_quarter = tie(self_landed, cross_quarter)
    self_total = add_low([self_total, self_landed])
    self_landed = seq_send(plan, self_total, 2)
    cross_landed, self_total, out_landed, memory_landed = tie(
        cross_landed, self_total, out_landed, memory_landed
    )
    cross_half = join(plan, cross_quarter, cross_landed, 2)
    cross_landed = seq_send(plan, cross_half, 1)
    out_tokens = order_home(plan, out_landed, LOW)
    grad_memory = order_home(plan, memory_landed, WIDE)
    grad_tokens = order_home(plan, token_landed, WIDE)
    self_landed, cross_landed, out_tokens, grad_memory, grad_tokens = tie(
        self_landed, cross_landed, out_tokens, grad_memory, grad_tokens
    )
    feed_total = join(plan, feed_half, feed_landed, 1).astype(WIDE)
    cross_total = join(plan, cross_half, cross_landed, 1).astype(WIDE)
    self_total = add_wide(self_total, self_landed)

    scale = 1.0 / (plan.batches * plan.dp)
    feed_grads, cross_grads, self_grads = (
        feed_total * scale,
        cross_total * scale,
        self_total * scale,
    )
    inner_grads = [
        feed_grads[block * shard : (block + 1) * shard] for block in range(plan.hidden_blocks)
    ]
    vector_grads = lax.dynamic_slice(self_grads, (3 * shard, dp * shard), (TILE, shard))
    return (
        out_tokens[:, None],
        grad_tokens[:, None],
        grad_memory[:, None],
        *[self_grads[which * shard : (which + 1) * shard] for which in range(3)],
        cross_grads[4 * shard : 5 * shard],
        *[cross_grads[which * shard : (which + 1) * shard] for which in range(4)],
        jnp.concatenate(inner_grads, axis=1),
        feed_grads[plan.hidden_blocks * shard :],
        *[vector_grads[which] for which in range(6)],
    )


def send_mates(plan, mates):
    return [permute(part, mate(plan, turn)) for turn, part in enumerate(mates, 1)]


def sum_mates(plan, own, landed):
    own = own.astype(WIDE)
    for part in landed:
        own = own + part.astype(WIDE)
    own = own.reshape(plan.batches, plan.chunk, plan.width)
    return [
        lax.dynamic_index_in_dim(own, place, 0, keepdims=False).astype(LOW)
        for place in plan.places
    ]


def add_mates(plan, own, mates):
    return sum_mates(plan, own, send_mates(plan, mates))


def solution(mesh):
    tokens = P(None, "dp", "seq", None)
    ids = P(None, "dp", "seq")
    weight = P("dp", None)
    vector = P("dp")
    return jax.shard_map(
        on_device,
        mesh=mesh,
        in_specs=(tokens, tokens, ids, ids, tokens) + (weight,) * 10 + (vector,) * 6,
        out_specs=(tokens,) * 3 + (weight,) * 10 + (vector,) * 6,
        check_vma=False,
    )
```

```python
import functools

import jax
import jax.numpy as jnp
from jax import lax
from jax.experimental import pallas as pl
from jax.experimental.pallas import tpu as pltpu
from jax.sharding import PartitionSpec as P

DH = 64
PAIR = 2 * DH
BLOCK = 256
TILE = 16
VECTOR_ROWS = 16
FORWARD_COST = 10**6
EPSILON = 1e-05
NEGATIVE = -1e30
FACTOR = DH ** (-0.5)
AXES = ("dp", "seq")
LOW = jnp.bfloat16
WIDE = jnp.float32
MEGABYTE = 1024 * 1024


def dot_nn(a, b):
    return jnp.dot(a, b, preferred_element_type=WIDE)


def dot_nt(a, b):
    return lax.dot_general(a, b, (((1,), (1,)), ((), ())), preferred_element_type=WIDE)


def dot_tn(a, b):
    return lax.dot_general(a, b, (((0,), (0,)), ((), ())), preferred_element_type=WIDE)


def normalise(values):
    centred = values - jnp.mean(values, axis=-1, keepdims=True)
    inverse = lax.rsqrt(jnp.mean(centred * centred, axis=-1, keepdims=True) + EPSILON)
    return centred * inverse, inverse


def norm_backward(upstream, normed, inverse, gain_row):
    scaled = upstream * gain_row
    plain_mean = jnp.mean(scaled, axis=-1, keepdims=True)
    along_mean = jnp.mean(scaled * normed, axis=-1, keepdims=True)
    return inverse * (scaled - plain_mean - normed * along_mean)


def row_blocks(length, size=BLOCK):
    return [pl.ds(start, size) for start in range(0, length, size)]


def copy_all(copies):
    for copy in copies:
        copy.start()
    for copy in copies:
        copy.wait()


def piece_copies(plan, pieces, info_ref, w_ref, semaphores):
    copies = []
    for piece in pieces:
        for slab in range(piece.shape[0]):
            number = len(copies)
            owner = info_ref[plan.order + number]
            copies.append(
                pltpu.make_async_copy(piece.at[slab], w_ref.at[owner], semaphores.at[number])
            )
    return copies


def weight_of(weight_ref, which, rows):
    count, _, width = weight_ref.shape
    return weight_ref[:, which * rows : (which + 1) * rows, :].reshape(count * rows, width)


def seg_columns(seg_row):
    return jnp.transpose(jnp.broadcast_to(seg_row, (128, seg_row.shape[1])))


def stack_heads(pair):
    lane = lax.broadcasted_iota(jnp.int32, pair.shape, 1)
    zero = jnp.zeros_like(pair)
    return jnp.concatenate(
        [jnp.where(lane < DH, pair, zero), jnp.where(lane < DH, zero, pair)], axis=0
    )


def unstack_heads(columns):
    row = lax.broadcasted_iota(jnp.int32, (PAIR, BLOCK), 0)
    return jnp.where(row < DH, columns[:, :BLOCK], columns[:, BLOCK:])


def mask_bias(key_ids, query_ids, key_start, query_start, causal):
    ids = jnp.concatenate([key_ids, key_ids], axis=1)
    allowed = ids == query_ids
    if causal:
        key_place = key_start + lax.broadcasted_iota(jnp.int32, (BLOCK, BLOCK), 0)
        query_place = query_start + lax.broadcasted_iota(jnp.int32, (BLOCK, BLOCK), 1)
        allowed = jnp.logical_and(allowed, key_place <= query_place)
    bias = jnp.where(allowed, 0.0, NEGATIVE)
    return jnp.concatenate([bias, bias], axis=1)


def key_bounds(key_row, query_ids, query_start, causal):
    below = jnp.sum(jnp.where(key_row < jnp.min(query_ids), 1.0, 0.0)).astype(jnp.int32)
    first = lax.div(below, BLOCK)
    if causal:
        return first, lax.div(query_start, BLOCK) + 1
    upto = jnp.sum(jnp.where(key_row <= jnp.max(query_ids), 1.0, 0.0)).astype(jnp.int32)
    return first, lax.div(upto + (BLOCK - 1), BLOCK)


def attend_forward(
    q_ref, k_ref, v_ref, o_ref, lse_ref, key_row, columns_ref, query_row, start, causal, scratch
):
    stack_ref, sum_ref, top_ref, total_ref = scratch
    pairs = q_ref.shape[1] // PAIR
    for number, rows in enumerate(row_blocks(q_ref.shape[0])):
        query_ids = query_row[:, number * BLOCK : (number + 1) * BLOCK]
        query_start = start + number * BLOCK
        low, high = key_bounds(key_row, query_ids, query_start, causal)
        for pair in range(pairs):
            stack_ref[pair] = stack_heads(q_ref[rows, pair * PAIR : (pair + 1) * PAIR])
        sum_ref[...] = jnp.zeros_like(sum_ref)
        top_ref[...] = jnp.full_like(top_ref, NEGATIVE)
        total_ref[...] = jnp.zeros_like(total_ref)

        def one_block(block, carry):
            key_start = pl.multiple_of(block * BLOCK, BLOCK)
            keys = pl.ds(key_start, BLOCK)
            bias = mask_bias(columns_ref[keys, :], query_ids, key_start, query_start, causal)
            values = [
                (
                    k_ref[keys, pair * PAIR : (pair + 1) * PAIR],
                    v_ref[keys, pair * PAIR : (pair + 1) * PAIR],
                    stack_ref[pair],
                    top_ref[pair : pair + 1, :],
                    total_ref[pair : pair + 1, :],
                    sum_ref[pair],
                )
                for pair in range(pairs)
            ]
            scores = [dot_nt(key_pair, queries) + bias for key_pair, _, queries, *_ in values]
            tops = [
                jnp.maximum(value[3], jnp.max(score, axis=0, keepdims=True))
                for value, score in zip(values, scores)
            ]
            exponents = [jnp.exp(score - top) for score, top in zip(scores, tops)]
            shrinks = [jnp.exp(value[3] - top) for value, top in zip(values, tops)]
            totals = [
                value[4] * shrink + jnp.sum(exponent, axis=0, keepdims=True)
                for value, shrink, exponent in zip(values, shrinks, exponents)
            ]
            sums = [
                value[5] * shrink + dot_tn(value[1], exponent.astype(LOW))
                for value, shrink, exponent in zip(values, shrinks, exponents)
            ]
            for pair in range(pairs):
                top_ref[pair : pair + 1, :] = tops[pair]
                total_ref[pair : pair + 1, :] = totals[pair]
                sum_ref[pair] = sums[pair]
            return carry

        lax.fori_loop(low, high, one_block, 0)
        for pair in range(pairs):
            total = total_ref[pair : pair + 1, :]
            context = unstack_heads(sum_ref[pair] / total)
            o_ref[rows, pair * PAIR : (pair + 1) * PAIR] = jnp.transpose(context).astype(LOW)
            place = number * pairs + pair
            lse_ref[place : place + 1, :] = top_ref[pair : pair + 1, :] + jnp.log(total)


def attend_backward(
    q_ref,
    k_ref,
    v_ref,
    o_ref,
    grad_ref,
    lse_ref,
    dq_ref,
    dk_ref,
    dv_ref,
    key_row,
    columns_ref,
    query_row,
    start,
    causal,
    scratch,
):
    stack_ref, stack_grad_ref, sum_ref, along_ref = scratch
    pairs = q_ref.shape[1] // PAIR
    dk_ref[...] = jnp.zeros_like(dk_ref)
    dv_ref[...] = jnp.zeros_like(dv_ref)
    for number, rows in enumerate(row_blocks(q_ref.shape[0])):
        query_ids = query_row[:, number * BLOCK : (number + 1) * BLOCK]
        query_start = start + number * BLOCK
        low, high = key_bounds(key_row, query_ids, query_start, causal)
        for pair in range(pairs):
            lanes = slice(pair * PAIR, (pair + 1) * PAIR)
            grad = grad_ref[rows, lanes]
            stack_ref[pair] = stack_heads(q_ref[rows, lanes])
            stack_grad_ref[pair] = stack_heads(grad)
            along = jnp.transpose(grad.astype(WIDE) * o_ref[rows, lanes].astype(WIDE))
            along_ref[pair : pair + 1, :] = jnp.concatenate(
                [
                    jnp.sum(along[:DH], axis=0, keepdims=True),
                    jnp.sum(along[DH:], axis=0, keepdims=True),
                ],
                axis=1,
            )
        sum_ref[...] = jnp.zeros_like(sum_ref)

        def one_block(block, carry):
            key_start = pl.multiple_of(block * BLOCK, BLOCK)
            keys = pl.ds(key_start, BLOCK)
            bias = mask_bias(columns_ref[keys, :], query_ids, key_start, query_start, causal)
            for pair in range(pairs):
                lanes = slice(pair * PAIR, (pair + 1) * PAIR)
                place = number * pairs + pair
                key_pair = k_ref[keys, lanes]
                scores = dot_nt(key_pair, stack_ref[pair]) + bias
                probs = jnp.exp(scores - lse_ref[place : place + 1, :])
                prob_grad = dot_nt(v_ref[keys, lanes], stack_grad_ref[pair])
                score_grad = (probs * (prob_grad - along_ref[pair : pair + 1, :])).astype(LOW)
                dv_ref[keys, lanes] += dot_nn(probs.astype(LOW), stack_grad_ref[pair])
                dk_ref[keys, lanes] += dot_nn(score_grad, stack_ref[pair])
                sum_ref[pair] += dot_tn(key_pair, score_grad)
            return carry

        lax.fori_loop(low, high, one_block, 0)
        for pair in range(pairs):
            grad = jnp.transpose(unstack_heads(sum_ref[pair])) * FACTOR
            dq_ref[rows, pair * PAIR : (pair + 1) * PAIR] = grad.astype(LOW)


def store_pieces(grad_ref, keep_ref, send_ref, info_ref, order, offset, count, rows):
    half = count // 2
    for number in range(count):
        owner = info_ref[order + number]
        block = grad_ref[pl.ds(pl.multiple_of(owner * rows, rows), rows), :]
        target = keep_ref if number < half else send_ref
        target[number % half, offset : offset + rows, :] = block


class Plan:
    def __init__(self, tokens, inner_weight):
        self.dp = lax.axis_size("dp")
        self.seq = lax.axis_size("seq")
        self.batches, _, self.chunk, self.width = tokens.shape
        self.hidden = inner_weight.shape[1]
        self.length = self.chunk * self.seq
        self.group = self.seq // self.batches
        self.rows = self.batches * self.chunk
        self.chunks = self.seq
        self.shard = self.width // self.dp
        self.outer_shard = self.hidden // self.dp
        self.hidden_blocks = self.hidden // self.width
        self.pairs = self.width // PAIR
        self.query_blocks = self.rows // BLOCK
        self.order = 0
        self.grad_order = self.dp
        self.chunk_order = 2 * self.dp
        self.own = self.chunk_order + self.chunks
        self.round = self.own + 1
        self.mates = self.round + self.batches
        self.batch = self.mates + self.group
        self.own_dp = self.batch + self.batches


def megabytes(plan, fixed, by_length):
    return fixed + -(-by_length * plan.length // 1024)


def seg_rows(plan, raw_ref, seg_ref):
    for number in range(plan.chunks):
        lanes = slice(number * plan.chunk, (number + 1) * plan.chunk)
        seg_ref[0:1, lanes] = raw_ref[number, 0:1, : plan.chunk].astype(WIDE)
        seg_ref[1:2, lanes] = raw_ref[number, 0:1, plan.chunk : 2 * plan.chunk].astype(WIDE)


def own_rows(plan, info_ref):
    return pl.multiple_of(info_ref[plan.own] * plan.rows, plan.rows)


def chunk_copies(plan, chunks, info_ref, first, x_ref, raw_ref, semaphores):
    copies = []
    for number, chunk in enumerate(chunks):
        index = info_ref[plan.chunk_order + number]
        rows = pl.ds(pl.multiple_of(index * plan.chunk, plan.chunk), plan.chunk)
        copies.append(
            pltpu.make_async_copy(
                chunk.at[pl.ds(first, plan.chunk)], x_ref.at[rows], semaphores.at[0, number]
            )
        )
        if raw_ref is not None:
            copies.append(
                pltpu.make_async_copy(
                    chunk.at[pl.ds(2 * plan.chunk, TILE)],
                    raw_ref.at[index],
                    semaphores.at[1, number],
                )
            )
    return copies


def project_rows(length, source_ref, key_weight, value_weight, k_ref, v_ref):
    for rows in row_blocks(length, 2 * BLOCK):
        k_ref[rows, :] = dot_nn(source_ref[rows, :], key_weight).astype(LOW)
        v_ref[rows, :] = dot_nn(source_ref[rows, :], value_weight).astype(LOW)


def forward_kernel(plan, chunk_count, piece_count, info_ref, *refs):
    chunks, refs = refs[:chunk_count], refs[chunk_count:]
    pieces, refs = refs[:piece_count], refs[piece_count:]
    (q_ref, o_ref, lse_ref, a_ref, seg_ref, vec_ref), refs = refs[:6], refs[6:]
    (cq_ref, co_ref, cross_lse_ref, z_ref, k_ref, v_ref), refs = refs[:6], refs[6:]
    x_ref, m_ref, raw_ref, w_ref, columns_ref, chunk_sems, m_sems, piece_sems, *scratch = refs
    load = chunk_copies(plan, chunks, info_ref, 0, x_ref, raw_ref, chunk_sems)
    load += chunk_copies(plan, chunks, info_ref, plan.chunk, m_ref, None, m_sems)
    load += piece_copies(plan, pieces, info_ref, w_ref, piece_sems)
    copy_all(load)
    shard = plan.shard
    start = own_rows(plan, info_ref)
    vec_ref[...] = jnp.sum(w_ref[:, 8 * shard :, :].astype(WIDE), axis=0)
    seg_rows(plan, raw_ref, seg_ref)
    columns_ref[...] = seg_columns(seg_ref[0:1, :])
    for rows in row_blocks(plan.rows):
        own = x_ref[pl.ds(start + rows.start, BLOCK), :]
        q_ref[rows, :] = (dot_nn(own, weight_of(w_ref, 0, shard)) * FACTOR).astype(LOW)
    project_rows(
        plan.length,
        x_ref,
        weight_of(w_ref, 1, shard),
        weight_of(w_ref, 2, shard),
        k_ref,
        v_ref,
    )
    attend_forward(
        q_ref,
        k_ref,
        v_ref,
        o_ref,
        lse_ref,
        seg_ref[0:1, :],
        columns_ref,
        seg_ref[0:1, pl.ds(start, plan.rows)],
        start,
        True,
        scratch,
    )
    gain, shift = vec_ref[0:1, :], vec_ref[1:2, :]
    for rows in row_blocks(plan.rows):
        own = x_ref[pl.ds(start + rows.start, BLOCK), :].astype(WIDE)
        a = own + dot_nn(o_ref[rows, :], weight_of(w_ref, 3, shard))
        a_ref[rows, :] = a
        normed, _ = normalise(a)
        first = normed * gain + shift
        z_ref[rows, :] = first
        cq_ref[rows, :] = (
            dot_nn(first.astype(LOW), weight_of(w_ref, 4, shard)) * FACTOR
        ).astype(LOW)
    project_rows(
        plan.length,
        m_ref,
        weight_of(w_ref, 5, shard),
        weight_of(w_ref, 6, shard),
        k_ref,
        v_ref,
    )
    columns_ref[...] = seg_columns(seg_ref[1:2, :])
    attend_forward(
        cq_ref,
        k_ref,
        v_ref,
        co_ref,
        cross_lse_ref,
        seg_ref[1:2, :],
        columns_ref,
        seg_ref[0:1, pl.ds(start, plan.rows)],
        start,
        False,
        scratch,
    )
    for rows in row_blocks(plan.rows):
        z_ref[rows, :] += dot_nn(co_ref[rows, :], weight_of(w_ref, 7, shard))


def feed_kernel(plan, piece_count, info_ref, *refs):
    batches = plan.batches
    upstreams, refs = refs[:batches], refs[batches:]
    pieces, refs = refs[:piece_count], refs[piece_count:]
    (z_ref, vec_ref), refs = refs[:2], refs[2:]
    outs, refs = refs[:batches], refs[batches:]
    (dh_ref, dvec_ref, keep_ref, send_ref), refs = refs[:4], refs[4:]
    inner_ref, outer_ref, low_ref, u_ref, r_ref, du_ref, f_ref, up_ref, res_ref, *refs = refs
    inner_gw_ref, outer_gw_ref, piece_sems, up_sems = refs
    width, shard, blocks, outer_shard = (
        plan.width,
        plan.shard,
        plan.hidden_blocks,
        plan.outer_shard,
    )
    copies = []
    number = 0
    for piece in pieces:
        for slab in range(piece.shape[0]):
            owner = info_ref[plan.order + number]
            for block in range(blocks):
                copies.append(
                    pltpu.make_async_copy(
                        piece.at[slab, pl.ds(block * shard, shard)],
                        inner_ref.at[
                            pl.ds(pl.multiple_of(owner * shard, shard), shard),
                            pl.ds(block * width, width),
                        ],
                        piece_sems.at[block, number],
                    )
                )
            copies.append(
                pltpu.make_async_copy(
                    piece.at[slab, pl.ds(blocks * shard, outer_shard)],
                    outer_ref.at[pl.ds(pl.multiple_of(owner * outer_shard, outer_shard), outer_shard)],
                    piece_sems.at[blocks, number],
                )
            )
            number += 1
    for number in range(batches):
        index = info_ref[plan.round + number]
        rows = pl.ds(pl.multiple_of(index * plan.chunk, plan.chunk), plan.chunk)
        copies.append(
            pltpu.make_async_copy(upstreams[number], up_ref.at[rows], up_sems.at[number])
        )
    for copy in copies:
        copy.start()
    gain_two, shift_two = vec_ref[2:3, :], vec_ref[3:4, :]
    gain_three, shift_three = vec_ref[4:5, :], vec_ref[5:6, :]
    gain_grad = jnp.zeros((1, width), WIDE)
    shift_grad = jnp.zeros((1, width), WIDE)
    for rows in row_blocks(plan.rows):
        normed, _ = normalise(z_ref[rows, :])
        second = normed * gain_two + shift_two
        f_ref[rows, :] = second
        low_ref[rows, :] = second.astype(LOW)
    for copy in copies:
        copy.wait()
    lanes = [slice(block * width, (block + 1) * width) for block in range(blocks)]
    for part in lanes:
        u = dot_nn(low_ref[...], inner_ref[:, part])
        phi = 0.5 + 0.5 * lax.erf(u * (0.5**0.5))
        r_ref[:, part] = (u * phi).astype(LOW)
        u_ref[:, part] = phi + u * (jnp.exp(-0.5 * u * u) * 0.3989422804014327)
    for rows in row_blocks(plan.rows):
        f = f_ref[rows, :] + dot_nn(r_ref[rows, :], outer_ref[...])
        normed, inverse = normalise(f)
        res_ref[rows, :] = (normed * gain_three + shift_three).astype(LOW)
        upstream = up_ref[rows, :].astype(WIDE)
        gain_grad += jnp.sum(upstream * normed, axis=0, keepdims=True)
        shift_grad += jnp.sum(upstream, axis=0, keepdims=True)
        feed_grad = norm_backward(upstream, normed, inverse, gain_three)
        dh_ref[rows, :] = feed_grad
        up_ref[rows, :] = feed_grad.astype(LOW)
    for number in range(batches):
        index = info_ref[plan.round + number]
        outs[number][...] = res_ref[pl.ds(pl.multiple_of(index * plan.chunk, plan.chunk), plan.chunk), :]
    for part in lanes:
        dr = dot_nt(up_ref[...], outer_ref[part, :]).astype(LOW).astype(WIDE)
        du_ref[:, part] = (dr * u_ref[:, part]).astype(LOW)
        outer_gw_ref[part, :] = dot_tn(r_ref[:, part], up_ref[...]).astype(LOW)
    for block, part in enumerate(lanes):
        inner_gw_ref[block] = dot_tn(low_ref[...], du_ref[:, part]).astype(LOW)
    for rows in row_blocks(plan.rows):
        dh_ref[rows, :] += dot_nt(du_ref[rows, :], inner_ref[...])
    for block in range(blocks):
        store_pieces(
            inner_gw_ref.at[block],
            keep_ref,
            send_ref,
            info_ref,
            plan.grad_order,
            block * shard,
            plan.dp,
            shard,
        )
    store_pieces(
        outer_gw_ref,
        keep_ref,
        send_ref,
        info_ref,
        plan.grad_order,
        blocks * shard,
        plan.dp,
        outer_shard,
    )
    dvec_ref[...] = jnp.zeros_like(dvec_ref)
    dvec_ref[4:5, :] = gain_grad
    dvec_ref[5:6, :] = shift_grad


def norm_back(plan, line, z_ref, upstream_ref, vec_ref, grad_ref, low_ref):
    gain_grad = jnp.zeros((1, plan.width), WIDE)
    shift_grad = jnp.zeros((1, plan.width), WIDE)
    for rows in row_blocks(plan.rows):
        normed, inverse = normalise(z_ref[rows, :])
        upstream = upstream_ref[rows, :]
        gain_grad += jnp.sum(upstream * normed, axis=0, keepdims=True)
        shift_grad += jnp.sum(upstream, axis=0, keepdims=True)
        grad = norm_backward(upstream, normed, inverse, vec_ref[2 * line : 2 * line + 1, :])
        if grad_ref is not None:
            grad_ref[rows, :] = grad
        low_ref[rows, :] = grad.astype(LOW)
    return gain_grad, shift_grad


def attention_back(plan, causal, info_ref, seg_ref, operands, results, buffers):
    q_ref, k_ref, v_ref, o_ref, do_ref, lse_ref = operands
    dq_ref, dkl_ref, dvl_ref = results
    columns_ref, dk_ref, dv_ref, *scratch = buffers
    start = own_rows(plan, info_ref)
    line = 0 if causal else 1
    columns_ref[...] = seg_columns(seg_ref[line : line + 1, :])
    attend_backward(
        q_ref,
        k_ref,
        v_ref,
        o_ref,
        do_ref,
        lse_ref,
        dq_ref,
        dk_ref,
        dv_ref,
        seg_ref[line : line + 1, :],
        columns_ref,
        seg_ref[0:1, pl.ds(start, plan.rows)],
        start,
        causal,
        scratch,
    )

    def round_block(block, carry):
        rows = pl.ds(pl.multiple_of(block * BLOCK, BLOCK), BLOCK)
        dkl_ref[rows, :] = dk_ref[rows, :].astype(LOW)
        dvl_ref[rows, :] = dv_ref[rows, :].astype(LOW)
        return carry

    lax.fori_loop(0, plan.length // BLOCK, round_block, 0)


def source_parts(plan, info_ref, dkl_ref, dvl_ref, w_ref, which, own_ref, base_ref, mates):
    shard = plan.shard
    for number in range(plan.group):
        first = pl.multiple_of(info_ref[plan.mates + number] * plan.rows, plan.rows)
        for rows in row_blocks(plan.rows):
            source = pl.ds(first + rows.start, BLOCK)
            part = dot_nt(dkl_ref[source, :], weight_of(w_ref, which, shard)) + dot_nt(
                dvl_ref[source, :], weight_of(w_ref, which + 1, shard)
            )
            if number == 0 and base_ref is not None:
                part = part + base_ref[rows, :]
            target = mates[number - 1] if number else own_ref
            target[rows, :] = part.astype(LOW)


def weight_products(plan, info_ref, products, gw_ref, keep_ref, send_ref):
    for which, (left, right) in enumerate(products):
        gw_ref[which] = dot_tn(left[...], right[...]).astype(LOW)
    for which in range(len(products)):
        store_pieces(
            gw_ref.at[which],
            keep_ref,
            send_ref,
            info_ref,
            plan.grad_order,
            which * plan.shard,
            plan.dp,
            plan.shard,
        )


def cross_backward_kernel(plan, chunk_count, piece_count, info_ref, *refs):
    chunks, refs = refs[:chunk_count], refs[chunk_count:]
    pieces, refs = refs[:piece_count], refs[piece_count:]
    (a_ref, z_ref, seg_ref, vec_ref, dvec_ref, dsecond_ref, context_ref), refs = refs[:7], refs[7:]
    (q_ref, o_ref, lse_ref), refs = refs[:3], refs[3:]
    own_ref, refs = refs[0], refs[1:]
    mates, refs = refs[: plan.group - 1], refs[plan.group - 1 :]
    (self_low_ref, terms_ref, keep_ref, send_ref), refs = refs[:4], refs[4:]
    m_ref, w_ref, h_ref, gw_ref, grad_ref, low_ref, *refs = refs
    k_ref, v_ref, do_ref, dq_ref, dkl_ref, dvl_ref, chunk_sems, piece_sems, *buffers = refs
    shard = plan.shard
    copies = chunk_copies(plan, chunks, info_ref, plan.chunk, m_ref, None, chunk_sems)
    copies += piece_copies(
        plan,
        [piece.at[:, pl.ds(3 * shard, 5 * shard)] for piece in pieces],
        info_ref,
        w_ref,
        piece_sems,
    )
    copy_all(copies)
    project_rows(
        plan.length, m_ref, weight_of(w_ref, 2, shard), weight_of(w_ref, 3, shard), k_ref, v_ref
    )
    cross_terms = norm_back(plan, 1, z_ref, dsecond_ref, vec_ref, grad_ref, low_ref)
    for rows in row_blocks(plan.rows):
        do_ref[rows, :] = dot_nt(low_ref[rows, :], weight_of(w_ref, 4, shard)).astype(LOW)
    attention_back(
        plan,
        False,
        info_ref,
        seg_ref,
        (q_ref, k_ref, v_ref, o_ref, do_ref, lse_ref),
        (dq_ref, dkl_ref, dvl_ref),
        buffers,
    )
    for rows in row_blocks(plan.rows):
        grad_ref[rows, :] += dot_nt(dq_ref[rows, :], weight_of(w_ref, 1, shard))
        normed, _ = normalise(a_ref[rows, :])
        h_ref[rows, :] = (normed * vec_ref[0:1, :] + vec_ref[1:2, :]).astype(LOW)
    self_terms = norm_back(plan, 0, a_ref, grad_ref, vec_ref, None, self_low_ref)
    source_parts(plan, info_ref, dkl_ref, dvl_ref, w_ref, 2, own_ref, None, mates)
    products = (
        (h_ref, dq_ref),
        (m_ref, dkl_ref),
        (m_ref, dvl_ref),
        (o_ref, low_ref),
        (context_ref, self_low_ref),
    )
    weight_products(plan, info_ref, products, gw_ref, keep_ref, send_ref)
    terms_ref[...] = dvec_ref[...]
    for place, term in enumerate([*self_terms, *cross_terms]):
        terms_ref[place : place + 1, :] = term


def self_backward_kernel(plan, chunk_count, piece_count, info_ref, *refs):
    chunks, refs = refs[:chunk_count], refs[chunk_count:]
    pieces, refs = refs[:piece_count], refs[piece_count:]
    (seg_ref, da_ref, terms_ref, q_ref, o_ref, lse_ref), refs = refs[:6], refs[6:]
    own_ref, refs = refs[0], refs[1:]
    mates, refs = refs[: plan.group - 1], refs[plan.group - 1 :]
    keep_ref, send_ref, x_ref, own_x_ref, gw_ref, w_ref, *refs = refs
    do_ref, k_ref, v_ref, base_ref, dq_ref, dkl_ref, dvl_ref, chunk_sems, piece_sems, *buffers = refs
    copies = piece_copies(
        plan,
        [piece.at[:, pl.ds(0, 4 * plan.shard)] for piece in pieces],
        info_ref,
        w_ref,
        piece_sems,
    )
    copies += chunk_copies(plan, chunks, info_ref, 0, x_ref, None, chunk_sems)
    copy_all(copies)
    project_rows(
        plan.length,
        x_ref,
        weight_of(w_ref, 1, plan.shard),
        weight_of(w_ref, 2, plan.shard),
        k_ref,
        v_ref,
    )
    for rows in row_blocks(plan.rows):
        do_ref[rows, :] = dot_nt(da_ref[rows, :], weight_of(w_ref, 3, plan.shard)).astype(LOW)
    attention_back(
        plan,
        True,
        info_ref,
        seg_ref,
        (q_ref, k_ref, v_ref, o_ref, do_ref, lse_ref),
        (dq_ref, dkl_ref, dvl_ref),
        buffers,
    )
    for rows in row_blocks(plan.rows):
        base_ref[rows, :] = da_ref[rows, :].astype(WIDE) + dot_nt(
            dq_ref[rows, :], weight_of(w_ref, 0, plan.shard)
        )
    source_parts(plan, info_ref, dkl_ref, dvl_ref, w_ref, 1, own_ref, base_ref, mates)
    start = own_rows(plan, info_ref)
    for rows in row_blocks(plan.rows):
        own_x_ref[rows, :] = x_ref[pl.ds(start + rows.start, BLOCK), :]
    products = ((own_x_ref, dq_ref), (x_ref, dkl_ref), (x_ref, dvl_ref))
    weight_products(plan, info_ref, products, gw_ref, keep_ref, send_ref)
    tail = jnp.concatenate(
        [terms_ref[...], jnp.zeros((VECTOR_ROWS - 8, plan.width), WIDE)], axis=0
    ).astype(LOW)
    for number in range(plan.dp // 2):
        keep_ref[number, 3 * plan.shard :, :] = tail
        send_ref[number, 3 * plan.shard :, :] = tail


SMEM = pl.BlockSpec(memory_space=pltpu.SMEM)
VMEM = pl.BlockSpec(memory_space=pltpu.VMEM)
ANY = pl.BlockSpec(memory_space=pl.ANY)
HBM = pl.BlockSpec(memory_space=pltpu.HBM)


def call(kernel, specs, operands, outs, scratch, flops, moved, megabytes, out_specs=None):
    return pl.pallas_call(
        kernel,
        in_specs=specs,
        out_specs=out_specs or [VMEM] * len(outs),
        out_shape=outs,
        scratch_shapes=scratch,
        compiler_params=pltpu.CompilerParams(vmem_limit_bytes=megabytes * MEGABYTE),
        cost_estimate=pl.CostEstimate(flops=flops, bytes_accessed=moved, transcendentals=0),
    )(*operands)


def shape(dims, dtype):
    return jax.ShapeDtypeStruct(dims, dtype)


def forward_scratch(plan):
    return [
        pltpu.VMEM((plan.pairs, 2 * BLOCK, PAIR), LOW),
        pltpu.VMEM((plan.pairs, PAIR, 2 * BLOCK), WIDE),
        pltpu.VMEM((8, 2 * BLOCK), WIDE),
        pltpu.VMEM((8, 2 * BLOCK), WIDE),
    ]


def backward_scratch(plan):
    return [
        pltpu.VMEM((plan.pairs, 2 * BLOCK, PAIR), LOW),
        pltpu.VMEM((plan.pairs, 2 * BLOCK, PAIR), LOW),
        pltpu.VMEM((plan.pairs, PAIR, 2 * BLOCK), WIDE),
        pltpu.VMEM((8, 2 * BLOCK), WIDE),
    ]


def flat(pieces):
    return sum(piece.shape[0] for piece in pieces)


def hold_kernel(info_ref, held_ref):
    for place in range(info_ref.shape[0]):
        held_ref[place] = info_ref[place]


def hold(info):
    return call(
        hold_kernel, [SMEM], [info], [shape(info.shape, jnp.int32)], [], 40 * 10**9, 10**5, 1, [SMEM]
    )[0]


def forward(plan, info, chunks, pieces):
    rows, length, width = plan.rows, plan.length, plan.width
    heads = [
        shape((rows, width), LOW),
        shape((rows, width), LOW),
        shape((plan.query_blocks * plan.pairs, 2 * BLOCK), WIDE),
        shape((rows, width), WIDE),
    ]
    outs = heads + [shape((8, length), WIDE), shape((TILE, width), WIDE)] + heads
    scratch = [
        pltpu.VMEM((length, width), LOW),
        pltpu.VMEM((length, width), LOW),
        pltpu.VMEM((length, width), LOW),
        pltpu.VMEM((length, width), LOW),
        pltpu.VMEM((plan.chunks, TILE, width), LOW),
        pltpu.VMEM((plan.dp, 8 * plan.shard + TILE, width), LOW),
        pltpu.VMEM((length, 128), WIDE),
        pltpu.SemaphoreType.DMA((2, plan.chunks)),
        pltpu.SemaphoreType.DMA((2, plan.chunks)),
        pltpu.SemaphoreType.DMA((plan.dp,)),
    ] + forward_scratch(plan)
    return call(
        functools.partial(forward_kernel, plan, len(chunks), len(pieces)),
        [SMEM] + [ANY] * (len(chunks) + len(pieces)),
        [info, *chunks, *pieces],
        outs,
        scratch,
        FORWARD_COST,
        10**5,
        megabytes(plan, 18, 10),
    )


def feed(plan, info, upstreams, pieces, z, vecs):
    rows, width, blocks = plan.rows, plan.width, plan.hidden_blocks
    piece_rows = blocks * plan.shard + plan.outer_shard
    outs = (
        [shape((plan.chunk, width), LOW)] * plan.batches
        + [shape((rows, width), WIDE), shape((8, width), WIDE)]
        + [shape((plan.dp // 2, piece_rows, width), LOW)] * 2
    )
    scratch = [
        pltpu.VMEM((width, plan.hidden), LOW),
        pltpu.VMEM((plan.hidden, width), LOW),
        pltpu.VMEM((rows, width), LOW),
        pltpu.VMEM((rows, plan.hidden), WIDE),
        pltpu.VMEM((rows, plan.hidden), LOW),
        pltpu.VMEM((rows, plan.hidden), LOW),
        pltpu.VMEM((rows, width), WIDE),
        pltpu.VMEM((rows, width), LOW),
        pltpu.VMEM((rows, width), LOW),
        pltpu.VMEM((blocks, width, width), LOW),
        pltpu.VMEM((plan.hidden, width), LOW),
        pltpu.SemaphoreType.DMA((blocks + 1, plan.dp)),
        pltpu.SemaphoreType.DMA((plan.batches,)),
    ]
    return call(
        functools.partial(feed_kernel, plan, len(pieces)),
        [SMEM] + [ANY] * (plan.batches + len(pieces)) + [VMEM] * 2,
        [info, *upstreams, *pieces, z, vecs],
        outs,
        scratch,
        20 * 10**9,
        12 * 10**6,
        28,
    )


def backward_buffers(plan):
    length, width = plan.length, plan.width
    return [
        pltpu.VMEM((length, 128), WIDE),
        pltpu.VMEM((length, width), WIDE),
        pltpu.VMEM((length, width), WIDE),
        pltpu.VMEM((plan.pairs, 2 * BLOCK, PAIR), LOW),
        pltpu.VMEM((plan.pairs, 2 * BLOCK, PAIR), LOW),
        pltpu.VMEM((plan.pairs, PAIR, 2 * BLOCK), WIDE),
        pltpu.VMEM((8, 2 * BLOCK), WIDE),
    ]


def cross_backward(plan, info, chunks, pieces, operands):
    rows, length, width = plan.rows, plan.length, plan.width
    outs = (
        [shape((rows, width), LOW)]
        + [shape((rows, width), LOW)] * (plan.group - 1)
        + [shape((rows, width), LOW), shape((8, width), WIDE)]
        + [shape((plan.dp // 2, 5 * plan.shard, width), LOW)] * 2
    )
    scratch = [
        pltpu.VMEM((length, width), LOW),
        pltpu.VMEM((plan.dp, 5 * plan.shard, width), LOW),
        pltpu.VMEM((rows, width), LOW),
        pltpu.VMEM((5, width, width), LOW),
        pltpu.VMEM((rows, width), WIDE),
        pltpu.VMEM((rows, width), LOW),
        pltpu.VMEM((length, width), LOW),
        pltpu.VMEM((length, width), LOW),
        pltpu.VMEM((rows, width), LOW),
        pltpu.VMEM((rows, width), LOW),
        pltpu.VMEM((length, width), LOW),
        pltpu.VMEM((length, width), LOW),
        pltpu.SemaphoreType.DMA((2, plan.chunks)),
        pltpu.SemaphoreType.DMA((plan.dp,)),
    ] + backward_buffers(plan)
    return call(
        functools.partial(cross_backward_kernel, plan, len(chunks), len(pieces)),
        [SMEM] + [ANY] * (len(chunks) + len(pieces)) + [VMEM] * len(operands),
        [info, *chunks, *pieces, *operands],
        outs,
        scratch,
        22 * 10**9,
        12 * 10**6,
        megabytes(plan, 18, 16),
    )


def self_backward(plan, info, chunks, pieces, operands):
    rows, length, width = plan.rows, plan.length, plan.width
    outs = (
        [shape((rows, width), LOW)]
        + [shape((rows, width), LOW)] * (plan.group - 1)
        + [shape((plan.dp // 2, 3 * plan.shard + VECTOR_ROWS, width), LOW)] * 2
    )
    scratch = [
        pltpu.VMEM((length, width), LOW),
        pltpu.VMEM((rows, width), LOW),
        pltpu.VMEM((3, width, width), LOW),
        pltpu.VMEM((plan.dp, 4 * plan.shard, width), LOW),
        pltpu.VMEM((rows, width), LOW),
        pltpu.VMEM((length, width), LOW),
        pltpu.VMEM((length, width), LOW),
        pltpu.VMEM((rows, width), WIDE),
        pltpu.VMEM((rows, width), LOW),
        pltpu.VMEM((length, width), LOW),
        pltpu.VMEM((length, width), LOW),
        pltpu.SemaphoreType.DMA((2, plan.chunks)),
        pltpu.SemaphoreType.DMA((plan.dp,)),
    ] + backward_buffers(plan)
    return call(
        functools.partial(self_backward_kernel, plan, len(chunks), len(pieces)),
        [SMEM] + [ANY] * (len(chunks) + len(pieces)) + [VMEM] * len(operands),
        [info, *chunks, *pieces, *operands],
        outs,
        scratch,
        18 * 10**9,
        12 * 10**6,
        megabytes(plan, 12, 12),
    )


def pack_tokens_kernel(plan, info_ref, tokens, memory, target, source, *refs):
    rounds, semaphores = refs[: plan.batches], refs[-1]
    chunk, width = plan.chunk, plan.width
    moves = []
    for number in range(plan.batches):
        batch = info_ref[plan.batch + number]
        moves.append((tokens.at[batch, 0], rounds[number].at[pl.ds(0, chunk)]))
        moves.append((memory.at[batch, 0], rounds[number].at[pl.ds(chunk, chunk)]))
    copies = [
        pltpu.make_async_copy(here, there, semaphores.at[number])
        for number, (here, there) in enumerate(moves)
    ]
    for copy in copies:
        copy.start()
    first_row = lax.broadcasted_iota(jnp.int32, (TILE, width), 0) == 0
    for number in range(plan.batches):
        batch = info_ref[plan.batch + number]
        row = jnp.concatenate([target[batch], source[batch]], axis=1).astype(WIDE)
        if width > 2 * chunk:
            row = jnp.concatenate([row, jnp.zeros((1, width - 2 * chunk), WIDE)], axis=1)
        rounds[number][2 * chunk :, :] = jnp.where(first_row, row, 0.0).astype(LOW)
    for copy in copies:
        copy.wait()


def pack_tokens(plan, info, tokens, memory, target, source):
    return call(
        functools.partial(pack_tokens_kernel, plan),
        [SMEM] + [HBM] * 2 + [VMEM] * 2,
        [info, tokens, memory, target, source],
        [shape((2 * plan.chunk + TILE, plan.width), LOW)] * plan.batches,
        [pltpu.SemaphoreType.DMA((2 * plan.batches,))],
        0,
        10**6,
        60,
    )


def pack_weights_kernel(plan, info_ref, *refs):
    weights, (vectors, piece_ref, lines_ref, semaphores) = refs[:8], refs[8:]
    shard = plan.shard
    copies = [
        pltpu.make_async_copy(
            weight, piece_ref.at[0, pl.ds(which * shard, shard)], semaphores.at[which]
        )
        for which, weight in enumerate(weights)
    ]
    for copy in copies:
        copy.start()
    lines_ref[...] = jnp.zeros_like(lines_ref)
    lines_ref[0:6, 0:shard] = vectors[...].astype(WIDE)
    lanes = pltpu.roll(lines_ref[...], info_ref[plan.own_dp] * shard, 1)
    piece_ref[0, 8 * shard :, :] = lanes.astype(LOW)
    for copy in copies:
        copy.wait()


def pack_weights(plan, info, weights, vectors):
    return call(
        functools.partial(pack_weights_kernel, plan),
        [SMEM] + [HBM] * 8 + [VMEM],
        [info, *weights, vectors],
        [shape((1, 8 * plan.shard + TILE, plan.width), LOW)],
        [pltpu.VMEM((TILE, plan.width), WIDE), pltpu.SemaphoreType.DMA((8,))],
        20 * 10**9,
        10**6,
        60,
    )[0]


def pack_rest_kernel(plan, info_ref, inner, outer, cotangent, feed_ref, *refs):
    rounds, semaphores = refs[: plan.batches], refs[-1]
    shard, width, blocks = plan.shard, plan.width, plan.hidden_blocks
    moves = [
        (
            inner.at[:, pl.ds(block * width, width)],
            feed_ref.at[0, pl.ds(block * shard, shard)],
        )
        for block in range(blocks)
    ]
    moves.append((outer, feed_ref.at[0, pl.ds(blocks * shard, plan.outer_shard)]))
    for number in range(plan.batches):
        moves.append((cotangent.at[info_ref[plan.batch + number], 0], rounds[number]))
    copy_all(
        [
            pltpu.make_async_copy(here, there, semaphores.at[number])
            for number, (here, there) in enumerate(moves)
        ]
    )


def pack_rest(plan, info, inner, outer, cotangent):
    outs = [shape((1, plan.hidden_blocks * plan.shard + plan.outer_shard, plan.width), LOW)]
    outs += [shape((plan.chunk, plan.width), LOW)] * plan.batches
    return call(
        functools.partial(pack_rest_kernel, plan),
        [SMEM] + [HBM] * 3,
        [info, inner, outer, cotangent],
        outs,
        [pltpu.SemaphoreType.DMA((plan.hidden_blocks + 1 + plan.batches,))],
        0,
        2 * 10**6,
        60,
    )


def pairs_of(plan, move):
    return [
        (dp * plan.seq + seq, to[0] * plan.seq + to[1])
        for dp in range(plan.dp)
        for seq in range(plan.seq)
        for to in [move(dp, seq)]
    ]


def home(plan, dp, batch, seq):
    position = (2 * batch + dp % 2) * plan.group + seq // plan.batches
    return (dp - dp % 2 + position % 2, position // 2)


def round_batch(plan, seq, number):
    return (seq + number) % plan.batches


def inward(plan, number):
    return pairs_of(plan, lambda dp, seq: home(plan, dp, round_batch(plan, seq, number), seq))


def outward(plan, number):
    return [(to, source) for source, to in inward(plan, number)]


def mate(plan, turn):
    def move(dp, seq):
        position = 2 * seq + dp % 2
        group, own = position // plan.group, position % plan.group
        to = group * plan.group + (own + turn) % plan.group
        return (dp - dp % 2 + to % 2, to // 2)

    return pairs_of(plan, move)


def permute(values, pairs):
    return lax.ppermute(values, AXES, pairs)


def dp_flip(plan, bits):
    return pairs_of(plan, lambda dp, seq: (dp ^ bits, seq))


def seq_flip(plan, bits):
    return pairs_of(plan, lambda dp, seq: (dp, seq ^ bits))


def share_inputs(plan, rounds):
    return [permute(piece, inward(plan, number)) for number, piece in enumerate(rounds)]


def share_mates(plan, received):
    chunks = list(received)
    for turn in range(1, plan.group):
        chunks += [permute(piece, mate(plan, turn)) for piece in received]
    return chunks


def send_home(plan, pieces):
    return [permute(piece, outward(plan, number)) for number, piece in enumerate(pieces)]


def order_home(plan, landed, dtype):
    seq = lax.axis_index("seq")
    landed = jnp.stack(landed).astype(dtype)
    order = [(batch - seq) % plan.batches for batch in range(plan.batches)]
    return jnp.stack(
        [lax.dynamic_index_in_dim(landed, index, 0, keepdims=False) for index in order]
    )


def gather_direct(plan, shard):
    if plan.dp != 8:
        return [lax.all_gather(shard[0], "dp", axis=0)]
    return [shard] + [permute(shard, dp_flip(plan, bits)) for bits in (2, 4, 6)]


def gather_own(plan, shard):
    return permute(shard, dp_flip(plan, 1)) if plan.dp == 8 else None


def gather_rest(plan, direct, own_other):
    if plan.dp != 8:
        return direct
    pieces = [direct[0], own_other]
    for piece in direct[1:]:
        pieces += [piece, permute(piece, dp_flip(plan, 1))]
    return pieces


def add_low(values):
    total = values[0].astype(WIDE)
    for value in values[1:]:
        total = total + value.astype(WIDE)
    return total.astype(LOW)


def core_send(plan, send):
    return permute(send, dp_flip(plan, 1)) if plan.dp == 8 else send


def core_sum(plan, keep, other):
    if plan.dp != 8:
        return [jnp.concatenate([keep, other], axis=0)]
    return [add_low([keep[number], other[number]]) for number in range(4)]


def plane_send(plan, parts):
    if plan.dp != 8:
        return [lax.psum_scatter(parts[0], "dp", scatter_dimension=0)]
    return [permute(parts[number], dp_flip(plan, 2 * number)) for number in range(1, 4)]


def plane_sum(plan, parts, landed):
    total = landed[0] if plan.dp != 8 else add_low([parts[0], *landed])
    return total if plan.seq == 4 else lax.psum(total, "seq")


def halves(plan, total, bits):
    if plan.seq != 4:
        return total, jnp.zeros_like(total)
    half = total.shape[0] // 2
    own = lax.axis_index("seq") // bits % 2
    return (
        lax.dynamic_slice_in_dim(total, own * half, half),
        lax.dynamic_slice_in_dim(total, (1 - own) * half, half),
    )


def seq_send(plan, values, bits):
    return permute(values, seq_flip(plan, bits)) if plan.seq == 4 else jnp.zeros_like(values)


def join(plan, own_part, other, bits):
    if plan.seq != 4:
        return own_part
    own = lax.axis_index("seq") // bits % 2
    return jnp.where(
        own == 0, jnp.concatenate([own_part, other]), jnp.concatenate([other, own_part])
    )


def add_wide(first, second):
    return first.astype(WIDE) + second.astype(WIDE)


def tie(*values):
    return lax.optimization_barrier(values)


def after(values, *others):
    return lax.optimization_barrier((values, others))[0]


def plan_info(plan):
    dp, seq = lax.axis_index("dp"), lax.axis_index("seq")
    position = 2 * seq + dp % 2
    own = position % plan.group
    batch = position // plan.group // 2
    flips = list(range(8)) if plan.dp == 8 else None
    entries = []
    if flips:
        entries += [dp ^ bits for bits in (0, 1, 2, 3, 4, 5, 6, 7)]
        entries += [dp ^ bits for bits in (0, 2, 4, 6, 1, 3, 5, 7)]
    else:
        entries += list(range(plan.dp)) * 2
    places = [(batch - number) % plan.batches for number in range(plan.batches)]
    for turn in range(plan.group):
        source = (own - turn) % plan.group
        entries += [source * plan.batches + place for place in places]
    entries.append(own)
    entries += places
    entries += [(own + turn) % plan.group for turn in range(plan.group)]
    entries += [(seq + number) % plan.batches for number in range(plan.batches)]
    entries.append(dp)
    plan.places = [place.astype(jnp.uint32) for place in places]
    return jnp.stack([jnp.asarray(entry, jnp.int32) for entry in entries])


def on_device(
    tokens,
    memory,
    target_segments,
    source_segments,
    cotangent,
    query_weight,
    key_weight,
    value_weight,
    output_weight,
    cross_query,
    cross_key,
    cross_value,
    cross_output,
    inner_weight,
    outer_weight,
    self_gain,
    self_shift,
    cross_gain,
    cross_shift,
    feed_gain,
    feed_shift,
):
    plan = Plan(tokens, inner_weight)
    width, shard = plan.width, plan.shard
    info = plan_info(plan)
    dp = lax.axis_index("dp")

    vectors = jnp.stack([self_gain, self_shift, cross_gain, cross_shift, feed_gain, feed_shift])
    rounds = pack_tokens(plan, info, tokens, memory, target_segments, source_segments)
    shard_piece = pack_weights(
        plan,
        info,
        [
            query_weight,
            key_weight,
            value_weight,
            output_weight,
            cross_query,
            cross_key,
            cross_value,
            cross_output,
        ],
        vectors,
    )
    direct = gather_direct(plan, shard_piece)
    own_other = gather_own(plan, shard_piece)
    landed = share_inputs(plan, rounds)

    feed_shard, *rounds = pack_rest(plan, info, inner_weight, outer_weight, cotangent)
    feed_shard, rounds, landed[0] = lax.optimization_barrier((feed_shard, rounds, landed[0]))
    info, feed_shard = lax.optimization_barrier((info, feed_shard))
    feed_direct = gather_direct(plan, feed_shard)
    feed_other = gather_own(plan, feed_shard)
    upstreams = share_inputs(plan, rounds)
    direct, landed, info = lax.optimization_barrier((direct, landed, hold(info)))
    pieces = gather_rest(plan, direct, own_other)
    chunks = share_mates(plan, landed)
    q, o, lse, a, segs, vecs, cq, co, cross_lse, z = forward(
        plan, info, chunks, pieces
    )

    feed_direct, upstreams = after((feed_direct, upstreams), z)
    feed_pieces = gather_rest(plan, feed_direct, feed_other)
    *results, dsecond, dvec, feed_keep, feed_send = feed(
        plan, info, upstreams, feed_pieces, z, vecs
    )

    feed_parts = core_sum(plan, feed_keep, core_send(plan, feed_send))
    out_landed = send_home(plan, results)
    feed_landed = plane_send(plan, feed_parts)
    dsecond = after(dsecond, feed_parts)
    back = cross_backward(
        plan,
        info,
        chunks,
        pieces,
        [a, z, segs, vecs, dvec, dsecond, o, cq, co, cross_lse],
    )
    back, feed_landed, out_landed = lax.optimization_barrier((back, feed_landed, out_landed))
    own_memory, *others = back
    mate_memory, (da, terms, cross_keep, cross_send) = (
        others[: plan.group - 1],
        others[plan.group - 1 :],
    )

    feed_keep, feed_send = halves(plan, plane_sum(plan, feed_parts, feed_landed), 1)
    cross_parts = core_sum(plan, cross_keep, core_send(plan, cross_send))
    memory_pieces = add_mates(plan, own_memory, mate_memory)
    feed_landed = seq_send(plan, feed_send, 1)
    cross_landed = plane_send(plan, cross_parts)
    memory_landed = send_home(plan, memory_pieces)
    feed_landed, cross_parts[0], memory_pieces = tie(feed_landed, cross_parts[0], memory_pieces)
    feed_keep, feed_send = halves(plan, add_low([feed_keep, feed_landed]), 2)
    feed_landed = seq_send(plan, feed_send, 2)
    da, feed_keep = tie(da, feed_keep)
    back = self_backward(plan, info, chunks, pieces, [segs, da, terms, q, o, lse])
    back, feed_landed, cross_landed, memory_landed = lax.optimization_barrier(
        (back, feed_landed, cross_landed, memory_landed)
    )
    own_tokens, *mate_tokens, self_keep, self_send = back

    mate_landed = send_mates(plan, mate_tokens)
    self_landed = core_send(plan, self_send)
    feed_quarter = add_low([feed_keep, feed_landed])
    feed_landed = seq_send(plan, feed_quarter, 2)
    cross_keep, cross_send = halves(plan, plane_sum(plan, cross_parts, cross_landed), 1)
    cross_landed = seq_send(plan, cross_send, 1)
    token_pieces = sum_mates(plan, own_tokens, mate_landed)
    token_landed = send_home(plan, token_pieces)
    self_landed, cross_keep, feed_quarter = tie(self_landed, cross_keep, feed_quarter)
    self_parts = core_sum(plan, self_keep, self_landed)
    self_landed = plane_send(plan, self_parts)
    feed_landed, cross_landed = after((feed_landed, cross_landed), self_parts)
    feed_half = join(plan, feed_quarter, feed_landed, 2)
    feed_landed = seq_send(plan, feed_half, 1)
    cross_keep, cross_send = halves(plan, add_low([cross_keep, cross_landed]), 2)
    cross_landed = seq_send(plan, cross_send, 2)
    self_landed, feed_half, cross_keep, token_landed[0] = tie(
        self_landed, feed_half, cross_keep, token_landed[0]
    )
    self_total = plane_sum(plan, self_parts, self_landed)
    self_landed = seq_send(plan, self_total, 1)
    cross_landed, self_total = tie(cross_landed, self_total)
    cross_quarter = add_low([cross_keep, cross_landed])
    cross_landed = seq_send(plan, cross_quarter, 2)
    self_landed, cross_quarter = tie(self_landed, cross_quarter)
    self_total = add_low([self_total, self_landed])
    self_landed = seq_send(plan, self_total, 2)
    cross_landed, self_total, out_landed, memory_landed = tie(
        cross_landed, self_total, out_landed, memory_landed
    )
    cross_half = join(plan, cross_quarter, cross_landed, 2)
    cross_landed = seq_send(plan, cross_half, 1)
    out_tokens = order_home(plan, out_landed, LOW)
    grad_memory = order_home(plan, memory_landed, WIDE)
    grad_tokens = order_home(plan, token_landed, WIDE)
    self_landed, cross_landed, out_tokens, grad_memory, grad_tokens = tie(
        self_landed, cross_landed, out_tokens, grad_memory, grad_tokens
    )
    feed_total = join(plan, feed_half, feed_landed, 1).astype(WIDE)
    cross_total = join(plan, cross_half, cross_landed, 1).astype(WIDE)
    self_total = add_wide(self_total, self_landed)

    scale = 1.0 / (plan.batches * plan.dp)
    feed_grads, cross_grads, self_grads = (
        feed_total * scale,
        cross_total * scale,
        self_total * scale,
    )
    inner_grads = [
        feed_grads[block * shard : (block + 1) * shard] for block in range(plan.hidden_blocks)
    ]
    vector_grads = lax.dynamic_slice(self_grads, (3 * shard, dp * shard), (TILE, shard))
    return (
        out_tokens[:, None],
        grad_tokens[:, None],
        grad_memory[:, None],
        *[self_grads[which * shard : (which + 1) * shard] for which in range(3)],
        cross_grads[4 * shard : 5 * shard],
        *[cross_grads[which * shard : (which + 1) * shard] for which in range(4)],
        jnp.concatenate(inner_grads, axis=1),
        feed_grads[plan.hidden_blocks * shard :],
        *[vector_grads[which] for which in range(6)],
    )


def send_mates(plan, mates):
    return [permute(part, mate(plan, turn)) for turn, part in enumerate(mates, 1)]


def sum_mates(plan, own, landed):
    own = own.astype(WIDE)
    for part in landed:
        own = own + part.astype(WIDE)
    own = own.reshape(plan.batches, plan.chunk, plan.width)
    return [
        lax.dynamic_index_in_dim(own, place, 0, keepdims=False).astype(LOW)
        for place in plan.places
    ]


def add_mates(plan, own, mates):
    return sum_mates(plan, own, send_mates(plan, mates))


def solution(mesh):
    tokens = P(None, "dp", "seq", None)
    ids = P(None, "dp", "seq")
    weight = P("dp", None)
    vector = P("dp")
    return jax.shard_map(
        on_device,
        mesh=mesh,
        in_specs=(tokens, tokens, ids, ids, tokens) + (weight,) * 10 + (vector,) * 6,
        out_specs=(tokens,) * 3 + (weight,) * 10 + (vector,) * 6,
        check_vma=False,
    )
```

```python
import functools

import jax
import jax.numpy as jnp
from jax import lax
from jax.experimental import pallas as pl
from jax.experimental.pallas import tpu as pltpu
from jax.sharding import PartitionSpec as P

DH = 64
PAIR = 2 * DH
BLOCK = 256
TILE = 16
VECTOR_ROWS = 16
FORWARD_COST = 10**6
EPSILON = 1e-05
NEGATIVE = -1e30
FACTOR = DH ** (-0.5)
AXES = ("dp", "seq")
LOW = jnp.bfloat16
WIDE = jnp.float32
MEGABYTE = 1024 * 1024


def dot_nn(a, b):
    return jnp.dot(a, b, preferred_element_type=WIDE)


def dot_nt(a, b):
    return lax.dot_general(a, b, (((1,), (1,)), ((), ())), preferred_element_type=WIDE)


def dot_tn(a, b):
    return lax.dot_general(a, b, (((0,), (0,)), ((), ())), preferred_element_type=WIDE)


def normalise(values):
    centred = values - jnp.mean(values, axis=-1, keepdims=True)
    inverse = lax.rsqrt(jnp.mean(centred * centred, axis=-1, keepdims=True) + EPSILON)
    return centred * inverse, inverse


def norm_backward(upstream, normed, inverse, gain_row):
    scaled = upstream * gain_row
    plain_mean = jnp.mean(scaled, axis=-1, keepdims=True)
    along_mean = jnp.mean(scaled * normed, axis=-1, keepdims=True)
    return inverse * (scaled - plain_mean - normed * along_mean)


def row_blocks(length, size=BLOCK):
    return [pl.ds(start, size) for start in range(0, length, size)]


def copy_all(copies):
    for copy in copies:
        copy.start()
    for copy in copies:
        copy.wait()


def piece_copies(plan, pieces, info_ref, w_ref, semaphores):
    copies = []
    for piece in pieces:
        for slab in range(piece.shape[0]):
            number = len(copies)
            owner = info_ref[plan.order + number]
            copies.append(
                pltpu.make_async_copy(piece.at[slab], w_ref.at[owner], semaphores.at[number])
            )
    return copies


def weight_of(weight_ref, which, rows):
    count, _, width = weight_ref.shape
    return weight_ref[:, which * rows : (which + 1) * rows, :].reshape(count * rows, width)


def seg_columns(seg_row):
    return jnp.transpose(jnp.broadcast_to(seg_row, (128, seg_row.shape[1])))


def stack_heads(pair):
    lane = lax.broadcasted_iota(jnp.int32, pair.shape, 1)
    zero = jnp.zeros_like(pair)
    return jnp.concatenate(
        [jnp.where(lane < DH, pair, zero), jnp.where(lane < DH, zero, pair)], axis=0
    )


def unstack_heads(columns):
    row = lax.broadcasted_iota(jnp.int32, (PAIR, BLOCK), 0)
    return jnp.where(row < DH, columns[:, :BLOCK], columns[:, BLOCK:])


def mask_bias(key_ids, query_ids, key_start, query_start, causal):
    ids = jnp.concatenate([key_ids, key_ids], axis=1)
    allowed = ids == query_ids
    if causal:
        key_place = key_start + lax.broadcasted_iota(jnp.int32, (BLOCK, BLOCK), 0)
        query_place = query_start + lax.broadcasted_iota(jnp.int32, (BLOCK, BLOCK), 1)
        allowed = jnp.logical_and(allowed, key_place <= query_place)
    bias = jnp.where(allowed, 0.0, NEGATIVE)
    return jnp.concatenate([bias, bias], axis=1)


def key_bounds(key_row, query_ids, query_start, causal):
    below = jnp.sum(jnp.where(key_row < jnp.min(query_ids), 1.0, 0.0)).astype(jnp.int32)
    first = lax.div(below, BLOCK)
    if causal:
        return first, lax.div(query_start, BLOCK) + 1
    upto = jnp.sum(jnp.where(key_row <= jnp.max(query_ids), 1.0, 0.0)).astype(jnp.int32)
    return first, lax.div(upto + (BLOCK - 1), BLOCK)


def attend_forward(
    q_ref, k_ref, v_ref, o_ref, lse_ref, key_row, columns_ref, query_row, start, causal, scratch
):
    stack_ref, sum_ref, top_ref, total_ref = scratch
    pairs = q_ref.shape[1] // PAIR
    for number, rows in enumerate(row_blocks(q_ref.shape[0])):
        query_ids = query_row[:, number * BLOCK : (number + 1) * BLOCK]
        query_start = start + number * BLOCK
        low, high = key_bounds(key_row, query_ids, query_start, causal)
        for pair in range(pairs):
            stack_ref[pair] = stack_heads(q_ref[rows, pair * PAIR : (pair + 1) * PAIR])
        sum_ref[...] = jnp.zeros_like(sum_ref)
        top_ref[...] = jnp.full_like(top_ref, NEGATIVE)
        total_ref[...] = jnp.zeros_like(total_ref)

        def one_block(block, carry):
            key_start = pl.multiple_of(block * BLOCK, BLOCK)
            keys = pl.ds(key_start, BLOCK)
            bias = mask_bias(columns_ref[keys, :], query_ids, key_start, query_start, causal)
            values = [
                (
                    k_ref[keys, pair * PAIR : (pair + 1) * PAIR],
                    v_ref[keys, pair * PAIR : (pair + 1) * PAIR],
                    stack_ref[pair],
                    top_ref[pair : pair + 1, :],
                    total_ref[pair : pair + 1, :],
                    sum_ref[pair],
                )
                for pair in range(pairs)
            ]
            scores = [dot_nt(key_pair, queries) + bias for key_pair, _, queries, *_ in values]
            tops = [
                jnp.maximum(value[3], jnp.max(score, axis=0, keepdims=True))
                for value, score in zip(values, scores)
            ]
            exponents = [jnp.exp(score - top) for score, top in zip(scores, tops)]
            shrinks = [jnp.exp(value[3] - top) for value, top in zip(values, tops)]
            totals = [
                value[4] * shrink + jnp.sum(exponent, axis=0, keepdims=True)
                for value, shrink, exponent in zip(values, shrinks, exponents)
            ]
            sums = [
                value[5] * shrink + dot_tn(value[1], exponent.astype(LOW))
                for value, shrink, exponent in zip(values, shrinks, exponents)
            ]
            for pair in range(pairs):
                top_ref[pair : pair + 1, :] = tops[pair]
                total_ref[pair : pair + 1, :] = totals[pair]
                sum_ref[pair] = sums[pair]
            return carry

        lax.fori_loop(low, high, one_block, 0)
        for pair in range(pairs):
            total = total_ref[pair : pair + 1, :]
            context = unstack_heads(sum_ref[pair] / total)
            o_ref[rows, pair * PAIR : (pair + 1) * PAIR] = jnp.transpose(context).astype(LOW)
            place = number * pairs + pair
            lse_ref[place : place + 1, :] = top_ref[pair : pair + 1, :] + jnp.log(total)


def attend_backward(
    q_ref,
    k_ref,
    v_ref,
    o_ref,
    grad_ref,
    lse_ref,
    dq_ref,
    dk_ref,
    dv_ref,
    key_row,
    columns_ref,
    query_row,
    start,
    causal,
    scratch,
):
    stack_ref, stack_grad_ref, sum_ref, along_ref = scratch
    pairs = q_ref.shape[1] // PAIR
    dk_ref[...] = jnp.zeros_like(dk_ref)
    dv_ref[...] = jnp.zeros_like(dv_ref)
    for number, rows in enumerate(row_blocks(q_ref.shape[0])):
        query_ids = query_row[:, number * BLOCK : (number + 1) * BLOCK]
        query_start = start + number * BLOCK
        low, high = key_bounds(key_row, query_ids, query_start, causal)
        for pair in range(pairs):
            lanes = slice(pair * PAIR, (pair + 1) * PAIR)
            grad = grad_ref[rows, lanes]
            stack_ref[pair] = stack_heads(q_ref[rows, lanes])
            stack_grad_ref[pair] = stack_heads(grad)
            along = jnp.transpose(grad.astype(WIDE) * o_ref[rows, lanes].astype(WIDE))
            along_ref[pair : pair + 1, :] = jnp.concatenate(
                [
                    jnp.sum(along[:DH], axis=0, keepdims=True),
                    jnp.sum(along[DH:], axis=0, keepdims=True),
                ],
                axis=1,
            )
        sum_ref[...] = jnp.zeros_like(sum_ref)

        def one_block(block, carry):
            key_start = pl.multiple_of(block * BLOCK, BLOCK)
            keys = pl.ds(key_start, BLOCK)
            bias = mask_bias(columns_ref[keys, :], query_ids, key_start, query_start, causal)
            for pair in range(pairs):
                lanes = slice(pair * PAIR, (pair + 1) * PAIR)
                place = number * pairs + pair
                key_pair = k_ref[keys, lanes]
                scores = dot_nt(key_pair, stack_ref[pair]) + bias
                probs = jnp.exp(scores - lse_ref[place : place + 1, :])
                prob_grad = dot_nt(v_ref[keys, lanes], stack_grad_ref[pair])
                score_grad = (probs * (prob_grad - along_ref[pair : pair + 1, :])).astype(LOW)
                dv_ref[keys, lanes] += dot_nn(probs.astype(LOW), stack_grad_ref[pair])
                dk_ref[keys, lanes] += dot_nn(score_grad, stack_ref[pair])
                sum_ref[pair] += dot_tn(key_pair, score_grad)
            return carry

        lax.fori_loop(low, high, one_block, 0)
        for pair in range(pairs):
            grad = jnp.transpose(unstack_heads(sum_ref[pair])) * FACTOR
            dq_ref[rows, pair * PAIR : (pair + 1) * PAIR] = grad.astype(LOW)


def store_pieces(grad_ref, keep_ref, send_ref, info_ref, order, offset, count, rows):
    half = count // 2
    for number in range(count):
        owner = info_ref[order + number]
        block = grad_ref[pl.ds(pl.multiple_of(owner * rows, rows), rows), :]
        target = keep_ref if number < half else send_ref
        target[number % half, offset : offset + rows, :] = block


class Plan:
    def __init__(self, tokens, inner_weight):
        self.dp = lax.axis_size("dp")
        self.seq = lax.axis_size("seq")
        self.batches, _, self.chunk, self.width = tokens.shape
        self.hidden = inner_weight.shape[1]
        self.length = self.chunk * self.seq
        self.group = self.seq // self.batches
        self.rows = self.batches * self.chunk
        self.chunks = self.seq
        self.shard = self.width // self.dp
        self.outer_shard = self.hidden // self.dp
        self.hidden_blocks = self.hidden // self.width
        self.pairs = self.width // PAIR
        self.query_blocks = self.rows // BLOCK
        self.order = 0
        self.grad_order = self.dp
        self.chunk_order = 2 * self.dp
        self.own = self.chunk_order + self.chunks
        self.round = self.own + 1
        self.mates = self.round + self.batches
        self.batch = self.mates + self.group
        self.own_dp = self.batch + self.batches


def megabytes(plan, fixed, by_length):
    return fixed + -(-by_length * plan.length // 1024)


def seg_rows(plan, raw_ref, seg_ref):
    for number in range(plan.chunks):
        lanes = slice(number * plan.chunk, (number + 1) * plan.chunk)
        seg_ref[0:1, lanes] = raw_ref[number, 0:1, : plan.chunk].astype(WIDE)
        seg_ref[1:2, lanes] = raw_ref[number, 0:1, plan.chunk : 2 * plan.chunk].astype(WIDE)


def own_rows(plan, info_ref):
    return pl.multiple_of(info_ref[plan.own] * plan.rows, plan.rows)


def chunk_copies(plan, chunks, info_ref, first, x_ref, raw_ref, semaphores):
    copies = []
    for number, chunk in enumerate(chunks):
        index = info_ref[plan.chunk_order + number]
        rows = pl.ds(pl.multiple_of(index * plan.chunk, plan.chunk), plan.chunk)
        copies.append(
            pltpu.make_async_copy(
                chunk.at[pl.ds(first, plan.chunk)], x_ref.at[rows], semaphores.at[0, number]
            )
        )
        if raw_ref is not None:
            copies.append(
                pltpu.make_async_copy(
                    chunk.at[pl.ds(2 * plan.chunk, TILE)],
                    raw_ref.at[index],
                    semaphores.at[1, number],
                )
            )
    return copies


def project_rows(length, source_ref, key_weight, value_weight, k_ref, v_ref):
    for rows in row_blocks(length, 2 * BLOCK):
        k_ref[rows, :] = dot_nn(source_ref[rows, :], key_weight).astype(LOW)
        v_ref[rows, :] = dot_nn(source_ref[rows, :], value_weight).astype(LOW)


def forward_kernel(plan, chunk_count, piece_count, info_ref, *refs):
    chunks, refs = refs[:chunk_count], refs[chunk_count:]
    pieces, refs = refs[:piece_count], refs[piece_count:]
    (q_ref, o_ref, lse_ref, a_ref, seg_ref, vec_ref), refs = refs[:6], refs[6:]
    (cq_ref, co_ref, cross_lse_ref, z_ref, k_ref, v_ref), refs = refs[:6], refs[6:]
    x_ref, m_ref, raw_ref, w_ref, columns_ref, chunk_sems, m_sems, piece_sems, *scratch = refs
    load = chunk_copies(plan, chunks, info_ref, 0, x_ref, raw_ref, chunk_sems)
    load += chunk_copies(plan, chunks, info_ref, plan.chunk, m_ref, None, m_sems)
    load += piece_copies(plan, pieces, info_ref, w_ref, piece_sems)
    copy_all(load)
    shard = plan.shard
    start = own_rows(plan, info_ref)
    vec_ref[...] = jnp.sum(w_ref[:, 8 * shard :, :].astype(WIDE), axis=0)
    seg_rows(plan, raw_ref, seg_ref)
    columns_ref[...] = seg_columns(seg_ref[0:1, :])
    for rows in row_blocks(plan.rows):
        own = x_ref[pl.ds(start + rows.start, BLOCK), :]
        q_ref[rows, :] = (dot_nn(own, weight_of(w_ref, 0, shard)) * FACTOR).astype(LOW)
    project_rows(
        plan.length,
        x_ref,
        weight_of(w_ref, 1, shard),
        weight_of(w_ref, 2, shard),
        k_ref,
        v_ref,
    )
    attend_forward(
        q_ref,
        k_ref,
        v_ref,
        o_ref,
        lse_ref,
        seg_ref[0:1, :],
        columns_ref,
        seg_ref[0:1, pl.ds(start, plan.rows)],
        start,
        True,
        scratch,
    )
    gain, shift = vec_ref[0:1, :], vec_ref[1:2, :]
    for rows in row_blocks(plan.rows):
        own = x_ref[pl.ds(start + rows.start, BLOCK), :].astype(WIDE)
        a = own + dot_nn(o_ref[rows, :], weight_of(w_ref, 3, shard))
        a_ref[rows, :] = a
        normed, _ = normalise(a)
        first = normed * gain + shift
        z_ref[rows, :] = first
        cq_ref[rows, :] = (
            dot_nn(first.astype(LOW), weight_of(w_ref, 4, shard)) * FACTOR
        ).astype(LOW)
    project_rows(
        plan.length,
        m_ref,
        weight_of(w_ref, 5, shard),
        weight_of(w_ref, 6, shard),
        k_ref,
        v_ref,
    )
    columns_ref[...] = seg_columns(seg_ref[1:2, :])
    attend_forward(
        cq_ref,
        k_ref,
        v_ref,
        co_ref,
        cross_lse_ref,
        seg_ref[1:2, :],
        columns_ref,
        seg_ref[0:1, pl.ds(start, plan.rows)],
        start,
        False,
        scratch,
    )
    for rows in row_blocks(plan.rows):
        z_ref[rows, :] += dot_nn(co_ref[rows, :], weight_of(w_ref, 7, shard))


def feed_kernel(plan, piece_count, info_ref, *refs):
    batches = plan.batches
    upstreams, refs = refs[:batches], refs[batches:]
    pieces, refs = refs[:piece_count], refs[piece_count:]
    (z_ref, vec_ref), refs = refs[:2], refs[2:]
    outs, refs = refs[:batches], refs[batches:]
    (dh_ref, dvec_ref, keep_ref, send_ref), refs = refs[:4], refs[4:]
    inner_ref, outer_ref, low_ref, u_ref, r_ref, du_ref, f_ref, up_ref, res_ref, *refs = refs
    inner_gw_ref, outer_gw_ref, piece_sems, up_sems = refs
    width, shard, blocks, outer_shard = (
        plan.width,
        plan.shard,
        plan.hidden_blocks,
        plan.outer_shard,
    )
    copies = []
    number = 0
    for piece in pieces:
        for slab in range(piece.shape[0]):
            owner = info_ref[plan.order + number]
            for block in range(blocks):
                copies.append(
                    pltpu.make_async_copy(
                        piece.at[slab, pl.ds(block * shard, shard)],
                        inner_ref.at[
                            pl.ds(pl.multiple_of(owner * shard, shard), shard),
                            pl.ds(block * width, width),
                        ],
                        piece_sems.at[block, number],
                    )
                )
            copies.append(
                pltpu.make_async_copy(
                    piece.at[slab, pl.ds(blocks * shard, outer_shard)],
                    outer_ref.at[pl.ds(pl.multiple_of(owner * outer_shard, outer_shard), outer_shard)],
                    piece_sems.at[blocks, number],
                )
            )
            number += 1
    for number in range(batches):
        index = info_ref[plan.round + number]
        rows = pl.ds(pl.multiple_of(index * plan.chunk, plan.chunk), plan.chunk)
        copies.append(
            pltpu.make_async_copy(upstreams[number], up_ref.at[rows], up_sems.at[number])
        )
    for copy in copies:
        copy.start()
    gain_two, shift_two = vec_ref[2:3, :], vec_ref[3:4, :]
    gain_three, shift_three = vec_ref[4:5, :], vec_ref[5:6, :]
    gain_grad = jnp.zeros((1, width), WIDE)
    shift_grad = jnp.zeros((1, width), WIDE)
    for rows in row_blocks(plan.rows):
        normed, _ = normalise(z_ref[rows, :])
        second = normed * gain_two + shift_two
        f_ref[rows, :] = second
        low_ref[rows, :] = second.astype(LOW)
    for copy in copies:
        copy.wait()
    lanes = [slice(block * width, (block + 1) * width) for block in range(blocks)]
    for part in lanes:
        u = dot_nn(low_ref[...], inner_ref[:, part])
        phi = 0.5 + 0.5 * lax.erf(u * (0.5**0.5))
        r_ref[:, part] = (u * phi).astype(LOW)
        u_ref[:, part] = phi + u * (jnp.exp(-0.5 * u * u) * 0.3989422804014327)
    for rows in row_blocks(plan.rows):
        f = f_ref[rows, :] + dot_nn(r_ref[rows, :], outer_ref[...])
        normed, inverse = normalise(f)
        res_ref[rows, :] = (normed * gain_three + shift_three).astype(LOW)
        upstream = up_ref[rows, :].astype(WIDE)
        gain_grad += jnp.sum(upstream * normed, axis=0, keepdims=True)
        shift_grad += jnp.sum(upstream, axis=0, keepdims=True)
        feed_grad = norm_backward(upstream, normed, inverse, gain_three)
        dh_ref[rows, :] = feed_grad
        up_ref[rows, :] = feed_grad.astype(LOW)
    for number in range(batches):
        index = info_ref[plan.round + number]
        outs[number][...] = res_ref[pl.ds(pl.multiple_of(index * plan.chunk, plan.chunk), plan.chunk), :]
    for part in lanes:
        dr = dot_nt(up_ref[...], outer_ref[part, :]).astype(LOW).astype(WIDE)
        du_ref[:, part] = (dr * u_ref[:, part]).astype(LOW)
        outer_gw_ref[part, :] = dot_tn(r_ref[:, part], up_ref[...]).astype(LOW)
    for block, part in enumerate(lanes):
        inner_gw_ref[block] = dot_tn(low_ref[...], du_ref[:, part]).astype(LOW)
    for rows in row_blocks(plan.rows):
        dh_ref[rows, :] += dot_nt(du_ref[rows, :], inner_ref[...])
    for block in range(blocks):
        store_pieces(
            inner_gw_ref.at[block],
            keep_ref,
            send_ref,
            info_ref,
            plan.grad_order,
            block * shard,
            plan.dp,
            shard,
        )
    store_pieces(
        outer_gw_ref,
        keep_ref,
        send_ref,
        info_ref,
        plan.grad_order,
        blocks * shard,
        plan.dp,
        outer_shard,
    )
    dvec_ref[...] = jnp.zeros_like(dvec_ref)
    dvec_ref[4:5, :] = gain_grad
    dvec_ref[5:6, :] = shift_grad


def norm_back(plan, line, z_ref, upstream_ref, vec_ref, grad_ref, low_ref):
    gain_grad = jnp.zeros((1, plan.width), WIDE)
    shift_grad = jnp.zeros((1, plan.width), WIDE)
    for rows in row_blocks(plan.rows):
        normed, inverse = normalise(z_ref[rows, :])
        upstream = upstream_ref[rows, :]
        gain_grad += jnp.sum(upstream * normed, axis=0, keepdims=True)
        shift_grad += jnp.sum(upstream, axis=0, keepdims=True)
        grad = norm_backward(upstream, normed, inverse, vec_ref[2 * line : 2 * line + 1, :])
        if grad_ref is not None:
            grad_ref[rows, :] = grad
        low_ref[rows, :] = grad.astype(LOW)
    return gain_grad, shift_grad


def attention_back(plan, causal, info_ref, seg_ref, operands, results, buffers):
    q_ref, k_ref, v_ref, o_ref, do_ref, lse_ref = operands
    dq_ref, dkl_ref, dvl_ref = results
    columns_ref, dk_ref, dv_ref, *scratch = buffers
    start = own_rows(plan, info_ref)
    line = 0 if causal else 1
    columns_ref[...] = seg_columns(seg_ref[line : line + 1, :])
    attend_backward(
        q_ref,
        k_ref,
        v_ref,
        o_ref,
        do_ref,
        lse_ref,
        dq_ref,
        dk_ref,
        dv_ref,
        seg_ref[line : line + 1, :],
        columns_ref,
        seg_ref[0:1, pl.ds(start, plan.rows)],
        start,
        causal,
        scratch,
    )

    def round_block(block, carry):
        rows = pl.ds(pl.multiple_of(block * BLOCK, BLOCK), BLOCK)
        dkl_ref[rows, :] = dk_ref[rows, :].astype(LOW)
        dvl_ref[rows, :] = dv_ref[rows, :].astype(LOW)
        return carry

    lax.fori_loop(0, plan.length // BLOCK, round_block, 0)


def source_parts(plan, info_ref, dkl_ref, dvl_ref, w_ref, which, own_ref, base_ref, mates):
    shard = plan.shard
    for number in range(plan.group):
        first = pl.multiple_of(info_ref[plan.mates + number] * plan.rows, plan.rows)
        for rows in row_blocks(plan.rows):
            source = pl.ds(first + rows.start, BLOCK)
            part = dot_nt(dkl_ref[source, :], weight_of(w_ref, which, shard)) + dot_nt(
                dvl_ref[source, :], weight_of(w_ref, which + 1, shard)
            )
            if number == 0 and base_ref is not None:
                part = part + base_ref[rows, :]
            target = mates[number - 1] if number else own_ref
            target[rows, :] = part.astype(LOW)


def weight_products(plan, info_ref, products, gw_ref, keep_ref, send_ref):
    for which, (left, right) in enumerate(products):
        gw_ref[which] = dot_tn(left[...], right[...]).astype(LOW)
    for which in range(len(products)):
        store_pieces(
            gw_ref.at[which],
            keep_ref,
            send_ref,
            info_ref,
            plan.grad_order,
            which * plan.shard,
            plan.dp,
            plan.shard,
        )


def cross_backward_kernel(plan, chunk_count, piece_count, info_ref, *refs):
    chunks, refs = refs[:chunk_count], refs[chunk_count:]
    pieces, refs = refs[:piece_count], refs[piece_count:]
    (a_ref, z_ref, seg_ref, vec_ref, dvec_ref, dsecond_ref, context_ref), refs = refs[:7], refs[7:]
    (q_ref, o_ref, lse_ref), refs = refs[:3], refs[3:]
    own_ref, refs = refs[0], refs[1:]
    mates, refs = refs[: plan.group - 1], refs[plan.group - 1 :]
    (self_low_ref, terms_ref, keep_ref, send_ref), refs = refs[:4], refs[4:]
    m_ref, w_ref, h_ref, gw_ref, grad_ref, low_ref, *refs = refs
    k_ref, v_ref, do_ref, dq_ref, dkl_ref, dvl_ref, chunk_sems, piece_sems, *buffers = refs
    shard = plan.shard
    copies = chunk_copies(plan, chunks, info_ref, plan.chunk, m_ref, None, chunk_sems)
    copies += piece_copies(
        plan,
        [piece.at[:, pl.ds(3 * shard, 5 * shard)] for piece in pieces],
        info_ref,
        w_ref,
        piece_sems,
    )
    copy_all(copies)
    project_rows(
        plan.length, m_ref, weight_of(w_ref, 2, shard), weight_of(w_ref, 3, shard), k_ref, v_ref
    )
    cross_terms = norm_back(plan, 1, z_ref, dsecond_ref, vec_ref, grad_ref, low_ref)
    for rows in row_blocks(plan.rows):
        do_ref[rows, :] = dot_nt(low_ref[rows, :], weight_of(w_ref, 4, shard)).astype(LOW)
    attention_back(
        plan,
        False,
        info_ref,
        seg_ref,
        (q_ref, k_ref, v_ref, o_ref, do_ref, lse_ref),
        (dq_ref, dkl_ref, dvl_ref),
        buffers,
    )
    for rows in row_blocks(plan.rows):
        grad_ref[rows, :] += dot_nt(dq_ref[rows, :], weight_of(w_ref, 1, shard))
        normed, _ = normalise(a_ref[rows, :])
        h_ref[rows, :] = (normed * vec_ref[0:1, :] + vec_ref[1:2, :]).astype(LOW)
    self_terms = norm_back(plan, 0, a_ref, grad_ref, vec_ref, None, self_low_ref)
    source_parts(plan, info_ref, dkl_ref, dvl_ref, w_ref, 2, own_ref, None, mates)
    products = (
        (h_ref, dq_ref),
        (m_ref, dkl_ref),
        (m_ref, dvl_ref),
        (o_ref, low_ref),
        (context_ref, self_low_ref),
    )
    weight_products(plan, info_ref, products, gw_ref, keep_ref, send_ref)
    terms_ref[...] = dvec_ref[...]
    for place, term in enumerate([*self_terms, *cross_terms]):
        terms_ref[place : place + 1, :] = term


def self_backward_kernel(plan, chunk_count, piece_count, info_ref, *refs):
    chunks, refs = refs[:chunk_count], refs[chunk_count:]
    pieces, refs = refs[:piece_count], refs[piece_count:]
    (seg_ref, da_ref, terms_ref, q_ref, o_ref, lse_ref), refs = refs[:6], refs[6:]
    own_ref, refs = refs[0], refs[1:]
    mates, refs = refs[: plan.group - 1], refs[plan.group - 1 :]
    keep_ref, send_ref, x_ref, own_x_ref, gw_ref, w_ref, *refs = refs
    do_ref, k_ref, v_ref, base_ref, dq_ref, dkl_ref, dvl_ref, chunk_sems, piece_sems, *buffers = refs
    copies = piece_copies(
        plan,
        [piece.at[:, pl.ds(0, 4 * plan.shard)] for piece in pieces],
        info_ref,
        w_ref,
        piece_sems,
    )
    copies += chunk_copies(plan, chunks, info_ref, 0, x_ref, None, chunk_sems)
    copy_all(copies)
    project_rows(
        plan.length,
        x_ref,
        weight_of(w_ref, 1, plan.shard),
        weight_of(w_ref, 2, plan.shard),
        k_ref,
        v_ref,
    )
    for rows in row_blocks(plan.rows):
        do_ref[rows, :] = dot_nt(da_ref[rows, :], weight_of(w_ref, 3, plan.shard)).astype(LOW)
    attention_back(
        plan,
        True,
        info_ref,
        seg_ref,
        (q_ref, k_ref, v_ref, o_ref, do_ref, lse_ref),
        (dq_ref, dkl_ref, dvl_ref),
        buffers,
    )
    for rows in row_blocks(plan.rows):
        base_ref[rows, :] = da_ref[rows, :].astype(WIDE) + dot_nt(
            dq_ref[rows, :], weight_of(w_ref, 0, plan.shard)
        )
    source_parts(plan, info_ref, dkl_ref, dvl_ref, w_ref, 1, own_ref, base_ref, mates)
    start = own_rows(plan, info_ref)
    for rows in row_blocks(plan.rows):
        own_x_ref[rows, :] = x_ref[pl.ds(start + rows.start, BLOCK), :]
    products = ((own_x_ref, dq_ref), (x_ref, dkl_ref), (x_ref, dvl_ref))
    weight_products(plan, info_ref, products, gw_ref, keep_ref, send_ref)
    tail = jnp.concatenate(
        [terms_ref[...], jnp.zeros((VECTOR_ROWS - 8, plan.width), WIDE)], axis=0
    ).astype(LOW)
    for number in range(plan.dp // 2):
        keep_ref[number, 3 * plan.shard :, :] = tail
        send_ref[number, 3 * plan.shard :, :] = tail


SMEM = pl.BlockSpec(memory_space=pltpu.SMEM)
VMEM = pl.BlockSpec(memory_space=pltpu.VMEM)
ANY = pl.BlockSpec(memory_space=pl.ANY)
HBM = pl.BlockSpec(memory_space=pltpu.HBM)


def call(kernel, specs, operands, outs, scratch, flops, moved, megabytes, out_specs=None):
    return pl.pallas_call(
        kernel,
        in_specs=specs,
        out_specs=out_specs or [VMEM] * len(outs),
        out_shape=outs,
        scratch_shapes=scratch,
        compiler_params=pltpu.CompilerParams(vmem_limit_bytes=megabytes * MEGABYTE),
        cost_estimate=pl.CostEstimate(flops=flops, bytes_accessed=moved, transcendentals=0),
    )(*operands)


def shape(dims, dtype):
    return jax.ShapeDtypeStruct(dims, dtype)


def forward_scratch(plan):
    return [
        pltpu.VMEM((plan.pairs, 2 * BLOCK, PAIR), LOW),
        pltpu.VMEM((plan.pairs, PAIR, 2 * BLOCK), WIDE),
        pltpu.VMEM((8, 2 * BLOCK), WIDE),
        pltpu.VMEM((8, 2 * BLOCK), WIDE),
    ]


def backward_scratch(plan):
    return [
        pltpu.VMEM((plan.pairs, 2 * BLOCK, PAIR), LOW),
        pltpu.VMEM((plan.pairs, 2 * BLOCK, PAIR), LOW),
        pltpu.VMEM((plan.pairs, PAIR, 2 * BLOCK), WIDE),
        pltpu.VMEM((8, 2 * BLOCK), WIDE),
    ]


def flat(pieces):
    return sum(piece.shape[0] for piece in pieces)


def hold_kernel(info_ref, held_ref):
    for place in range(info_ref.shape[0]):
        held_ref[place] = info_ref[place]


def hold(info):
    return call(
        hold_kernel, [SMEM], [info], [shape(info.shape, jnp.int32)], [], 40 * 10**9, 10**5, 1, [SMEM]
    )[0]


def forward(plan, info, chunks, pieces):
    rows, length, width = plan.rows, plan.length, plan.width
    heads = [
        shape((rows, width), LOW),
        shape((rows, width), LOW),
        shape((plan.query_blocks * plan.pairs, 2 * BLOCK), WIDE),
        shape((rows, width), WIDE),
    ]
    outs = heads + [shape((8, length), WIDE), shape((TILE, width), WIDE)] + heads
    scratch = [
        pltpu.VMEM((length, width), LOW),
        pltpu.VMEM((length, width), LOW),
        pltpu.VMEM((length, width), LOW),
        pltpu.VMEM((length, width), LOW),
        pltpu.VMEM((plan.chunks, TILE, width), LOW),
        pltpu.VMEM((plan.dp, 8 * plan.shard + TILE, width), LOW),
        pltpu.VMEM((length, 128), WIDE),
        pltpu.SemaphoreType.DMA((2, plan.chunks)),
        pltpu.SemaphoreType.DMA((2, plan.chunks)),
        pltpu.SemaphoreType.DMA((plan.dp,)),
    ] + forward_scratch(plan)
    return call(
        functools.partial(forward_kernel, plan, len(chunks), len(pieces)),
        [SMEM] + [ANY] * (len(chunks) + len(pieces)),
        [info, *chunks, *pieces],
        outs,
        scratch,
        FORWARD_COST,
        10**5,
        megabytes(plan, 18, 10),
    )


def feed(plan, info, upstreams, pieces, z, vecs):
    rows, width, blocks = plan.rows, plan.width, plan.hidden_blocks
    piece_rows = blocks * plan.shard + plan.outer_shard
    outs = (
        [shape((plan.chunk, width), LOW)] * plan.batches
        + [shape((rows, width), WIDE), shape((8, width), WIDE)]
        + [shape((plan.dp // 2, piece_rows, width), LOW)] * 2
    )
    scratch = [
        pltpu.VMEM((width, plan.hidden), LOW),
        pltpu.VMEM((plan.hidden, width), LOW),
        pltpu.VMEM((rows, width), LOW),
        pltpu.VMEM((rows, plan.hidden), WIDE),
        pltpu.VMEM((rows, plan.hidden), LOW),
        pltpu.VMEM((rows, plan.hidden), LOW),
        pltpu.VMEM((rows, width), WIDE),
        pltpu.VMEM((rows, width), LOW),
        pltpu.VMEM((rows, width), LOW),
        pltpu.VMEM((blocks, width, width), LOW),
        pltpu.VMEM((plan.hidden, width), LOW),
        pltpu.SemaphoreType.DMA((blocks + 1, plan.dp)),
        pltpu.SemaphoreType.DMA((plan.batches,)),
    ]
    return call(
        functools.partial(feed_kernel, plan, len(pieces)),
        [SMEM] + [ANY] * (plan.batches + len(pieces)) + [VMEM] * 2,
        [info, *upstreams, *pieces, z, vecs],
        outs,
        scratch,
        20 * 10**9,
        12 * 10**6,
        28,
    )


def backward_buffers(plan):
    length, width = plan.length, plan.width
    return [
        pltpu.VMEM((length, 128), WIDE),
        pltpu.VMEM((length, width), WIDE),
        pltpu.VMEM((length, width), WIDE),
        pltpu.VMEM((plan.pairs, 2 * BLOCK, PAIR), LOW),
        pltpu.VMEM((plan.pairs, 2 * BLOCK, PAIR), LOW),
        pltpu.VMEM((plan.pairs, PAIR, 2 * BLOCK), WIDE),
        pltpu.VMEM((8, 2 * BLOCK), WIDE),
    ]


def cross_backward(plan, info, chunks, pieces, operands):
    rows, length, width = plan.rows, plan.length, plan.width
    outs = (
        [shape((rows, width), LOW)]
        + [shape((rows, width), LOW)] * (plan.group - 1)
        + [shape((rows, width), LOW), shape((8, width), WIDE)]
        + [shape((plan.dp // 2, 5 * plan.shard, width), LOW)] * 2
    )
    scratch = [
        pltpu.VMEM((length, width), LOW),
        pltpu.VMEM((plan.dp, 5 * plan.shard, width), LOW),
        pltpu.VMEM((rows, width), LOW),
        pltpu.VMEM((5, width, width), LOW),
        pltpu.VMEM((rows, width), WIDE),
        pltpu.VMEM((rows, width), LOW),
        pltpu.VMEM((length, width), LOW),
        pltpu.VMEM((length, width), LOW),
        pltpu.VMEM((rows, width), LOW),
        pltpu.VMEM((rows, width), LOW),
        pltpu.VMEM((length, width), LOW),
        pltpu.VMEM((length, width), LOW),
        pltpu.SemaphoreType.DMA((2, plan.chunks)),
        pltpu.SemaphoreType.DMA((plan.dp,)),
    ] + backward_buffers(plan)
    return call(
        functools.partial(cross_backward_kernel, plan, len(chunks), len(pieces)),
        [SMEM] + [ANY] * (len(chunks) + len(pieces)) + [VMEM] * len(operands),
        [info, *chunks, *pieces, *operands],
        outs,
        scratch,
        22 * 10**9,
        12 * 10**6,
        megabytes(plan, 18, 16),
    )


def self_backward(plan, info, chunks, pieces, operands):
    rows, length, width = plan.rows, plan.length, plan.width
    outs = (
        [shape((rows, width), LOW)]
        + [shape((rows, width), LOW)] * (plan.group - 1)
        + [shape((plan.dp // 2, 3 * plan.shard + VECTOR_ROWS, width), LOW)] * 2
    )
    scratch = [
        pltpu.VMEM((length, width), LOW),
        pltpu.VMEM((rows, width), LOW),
        pltpu.VMEM((3, width, width), LOW),
        pltpu.VMEM((plan.dp, 4 * plan.shard, width), LOW),
        pltpu.VMEM((rows, width), LOW),
        pltpu.VMEM((length, width), LOW),
        pltpu.VMEM((length, width), LOW),
        pltpu.VMEM((rows, width), WIDE),
        pltpu.VMEM((rows, width), LOW),
        pltpu.VMEM((length, width), LOW),
        pltpu.VMEM((length, width), LOW),
        pltpu.SemaphoreType.DMA((2, plan.chunks)),
        pltpu.SemaphoreType.DMA((plan.dp,)),
    ] + backward_buffers(plan)
    return call(
        functools.partial(self_backward_kernel, plan, len(chunks), len(pieces)),
        [SMEM] + [ANY] * (len(chunks) + len(pieces)) + [VMEM] * len(operands),
        [info, *chunks, *pieces, *operands],
        outs,
        scratch,
        18 * 10**9,
        12 * 10**6,
        megabytes(plan, 12, 12),
    )


def pack_tokens_kernel(plan, tokens, memory, target, source, *refs):
    rounds, semaphores = refs[: plan.batches], refs[-1]
    chunk, width = plan.chunk, plan.width
    moves = []
    for number in range(plan.batches):
        batch = lax.rem(lax.axis_index("seq") + number, plan.batches)
        moves.append((tokens.at[batch, 0], rounds[number].at[pl.ds(0, chunk)]))
        moves.append((memory.at[batch, 0], rounds[number].at[pl.ds(chunk, chunk)]))
    copies = [
        pltpu.make_async_copy(here, there, semaphores.at[number])
        for number, (here, there) in enumerate(moves)
    ]
    for copy in copies:
        copy.start()
    first_row = lax.broadcasted_iota(jnp.int32, (TILE, width), 0) == 0
    for number in range(plan.batches):
        batch = lax.rem(lax.axis_index("seq") + number, plan.batches)
        row = jnp.concatenate([target[batch], source[batch]], axis=1).astype(WIDE)
        if width > 2 * chunk:
            row = jnp.concatenate([row, jnp.zeros((1, width - 2 * chunk), WIDE)], axis=1)
        rounds[number][2 * chunk :, :] = jnp.where(first_row, row, 0.0).astype(LOW)
    for copy in copies:
        copy.wait()


def pack_tokens(plan, tokens, memory, target, source):
    return call(
        functools.partial(pack_tokens_kernel, plan),
        [HBM] * 2 + [VMEM] * 2,
        [tokens, memory, target, source],
        [shape((2 * plan.chunk + TILE, plan.width), LOW)] * plan.batches,
        [pltpu.SemaphoreType.DMA((2 * plan.batches,))],
        0,
        10**6,
        60,
    )


def pack_weights_kernel(plan, info_ref, *refs):
    weights, (vectors, piece_ref, lines_ref, semaphores) = refs[:8], refs[8:]
    shard = plan.shard
    copies = [
        pltpu.make_async_copy(
            weight, piece_ref.at[0, pl.ds(which * shard, shard)], semaphores.at[which]
        )
        for which, weight in enumerate(weights)
    ]
    for copy in copies:
        copy.start()
    lines_ref[...] = jnp.zeros_like(lines_ref)
    lines_ref[0:6, 0:shard] = vectors[...].astype(WIDE)
    lanes = pltpu.roll(lines_ref[...], info_ref[plan.own_dp] * shard, 1)
    piece_ref[0, 8 * shard :, :] = lanes.astype(LOW)
    for copy in copies:
        copy.wait()


def pack_weights(plan, info, weights, vectors):
    return call(
        functools.partial(pack_weights_kernel, plan),
        [SMEM] + [HBM] * 8 + [VMEM],
        [info, *weights, vectors],
        [shape((1, 8 * plan.shard + TILE, plan.width), LOW)],
        [pltpu.VMEM((TILE, plan.width), WIDE), pltpu.SemaphoreType.DMA((8,))],
        20 * 10**9,
        10**6,
        60,
    )[0]


def pack_rest_kernel(plan, info_ref, inner, outer, cotangent, feed_ref, *refs):
    rounds, semaphores = refs[: plan.batches], refs[-1]
    shard, width, blocks = plan.shard, plan.width, plan.hidden_blocks
    moves = [
        (
            inner.at[:, pl.ds(block * width, width)],
            feed_ref.at[0, pl.ds(block * shard, shard)],
        )
        for block in range(blocks)
    ]
    moves.append((outer, feed_ref.at[0, pl.ds(blocks * shard, plan.outer_shard)]))
    for number in range(plan.batches):
        moves.append((cotangent.at[info_ref[plan.batch + number], 0], rounds[number]))
    copy_all(
        [
            pltpu.make_async_copy(here, there, semaphores.at[number])
            for number, (here, there) in enumerate(moves)
        ]
    )


def pack_rest(plan, info, inner, outer, cotangent):
    outs = [shape((1, plan.hidden_blocks * plan.shard + plan.outer_shard, plan.width), LOW)]
    outs += [shape((plan.chunk, plan.width), LOW)] * plan.batches
    return call(
        functools.partial(pack_rest_kernel, plan),
        [SMEM] + [HBM] * 3,
        [info, inner, outer, cotangent],
        outs,
        [pltpu.SemaphoreType.DMA((plan.hidden_blocks + 1 + plan.batches,))],
        0,
        2 * 10**6,
        60,
    )


def pairs_of(plan, move):
    return [
        (dp * plan.seq + seq, to[0] * plan.seq + to[1])
        for dp in range(plan.dp)
        for seq in range(plan.seq)
        for to in [move(dp, seq)]
    ]


def home(plan, dp, batch, seq):
    position = (2 * batch + dp % 2) * plan.group + seq // plan.batches
    return (dp - dp % 2 + position % 2, position // 2)


def round_batch(plan, seq, number):
    return (seq + number) % plan.batches


def inward(plan, number):
    return pairs_of(plan, lambda dp, seq: home(plan, dp, round_batch(plan, seq, number), seq))


def outward(plan, number):
    return [(to, source) for source, to in inward(plan, number)]


def mate(plan, turn):
    def move(dp, seq):
        position = 2 * seq + dp % 2
        group, own = position // plan.group, position % plan.group
        to = group * plan.group + (own + turn) % plan.group
        return (dp - dp % 2 + to % 2, to // 2)

    return pairs_of(plan, move)


def permute(values, pairs):
    return lax.ppermute(values, AXES, pairs)


def dp_flip(plan, bits):
    return pairs_of(plan, lambda dp, seq: (dp ^ bits, seq))


def seq_flip(plan, bits):
    return pairs_of(plan, lambda dp, seq: (dp, seq ^ bits))


def share_inputs(plan, rounds):
    landed = [permute(rounds[number], inward(plan, number)) for number in reversed(range(plan.batches))]
    return landed[::-1]


def share_mates(plan, received):
    chunks = list(received)
    for turn in range(1, plan.group):
        chunks += [permute(piece, mate(plan, turn)) for piece in received]
    return chunks


def send_home(plan, pieces):
    return [permute(piece, outward(plan, number)) for number, piece in enumerate(pieces)]


def order_home(plan, landed, dtype):
    seq = lax.axis_index("seq")
    landed = jnp.stack(landed).astype(dtype)
    order = [(batch - seq) % plan.batches for batch in range(plan.batches)]
    return jnp.stack(
        [lax.dynamic_index_in_dim(landed, index, 0, keepdims=False) for index in order]
    )


def gather_direct(plan, shard):
    if plan.dp != 8:
        return [lax.all_gather(shard[0], "dp", axis=0)]
    return [shard] + [permute(shard, dp_flip(plan, bits)) for bits in (2, 4, 6)]


def gather_own(plan, shard):
    return permute(shard, dp_flip(plan, 1)) if plan.dp == 8 else None


def gather_rest(plan, direct, own_other):
    if plan.dp != 8:
        return direct
    pieces = [direct[0], own_other]
    for piece in direct[1:]:
        pieces += [piece, permute(piece, dp_flip(plan, 1))]
    return pieces


def add_low(values):
    total = values[0].astype(WIDE)
    for value in values[1:]:
        total = total + value.astype(WIDE)
    return total.astype(LOW)


def core_send(plan, send):
    return permute(send, dp_flip(plan, 1)) if plan.dp == 8 else send


def core_sum(plan, keep, other):
    if plan.dp != 8:
        return [jnp.concatenate([keep, other], axis=0)]
    return [add_low([keep[number], other[number]]) for number in range(4)]


def plane_send(plan, parts):
    if plan.dp != 8:
        return [lax.psum_scatter(parts[0], "dp", scatter_dimension=0)]
    return [permute(parts[number], dp_flip(plan, 2 * number)) for number in range(1, 4)]


def plane_sum(plan, parts, landed):
    total = landed[0] if plan.dp != 8 else add_low([parts[0], *landed])
    return total if plan.seq == 4 else lax.psum(total, "seq")


def halves(plan, total, bits):
    if plan.seq != 4:
        return total, jnp.zeros_like(total)
    half = total.shape[0] // 2
    own = lax.axis_index("seq") // bits % 2
    return (
        lax.dynamic_slice_in_dim(total, own * half, half),
        lax.dynamic_slice_in_dim(total, (1 - own) * half, half),
    )


def seq_send(plan, values, bits):
    return permute(values, seq_flip(plan, bits)) if plan.seq == 4 else jnp.zeros_like(values)


def join(plan, own_part, other, bits):
    if plan.seq != 4:
        return own_part
    own = lax.axis_index("seq") // bits % 2
    return jnp.where(
        own == 0, jnp.concatenate([own_part, other]), jnp.concatenate([other, own_part])
    )


def add_wide(first, second):
    return first.astype(WIDE) + second.astype(WIDE)


def tie(*values):
    return lax.optimization_barrier(values)


def after(values, *others):
    return lax.optimization_barrier((values, others))[0]


def plan_info(plan):
    dp, seq = lax.axis_index("dp"), lax.axis_index("seq")
    position = 2 * seq + dp % 2
    own = position % plan.group
    batch = position // plan.group // 2
    flips = list(range(8)) if plan.dp == 8 else None
    entries = []
    if flips:
        entries += [dp ^ bits for bits in (0, 1, 2, 3, 4, 5, 6, 7)]
        entries += [dp ^ bits for bits in (0, 2, 4, 6, 1, 3, 5, 7)]
    else:
        entries += list(range(plan.dp)) * 2
    places = [(batch - number) % plan.batches for number in range(plan.batches)]
    for turn in range(plan.group):
        source = (own - turn) % plan.group
        entries += [source * plan.batches + place for place in places]
    entries.append(own)
    entries += places
    entries += [(own + turn) % plan.group for turn in range(plan.group)]
    entries += [(seq + number) % plan.batches for number in range(plan.batches)]
    entries.append(dp)
    plan.places = [place.astype(jnp.uint32) for place in places]
    return jnp.stack([jnp.asarray(entry, jnp.int32) for entry in entries])


def on_device(
    tokens,
    memory,
    target_segments,
    source_segments,
    cotangent,
    query_weight,
    key_weight,
    value_weight,
    output_weight,
    cross_query,
    cross_key,
    cross_value,
    cross_output,
    inner_weight,
    outer_weight,
    self_gain,
    self_shift,
    cross_gain,
    cross_shift,
    feed_gain,
    feed_shift,
):
    plan = Plan(tokens, inner_weight)
    width, shard = plan.width, plan.shard
    info = plan_info(plan)
    dp = lax.axis_index("dp")

    vectors = jnp.stack([self_gain, self_shift, cross_gain, cross_shift, feed_gain, feed_shift])
    rounds = pack_tokens(plan, tokens, memory, target_segments, source_segments)
    shard_piece = pack_weights(
        plan,
        info,
        [
            query_weight,
            key_weight,
            value_weight,
            output_weight,
            cross_query,
            cross_key,
            cross_value,
            cross_output,
        ],
        vectors,
    )
    direct = gather_direct(plan, shard_piece)
    own_other = gather_own(plan, shard_piece)
    landed = share_inputs(plan, rounds)

    feed_shard, *rounds = pack_rest(plan, info, inner_weight, outer_weight, cotangent)
    feed_shard, rounds, landed[-1] = lax.optimization_barrier((feed_shard, rounds, landed[-1]))
    info, feed_shard = lax.optimization_barrier((info, feed_shard))
    feed_direct = gather_direct(plan, feed_shard)
    feed_other = gather_own(plan, feed_shard)
    upstreams = share_inputs(plan, rounds)
    direct, landed, info = lax.optimization_barrier((direct, landed, hold(info)))
    pieces = gather_rest(plan, direct, own_other)
    chunks = share_mates(plan, landed)
    q, o, lse, a, segs, vecs, cq, co, cross_lse, z = forward(
        plan, info, chunks, pieces
    )

    feed_direct, upstreams = after((feed_direct, upstreams), z)
    feed_pieces = gather_rest(plan, feed_direct, feed_other)
    *results, dsecond, dvec, feed_keep, feed_send = feed(
        plan, info, upstreams, feed_pieces, z, vecs
    )

    feed_parts = core_sum(plan, feed_keep, core_send(plan, feed_send))
    out_landed = send_home(plan, results)
    feed_landed = plane_send(plan, feed_parts)
    dsecond = after(dsecond, feed_parts)
    back = cross_backward(
        plan,
        info,
        chunks,
        pieces,
        [a, z, segs, vecs, dvec, dsecond, o, cq, co, cross_lse],
    )
    back, feed_landed, out_landed = lax.optimization_barrier((back, feed_landed, out_landed))
    own_memory, *others = back
    mate_memory, (da, terms, cross_keep, cross_send) = (
        others[: plan.group - 1],
        others[plan.group - 1 :],
    )

    feed_keep, feed_send = halves(plan, plane_sum(plan, feed_parts, feed_landed), 1)
    cross_parts = core_sum(plan, cross_keep, core_send(plan, cross_send))
    memory_pieces = add_mates(plan, own_memory, mate_memory)
    feed_landed = seq_send(plan, feed_send, 1)
    cross_landed = plane_send(plan, cross_parts)
    memory_landed = send_home(plan, memory_pieces)
    feed_landed, cross_parts[0], memory_pieces = tie(feed_landed, cross_parts[0], memory_pieces)
    feed_keep, feed_send = halves(plan, add_low([feed_keep, feed_landed]), 2)
    feed_landed = seq_send(plan, feed_send, 2)
    da, feed_keep = tie(da, feed_keep)
    back = self_backward(plan, info, chunks, pieces, [segs, da, terms, q, o, lse])
    back, feed_landed, cross_landed, memory_landed = lax.optimization_barrier(
        (back, feed_landed, cross_landed, memory_landed)
    )
    own_tokens, *mate_tokens, self_keep, self_send = back

    mate_landed = send_mates(plan, mate_tokens)
    self_landed = core_send(plan, self_send)
    feed_quarter = add_low([feed_keep, feed_landed])
    feed_landed = seq_send(plan, feed_quarter, 2)
    cross_keep, cross_send = halves(plan, plane_sum(plan, cross_parts, cross_landed), 1)
    cross_landed = seq_send(plan, cross_send, 1)
    token_pieces = sum_mates(plan, own_tokens, mate_landed)
    token_landed = send_home(plan, token_pieces)
    self_landed, cross_keep, feed_quarter = tie(self_landed, cross_keep, feed_quarter)
    self_parts = core_sum(plan, self_keep, self_landed)
    self_landed = plane_send(plan, self_parts)
    feed_landed, cross_landed = after((feed_landed, cross_landed), self_parts)
    feed_half = join(plan, feed_quarter, feed_landed, 2)
    feed_landed = seq_send(plan, feed_half, 1)
    cross_keep, cross_send = halves(plan, add_low([cross_keep, cross_landed]), 2)
    cross_landed = seq_send(plan, cross_send, 2)
    self_landed, feed_half, cross_keep, token_landed[0] = tie(
        self_landed, feed_half, cross_keep, token_landed[0]
    )
    self_total = plane_sum(plan, self_parts, self_landed)
    self_landed = seq_send(plan, self_total, 1)
    cross_landed, self_total = tie(cross_landed, self_total)
    cross_quarter = add_low([cross_keep, cross_landed])
    cross_landed = seq_send(plan, cross_quarter, 2)
    self_landed, cross_quarter = tie(self_landed, cross_quarter)
    self_total = add_low([self_total, self_landed])
    self_landed = seq_send(plan, self_total, 2)
    cross_landed, self_total, out_landed, memory_landed = tie(
        cross_landed, self_total, out_landed, memory_landed
    )
    cross_half = join(plan, cross_quarter, cross_landed, 2)
    cross_landed = seq_send(plan, cross_half, 1)
    out_tokens = order_home(plan, out_landed, LOW)
    grad_memory = order_home(plan, memory_landed, WIDE)
    grad_tokens = order_home(plan, token_landed, WIDE)
    self_landed, cross_landed, out_tokens, grad_memory, grad_tokens = tie(
        self_landed, cross_landed, out_tokens, grad_memory, grad_tokens
    )
    feed_total = join(plan, feed_half, feed_landed, 1).astype(WIDE)
    cross_total = join(plan, cross_half, cross_landed, 1).astype(WIDE)
    self_total = add_wide(self_total, self_landed)

    scale = 1.0 / (plan.batches * plan.dp)
    feed_grads, cross_grads, self_grads = (
        feed_total * scale,
        cross_total * scale,
        self_total * scale,
    )
    inner_grads = [
        feed_grads[block * shard : (block + 1) * shard] for block in range(plan.hidden_blocks)
    ]
    vector_grads = lax.dynamic_slice(self_grads, (3 * shard, dp * shard), (TILE, shard))
    return (
        out_tokens[:, None],
        grad_tokens[:, None],
        grad_memory[:, None],
        *[self_grads[which * shard : (which + 1) * shard] for which in range(3)],
        cross_grads[4 * shard : 5 * shard],
        *[cross_grads[which * shard : (which + 1) * shard] for which in range(4)],
        jnp.concatenate(inner_grads, axis=1),
        feed_grads[plan.hidden_blocks * shard :],
        *[vector_grads[which] for which in range(6)],
    )


def send_mates(plan, mates):
    return [permute(part, mate(plan, turn)) for turn, part in enumerate(mates, 1)]


def sum_mates(plan, own, landed):
    own = own.astype(WIDE)
    for part in landed:
        own = own + part.astype(WIDE)
    own = own.reshape(plan.batches, plan.chunk, plan.width)
    return [
        lax.dynamic_index_in_dim(own, place, 0, keepdims=False).astype(LOW)
        for place in plan.places
    ]


def add_mates(plan, own, mates):
    return sum_mates(plan, own, send_mates(plan, mates))


def solution(mesh):
    tokens = P(None, "dp", "seq", None)
    ids = P(None, "dp", "seq")
    weight = P("dp", None)
    vector = P("dp")
    return jax.shard_map(
        on_device,
        mesh=mesh,
        in_specs=(tokens, tokens, ids, ids, tokens) + (weight,) * 10 + (vector,) * 6,
        out_specs=(tokens,) * 3 + (weight,) * 10 + (vector,) * 6,
        check_vma=False,
    )
```

```python
import functools

import jax
import jax.numpy as jnp
from jax import lax
from jax.experimental import pallas as pl
from jax.experimental.pallas import tpu as pltpu
from jax.sharding import PartitionSpec as P

DH = 64
PAIR = 2 * DH
BLOCK = 256
TILE = 16
VECTOR_ROWS = 16
FORWARD_COST = 10**6
EPSILON = 1e-05
NEGATIVE = -1e30
FACTOR = DH ** (-0.5)
AXES = ("dp", "seq")
LOW = jnp.bfloat16
WIDE = jnp.float32
MEGABYTE = 1024 * 1024


def dot_nn(a, b):
    return jnp.dot(a, b, preferred_element_type=WIDE)


def dot_nt(a, b):
    return lax.dot_general(a, b, (((1,), (1,)), ((), ())), preferred_element_type=WIDE)


def dot_tn(a, b):
    return lax.dot_general(a, b, (((0,), (0,)), ((), ())), preferred_element_type=WIDE)


def normalise(values):
    centred = values - jnp.mean(values, axis=-1, keepdims=True)
    inverse = lax.rsqrt(jnp.mean(centred * centred, axis=-1, keepdims=True) + EPSILON)
    return centred * inverse, inverse


def norm_backward(upstream, normed, inverse, gain_row):
    scaled = upstream * gain_row
    plain_mean = jnp.mean(scaled, axis=-1, keepdims=True)
    along_mean = jnp.mean(scaled * normed, axis=-1, keepdims=True)
    return inverse * (scaled - plain_mean - normed * along_mean)


def row_blocks(length, size=BLOCK):
    return [pl.ds(start, size) for start in range(0, length, size)]


def copy_all(copies):
    for copy in copies:
        copy.start()
    for copy in copies:
        copy.wait()


def piece_copies(plan, pieces, info_ref, w_ref, semaphores):
    copies = []
    for piece in pieces:
        for slab in range(piece.shape[0]):
            number = len(copies)
            owner = info_ref[plan.order + number]
            copies.append(
                pltpu.make_async_copy(piece.at[slab], w_ref.at[owner], semaphores.at[number])
            )
    return copies


def weight_of(weight_ref, which, rows):
    count, _, width = weight_ref.shape
    return weight_ref[:, which * rows : (which + 1) * rows, :].reshape(count * rows, width)


def seg_columns(seg_row):
    return jnp.transpose(jnp.broadcast_to(seg_row, (128, seg_row.shape[1])))


def stack_heads(pair):
    lane = lax.broadcasted_iota(jnp.int32, pair.shape, 1)
    zero = jnp.zeros_like(pair)
    return jnp.concatenate(
        [jnp.where(lane < DH, pair, zero), jnp.where(lane < DH, zero, pair)], axis=0
    )


def unstack_heads(columns):
    row = lax.broadcasted_iota(jnp.int32, (PAIR, BLOCK), 0)
    return jnp.where(row < DH, columns[:, :BLOCK], columns[:, BLOCK:])


def mask_bias(key_ids, query_ids, key_start, query_start, causal):
    ids = jnp.concatenate([key_ids, key_ids], axis=1)
    allowed = ids == query_ids
    if causal:
        key_place = key_start + lax.broadcasted_iota(jnp.int32, (BLOCK, BLOCK), 0)
        query_place = query_start + lax.broadcasted_iota(jnp.int32, (BLOCK, BLOCK), 1)
        allowed = jnp.logical_and(allowed, key_place <= query_place)
    bias = jnp.where(allowed, 0.0, NEGATIVE)
    return jnp.concatenate([bias, bias], axis=1)


def key_bounds(key_row, query_ids, query_start, causal):
    below = jnp.sum(jnp.where(key_row < jnp.min(query_ids), 1.0, 0.0)).astype(jnp.int32)
    first = lax.div(below, BLOCK)
    if causal:
        return first, lax.div(query_start, BLOCK) + 1
    upto = jnp.sum(jnp.where(key_row <= jnp.max(query_ids), 1.0, 0.0)).astype(jnp.int32)
    return first, lax.div(upto + (BLOCK - 1), BLOCK)


def attend_forward(
    q_ref, k_ref, v_ref, o_ref, lse_ref, key_row, columns_ref, query_row, start, causal, scratch
):
    stack_ref, sum_ref, top_ref, total_ref = scratch
    pairs = q_ref.shape[1] // PAIR
    for number, rows in enumerate(row_blocks(q_ref.shape[0])):
        query_ids = query_row[:, number * BLOCK : (number + 1) * BLOCK]
        query_start = start + number * BLOCK
        low, high = key_bounds(key_row, query_ids, query_start, causal)
        for pair in range(pairs):
            stack_ref[pair] = stack_heads(q_ref[rows, pair * PAIR : (pair + 1) * PAIR])
        sum_ref[...] = jnp.zeros_like(sum_ref)
        top_ref[...] = jnp.full_like(top_ref, NEGATIVE)
        total_ref[...] = jnp.zeros_like(total_ref)

        def one_block(block, carry):
            key_start = pl.multiple_of(block * BLOCK, BLOCK)
            keys = pl.ds(key_start, BLOCK)
            bias = mask_bias(columns_ref[keys, :], query_ids, key_start, query_start, causal)
            values = [
                (
                    k_ref[keys, pair * PAIR : (pair + 1) * PAIR],
                    v_ref[keys, pair * PAIR : (pair + 1) * PAIR],
                    stack_ref[pair],
                    top_ref[pair : pair + 1, :],
                    total_ref[pair : pair + 1, :],
                    sum_ref[pair],
                )
                for pair in range(pairs)
            ]
            scores = [dot_nt(key_pair, queries) + bias for key_pair, _, queries, *_ in values]
            tops = [
                jnp.maximum(value[3], jnp.max(score, axis=0, keepdims=True))
                for value, score in zip(values, scores)
            ]
            exponents = [jnp.exp(score - top) for score, top in zip(scores, tops)]
            shrinks = [jnp.exp(value[3] - top) for value, top in zip(values, tops)]
            totals = [
                value[4] * shrink + jnp.sum(exponent, axis=0, keepdims=True)
                for value, shrink, exponent in zip(values, shrinks, exponents)
            ]
            sums = [
                value[5] * shrink + dot_tn(value[1], exponent.astype(LOW))
                for value, shrink, exponent in zip(values, shrinks, exponents)
            ]
            for pair in range(pairs):
                top_ref[pair : pair + 1, :] = tops[pair]
                total_ref[pair : pair + 1, :] = totals[pair]
                sum_ref[pair] = sums[pair]
            return carry

        lax.fori_loop(low, high, one_block, 0)
        for pair in range(pairs):
            total = total_ref[pair : pair + 1, :]
            context = unstack_heads(sum_ref[pair] / total)
            o_ref[rows, pair * PAIR : (pair + 1) * PAIR] = jnp.transpose(context).astype(LOW)
            place = number * pairs + pair
            lse_ref[place : place + 1, :] = top_ref[pair : pair + 1, :] + jnp.log(total)


def attend_backward(
    q_ref,
    k_ref,
    v_ref,
    o_ref,
    grad_ref,
    lse_ref,
    dq_ref,
    dk_ref,
    dv_ref,
    key_row,
    columns_ref,
    query_row,
    start,
    causal,
    scratch,
):
    stack_ref, stack_grad_ref, sum_ref, along_ref = scratch
    pairs = q_ref.shape[1] // PAIR
    dk_ref[...] = jnp.zeros_like(dk_ref)
    dv_ref[...] = jnp.zeros_like(dv_ref)
    for number, rows in enumerate(row_blocks(q_ref.shape[0])):
        query_ids = query_row[:, number * BLOCK : (number + 1) * BLOCK]
        query_start = start + number * BLOCK
        low, high = key_bounds(key_row, query_ids, query_start, causal)
        for pair in range(pairs):
            lanes = slice(pair * PAIR, (pair + 1) * PAIR)
            grad = grad_ref[rows, lanes]
            stack_ref[pair] = stack_heads(q_ref[rows, lanes])
            stack_grad_ref[pair] = stack_heads(grad)
            along = jnp.transpose(grad.astype(WIDE) * o_ref[rows, lanes].astype(WIDE))
            along_ref[pair : pair + 1, :] = jnp.concatenate(
                [
                    jnp.sum(along[:DH], axis=0, keepdims=True),
                    jnp.sum(along[DH:], axis=0, keepdims=True),
                ],
                axis=1,
            )
        sum_ref[...] = jnp.zeros_like(sum_ref)

        def one_block(block, carry):
            key_start = pl.multiple_of(block * BLOCK, BLOCK)
            keys = pl.ds(key_start, BLOCK)
            bias = mask_bias(columns_ref[keys, :], query_ids, key_start, query_start, causal)
            for pair in range(pairs):
                lanes = slice(pair * PAIR, (pair + 1) * PAIR)
                place = number * pairs + pair
                key_pair = k_ref[keys, lanes]
                scores = dot_nt(key_pair, stack_ref[pair]) + bias
                probs = jnp.exp(scores - lse_ref[place : place + 1, :])
                prob_grad = dot_nt(v_ref[keys, lanes], stack_grad_ref[pair])
                score_grad = (probs * (prob_grad - along_ref[pair : pair + 1, :])).astype(LOW)
                dv_ref[keys, lanes] += dot_nn(probs.astype(LOW), stack_grad_ref[pair])
                dk_ref[keys, lanes] += dot_nn(score_grad, stack_ref[pair])
                sum_ref[pair] += dot_tn(key_pair, score_grad)
            return carry

        lax.fori_loop(low, high, one_block, 0)
        for pair in range(pairs):
            grad = jnp.transpose(unstack_heads(sum_ref[pair])) * FACTOR
            dq_ref[rows, pair * PAIR : (pair + 1) * PAIR] = grad.astype(LOW)


def store_pieces(grad_ref, keep_ref, send_ref, info_ref, order, offset, count, rows):
    half = count // 2
    for number in range(count):
        owner = info_ref[order + number]
        block = grad_ref[pl.ds(pl.multiple_of(owner * rows, rows), rows), :]
        target = keep_ref if number < half else send_ref
        target[number % half, offset : offset + rows, :] = block


class Plan:
    def __init__(self, tokens, inner_weight):
        self.dp = lax.axis_size("dp")
        self.seq = lax.axis_size("seq")
        self.batches, _, self.chunk, self.width = tokens.shape
        self.hidden = inner_weight.shape[1]
        self.length = self.chunk * self.seq
        self.group = self.seq // self.batches
        self.rows = self.batches * self.chunk
        self.chunks = self.seq
        self.shard = self.width // self.dp
        self.outer_shard = self.hidden // self.dp
        self.hidden_blocks = self.hidden // self.width
        self.pairs = self.width // PAIR
        self.query_blocks = self.rows // BLOCK
        self.order = 0
        self.grad_order = self.dp
        self.chunk_order = 2 * self.dp
        self.own = self.chunk_order + self.chunks
        self.round = self.own + 1
        self.mates = self.round + self.batches
        self.batch = self.mates + self.group
        self.own_dp = self.batch + self.batches


def megabytes(plan, fixed, by_length):
    return fixed + -(-by_length * plan.length // 1024)


def seg_rows(plan, raw_ref, seg_ref):
    for number in range(plan.chunks):
        lanes = slice(number * plan.chunk, (number + 1) * plan.chunk)
        seg_ref[0:1, lanes] = raw_ref[number, 0:1, : plan.chunk].astype(WIDE)
        seg_ref[1:2, lanes] = raw_ref[number, 0:1, plan.chunk : 2 * plan.chunk].astype(WIDE)


def own_rows(plan, info_ref):
    return pl.multiple_of(info_ref[plan.own] * plan.rows, plan.rows)


def chunk_copies(plan, chunks, info_ref, first, x_ref, raw_ref, semaphores):
    copies = []
    for number, chunk in enumerate(chunks):
        index = info_ref[plan.chunk_order + number]
        rows = pl.ds(pl.multiple_of(index * plan.chunk, plan.chunk), plan.chunk)
        copies.append(
            pltpu.make_async_copy(
                chunk.at[pl.ds(first, plan.chunk)], x_ref.at[rows], semaphores.at[0, number]
            )
        )
        if raw_ref is not None:
            copies.append(
                pltpu.make_async_copy(
                    chunk.at[pl.ds(2 * plan.chunk, TILE)],
                    raw_ref.at[index],
                    semaphores.at[1, number],
                )
            )
    return copies


def project_rows(length, source_ref, key_weight, value_weight, k_ref, v_ref):
    for rows in row_blocks(length, 2 * BLOCK):
        k_ref[rows, :] = dot_nn(source_ref[rows, :], key_weight).astype(LOW)
        v_ref[rows, :] = dot_nn(source_ref[rows, :], value_weight).astype(LOW)


def forward_kernel(plan, chunk_count, piece_count, info_ref, *refs):
    chunks, refs = refs[:chunk_count], refs[chunk_count:]
    pieces, refs = refs[:piece_count], refs[piece_count:]
    (q_ref, o_ref, lse_ref, a_ref, seg_ref, vec_ref), refs = refs[:6], refs[6:]
    (cq_ref, co_ref, cross_lse_ref, z_ref, k_ref, v_ref), refs = refs[:6], refs[6:]
    x_ref, m_ref, raw_ref, w_ref, columns_ref, chunk_sems, m_sems, piece_sems, *scratch = refs
    load = chunk_copies(plan, chunks, info_ref, 0, x_ref, raw_ref, chunk_sems)
    load += chunk_copies(plan, chunks, info_ref, plan.chunk, m_ref, None, m_sems)
    load += piece_copies(plan, pieces, info_ref, w_ref, piece_sems)
    copy_all(load)
    shard = plan.shard
    start = own_rows(plan, info_ref)
    vec_ref[...] = jnp.sum(w_ref[:, 8 * shard :, :].astype(WIDE), axis=0)
    seg_rows(plan, raw_ref, seg_ref)
    columns_ref[...] = seg_columns(seg_ref[0:1, :])
    for rows in row_blocks(plan.rows):
        own = x_ref[pl.ds(start + rows.start, BLOCK), :]
        q_ref[rows, :] = (dot_nn(own, weight_of(w_ref, 0, shard)) * FACTOR).astype(LOW)
    project_rows(
        plan.length,
        x_ref,
        weight_of(w_ref, 1, shard),
        weight_of(w_ref, 2, shard),
        k_ref,
        v_ref,
    )
    attend_forward(
        q_ref,
        k_ref,
        v_ref,
        o_ref,
        lse_ref,
        seg_ref[0:1, :],
        columns_ref,
        seg_ref[0:1, pl.ds(start, plan.rows)],
        start,
        True,
        scratch,
    )
    gain, shift = vec_ref[0:1, :], vec_ref[1:2, :]
    for rows in row_blocks(plan.rows):
        own = x_ref[pl.ds(start + rows.start, BLOCK), :].astype(WIDE)
        a = own + dot_nn(o_ref[rows, :], weight_of(w_ref, 3, shard))
        a_ref[rows, :] = a
        normed, _ = normalise(a)
        first = normed * gain + shift
        z_ref[rows, :] = first
        cq_ref[rows, :] = (
            dot_nn(first.astype(LOW), weight_of(w_ref, 4, shard)) * FACTOR
        ).astype(LOW)
    project_rows(
        plan.length,
        m_ref,
        weight_of(w_ref, 5, shard),
        weight_of(w_ref, 6, shard),
        k_ref,
        v_ref,
    )
    columns_ref[...] = seg_columns(seg_ref[1:2, :])
    attend_forward(
        cq_ref,
        k_ref,
        v_ref,
        co_ref,
        cross_lse_ref,
        seg_ref[1:2, :],
        columns_ref,
        seg_ref[0:1, pl.ds(start, plan.rows)],
        start,
        False,
        scratch,
    )
    for rows in row_blocks(plan.rows):
        z_ref[rows, :] += dot_nn(co_ref[rows, :], weight_of(w_ref, 7, shard))


def feed_kernel(plan, piece_count, info_ref, *refs):
    batches = plan.batches
    upstreams, refs = refs[:batches], refs[batches:]
    pieces, refs = refs[:piece_count], refs[piece_count:]
    (z_ref, vec_ref), refs = refs[:2], refs[2:]
    outs, refs = refs[:batches], refs[batches:]
    (dh_ref, dvec_ref, keep_ref, send_ref), refs = refs[:4], refs[4:]
    inner_ref, outer_ref, low_ref, u_ref, r_ref, du_ref, f_ref, up_ref, res_ref, *refs = refs
    inner_gw_ref, outer_gw_ref, piece_sems, up_sems = refs
    width, shard, blocks, outer_shard = (
        plan.width,
        plan.shard,
        plan.hidden_blocks,
        plan.outer_shard,
    )
    copies = []
    number = 0
    for piece in pieces:
        for slab in range(piece.shape[0]):
            owner = info_ref[plan.order + number]
            for block in range(blocks):
                copies.append(
                    pltpu.make_async_copy(
                        piece.at[slab, pl.ds(block * shard, shard)],
                        inner_ref.at[
                            pl.ds(pl.multiple_of(owner * shard, shard), shard),
                            pl.ds(block * width, width),
                        ],
                        piece_sems.at[block, number],
                    )
                )
            copies.append(
                pltpu.make_async_copy(
                    piece.at[slab, pl.ds(blocks * shard, outer_shard)],
                    outer_ref.at[pl.ds(pl.multiple_of(owner * outer_shard, outer_shard), outer_shard)],
                    piece_sems.at[blocks, number],
                )
            )
            number += 1
    for number in range(batches):
        index = info_ref[plan.round + number]
        rows = pl.ds(pl.multiple_of(index * plan.chunk, plan.chunk), plan.chunk)
        copies.append(
            pltpu.make_async_copy(upstreams[number], up_ref.at[rows], up_sems.at[number])
        )
    for copy in copies:
        copy.start()
    gain_two, shift_two = vec_ref[2:3, :], vec_ref[3:4, :]
    gain_three, shift_three = vec_ref[4:5, :], vec_ref[5:6, :]
    gain_grad = jnp.zeros((1, width), WIDE)
    shift_grad = jnp.zeros((1, width), WIDE)
    for rows in row_blocks(plan.rows):
        normed, _ = normalise(z_ref[rows, :])
        second = normed * gain_two + shift_two
        f_ref[rows, :] = second
        low_ref[rows, :] = second.astype(LOW)
    for copy in copies:
        copy.wait()
    lanes = [slice(block * width, (block + 1) * width) for block in range(blocks)]
    for part in lanes:
        u = dot_nn(low_ref[...], inner_ref[:, part])
        phi = 0.5 + 0.5 * lax.erf(u * (0.5**0.5))
        r_ref[:, part] = (u * phi).astype(LOW)
        u_ref[:, part] = phi + u * (jnp.exp(-0.5 * u * u) * 0.3989422804014327)
    for rows in row_blocks(plan.rows):
        f = f_ref[rows, :] + dot_nn(r_ref[rows, :], outer_ref[...])
        normed, inverse = normalise(f)
        res_ref[rows, :] = (normed * gain_three + shift_three).astype(LOW)
        upstream = up_ref[rows, :].astype(WIDE)
        gain_grad += jnp.sum(upstream * normed, axis=0, keepdims=True)
        shift_grad += jnp.sum(upstream, axis=0, keepdims=True)
        feed_grad = norm_backward(upstream, normed, inverse, gain_three)
        dh_ref[rows, :] = feed_grad
        up_ref[rows, :] = feed_grad.astype(LOW)
    for number in range(batches):
        index = info_ref[plan.round + number]
        outs[number][...] = res_ref[pl.ds(pl.multiple_of(index * plan.chunk, plan.chunk), plan.chunk), :]
    for part in lanes:
        dr = dot_nt(up_ref[...], outer_ref[part, :]).astype(LOW).astype(WIDE)
        du_ref[:, part] = (dr * u_ref[:, part]).astype(LOW)
        outer_gw_ref[part, :] = dot_tn(r_ref[:, part], up_ref[...]).astype(LOW)
    for block, part in enumerate(lanes):
        inner_gw_ref[block] = dot_tn(low_ref[...], du_ref[:, part]).astype(LOW)
    for rows in row_blocks(plan.rows):
        dh_ref[rows, :] += dot_nt(du_ref[rows, :], inner_ref[...])
    for block in range(blocks):
        store_pieces(
            inner_gw_ref.at[block],
            keep_ref,
            send_ref,
            info_ref,
            plan.grad_order,
            block * shard,
            plan.dp,
            shard,
        )
    store_pieces(
        outer_gw_ref,
        keep_ref,
        send_ref,
        info_ref,
        plan.grad_order,
        blocks * shard,
        plan.dp,
        outer_shard,
    )
    dvec_ref[...] = jnp.zeros_like(dvec_ref)
    dvec_ref[4:5, :] = gain_grad
    dvec_ref[5:6, :] = shift_grad


def norm_back(plan, line, z_ref, upstream_ref, vec_ref, grad_ref, low_ref):
    gain_grad = jnp.zeros((1, plan.width), WIDE)
    shift_grad = jnp.zeros((1, plan.width), WIDE)
    for rows in row_blocks(plan.rows):
        normed, inverse = normalise(z_ref[rows, :])
        upstream = upstream_ref[rows, :]
        gain_grad += jnp.sum(upstream * normed, axis=0, keepdims=True)
        shift_grad += jnp.sum(upstream, axis=0, keepdims=True)
        grad = norm_backward(upstream, normed, inverse, vec_ref[2 * line : 2 * line + 1, :])
        if grad_ref is not None:
            grad_ref[rows, :] = grad
        low_ref[rows, :] = grad.astype(LOW)
    return gain_grad, shift_grad


def attention_back(plan, causal, info_ref, seg_ref, operands, results, buffers):
    q_ref, k_ref, v_ref, o_ref, do_ref, lse_ref = operands
    dq_ref, dkl_ref, dvl_ref = results
    columns_ref, dk_ref, dv_ref, *scratch = buffers
    start = own_rows(plan, info_ref)
    line = 0 if causal else 1
    columns_ref[...] = seg_columns(seg_ref[line : line + 1, :])
    attend_backward(
        q_ref,
        k_ref,
        v_ref,
        o_ref,
        do_ref,
        lse_ref,
        dq_ref,
        dk_ref,
        dv_ref,
        seg_ref[line : line + 1, :],
        columns_ref,
        seg_ref[0:1, pl.ds(start, plan.rows)],
        start,
        causal,
        scratch,
    )

    def round_block(block, carry):
        rows = pl.ds(pl.multiple_of(block * BLOCK, BLOCK), BLOCK)
        dkl_ref[rows, :] = dk_ref[rows, :].astype(LOW)
        dvl_ref[rows, :] = dv_ref[rows, :].astype(LOW)
        return carry

    lax.fori_loop(0, plan.length // BLOCK, round_block, 0)


def source_parts(plan, info_ref, dkl_ref, dvl_ref, w_ref, which, own_ref, base_ref, mates):
    shard = plan.shard
    for number in range(plan.group):
        first = pl.multiple_of(info_ref[plan.mates + number] * plan.rows, plan.rows)
        for rows in row_blocks(plan.rows):
            source = pl.ds(first + rows.start, BLOCK)
            part = dot_nt(dkl_ref[source, :], weight_of(w_ref, which, shard)) + dot_nt(
                dvl_ref[source, :], weight_of(w_ref, which + 1, shard)
            )
            if number == 0 and base_ref is not None:
                part = part + base_ref[rows, :]
            target = mates[number - 1] if number else own_ref
            target[rows, :] = part.astype(LOW)


def weight_products(plan, info_ref, products, gw_ref, keep_ref, send_ref):
    for which, (left, right) in enumerate(products):
        gw_ref[which] = dot_tn(left[...], right[...]).astype(LOW)
    for which in range(len(products)):
        store_pieces(
            gw_ref.at[which],
            keep_ref,
            send_ref,
            info_ref,
            plan.grad_order,
            which * plan.shard,
            plan.dp,
            plan.shard,
        )


def cross_backward_kernel(plan, chunk_count, piece_count, info_ref, *refs):
    chunks, refs = refs[:chunk_count], refs[chunk_count:]
    pieces, refs = refs[:piece_count], refs[piece_count:]
    (a_ref, z_ref, seg_ref, vec_ref, dvec_ref, dsecond_ref, context_ref), refs = refs[:7], refs[7:]
    (q_ref, o_ref, lse_ref), refs = refs[:3], refs[3:]
    own_ref, refs = refs[0], refs[1:]
    mates, refs = refs[: plan.group - 1], refs[plan.group - 1 :]
    (self_low_ref, terms_ref, keep_ref, send_ref), refs = refs[:4], refs[4:]
    m_ref, w_ref, h_ref, gw_ref, grad_ref, low_ref, *refs = refs
    k_ref, v_ref, do_ref, dq_ref, dkl_ref, dvl_ref, chunk_sems, piece_sems, *buffers = refs
    shard = plan.shard
    copies = chunk_copies(plan, chunks, info_ref, plan.chunk, m_ref, None, chunk_sems)
    copies += piece_copies(
        plan,
        [piece.at[:, pl.ds(3 * shard, 5 * shard)] for piece in pieces],
        info_ref,
        w_ref,
        piece_sems,
    )
    copy_all(copies)
    project_rows(
        plan.length, m_ref, weight_of(w_ref, 2, shard), weight_of(w_ref, 3, shard), k_ref, v_ref
    )
    cross_terms = norm_back(plan, 1, z_ref, dsecond_ref, vec_ref, grad_ref, low_ref)
    for rows in row_blocks(plan.rows):
        do_ref[rows, :] = dot_nt(low_ref[rows, :], weight_of(w_ref, 4, shard)).astype(LOW)
    attention_back(
        plan,
        False,
        info_ref,
        seg_ref,
        (q_ref, k_ref, v_ref, o_ref, do_ref, lse_ref),
        (dq_ref, dkl_ref, dvl_ref),
        buffers,
    )
    for rows in row_blocks(plan.rows):
        grad_ref[rows, :] += dot_nt(dq_ref[rows, :], weight_of(w_ref, 1, shard))
        normed, _ = normalise(a_ref[rows, :])
        h_ref[rows, :] = (normed * vec_ref[0:1, :] + vec_ref[1:2, :]).astype(LOW)
    self_terms = norm_back(plan, 0, a_ref, grad_ref, vec_ref, None, self_low_ref)
    source_parts(plan, info_ref, dkl_ref, dvl_ref, w_ref, 2, own_ref, None, mates)
    products = (
        (h_ref, dq_ref),
        (m_ref, dkl_ref),
        (m_ref, dvl_ref),
        (o_ref, low_ref),
        (context_ref, self_low_ref),
    )
    weight_products(plan, info_ref, products, gw_ref, keep_ref, send_ref)
    terms_ref[...] = dvec_ref[...]
    for place, term in enumerate([*self_terms, *cross_terms]):
        terms_ref[place : place + 1, :] = term


def self_backward_kernel(plan, chunk_count, piece_count, info_ref, *refs):
    chunks, refs = refs[:chunk_count], refs[chunk_count:]
    pieces, refs = refs[:piece_count], refs[piece_count:]
    (seg_ref, da_ref, terms_ref, q_ref, o_ref, lse_ref), refs = refs[:6], refs[6:]
    own_ref, refs = refs[0], refs[1:]
    mates, refs = refs[: plan.group - 1], refs[plan.group - 1 :]
    keep_ref, send_ref, x_ref, own_x_ref, gw_ref, w_ref, *refs = refs
    do_ref, k_ref, v_ref, base_ref, dq_ref, dkl_ref, dvl_ref, chunk_sems, piece_sems, *buffers = refs
    copies = piece_copies(
        plan,
        [piece.at[:, pl.ds(0, 4 * plan.shard)] for piece in pieces],
        info_ref,
        w_ref,
        piece_sems,
    )
    copies += chunk_copies(plan, chunks, info_ref, 0, x_ref, None, chunk_sems)
    copy_all(copies)
    project_rows(
        plan.length,
        x_ref,
        weight_of(w_ref, 1, plan.shard),
        weight_of(w_ref, 2, plan.shard),
        k_ref,
        v_ref,
    )
    for rows in row_blocks(plan.rows):
        do_ref[rows, :] = dot_nt(da_ref[rows, :], weight_of(w_ref, 3, plan.shard)).astype(LOW)
    attention_back(
        plan,
        True,
        info_ref,
        seg_ref,
        (q_ref, k_ref, v_ref, o_ref, do_ref, lse_ref),
        (dq_ref, dkl_ref, dvl_ref),
        buffers,
    )
    for rows in row_blocks(plan.rows):
        base_ref[rows, :] = da_ref[rows, :].astype(WIDE) + dot_nt(
            dq_ref[rows, :], weight_of(w_ref, 0, plan.shard)
        )
    source_parts(plan, info_ref, dkl_ref, dvl_ref, w_ref, 1, own_ref, base_ref, mates)
    start = own_rows(plan, info_ref)
    for rows in row_blocks(plan.rows):
        own_x_ref[rows, :] = x_ref[pl.ds(start + rows.start, BLOCK), :]
    products = ((own_x_ref, dq_ref), (x_ref, dkl_ref), (x_ref, dvl_ref))
    weight_products(plan, info_ref, products, gw_ref, keep_ref, send_ref)
    tail = jnp.concatenate(
        [terms_ref[...], jnp.zeros((VECTOR_ROWS - 8, plan.width), WIDE)], axis=0
    ).astype(LOW)
    for number in range(plan.dp // 2):
        keep_ref[number, 3 * plan.shard :, :] = tail
        send_ref[number, 3 * plan.shard :, :] = tail


SMEM = pl.BlockSpec(memory_space=pltpu.SMEM)
VMEM = pl.BlockSpec(memory_space=pltpu.VMEM)
ANY = pl.BlockSpec(memory_space=pl.ANY)
HBM = pl.BlockSpec(memory_space=pltpu.HBM)


def call(kernel, specs, operands, outs, scratch, flops, moved, megabytes, out_specs=None):
    return pl.pallas_call(
        kernel,
        in_specs=specs,
        out_specs=out_specs or [VMEM] * len(outs),
        out_shape=outs,
        scratch_shapes=scratch,
        compiler_params=pltpu.CompilerParams(vmem_limit_bytes=megabytes * MEGABYTE),
        cost_estimate=pl.CostEstimate(flops=flops, bytes_accessed=moved, transcendentals=0),
    )(*operands)


def shape(dims, dtype):
    return jax.ShapeDtypeStruct(dims, dtype)


def forward_scratch(plan):
    return [
        pltpu.VMEM((plan.pairs, 2 * BLOCK, PAIR), LOW),
        pltpu.VMEM((plan.pairs, PAIR, 2 * BLOCK), WIDE),
        pltpu.VMEM((8, 2 * BLOCK), WIDE),
        pltpu.VMEM((8, 2 * BLOCK), WIDE),
    ]


def backward_scratch(plan):
    return [
        pltpu.VMEM((plan.pairs, 2 * BLOCK, PAIR), LOW),
        pltpu.VMEM((plan.pairs, 2 * BLOCK, PAIR), LOW),
        pltpu.VMEM((plan.pairs, PAIR, 2 * BLOCK), WIDE),
        pltpu.VMEM((8, 2 * BLOCK), WIDE),
    ]


def flat(pieces):
    return sum(piece.shape[0] for piece in pieces)


def hold_kernel(info_ref, held_ref):
    for place in range(info_ref.shape[0]):
        held_ref[place] = info_ref[place]


def hold(info):
    return call(
        hold_kernel, [SMEM], [info], [shape(info.shape, jnp.int32)], [], 40 * 10**9, 10**5, 1, [SMEM]
    )[0]


def forward(plan, info, chunks, pieces):
    rows, length, width = plan.rows, plan.length, plan.width
    heads = [
        shape((rows, width), LOW),
        shape((rows, width), LOW),
        shape((plan.query_blocks * plan.pairs, 2 * BLOCK), WIDE),
        shape((rows, width), WIDE),
    ]
    outs = heads + [shape((8, length), WIDE), shape((TILE, width), WIDE)] + heads
    scratch = [
        pltpu.VMEM((length, width), LOW),
        pltpu.VMEM((length, width), LOW),
        pltpu.VMEM((length, width), LOW),
        pltpu.VMEM((length, width), LOW),
        pltpu.VMEM((plan.chunks, TILE, width), LOW),
        pltpu.VMEM((plan.dp, 8 * plan.shard + TILE, width), LOW),
        pltpu.VMEM((length, 128), WIDE),
        pltpu.SemaphoreType.DMA((2, plan.chunks)),
        pltpu.SemaphoreType.DMA((2, plan.chunks)),
        pltpu.SemaphoreType.DMA((plan.dp,)),
    ] + forward_scratch(plan)
    return call(
        functools.partial(forward_kernel, plan, len(chunks), len(pieces)),
        [SMEM] + [ANY] * (len(chunks) + len(pieces)),
        [info, *chunks, *pieces],
        outs,
        scratch,
        FORWARD_COST,
        10**5,
        megabytes(plan, 18, 10),
    )


def feed(plan, info, upstreams, pieces, z, vecs):
    rows, width, blocks = plan.rows, plan.width, plan.hidden_blocks
    piece_rows = blocks * plan.shard + plan.outer_shard
    outs = (
        [shape((plan.chunk, width), LOW)] * plan.batches
        + [shape((rows, width), WIDE), shape((8, width), WIDE)]
        + [shape((plan.dp // 2, piece_rows, width), LOW)] * 2
    )
    scratch = [
        pltpu.VMEM((width, plan.hidden), LOW),
        pltpu.VMEM((plan.hidden, width), LOW),
        pltpu.VMEM((rows, width), LOW),
        pltpu.VMEM((rows, plan.hidden), WIDE),
        pltpu.VMEM((rows, plan.hidden), LOW),
        pltpu.VMEM((rows, plan.hidden), LOW),
        pltpu.VMEM((rows, width), WIDE),
        pltpu.VMEM((rows, width), LOW),
        pltpu.VMEM((rows, width), LOW),
        pltpu.VMEM((blocks, width, width), LOW),
        pltpu.VMEM((plan.hidden, width), LOW),
        pltpu.SemaphoreType.DMA((blocks + 1, plan.dp)),
        pltpu.SemaphoreType.DMA((plan.batches,)),
    ]
    return call(
        functools.partial(feed_kernel, plan, len(pieces)),
        [SMEM] + [ANY] * (plan.batches + len(pieces)) + [VMEM] * 2,
        [info, *upstreams, *pieces, z, vecs],
        outs,
        scratch,
        20 * 10**9,
        12 * 10**6,
        28,
    )


def backward_buffers(plan):
    length, width = plan.length, plan.width
    return [
        pltpu.VMEM((length, 128), WIDE),
        pltpu.VMEM((length, width), WIDE),
        pltpu.VMEM((length, width), WIDE),
        pltpu.VMEM((plan.pairs, 2 * BLOCK, PAIR), LOW),
        pltpu.VMEM((plan.pairs, 2 * BLOCK, PAIR), LOW),
        pltpu.VMEM((plan.pairs, PAIR, 2 * BLOCK), WIDE),
        pltpu.VMEM((8, 2 * BLOCK), WIDE),
    ]


def cross_backward(plan, info, chunks, pieces, operands):
    rows, length, width = plan.rows, plan.length, plan.width
    outs = (
        [shape((rows, width), LOW)]
        + [shape((rows, width), LOW)] * (plan.group - 1)
        + [shape((rows, width), LOW), shape((8, width), WIDE)]
        + [shape((plan.dp // 2, 5 * plan.shard, width), LOW)] * 2
    )
    scratch = [
        pltpu.VMEM((length, width), LOW),
        pltpu.VMEM((plan.dp, 5 * plan.shard, width), LOW),
        pltpu.VMEM((rows, width), LOW),
        pltpu.VMEM((5, width, width), LOW),
        pltpu.VMEM((rows, width), WIDE),
        pltpu.VMEM((rows, width), LOW),
        pltpu.VMEM((length, width), LOW),
        pltpu.VMEM((length, width), LOW),
        pltpu.VMEM((rows, width), LOW),
        pltpu.VMEM((rows, width), LOW),
        pltpu.VMEM((length, width), LOW),
        pltpu.VMEM((length, width), LOW),
        pltpu.SemaphoreType.DMA((2, plan.chunks)),
        pltpu.SemaphoreType.DMA((plan.dp,)),
    ] + backward_buffers(plan)
    return call(
        functools.partial(cross_backward_kernel, plan, len(chunks), len(pieces)),
        [SMEM] + [ANY] * (len(chunks) + len(pieces)) + [VMEM] * len(operands),
        [info, *chunks, *pieces, *operands],
        outs,
        scratch,
        22 * 10**9,
        12 * 10**6,
        megabytes(plan, 18, 16),
    )


def self_backward(plan, info, chunks, pieces, operands):
    rows, length, width = plan.rows, plan.length, plan.width
    outs = (
        [shape((rows, width), LOW)]
        + [shape((rows, width), LOW)] * (plan.group - 1)
        + [shape((plan.dp // 2, 3 * plan.shard + VECTOR_ROWS, width), LOW)] * 2
    )
    scratch = [
        pltpu.VMEM((length, width), LOW),
        pltpu.VMEM((rows, width), LOW),
        pltpu.VMEM((3, width, width), LOW),
        pltpu.VMEM((plan.dp, 4 * plan.shard, width), LOW),
        pltpu.VMEM((rows, width), LOW),
        pltpu.VMEM((length, width), LOW),
        pltpu.VMEM((length, width), LOW),
        pltpu.VMEM((rows, width), WIDE),
        pltpu.VMEM((rows, width), LOW),
        pltpu.VMEM((length, width), LOW),
        pltpu.VMEM((length, width), LOW),
        pltpu.SemaphoreType.DMA((2, plan.chunks)),
        pltpu.SemaphoreType.DMA((plan.dp,)),
    ] + backward_buffers(plan)
    return call(
        functools.partial(self_backward_kernel, plan, len(chunks), len(pieces)),
        [SMEM] + [ANY] * (len(chunks) + len(pieces)) + [VMEM] * len(operands),
        [info, *chunks, *pieces, *operands],
        outs,
        scratch,
        18 * 10**9,
        12 * 10**6,
        megabytes(plan, 12, 12),
    )


def pack_tokens_kernel(plan, tokens, memory, target, source, *refs):
    rounds, semaphores = refs[: plan.batches], refs[-1]
    chunk, width = plan.chunk, plan.width
    moves = []
    for number in range(plan.batches):
        batch = lax.rem(lax.axis_index("seq") + number, plan.batches)
        moves.append((tokens.at[batch, 0], rounds[number].at[pl.ds(0, chunk)]))
        moves.append((memory.at[batch, 0], rounds[number].at[pl.ds(chunk, chunk)]))
    copies = [
        pltpu.make_async_copy(here, there, semaphores.at[number])
        for number, (here, there) in enumerate(moves)
    ]
    for copy in copies:
        copy.start()
    first_row = lax.broadcasted_iota(jnp.int32, (TILE, width), 0) == 0
    for number in range(plan.batches):
        batch = lax.rem(lax.axis_index("seq") + number, plan.batches)
        row = jnp.concatenate([target[batch], source[batch]], axis=1).astype(WIDE)
        if width > 2 * chunk:
            row = jnp.concatenate([row, jnp.zeros((1, width - 2 * chunk), WIDE)], axis=1)
        rounds[number][2 * chunk :, :] = jnp.where(first_row, row, 0.0).astype(LOW)
    for copy in copies:
        copy.wait()


def pack_tokens(plan, tokens, memory, target, source):
    return call(
        functools.partial(pack_tokens_kernel, plan),
        [HBM] * 2 + [VMEM] * 2,
        [tokens, memory, target, source],
        [shape((2 * plan.chunk + TILE, plan.width), LOW)] * plan.batches,
        [pltpu.SemaphoreType.DMA((2 * plan.batches,))],
        0,
        10**6,
        60,
    )


def pack_weights_kernel(plan, *refs):
    weights, (vectors, piece_ref, lines_ref, semaphores) = refs[:8], refs[8:]
    shard = plan.shard
    copies = [
        pltpu.make_async_copy(
            weight, piece_ref.at[0, pl.ds(which * shard, shard)], semaphores.at[which]
        )
        for which, weight in enumerate(weights)
    ]
    for copy in copies:
        copy.start()
    lines_ref[...] = jnp.zeros_like(lines_ref)
    lines_ref[0:6, 0:shard] = vectors[...].astype(WIDE)
    lanes = pltpu.roll(lines_ref[...], lax.axis_index("dp") * shard, 1)
    piece_ref[0, 8 * shard :, :] = lanes.astype(LOW)
    for copy in copies:
        copy.wait()


def pack_weights(plan, weights, vectors):
    return call(
        functools.partial(pack_weights_kernel, plan),
        [HBM] * 8 + [VMEM],
        [*weights, vectors],
        [shape((1, 8 * plan.shard + TILE, plan.width), LOW)],
        [pltpu.VMEM((TILE, plan.width), WIDE), pltpu.SemaphoreType.DMA((8,))],
        20 * 10**9,
        10**6,
        60,
    )[0]


def pack_rest_kernel(plan, info_ref, inner, outer, cotangent, feed_ref, *refs):
    rounds, semaphores = refs[: plan.batches], refs[-1]
    shard, width, blocks = plan.shard, plan.width, plan.hidden_blocks
    moves = [
        (
            inner.at[:, pl.ds(block * width, width)],
            feed_ref.at[0, pl.ds(block * shard, shard)],
        )
        for block in range(blocks)
    ]
    moves.append((outer, feed_ref.at[0, pl.ds(blocks * shard, plan.outer_shard)]))
    for number in range(plan.batches):
        moves.append((cotangent.at[info_ref[plan.batch + number], 0], rounds[number]))
    copy_all(
        [
            pltpu.make_async_copy(here, there, semaphores.at[number])
            for number, (here, there) in enumerate(moves)
        ]
    )


def pack_rest(plan, info, inner, outer, cotangent):
    outs = [shape((1, plan.hidden_blocks * plan.shard + plan.outer_shard, plan.width), LOW)]
    outs += [shape((plan.chunk, plan.width), LOW)] * plan.batches
    return call(
        functools.partial(pack_rest_kernel, plan),
        [SMEM] + [HBM] * 3,
        [info, inner, outer, cotangent],
        outs,
        [pltpu.SemaphoreType.DMA((plan.hidden_blocks + 1 + plan.batches,))],
        0,
        2 * 10**6,
        60,
    )


def pairs_of(plan, move):
    return [
        (dp * plan.seq + seq, to[0] * plan.seq + to[1])
        for dp in range(plan.dp)
        for seq in range(plan.seq)
        for to in [move(dp, seq)]
    ]


def home(plan, dp, batch, seq):
    position = (2 * batch + dp % 2) * plan.group + seq // plan.batches
    return (dp - dp % 2 + position % 2, position // 2)


def round_batch(plan, seq, number):
    return (seq + number) % plan.batches


def inward(plan, number):
    return pairs_of(plan, lambda dp, seq: home(plan, dp, round_batch(plan, seq, number), seq))


def outward(plan, number):
    return [(to, source) for source, to in inward(plan, number)]


def mate(plan, turn):
    def move(dp, seq):
        position = 2 * seq + dp % 2
        group, own = position // plan.group, position % plan.group
        to = group * plan.group + (own + turn) % plan.group
        return (dp - dp % 2 + to % 2, to // 2)

    return pairs_of(plan, move)


def permute(values, pairs):
    return lax.ppermute(values, AXES, pairs)


def dp_flip(plan, bits):
    return pairs_of(plan, lambda dp, seq: (dp ^ bits, seq))


def seq_flip(plan, bits):
    return pairs_of(plan, lambda dp, seq: (dp, seq ^ bits))


def share_inputs(plan, rounds):
    landed = [permute(rounds[number], inward(plan, number)) for number in reversed(range(plan.batches))]
    return landed[::-1]


def share_mates(plan, received):
    chunks = list(received)
    for turn in range(1, plan.group):
        chunks += [permute(piece, mate(plan, turn)) for piece in received]
    return chunks


def send_home(plan, pieces):
    return [permute(piece, outward(plan, number)) for number, piece in enumerate(pieces)]


def order_home(plan, landed, dtype):
    seq = lax.axis_index("seq")
    landed = jnp.stack(landed).astype(dtype)
    order = [(batch - seq) % plan.batches for batch in range(plan.batches)]
    return jnp.stack(
        [lax.dynamic_index_in_dim(landed, index, 0, keepdims=False) for index in order]
    )


def gather_direct(plan, shard):
    if plan.dp != 8:
        return [lax.all_gather(shard[0], "dp", axis=0)]
    return [shard] + [permute(shard, dp_flip(plan, bits)) for bits in (2, 4, 6)]


def gather_own(plan, shard):
    return permute(shard, dp_flip(plan, 1)) if plan.dp == 8 else None


def gather_rest(plan, direct, own_other):
    if plan.dp != 8:
        return direct
    pieces = [direct[0], own_other]
    for piece in direct[1:]:
        pieces += [piece, permute(piece, dp_flip(plan, 1))]
    return pieces


def add_low(values):
    total = values[0].astype(WIDE)
    for value in values[1:]:
        total = total + value.astype(WIDE)
    return total.astype(LOW)


def core_send(plan, send):
    return permute(send, dp_flip(plan, 1)) if plan.dp == 8 else send


def core_sum(plan, keep, other):
    if plan.dp != 8:
        return [jnp.concatenate([keep, other], axis=0)]
    return [add_low([keep[number], other[number]]) for number in range(4)]


def plane_send(plan, parts):
    if plan.dp != 8:
        return [lax.psum_scatter(parts[0], "dp", scatter_dimension=0)]
    return [permute(parts[number], dp_flip(plan, 2 * number)) for number in range(1, 4)]


def plane_sum(plan, parts, landed):
    total = landed[0] if plan.dp != 8 else add_low([parts[0], *landed])
    return total if plan.seq == 4 else lax.psum(total, "seq")


def halves(plan, total, bits):
    if plan.seq != 4:
        return total, jnp.zeros_like(total)
    half = total.shape[0] // 2
    own = lax.axis_index("seq") // bits % 2
    return (
        lax.dynamic_slice_in_dim(total, own * half, half),
        lax.dynamic_slice_in_dim(total, (1 - own) * half, half),
    )


def seq_send(plan, values, bits):
    return permute(values, seq_flip(plan, bits)) if plan.seq == 4 else jnp.zeros_like(values)


def join(plan, own_part, other, bits):
    if plan.seq != 4:
        return own_part
    own = lax.axis_index("seq") // bits % 2
    return jnp.where(
        own == 0, jnp.concatenate([own_part, other]), jnp.concatenate([other, own_part])
    )


def add_wide(first, second):
    return first.astype(WIDE) + second.astype(WIDE)


def tie(*values):
    return lax.optimization_barrier(values)


def after(values, *others):
    return lax.optimization_barrier((values, others))[0]


def plan_info(plan):
    dp, seq = lax.axis_index("dp"), lax.axis_index("seq")
    position = 2 * seq + dp % 2
    own = position % plan.group
    batch = position // plan.group // 2
    flips = list(range(8)) if plan.dp == 8 else None
    entries = []
    if flips:
        entries += [dp ^ bits for bits in (0, 1, 2, 3, 4, 5, 6, 7)]
        entries += [dp ^ bits for bits in (0, 2, 4, 6, 1, 3, 5, 7)]
    else:
        entries += list(range(plan.dp)) * 2
    places = [(batch - number) % plan.batches for number in range(plan.batches)]
    for turn in range(plan.group):
        source = (own - turn) % plan.group
        entries += [source * plan.batches + place for place in places]
    entries.append(own)
    entries += places
    entries += [(own + turn) % plan.group for turn in range(plan.group)]
    entries += [(seq + number) % plan.batches for number in range(plan.batches)]
    entries.append(dp)
    plan.places = [place.astype(jnp.uint32) for place in places]
    return jnp.stack([jnp.asarray(entry, jnp.int32) for entry in entries])


def on_device(
    tokens,
    memory,
    target_segments,
    source_segments,
    cotangent,
    query_weight,
    key_weight,
    value_weight,
    output_weight,
    cross_query,
    cross_key,
    cross_value,
    cross_output,
    inner_weight,
    outer_weight,
    self_gain,
    self_shift,
    cross_gain,
    cross_shift,
    feed_gain,
    feed_shift,
):
    plan = Plan(tokens, inner_weight)
    width, shard = plan.width, plan.shard
    info = plan_info(plan)
    dp = lax.axis_index("dp")

    vectors = jnp.stack([self_gain, self_shift, cross_gain, cross_shift, feed_gain, feed_shift])
    rounds = pack_tokens(plan, tokens, memory, target_segments, source_segments)
    shard_piece = pack_weights(
        plan,
        [
            query_weight,
            key_weight,
            value_weight,
            output_weight,
            cross_query,
            cross_key,
            cross_value,
            cross_output,
        ],
        vectors,
    )
    direct = gather_direct(plan, shard_piece)
    own_other = gather_own(plan, shard_piece)
    landed = share_inputs(plan, rounds)

    feed_shard, *rounds = pack_rest(plan, info, inner_weight, outer_weight, cotangent)
    feed_shard, rounds, landed[-1] = lax.optimization_barrier((feed_shard, rounds, landed[-1]))
    info, feed_shard = lax.optimization_barrier((info, feed_shard))
    feed_direct = gather_direct(plan, feed_shard)
    feed_other = gather_own(plan, feed_shard)
    upstreams = share_inputs(plan, rounds)
    direct, landed, info = lax.optimization_barrier((direct, landed, hold(info)))
    pieces = gather_rest(plan, direct, own_other)
    chunks = share_mates(plan, landed)
    q, o, lse, a, segs, vecs, cq, co, cross_lse, z = forward(
        plan, info, chunks, pieces
    )

    feed_direct, upstreams = after((feed_direct, upstreams), z)
    feed_pieces = gather_rest(plan, feed_direct, feed_other)
    *results, dsecond, dvec, feed_keep, feed_send = feed(
        plan, info, upstreams, feed_pieces, z, vecs
    )

    feed_parts = core_sum(plan, feed_keep, core_send(plan, feed_send))
    out_landed = send_home(plan, results)
    feed_landed = plane_send(plan, feed_parts)
    dsecond = after(dsecond, feed_parts)
    back = cross_backward(
        plan,
        info,
        chunks,
        pieces,
        [a, z, segs, vecs, dvec, dsecond, o, cq, co, cross_lse],
    )
    back, feed_landed, out_landed = lax.optimization_barrier((back, feed_landed, out_landed))
    own_memory, *others = back
    mate_memory, (da, terms, cross_keep, cross_send) = (
        others[: plan.group - 1],
        others[plan.group - 1 :],
    )

    feed_keep, feed_send = halves(plan, plane_sum(plan, feed_parts, feed_landed), 1)
    cross_parts = core_sum(plan, cross_keep, core_send(plan, cross_send))
    memory_pieces = add_mates(plan, own_memory, mate_memory)
    feed_landed = seq_send(plan, feed_send, 1)
    cross_landed = plane_send(plan, cross_parts)
    memory_landed = send_home(plan, memory_pieces)
    feed_landed, cross_parts[0], memory_pieces = tie(feed_landed, cross_parts[0], memory_pieces)
    feed_keep, feed_send = halves(plan, add_low([feed_keep, feed_landed]), 2)
    feed_landed = seq_send(plan, feed_send, 2)
    da, feed_keep = tie(da, feed_keep)
    back = self_backward(plan, info, chunks, pieces, [segs, da, terms, q, o, lse])
    back, feed_landed, cross_landed, memory_landed = lax.optimization_barrier(
        (back, feed_landed, cross_landed, memory_landed)
    )
    own_tokens, *mate_tokens, self_keep, self_send = back

    mate_landed = send_mates(plan, mate_tokens)
    self_landed = core_send(plan, self_send)
    feed_quarter = add_low([feed_keep, feed_landed])
    feed_landed = seq_send(plan, feed_quarter, 2)
    cross_keep, cross_send = halves(plan, plane_sum(plan, cross_parts, cross_landed), 1)
    cross_landed = seq_send(plan, cross_send, 1)
    token_pieces = sum_mates(plan, own_tokens, mate_landed)
    token_landed = send_home(plan, token_pieces)
    self_landed, cross_keep, feed_quarter = tie(self_landed, cross_keep, feed_quarter)
    self_parts = core_sum(plan, self_keep, self_landed)
    self_landed = plane_send(plan, self_parts)
    feed_landed, cross_landed = after((feed_landed, cross_landed), self_parts)
    feed_half = join(plan, feed_quarter, feed_landed, 2)
    feed_landed = seq_send(plan, feed_half, 1)
    cross_keep, cross_send = halves(plan, add_low([cross_keep, cross_landed]), 2)
    cross_landed = seq_send(plan, cross_send, 2)
    self_landed, feed_half, cross_keep, token_landed[0] = tie(
        self_landed, feed_half, cross_keep, token_landed[0]
    )
    self_total = plane_sum(plan, self_parts, self_landed)
    self_landed = seq_send(plan, self_total, 1)
    cross_landed, self_total = tie(cross_landed, self_total)
    cross_quarter = add_low([cross_keep, cross_landed])
    cross_landed = seq_send(plan, cross_quarter, 2)
    self_landed, cross_quarter = tie(self_landed, cross_quarter)
    self_total = add_low([self_total, self_landed])
    self_landed = seq_send(plan, self_total, 2)
    cross_landed, self_total, out_landed, memory_landed = tie(
        cross_landed, self_total, out_landed, memory_landed
    )
    cross_half = join(plan, cross_quarter, cross_landed, 2)
    cross_landed = seq_send(plan, cross_half, 1)
    out_tokens = order_home(plan, out_landed, LOW)
    grad_memory = order_home(plan, memory_landed, WIDE)
    grad_tokens = order_home(plan, token_landed, WIDE)
    self_landed, cross_landed, out_tokens, grad_memory, grad_tokens = tie(
        self_landed, cross_landed, out_tokens, grad_memory, grad_tokens
    )
    feed_total = join(plan, feed_half, feed_landed, 1).astype(WIDE)
    cross_total = join(plan, cross_half, cross_landed, 1).astype(WIDE)
    self_total = add_wide(self_total, self_landed)

    scale = 1.0 / (plan.batches * plan.dp)
    feed_grads, cross_grads, self_grads = (
        feed_total * scale,
        cross_total * scale,
        self_total * scale,
    )
    inner_grads = [
        feed_grads[block * shard : (block + 1) * shard] for block in range(plan.hidden_blocks)
    ]
    vector_grads = lax.dynamic_slice(self_grads, (3 * shard, dp * shard), (TILE, shard))
    return (
        out_tokens[:, None],
        grad_tokens[:, None],
        grad_memory[:, None],
        *[self_grads[which * shard : (which + 1) * shard] for which in range(3)],
        cross_grads[4 * shard : 5 * shard],
        *[cross_grads[which * shard : (which + 1) * shard] for which in range(4)],
        jnp.concatenate(inner_grads, axis=1),
        feed_grads[plan.hidden_blocks * shard :],
        *[vector_grads[which] for which in range(6)],
    )


def send_mates(plan, mates):
    return [permute(part, mate(plan, turn)) for turn, part in enumerate(mates, 1)]


def sum_mates(plan, own, landed):
    own = own.astype(WIDE)
    for part in landed:
        own = own + part.astype(WIDE)
    own = own.reshape(plan.batches, plan.chunk, plan.width)
    return [
        lax.dynamic_index_in_dim(own, place, 0, keepdims=False).astype(LOW)
        for place in plan.places
    ]


def add_mates(plan, own, mates):
    return sum_mates(plan, own, send_mates(plan, mates))


def solution(mesh):
    tokens = P(None, "dp", "seq", None)
    ids = P(None, "dp", "seq")
    weight = P("dp", None)
    vector = P("dp")
    return jax.shard_map(
        on_device,
        mesh=mesh,
        in_specs=(tokens, tokens, ids, ids, tokens) + (weight,) * 10 + (vector,) * 6,
        out_specs=(tokens,) * 3 + (weight,) * 10 + (vector,) * 6,
        check_vma=False,
    )
```
